32 devices in a mesh: dp: 4 (over y, core), expert: 8 (over z, x).
Axes of the slice: x: 2, y: 2, z: 4, core: 2. Of those that a mesh axis runs over, the one named last changes fastest.
Arguments:
- tokens: bfloat16 [8192, 1536], P(('dp', 'expert')), may hold values from -6 to 6
- seq_lengths: int32 [32, 4], P(('dp', 'expert')), may hold values from 1 to 128, 256 in all within a row
- routes: int32 [8192, 8], P(('dp', 'expert')), may hold values from 0 to 15, all different within a row; in each aligned block of 256 rows (0 to 255, 256 to 511, ...) at most 160 rows name the same one
- w_query: bfloat16 [1536, 1536], P('dp'), may hold values from -0.15625 to 0.15625
- w_key: bfloat16 [1536, 512], P('dp'), may hold values from -0.15625 to 0.15625
- w_value: bfloat16 [1536, 512], P('dp'), may hold values from -0.15625 to 0.15625
- w_output: bfloat16 [1536, 1536], P('dp'), may hold values from -0.625 to 0.625
- w_router: bfloat16 [1536, 16], P('dp'), may hold values from -0.078125 to 0.078125
- attn_gain: bfloat16 [1536], P('dp'), may hold values from 0.099609375 to 1.8984375
- moe_gain: bfloat16 [1536], P('dp'), may hold values from 0.099609375 to 1.8984375
- expert_gate: bfloat16 [16, 1536, 512], P('expert'), may hold values from -0.15625 to 0.15625
- expert_up: bfloat16 [16, 1536, 512], P('expert'), may hold values from -0.15625 to 0.15625
- expert_down: bfloat16 [16, 1536, 512], P('expert'), may hold values from -1 to 1
- out_grad: bfloat16 [8192, 1536], P(('dp', 'expert')), may hold values from -6 to 6
Outputs:
- layer_out: bfloat16 [8192, 1536], P(('dp', 'expert'))
- in_grad: float32 [8192, 1536], P(('dp', 'expert'))
- grad_query: float32 [1536, 1536], P('dp')
- grad_key: float32 [1536, 512], P('dp')
- grad_value: float32 [1536, 512], P('dp')
- grad_output: float32 [1536, 1536], P('dp')
- grad_router: float32 [1536, 16], P('dp')
- grad_attn_gain: float32 [1536], P('dp')
- grad_moe_gain: float32 [1536], P('dp')
- grad_gate: float32 [16, 1536, 512], P('expert', 'dp')
- grad_up: float32 [16, 1536, 512], P('expert', 'dp')
- grad_down: float32 [16, 1536, 512], P('expert', 'dp')
The draws below stay inside these ranges and needn't reach their ends.
Inputs may be any that keep to these rules, and one draw needn't show every extreme that they name: `seq_lengths`: row b gives the lengths of the sequences of block b; they sum to 256, and the longest is 128. `routes`: each row names 8 different experts. In the rows of one block no expert is named more than 160 times, and in some block some expert is named exactly 160 times.
All inputs are finite; a program needn't handle non-finite values.
Results may differ from the reference program's by a relative error of at most 0.022.
Values may be sent and summed in bfloat16 or wider, within the bound.
A program may use at most 256 MiB of HBM per device.

```python
import math
import jax
import jax.numpy as jnp
import numpy as np
from jax import lax

D = 1536
QH = 24
KVH = 8
HD = 64
FF = 512
TOP = 8
SEQS = 4
TOK_DEV = 256
EXPERTS = 16
BLOCKS = 32
TOKENS = 8192
CAP = 160


def levels(key, shape, pieces, smallest, largest):
    loudness = 1.0
    for dim, shards_of in pieces:
        steps = jax.random.uniform(jax.random.fold_in(jax.random.fold_in(key, 6), dim), (shards_of,), jnp.float32, smallest / len(pieces), largest / len(pieces))
        loudness = loudness * jnp.repeat(jnp.exp(steps), shape[dim] // shards_of).reshape((-1,) + (1,) * (len(shape) - 1 - dim))
    return loudness


def profile(number_of, total, bound, lean):
    portions = [(1 << 20) // math.isqrt(standing ** lean) + 1 for standing in range(2, number_of + 1)]
    rest, counts = total - bound - (number_of - 1), [1] * (number_of - 1)
    while rest > 0:
        candidates = [i for i in range(number_of - 1) if counts[i] < bound]
        whole, budget = sum([portions[i] for i in candidates]), rest
        for i in candidates:
            more = min(bound - counts[i], max(1, budget * portions[i] // whole), rest)
            counts[i] = counts[i] + more
            rest = rest - more
    return np.array([bound] + counts)


def uneven_parts(key, number_of, total, reach, lean):
    if number_of == 2:
        one = jax.random.randint(key, (), max(1, total - reach), min(reach, total - 1) + 1)
        return jnp.stack([one, total - one])
    lengths = jnp.asarray(profile(number_of, total, reach, lean), jnp.int32)
    couples = (number_of - 1) // 2
    donor, receiver = lengths[1:1 + 2 * couples:2], lengths[2:2 + 2 * couples:2]
    slack = jnp.minimum(donor - 1, reach - receiver)
    moved = jax.random.randint(jax.random.fold_in(key, 1), (couples,), 0, 1 << 20) % (slack + 1)
    lengths = lengths.at[1:1 + 2 * couples:2].set(donor - moved).at[2:2 + 2 * couples:2].set(receiver + moved)
    return lengths[jax.random.permutation(jax.random.fold_in(key, 2), number_of)]


def assign_block(own_key, own, number, rows, amount, top, reach, slope):
    ranking = jax.random.permutation(own_key, amount)
    packed, common = load_shares(amount, rows * top, reach, slope, True), load_shares(amount, rows * top, reach, slope, False)
    places = jnp.arange(amount)

    def named(tallies, offset_by):
        used = int((tallies > 0).sum())
        fixed = max(1, used // 4)
        moved = fixed + (places - fixed + offset_by * (used - fixed)) % max(1, amount - fixed)
        return jnp.zeros((amount,), jnp.int32).at[ranking[jnp.where(places < fixed, places, moved)]].set(jnp.asarray(tallies, jnp.int32))

    tallies = jnp.where(number % 4 == 0, named(packed, number // 4), named(common, number - number // 4 - 1))
    mixed = jax.random.permutation(jax.random.fold_in(own, 3), amount)
    source_of, sink = mixed[0:amount // 2 * 2:2], mixed[1:amount // 2 * 2:2]
    margin = jnp.minimum(tallies[source_of] - 1, reach - tallies[sink]) // 2
    margin = jnp.where((source_of == ranking[0]) | (sink == ranking[0]) | (tallies[sink] == 0), 0, jnp.maximum(margin, 0))
    moved = jax.random.randint(jax.random.fold_in(own, 4), (amount // 2,), 0, 1 << 20) % (margin + 1)
    tallies = tallies.at[source_of].add(-moved).at[sink].add(moved)
    items = jnp.searchsorted(jnp.cumsum(tallies), jnp.arange(rows * top), side="right").astype(jnp.int32)
    listing = items.reshape(top, rows).T
    listing = listing[jax.random.permutation(jax.random.fold_in(own, 1), rows)]
    offset_by = jax.random.randint(jax.random.fold_in(own, 2), (rows, 1), 0, top)
    return jnp.take_along_axis(listing, (jnp.arange(top)[None, :] + offset_by) % top, axis=1)


def load_shares(number_of, total, limit, skew, full):
    loads = [(1 << 20) // math.isqrt(standing ** skew) + 1 for standing in range(1, number_of + 1)]
    largest = limit if full else min(limit, max(-(-total // number_of), total * loads[0] // sum(loads)))
    least = 1 if total - largest >= number_of - 1 else 0
    counts, surplus = [largest] + [least] * (number_of - 1), total - largest - least * (number_of - 1)
    while surplus > 0:
        free = [i for i in range(1, number_of) if counts[i] < largest] or [i for i in range(1, number_of) if counts[i] < limit]
        pool, budget = sum([loads[i] for i in free]), surplus
        for i in free:
            extra = min(limit - counts[i], max(1, budget * loads[i] // pool), surplus)
            counts[i] = counts[i] + extra
            surplus = surplus - extra
    return np.array(counts)


def noise(own_key, extent, deviation, limit, pieces=(), kind=jnp.bfloat16):
    entries = deviation * jax.random.normal(own_key, extent, jnp.float32)
    if pieces:
        entries = entries * levels(own_key, extent, pieces, -0.22, 0.18)
    return jnp.clip(entries, -limit, limit).astype(kind)


def setup_inputs(seed: int = 0) -> dict:
    streams_of = jax.random.split(jax.random.key(seed), 15)
    tokens = noise(streams_of[0], (TOKENS, D), 1.0, 6.0, ((0, 32),))
    seq_lengths = jax.vmap(lambda own: uneven_parts(own, SEQS, TOK_DEV, TOK_DEV // 2, 2))(jax.random.split(streams_of[1], BLOCKS)).reshape((BLOCKS, SEQS)).astype(jnp.int32)
    routes_keys = jax.random.split(jax.random.fold_in(streams_of[2], 1), TOKENS // TOK_DEV)
    routes_turns = jax.random.permutation(jax.random.fold_in(streams_of[2], 3), TOKENS // TOK_DEV)
    routes = jax.vmap(lambda own, number: assign_block(jax.random.fold_in(streams_of[2], 2), own, number, TOK_DEV, EXPERTS, TOP, CAP, 1))(routes_keys, routes_turns).reshape((TOKENS, TOP))
    w_query = noise(streams_of[3], (D, QH * HD), D ** -0.5, 0.15625, ((0, 4),))
    w_key = noise(streams_of[4], (D, KVH * HD), D ** -0.5, 0.15625, ((0, 4),))
    w_value = noise(streams_of[5], (D, KVH * HD), D ** -0.5, 0.15625, ((0, 4),))
    w_output = noise(streams_of[6], (QH * HD, D), (QH * HD // 16) ** -0.5, 0.625, ((0, 4),))
    w_router = noise(streams_of[7], (D, EXPERTS), (4 * D) ** -0.5, 0.078125, ((0, 4),))
    attn_gain = jnp.clip(1.0 + 0.18 * jax.random.normal(streams_of[8], (D,), jnp.float32), 0.099609375, 1.8984375).astype(jnp.bfloat16)
    moe_gain = jnp.clip(1.0 + 0.18 * jax.random.normal(streams_of[9], (D,), jnp.float32), 0.099609375, 1.8984375).astype(jnp.bfloat16)
    expert_gate = noise(streams_of[10], (EXPERTS, D, FF), D ** -0.5, 0.15625, ((0, 8),))
    expert_up = noise(streams_of[11], (EXPERTS, D, FF), D ** -0.5, 0.15625, ((0, 8),))
    expert_down = noise(streams_of[12], (EXPERTS, D, FF), (FF // 16) ** -0.5, 1.0, ((0, 8),))
    out_grad = noise(streams_of[13], (TOKENS, D), 1.0, 6.0, ((0, 32),))
    return {"tokens": tokens, "seq_lengths": seq_lengths, "routes": routes, "w_query": w_query, "w_key": w_key, "w_value": w_value, "w_output": w_output, "w_router": w_router, "attn_gain": attn_gain, "moe_gain": moe_gain, "expert_gate": expert_gate, "expert_up": expert_up, "expert_down": expert_down, "out_grad": out_grad}


@jax.custom_vjp
def low(v):
    return lax.optimization_barrier(v.astype(jnp.bfloat16)).astype(jnp.float32)

@jax.custom_vjp
def low_back(v):
    return v

def low_keep(v):
    return (low(v), None)

def low_pass(kept, grad):
    return (grad,)

def back_keep(v):
    return (v, None)

def back_low(kept, grad):
    return (low(grad),)
low.defvjp(low_keep, low_pass)
low_back.defvjp(back_keep, back_low)
eps = 1e-06
rope_base = 10000.0
masked_score = -1e+30
highest = lax.Precision.HIGHEST

def precise_dot(left_arr, right_arr):
    return jnp.dot(left_arr, right_arr, precision=highest)

def rms_scale(values):
    return lax.rsqrt(lax.optimization_barrier(jnp.mean(values * values, axis=-1, keepdims=True)) + eps)

def token_layout(lengths_row, row_count):
    token_index = jnp.arange(row_count, dtype=jnp.int32)
    seq_ends = jnp.cumsum(lengths_row).astype(jnp.int32)
    passed = (token_index[:, None] >= seq_ends[None, :]).astype(jnp.int32)
    doc_id = lax.optimization_barrier(jnp.sum(passed, axis=1)).astype(jnp.int32)
    seq_start = lax.optimization_barrier(jnp.sum(passed * lengths_row[None, :], axis=1)).astype(jnp.int32)
    return (doc_id, (token_index - seq_start).astype(jnp.int32))

def rope_tables(position):
    half_size = HD // 2
    frequency = rope_base ** (-2.0 * jnp.arange(half_size, dtype=jnp.float32) / HD)
    angles = position.astype(jnp.float32)[:, None] * frequency[None, :]
    return (jnp.cos(angles)[:, None, :], jnp.sin(angles)[:, None, :])

def rotate(values, cos_table, sin_table, head_count):
    half_size = HD // 2
    shaped = values.reshape(values.shape[0], head_count, HD)
    front_half = shaped[..., :half_size]
    back_half = shaped[..., half_size:]
    turned = jnp.concatenate([front_half * cos_table - back_half * sin_table, back_half * cos_table + front_half * sin_table], axis=-1)
    return turned.reshape(values.shape[0], head_count * HD)

def expert_slots(route_rows):
    flat_routes = route_rows.reshape(-1)
    pair_count = flat_routes.shape[0]
    matches = (flat_routes[:, None] == jnp.arange(EXPERTS, dtype=jnp.int32)[None, :]).astype(jnp.int32)
    earlier = jnp.cumsum(matches, axis=0).astype(jnp.int32) - matches
    slot_rank = lax.optimization_barrier(jnp.sum(earlier * matches, axis=1)).astype(jnp.int32)
    slot_table = jnp.full((EXPERTS, CAP), pair_count, jnp.int32)
    slot_table = slot_table.at[flat_routes, slot_rank].set(jnp.arange(pair_count, dtype=jnp.int32))
    return (slot_table, slot_rank)

def device_layer(block_in, lengths_row, route_rows, params):
    w_query, w_key, w_value, w_output, w_router, attn_gain, moe_gain, expert_gate, expert_up, expert_down = params
    row_count = block_in.shape[0]
    doc_id, position = token_layout(lengths_row, row_count)
    cos_table, sin_table = rope_tables(position)
    normed_one = block_in * rms_scale(block_in)
    hidden_one = low(normed_one * attn_gain)
    query_rot = low(rotate(low_back(precise_dot(hidden_one, w_query)), cos_table, sin_table, QH))
    key_rot = low(rotate(low_back(precise_dot(hidden_one, w_key)), cos_table, sin_table, KVH))
    value_rows = low(low_back(precise_dot(hidden_one, w_value)))
    group_size = QH // KVH
    query_heads = query_rot.reshape(row_count, KVH, group_size, HD)
    key_heads = key_rot.reshape(row_count, KVH, HD)
    value_heads = value_rows.reshape(row_count, KVH, HD)
    scores = jnp.einsum('tkgd,ukd->kgtu', query_heads, key_heads, precision=highest) * HD ** (-0.5)
    scores = low_back(scores)
    token_index = jnp.arange(row_count, dtype=jnp.int32)
    allowed = (doc_id[:, None] == doc_id[None, :]) & (token_index[None, :] <= token_index[:, None])
    scores = jnp.where(allowed, scores, masked_score)
    shifted = scores - lax.optimization_barrier(jnp.max(scores, axis=-1, keepdims=True))
    exp_terms = jnp.exp(shifted)
    attn_probs = low(exp_terms / lax.optimization_barrier(jnp.sum(exp_terms, axis=-1, keepdims=True)))
    attended = jnp.einsum('kgtu,ukd->tkgd', attn_probs, value_heads, precision=highest).reshape(row_count, QH * HD)
    attended = low(low_back(attended))
    residual = block_in + low_back(precise_dot(attended, w_output))
    normed_two = residual * rms_scale(residual)
    hidden_two = low(normed_two * moe_gain)
    logits = low_back(precise_dot(hidden_two, w_router))
    chosen = jnp.take_along_axis(logits, route_rows, axis=1)
    gate_probs = jax.nn.softmax(chosen, axis=-1)
    slot_table, slot_rank = expert_slots(route_rows)
    padded = jnp.concatenate([hidden_two, jnp.zeros((1, hidden_two.shape[1]), hidden_two.dtype)], axis=0)
    expert_rows = low_back(padded[slot_table // TOP])
    gate_pre = low_back(jnp.einsum('ecd,edf->ecf', expert_rows, expert_gate, precision=highest))
    up_pre = low_back(jnp.einsum('ecd,edf->ecf', expert_rows, expert_up, precision=highest))
    activation = low(jax.nn.silu(gate_pre) * up_pre)
    expert_out = low(low_back(jnp.einsum('ecf,edf->ecd', activation, expert_down, precision=highest)))
    flat_routes = route_rows.reshape(-1)
    per_pair = expert_out[flat_routes, slot_rank].reshape(row_count, TOP, expert_out.shape[2])
    mixture = lax.optimization_barrier(jnp.sum(gate_probs[:, :, None] * per_pair, axis=1))
    return residual + mixture

def reference(tokens, seq_lengths, routes, w_query, w_key, w_value, w_output, w_router, attn_gain, moe_gain, expert_gate, expert_up, expert_down, out_grad):
    block_total = seq_lengths.shape[0]
    blocks_in = tokens.astype(jnp.float32).reshape(block_total, TOK_DEV, D)
    route_blocks = routes.reshape(block_total, TOK_DEV, TOP)
    params = tuple((weight_arr.astype(jnp.float32) for weight_arr in (w_query, w_key, w_value, w_output, w_router, attn_gain, moe_gain, expert_gate, expert_up, expert_down)))
    layer_step = jax.checkpoint(device_layer)

    def forward(blocks, weights):

        def step(carry, slices):
            return (carry, layer_step(slices[0], slices[1], slices[2], weights))
        carry_out, outputs = lax.scan(step, None, (blocks, seq_lengths, route_blocks))
        return outputs
    outputs, pullback = jax.vjp(forward, blocks_in, params)
    block_grad, weight_grads = pullback(out_grad.astype(jnp.float32).reshape(block_total, TOK_DEV, D))
    return (outputs.reshape(block_total * TOK_DEV, D).astype(jnp.bfloat16), block_grad.reshape(block_total * TOK_DEV, D), weight_grads[0], weight_grads[1], weight_grads[2], weight_grads[3], weight_grads[4], weight_grads[5], weight_grads[6], weight_grads[7], weight_grads[8], weight_grads[9])
```

```python
import jax
import jax.numpy as jnp
from jax import lax
from jax.sharding import PartitionSpec as P

QH = 24
KVH = 8
HD = 64
TOP = 8


eps = 1e-06
rope_base = 10000.0
masked_score = -1e30


def shortened(value):
    return jax.tree.map(lambda a: a.astype(jnp.bfloat16) if a.dtype == jnp.float32 else a, value)


def rms_scale(values):
    return lax.rsqrt(jnp.mean(values * values, axis=-1, keepdims=True) + eps)


def token_layout(lengths_row, row_count):
    token_index = jnp.arange(row_count, dtype=jnp.int32)
    seq_ends = jnp.cumsum(lengths_row)
    passed = (token_index[:, None] >= seq_ends[None, :]).astype(jnp.int32)
    doc_id = jnp.sum(passed, axis=1)
    seq_start = jnp.sum(passed * lengths_row[None, :], axis=1)
    return (doc_id, token_index - seq_start)


def rope_tables(position):
    half_size = HD // 2
    frequency = rope_base ** (-2.0 * jnp.arange(half_size, dtype=jnp.float32) / HD)
    angles = position.astype(jnp.float32)[:, None] * frequency[None, :]
    return (jnp.cos(angles)[:, None, :], jnp.sin(angles)[:, None, :])


def rotate(values, cos_table, sin_table, head_count):
    half_size = HD // 2
    shaped = values.reshape(values.shape[0], head_count, HD)
    front_half = shaped[..., :half_size]
    back_half = shaped[..., half_size:]
    turned = jnp.concatenate(
        [
            front_half * cos_table - back_half * sin_table,
            back_half * cos_table + front_half * sin_table,
        ],
        axis=-1,
    )
    return turned.reshape(values.shape[0], head_count * HD)


def unrotate(values, cos_table, sin_table, head_count):
    half_size = HD // 2
    shaped = values.reshape(values.shape[0], head_count, HD)
    front_half = shaped[..., :half_size]
    back_half = shaped[..., half_size:]
    turned = jnp.concatenate(
        [
            front_half * cos_table + back_half * sin_table,
            back_half * cos_table - front_half * sin_table,
        ],
        axis=-1,
    )
    return turned.reshape(values.shape[0], head_count * HD)


def own_columns(values, local_count):
    start = lax.axis_index("expert") * local_count
    return lax.dynamic_slice_in_dim(values, start, local_count, axis=1)


def body(
    tokens,
    seq_lengths,
    routes,
    w_query,
    w_key,
    w_value,
    w_output,
    w_router,
    attn_gain,
    moe_gain,
    expert_gate,
    expert_up,
    expert_down,
    out_grad,
):
    shards = (w_query, w_key, w_value, w_output, w_router, attn_gain, moe_gain)
    gathered = (
        lax.all_gather(shards[0], "dp", axis=0, tiled=True),
        lax.all_gather(shards[1], "dp", axis=0, tiled=True),
        lax.all_gather(shards[2], "dp", axis=0, tiled=True),
        lax.all_gather(shards[3], "dp", axis=0, tiled=True),
        lax.all_gather(shards[4], "dp", axis=0, tiled=True),
        lax.all_gather(shards[5], "dp", axis=0, tiled=True),
        lax.all_gather(shards[6], "dp", axis=0, tiled=True),
    )
    query_w, key_w, value_w, output_w, router_w, gain_one, gain_two = gathered
    row_count = tokens.shape[0]
    expert_count = w_router.shape[1]
    group_size = QH // KVH
    block_rows = min(512, row_count)
    block_total = row_count // block_rows
    score_scale = HD ** (-0.5)
    doc_id, position = token_layout(seq_lengths[0], row_count)
    cos_table, sin_table = rope_tables(position)
    token_index = jnp.arange(row_count, dtype=jnp.int32)
    block_starts = jnp.arange(block_total, dtype=jnp.int32) * block_rows
    inputs = tokens.astype(jnp.float32)
    scale_one = rms_scale(inputs)
    normed_one = inputs * scale_one
    hidden_one = (normed_one * gain_one.astype(jnp.float32)).astype(jnp.bfloat16)
    query_rot = rotate(
        jnp.dot(hidden_one, query_w, preferred_element_type=jnp.float32), cos_table, sin_table, QH
    ).astype(jnp.bfloat16)
    key_rot = rotate(
        jnp.dot(hidden_one, key_w, preferred_element_type=jnp.float32), cos_table, sin_table, KVH
    ).astype(jnp.bfloat16)
    value_rows = jnp.dot(hidden_one, value_w, preferred_element_type=jnp.float32).astype(
        jnp.bfloat16
    )
    key_heads = key_rot.reshape(row_count, KVH, HD)
    value_heads = value_rows.reshape(row_count, KVH, HD)

    def block_scores(block_start):
        query_block = query_rot.reshape(block_rows, KVH, group_size, HD)
        raw_scores = (
            jnp.einsum("tkgd,ukd->kgtu", query_block, key_heads, preferred_element_type=jnp.float32)
            * score_scale
        )
        block_index = block_start + jnp.arange(block_rows, dtype=jnp.int32)
        allowed = (doc_id[:, None] == doc_id[None, :]) & (
            token_index[None, :] <= block_index[:, None]
        )
        return (query_block, jnp.where(allowed, raw_scores, masked_score))

    def attend_block(block_start):
        query_block, scores = block_scores(block_start)
        row_top = jnp.max(scores, axis=-1, keepdims=True)
        exp_terms = jnp.exp(scores - row_top)
        row_total = jnp.sum(exp_terms, axis=-1, keepdims=True)
        probs_low = (exp_terms / row_total).astype(jnp.bfloat16)
        attended_block = jnp.einsum(
            "kgtu,ukd->tkgd", probs_low, value_heads, preferred_element_type=jnp.float32
        )
        log_total = (row_top + jnp.log(row_total))[..., 0]
        return (attended_block.reshape(block_rows, QH * HD).astype(jnp.bfloat16), log_total)

    attended_blocks, log_blocks = lax.map(attend_block, block_starts)
    attended = attended_blocks.reshape(row_count, QH * HD)
    residual = inputs + jnp.dot(attended, output_w, preferred_element_type=jnp.float32)
    scale_two = rms_scale(residual)
    normed_two = residual * scale_two
    hidden_two = (normed_two * gain_two.astype(jnp.float32)).astype(jnp.bfloat16)
    logits = jnp.dot(hidden_two, router_w, preferred_element_type=jnp.float32)
    expert_ids = jnp.arange(expert_count, dtype=jnp.int32)
    route_hot = (routes[:, :, None] == expert_ids[None, None, :]).astype(jnp.float32)
    chosen = jnp.sum(route_hot * logits[:, None, :], axis=-1)
    gate_probs = jax.nn.softmax(chosen, axis=-1)
    dense_probs = jnp.sum(route_hot * gate_probs[:, :, None], axis=1)
    upstream = out_grad.astype(jnp.float32)
    local_count = expert_gate.shape[0]
    all_hidden = lax.all_gather(hidden_two, "expert", axis=0, tiled=True)
    all_probs = own_columns(lax.all_gather(dense_probs, "expert", axis=0, tiled=True), local_count)
    all_upstream = lax.all_gather(out_grad, "expert", axis=0, tiled=True)
    mix_part = jnp.zeros(all_hidden.shape, jnp.float32)
    row_part = jnp.zeros(all_hidden.shape, jnp.float32)
    grad_columns, down_parts, gate_parts, up_parts = [], [], [], []
    for e in range(local_count):
        prob = all_probs[:, e : e + 1]
        gate_pre = jnp.dot(all_hidden, expert_gate[e], preferred_element_type=jnp.float32)
        up_pre = jnp.dot(all_hidden, expert_up[e], preferred_element_type=jnp.float32)
        raw_grad = jnp.dot(all_upstream, expert_down[e], preferred_element_type=jnp.float32)
        gate_sig = jax.nn.sigmoid(gate_pre)
        gate_act = gate_pre * gate_sig
        activation = gate_act * up_pre
        grad_columns.append(jnp.sum(activation * raw_grad, axis=-1, keepdims=True))
        weighted = (activation * prob).astype(jnp.bfloat16)
        act_grad = raw_grad * prob
        gate_pre_grad = (act_grad * up_pre * gate_sig * (1.0 + gate_pre * (1.0 - gate_sig))).astype(
            jnp.bfloat16
        )
        up_pre_grad = (act_grad * gate_act).astype(jnp.bfloat16)
        mix_part = mix_part + jnp.dot(
            weighted, expert_down[e].T, preferred_element_type=jnp.float32
        )
        row_part = row_part + jnp.dot(
            gate_pre_grad, expert_gate[e].T, preferred_element_type=jnp.float32
        )
        row_part = row_part + jnp.dot(
            up_pre_grad, expert_up[e].T, preferred_element_type=jnp.float32
        )
        down_parts.append(jnp.dot(all_upstream.T, weighted, preferred_element_type=jnp.float32))
        gate_parts.append(jnp.dot(all_hidden.T, gate_pre_grad, preferred_element_type=jnp.float32))
        up_parts.append(jnp.dot(all_hidden.T, up_pre_grad, preferred_element_type=jnp.float32))
    down_partial = jnp.stack(down_parts)
    gate_partial = jnp.stack(gate_parts)
    up_partial = jnp.stack(up_parts)
    grad_dense = lax.all_to_all(
        jnp.concatenate(grad_columns, axis=1), "expert", split_axis=0, concat_axis=1, tiled=True
    )
    gate_grad = jnp.sum(route_hot * grad_dense[:, None, :], axis=-1)
    mixture = lax.psum_scatter(
        mix_part.astype(jnp.bfloat16), "expert", scatter_dimension=0, tiled=True
    ).astype(jnp.float32)
    layer_out = (residual + mixture).astype(jnp.bfloat16)
    hidden_two_grad = lax.psum_scatter(
        row_part.astype(jnp.bfloat16), "expert", scatter_dimension=0, tiled=True
    ).astype(jnp.float32)
    chosen_grad = gate_probs * (gate_grad - jnp.sum(gate_probs * gate_grad, axis=-1, keepdims=True))
    logit_grad = jnp.sum(route_hot * chosen_grad[:, :, None], axis=1).astype(jnp.bfloat16)
    hidden_two_grad = hidden_two_grad + jnp.dot(
        logit_grad, router_w.T, preferred_element_type=jnp.float32
    )
    gain_two_partial = jnp.sum(hidden_two_grad * normed_two, axis=0)
    normed_two_grad = hidden_two_grad * gain_two.astype(jnp.float32)
    residual_grad = upstream + scale_two * (
        normed_two_grad
        - normed_two * jnp.mean(normed_two_grad * normed_two, axis=-1, keepdims=True)
    )
    branch_grad = residual_grad.astype(jnp.bfloat16)
    attended_grad = jnp.dot(branch_grad, output_w.T, preferred_element_type=jnp.float32).astype(
        jnp.bfloat16
    )

    def attend_back(carry, block_data):
        key_acc, value_acc = carry
        block_start, log_total = block_data
        query_block, scores = block_scores(block_start)
        attn_probs = jnp.exp(scores - log_total[..., None])
        probs_low = attn_probs.astype(jnp.bfloat16)
        grad_block = attended_grad.reshape(block_rows, KVH, group_size, HD)
        prob_grad = jnp.einsum(
            "tkgd,ukd->kgtu", grad_block, value_heads, preferred_element_type=jnp.float32
        )
        score_grad = (
            attn_probs * (prob_grad - jnp.sum(attn_probs * prob_grad, axis=-1, keepdims=True))
        ).astype(jnp.bfloat16)
        query_part = (
            jnp.einsum("kgtu,ukd->tkgd", score_grad, key_heads, preferred_element_type=jnp.float32)
            * score_scale
        )
        key_acc = (
            key_acc
            + jnp.einsum(
                "kgtu,tkgd->ukd", score_grad, query_block, preferred_element_type=jnp.float32
            )
            * score_scale
        )
        value_acc = value_acc + jnp.einsum(
            "kgtu,tkgd->ukd", probs_low, grad_block, preferred_element_type=jnp.float32
        )
        return ((key_acc, value_acc), query_part.reshape(block_rows, QH * HD))

    zero_heads = jnp.zeros((row_count, KVH, HD), jnp.float32)
    (key_sums, value_sums), query_blocks = lax.scan(
        attend_back, (zero_heads, zero_heads), (block_starts, log_blocks)
    )
    query_grad = unrotate(
        query_blocks.reshape(row_count, QH * HD), cos_table, sin_table, QH
    ).astype(jnp.bfloat16)
    key_grad = unrotate(key_sums.reshape(row_count, KVH * HD), cos_table, sin_table, KVH).astype(
        jnp.bfloat16
    )
    value_grad = value_sums.reshape(row_count, KVH * HD).astype(jnp.bfloat16)
    hidden_one_grad = jnp.dot(query_grad, query_w.T, preferred_element_type=jnp.float32)
    hidden_one_grad = hidden_one_grad + jnp.dot(
        key_grad, key_w.T, preferred_element_type=jnp.float32
    )
    hidden_one_grad = hidden_one_grad + jnp.dot(
        value_grad, value_w.T, preferred_element_type=jnp.float32
    )
    gain_one_partial = jnp.sum(hidden_one_grad * normed_one, axis=0)
    normed_one_grad = hidden_one_grad * gain_one.astype(jnp.float32)
    in_grad = residual_grad + scale_one * (
        normed_one_grad
        - normed_one * jnp.mean(normed_one_grad * normed_one, axis=-1, keepdims=True)
    )
    query_partial = jnp.dot(hidden_one.T, query_grad, preferred_element_type=jnp.float32)
    key_partial = jnp.dot(hidden_one.T, key_grad, preferred_element_type=jnp.float32)
    value_partial = jnp.dot(hidden_one.T, value_grad, preferred_element_type=jnp.float32)
    output_partial = jnp.dot(attended.T, branch_grad, preferred_element_type=jnp.float32)
    router_partial = jnp.dot(hidden_two.T, logit_grad, preferred_element_type=jnp.float32)
    pieces = jax.tree.map(
        lambda part: part.astype(jnp.float32),
        lax.psum_scatter(
            shortened(
                (
                    query_partial,
                    key_partial,
                    value_partial,
                    output_partial,
                    router_partial,
                    gain_one_partial,
                    gain_two_partial,
                )
            ),
            "dp",
            scatter_dimension=0,
            tiled=True,
        ),
    )
    totals = (
        lax.psum(pieces[0].astype(jnp.bfloat16), "expert").astype(jnp.float32),
        lax.psum(pieces[1].astype(jnp.bfloat16), "expert").astype(jnp.float32),
        lax.psum(pieces[2].astype(jnp.bfloat16), "expert").astype(jnp.float32),
        lax.psum(pieces[3].astype(jnp.bfloat16), "expert").astype(jnp.float32),
        lax.psum(pieces[4].astype(jnp.bfloat16), "expert").astype(jnp.float32),
        lax.psum(pieces[5].astype(jnp.bfloat16), "expert").astype(jnp.float32),
        lax.psum(pieces[6].astype(jnp.bfloat16), "expert").astype(jnp.float32),
    )
    expert_totals = (
        lax.psum_scatter(
            gate_partial.astype(jnp.bfloat16), "dp", scatter_dimension=1, tiled=True
        ).astype(jnp.float32),
        lax.psum_scatter(
            up_partial.astype(jnp.bfloat16), "dp", scatter_dimension=1, tiled=True
        ).astype(jnp.float32),
        lax.psum_scatter(
            down_partial.astype(jnp.bfloat16), "dp", scatter_dimension=1, tiled=True
        ).astype(jnp.float32),
    )
    return (
        layer_out,
        in_grad,
        totals[0],
        totals[1],
        totals[2],
        totals[3],
        totals[4],
        totals[5],
        totals[6],
        expert_totals[0],
        expert_totals[1],
        expert_totals[2],
    )


def solution(mesh):
    placed = (
        P(("dp", "expert"), None),
        P(("dp", "expert"), None),
        P(("dp", "expert"), None),
        P("dp", None),
        P("dp", None),
        P("dp", None),
        P("dp", None),
        P("dp", None),
        P("dp"),
        P("dp"),
        P("expert", None, None),
        P("expert", None, None),
        P("expert", None, None),
        P(("dp", "expert"), None),
    )
    return jax.shard_map(
        body,
        mesh=mesh,
        in_specs=placed,
        out_specs=(
            P(("dp", "expert"), None),
            P(("dp", "expert"), None),
            P("dp", None),
            P("dp", None),
            P("dp", None),
            P("dp", None),
            P("dp", None),
            P("dp"),
            P("dp"),
            P("expert", "dp", None),
            P("expert", "dp", None),
            P("expert", "dp", None),
        ),
        check_vma=False,
    )
```

```python
import functools

import jax
import jax.numpy as jnp
from jax import lax
from jax.experimental import pallas as pl
from jax.experimental.pallas import tpu as pltpu
from jax.sharding import PartitionSpec as P

MESH = pl.DeviceIdType.MESH
QH = 24
KVH = 8
HD = 64
TOP = 8


eps = 1e-06
rope_base = 10000.0
masked_score = -1e30


def shortened(value):
    return jax.tree.map(lambda a: a.astype(jnp.bfloat16) if a.dtype == jnp.float32 else a, value)


def rms_scale(values):
    return lax.rsqrt(jnp.mean(values * values, axis=-1, keepdims=True) + eps)


def token_layout(lengths_row, row_count):
    token_index = jnp.arange(row_count, dtype=jnp.int32)
    seq_ends = jnp.cumsum(lengths_row)
    passed = (token_index[:, None] >= seq_ends[None, :]).astype(jnp.int32)
    doc_id = jnp.sum(passed, axis=1)
    seq_start = jnp.sum(passed * lengths_row[None, :], axis=1)
    return (doc_id, token_index - seq_start)


def rope_tables(position):
    half_size = HD // 2
    frequency = rope_base ** (-2.0 * jnp.arange(half_size, dtype=jnp.float32) / HD)
    angles = position.astype(jnp.float32)[:, None] * frequency[None, :]
    return (jnp.cos(angles)[:, None, :], jnp.sin(angles)[:, None, :])


def rotate(values, cos_table, sin_table, head_count):
    half_size = HD // 2
    shaped = values.reshape(values.shape[0], head_count, HD)
    front_half = shaped[..., :half_size]
    back_half = shaped[..., half_size:]
    turned = jnp.concatenate(
        [
            front_half * cos_table - back_half * sin_table,
            back_half * cos_table + front_half * sin_table,
        ],
        axis=-1,
    )
    return turned.reshape(values.shape[0], head_count * HD)


def unrotate(values, cos_table, sin_table, head_count):
    half_size = HD // 2
    shaped = values.reshape(values.shape[0], head_count, HD)
    front_half = shaped[..., :half_size]
    back_half = shaped[..., half_size:]
    turned = jnp.concatenate(
        [
            front_half * cos_table + back_half * sin_table,
            back_half * cos_table - front_half * sin_table,
        ],
        axis=-1,
    )
    return turned.reshape(values.shape[0], head_count * HD)


def own_columns(values, local_count):
    start = lax.axis_index("expert") * local_count
    return lax.dynamic_slice_in_dim(values, start, local_count, axis=1)


NT = (((1,), (1,)), ((), ()))
TN = (((0,), (0,)), ((), ()))


def dot_f32(left, right, dims=(((1,), (0,)), ((), ()))):
    return lax.dot_general(left, right, dims, preferred_element_type=jnp.float32)


def packed(rows, index, step, base=8):
    value = 0
    for place, row in enumerate(rows):
        number = sum(digit * base**power for power, digit in enumerate(row))
        value = value + jnp.where(index == place, number, 0)
    scale = 1
    for power in range(1, len(rows[0])):
        scale = jnp.where(step == power, base**power, scale)
    return (value // scale) % base


BLOCK_ORDER = (
    (0, 4, 1, 5, 2, 6, 3, 7),
    (1, 5, 0, 2, 4, 3, 6, 7),
    (2, 6, 3, 1, 7, 0, 5, 4),
    (3, 7, 2, 6, 1, 5, 0, 4),
)
TAKE_FIRST = (
    (7, 1, 7, 2, 7, 3, 7, 7),
    (7, 0, 7, 7, 3, 7, 7, 7),
    (7, 3, 7, 7, 0, 7, 7, 7),
    (7, 2, 7, 1, 7, 0, 7, 7),
)
TAKE_SECOND = (
    (7, 7, 7, 7, 7, 7, 7, 7),
    (7, 2, 7, 7, 7, 7, 7, 7),
    (7, 1, 7, 7, 7, 7, 7, 7),
    (7, 7, 7, 7, 7, 7, 7, 7),
)
SUM_ORDER = ((3, 2, 1, 0), (3, 2, 0, 1), (0, 1, 3, 2), (0, 1, 2, 3))


def moe_kernel(
    h_in, u_in, p_in, wg_in, wu_in, wd_in,
    d_out, e_out, gg_out, grads_out, core_got, y_got,
    h_all, u_all, p_all, wg, wu, wd, act, gu, ex, ez, rx, rz, d_stage, gg_stage, tile_bf, tile_f32, got_tile, got_y,
    load_sem, h_up, h_down, h_across, h_recv, p_send, p_recv, g_send, g_recv,
    x_send, x_recv, z_send, z_recv, d_sem, c_send, c_recv, y_send, y_recv, tile_sem, out_sem,
    *, comm
):
    A, B, n = 4, 2, 8
    R, D = h_in.shape
    F = wg.shape[2]
    shard = D // 4
    me = lax.axis_index("expert")
    dp = lax.axis_index("dp")
    a, b = me // B, me % B
    y, c = dp // 2, dp % 2
    partner_x = a * B + (1 - b)
    core_peer = 2 * y + (1 - c)
    y_peer = 2 * (1 - y) + c

    def copy(src, dst, send, recv, **target):
        return pltpu.make_async_remote_copy(
            src_ref=src, dst_ref=dst, send_sem=send, recv_sem=recv, device_id=target, device_id_type=MESH
        )

    loads = [
        pltpu.make_async_copy(h_in, h_all.at[me], load_sem.at[0]),
        pltpu.make_async_copy(u_in, u_all, load_sem.at[1]),
        pltpu.make_async_copy(wg_in, wg, load_sem.at[2]),
        pltpu.make_async_copy(wu_in, wu, load_sem.at[3]),
        pltpu.make_async_copy(wd_in, wd, load_sem.at[4]),
        pltpu.make_async_copy(p_in.at[me], p_all.at[me], load_sem.at[5]),
    ]
    for load in loads:
        load.start()

    barrier = pltpu.get_barrier_semaphore()
    for k in range(1, n):
        pl.semaphore_signal(barrier, inc=1, device_id={"expert": (me + k) % n}, device_id_type=MESH)
    pl.semaphore_signal(barrier, inc=1, device_id={"dp": core_peer}, device_id_type=MESH)
    pl.semaphore_signal(barrier, inc=1, device_id={"dp": y_peer}, device_id_type=MESH)
    pl.semaphore_wait(barrier, n + 1)
    loads[0].wait()
    loads[5].wait()

    def send_up(s):
        return copy(h_all.at[s], h_all.at[s], h_up.at[s], h_recv.at[s], expert=me + B)

    def send_down(s):
        return copy(h_all.at[s], h_all.at[s], h_down.at[s], h_recv.at[s], expert=me - B)

    def send_across(s):
        return copy(h_all.at[s], h_all.at[s], h_across.at[s], h_recv.at[s], expert=partner_x)

    def p_copy(peer):
        return copy(p_in.at[peer], p_all.at[me], p_send.at[peer], p_recv.at[me], expert=peer)

    @pl.when(a < A - 1)
    def _():
        send_up(me).start()

    @pl.when(a > 0)
    def _():
        send_down(me).start()

    send_across(me).start()
    for k in range(1, n):
        p_copy((me + k) % n).start()
    for k in range(1, n):
        s = (me + k) % n
        copy(p_in.at[s], p_all.at[s], p_send.at[s], p_recv.at[s], expert=s).wait_recv()
    for load in loads[1:5]:
        load.wait()

    def recv_block(s):
        send_across(s).wait_recv()

    def take(row):
        @pl.when(row < A)
        def _():
            s = row * B + b
            recv_block(s)
            send_across(s).start()

            @pl.when((row < a) & (a < A - 1))
            def _():
                send_up(s).start()

            @pl.when((row > a) & (a > 0))
            def _():
                send_down(s).start()

    def d_copy(s, slot):
        return pltpu.make_async_copy(d_stage.at[slot], d_out.at[s], d_sem.at[slot])

    def g_copy(s):
        return copy(gg_stage.at[s], gg_out.at[me], g_send.at[s], g_recv.at[me], expert=s)

    def compute(step, s, row, across):
        rows = pl.ds(pl.multiple_of(s * R, R), R)
        probs = jnp.transpose(p_all[s])
        grad_cols = []
        for e in range(2):
            gate_pre = dot_f32(h_all[s], wg[e])
            up_pre = dot_f32(h_all[s], wu[e])
            raw = dot_f32(u_all[s], wd[e])
            prob = probs[:, e : e + 1]
            sig = 1.0 / (1.0 + jnp.exp(-gate_pre))
            gate_act = gate_pre * sig
            activation = gate_act * up_pre
            grad_cols.append(jnp.sum(activation * raw, axis=1, keepdims=True))
            act[rows, e * F : (e + 1) * F] = (activation * prob).astype(jnp.bfloat16)
            act_grad = raw * prob
            gate_grad = act_grad * up_pre * sig * (1.0 + gate_pre * (1.0 - sig))
            gu[rows, 2 * e * F : (2 * e + 1) * F] = gate_grad.astype(jnp.bfloat16)
            gu[rows, (2 * e + 1) * F : (2 * e + 2) * F] = (act_grad * gate_act).astype(jnp.bfloat16)
        column = lax.broadcasted_iota(jnp.int32, (R, 128), 1)
        both = jnp.where(column == 0, grad_cols[0], jnp.where(column == 1, grad_cols[1], 0.0))
        gg_stage[s] = jnp.transpose(both)[:8]
        slot = step % 2

        @pl.when(step >= 2)
        def _():
            d_copy(s, slot).wait()

        def columns(tile, _):
            cols = pl.ds(pl.multiple_of(tile * 512, 512), 512)
            mixed = dot_f32(act[rows, 0:F], wd[0, cols, :], NT) + dot_f32(act[rows, F : 2 * F], wd[1, cols, :], NT)
            d_stage[slot, :, cols] = mixed.astype(jnp.bfloat16)
            back = dot_f32(gu[rows, 0:F], wg[0, cols, :], NT)
            back += dot_f32(gu[rows, F : 2 * F], wu[0, cols, :], NT)
            back += dot_f32(gu[rows, 2 * F : 3 * F], wg[1, cols, :], NT)
            back += dot_f32(gu[rows, 3 * F : 4 * F], wu[1, cols, :], NT)

            @pl.when(across)
            def _():
                ex[row, :, cols] = back.astype(jnp.bfloat16)

            @pl.when(jnp.logical_not(across))
            def _():
                ez[row, :, cols] = back.astype(jnp.bfloat16)

            return 0

        lax.fori_loop(0, D // 512, columns, 0)
        d_copy(s, slot).start()

        @pl.when(s != me)
        def _():
            g_copy(s).start()

        @pl.when(s == me)
        def _():
            pltpu.make_async_copy(gg_stage.at[s], gg_out.at[me], g_send.at[s]).start()

    def block_step(step, _):
        take(packed(TAKE_FIRST, a, step))
        take(packed(TAKE_SECOND, a, step))
        code = packed(BLOCK_ORDER, a, step)
        across = code >= A
        row = code % A
        s = row * B + jnp.where(across, 1 - b, b)

        @pl.when(across)
        def _():
            recv_block(s)

        compute(step, s, row, across)
        return 0

    lax.fori_loop(0, n, block_step, 0)

    def x_copy(row):
        return copy(ex.at[row], rx.at[row], x_send.at[row], x_recv.at[row], expert=partner_x)

    def z_up(row):
        return copy(ez.at[row], rz.at[row + 1], z_send.at[row], z_recv.at[row + 1], expert=me + B)

    def z_down(row):
        return copy(ez.at[row], rz.at[row], z_send.at[row], z_recv.at[row], expert=me - B)

    for place in range(A):
        x_copy(packed(SUM_ORDER, a, place)).start()

    def core_copy(slot, which, index):
        return copy(tile_bf.at[slot], core_got.at[which, index], c_send.at[slot], c_recv.at[which, index], dp=core_peer)

    def y_copy(slot, index):
        return copy(tile_bf.at[slot], y_got.at[index], y_send.at[slot], y_recv.at[index], dp=y_peer)

    def weight_tile(group, e, kind, left, right):
        owner = jnp.where(group == 0, core_peer, jnp.where(group == 1, 2 * (1 - y) + 1 - c, jnp.where(group == 2, y_peer, dp)))
        cols = pl.ds(pl.multiple_of(owner * shard, 128), shard)
        total = dot_f32(left[:, :, cols].reshape(n * R, shard), right, TN)
        index = kind * 2 + e
        slot = kind

        @pl.when(group < 2)
        def _():
            @pl.when((group > 0) | (e > 0))
            def _():
                core_copy(slot, 0, index).wait_send()

            tile_bf[slot] = total.astype(jnp.bfloat16)
            core_copy(slot, group, index).start()

        @pl.when(group == 2)
        def _():
            @pl.when(e == 0)
            def _():
                core_copy(slot, 0, index).wait_send()

            @pl.when(e > 0)
            def _():
                y_copy(slot, index).wait_send()

            core_copy(slot, 1, index).wait_recv()
            got = pltpu.make_async_copy(core_got.at[1, index], got_tile, tile_sem)
            got.start()
            got.wait()
            tile_bf[slot] = (total + got_tile[...].astype(jnp.float32)).astype(jnp.bfloat16)
            y_copy(slot, index).start()

        @pl.when(group == 3)
        def _():
            core_copy(slot, 0, index).wait_recv()
            got = pltpu.make_async_copy(core_got.at[0, index], got_tile, tile_sem)
            got.start()
            got.wait()
            tile_f32[index] = total + got_tile[...].astype(jnp.float32)

    def sum_step(place, _):
        def pair(e, _):
            weight_tile(place, e, 0, h_all, gu[:, pl.ds(pl.multiple_of(2 * e * F, 128), F)])
            weight_tile(place, e, 1, h_all, gu[:, pl.ds(pl.multiple_of((2 * e + 1) * F, 128), F)])
            weight_tile(place, e, 2, u_all, act[:, pl.ds(pl.multiple_of(e * F, 128), F)])
            return 0

        lax.fori_loop(0, 2, pair, 0)
        row = packed(SUM_ORDER, a, place)
        x_copy(row).wait_recv()
        below = (a > 0) & (row >= a)
        above = (a < A - 1) & (row <= a)

        @pl.when(below)
        def _():
            z_up(row).wait_recv()

        @pl.when(above)
        def _():
            z_down(row).wait_recv()

        def chunk(index, _):
            part = pl.ds(pl.multiple_of(index * 64, 64), 64)
            total = ez[row, part, :].astype(jnp.float32) + rx[row, part, :].astype(jnp.float32)

            @pl.when(row != a)
            def _():
                @pl.when(below)
                def _():
                    ez[row, part, :] = (total + rz[row + 1, part, :].astype(jnp.float32)).astype(jnp.bfloat16)

                @pl.when(above)
                def _():
                    ez[row, part, :] = (total + rz[row, part, :].astype(jnp.float32)).astype(jnp.bfloat16)

                @pl.when(jnp.logical_not(below | above))
                def _():
                    ez[row, part, :] = total.astype(jnp.bfloat16)

            @pl.when(row == a)
            def _():
                @pl.when(below & above)
                def _():
                    e_out[part, :] = total + rz[row + 1, part, :].astype(jnp.float32) + rz[row, part, :].astype(jnp.float32)

                @pl.when(below & jnp.logical_not(above))
                def _():
                    e_out[part, :] = total + rz[row + 1, part, :].astype(jnp.float32)

                @pl.when(above & jnp.logical_not(below))
                def _():
                    e_out[part, :] = total + rz[row, part, :].astype(jnp.float32)

            return 0

        lax.fori_loop(0, R // 64, chunk, 0)

        @pl.when(row > a)
        def _():
            z_up(row).start()

        @pl.when(row < a)
        def _():
            z_down(row).start()

        return 0

    lax.fori_loop(0, A, sum_step, 0)

    def finish(index, _):
        y_copy(0, index).wait_recv()
        got = pltpu.make_async_copy(y_got.at[index], got_y, tile_sem)
        got.start()
        got.wait()
        tile_f32[index] = tile_f32[index] + got_y[...].astype(jnp.float32)
        out = pltpu.make_async_copy(tile_f32.at[index], grads_out.at[index], out_sem.at[index])
        out.start()
        return 0

    lax.fori_loop(0, 6, finish, 0)

    for kind in range(3):
        y_copy(kind, 0).wait_send()
    for row in range(A):
        x_copy(row).wait_send()

        @pl.when(row != a)
        def _():
            z_up(row).wait_send()

    @pl.when(a < A - 1)
    def _():
        send_up(me).wait_send()

    @pl.when(a > 0)
    def _():
        send_down(me).wait_send()

    for row in range(A):
        s = row * B + b
        send_across(s).wait_send()

        @pl.when((row < a) & (a < A - 1))
        def _():
            send_up(s).wait_send()

        @pl.when((row > a) & (a > 0))
        def _():
            send_down(s).wait_send()

    for k in range(1, n):
        s = (me + k) % n
        p_copy(s).wait_send()
        g_copy(s).wait_send()
        copy(gg_stage.at[s], gg_out.at[s], g_send.at[s], g_recv.at[s], expert=s).wait_recv()
    pltpu.make_async_copy(gg_stage.at[me], gg_out.at[me], g_send.at[me]).wait()
    for slot in range(2):
        d_copy(0, slot).wait()
    for index in range(6):
        pltpu.make_async_copy(tile_f32.at[index], grads_out.at[index], out_sem.at[index]).wait()


def moe_call(hidden, all_upstream, probs, expert_gate, expert_up, expert_down):
    R, D = hidden.shape
    F = expert_gate.shape[2]
    A, n = 4, 8
    shard = D // 4
    bf, f32 = jnp.bfloat16, jnp.float32
    any_spec = pl.BlockSpec(memory_space=pl.ANY)
    vmem = pl.BlockSpec(memory_space=pltpu.VMEM)
    dma = pltpu.SemaphoreType.DMA
    out_shape = (
        jax.ShapeDtypeStruct((n, R, D), bf),
        jax.ShapeDtypeStruct((R, D), f32),
        jax.ShapeDtypeStruct((n, 8, R), f32),
        jax.ShapeDtypeStruct((6, shard, F), f32),
        jax.ShapeDtypeStruct((2, 6, shard, F), bf),
        jax.ShapeDtypeStruct((6, shard, F), bf),
    )
    return pl.pallas_call(
        functools.partial(moe_kernel, comm=True),
        out_shape=out_shape,
        in_specs=[any_spec] * 6,
        out_specs=(any_spec, vmem, any_spec, any_spec, any_spec, any_spec),
        scratch_shapes=[
            pltpu.VMEM((n, R, D), bf),
            pltpu.VMEM((n, R, D), bf),
            pltpu.VMEM((n, 8, R), f32),
            pltpu.VMEM((2, D, F), bf),
            pltpu.VMEM((2, D, F), bf),
            pltpu.VMEM((2, D, F), bf),
            pltpu.VMEM((n * R, 2 * F), bf),
            pltpu.VMEM((n * R, 4 * F), bf),
            pltpu.VMEM((A, R, D), bf),
            pltpu.VMEM((A, R, D), bf),
            pltpu.VMEM((A, R, D), bf),
            pltpu.VMEM((A + 1, R, D), bf),
            pltpu.VMEM((2, R, D), bf),
            pltpu.VMEM((n, 8, R), f32),
            pltpu.VMEM((3, shard, F), bf),
            pltpu.VMEM((6, shard, F), f32),
            pltpu.VMEM((shard, F), bf),
            pltpu.VMEM((shard, F), bf),
            dma((6,)), dma((n,)), dma((n,)), dma((n,)), dma((n,)), dma((n,)), dma((n,)), dma((n,)), dma((n,)),
            dma((A,)), dma((A,)), dma((A,)), dma((A + 1,)), dma((2,)),
            dma((3,)), dma((2, 6)), dma((3,)), dma((6,)), dma, dma((6,)),
        ],
        compiler_params=pltpu.CompilerParams(
            collective_id=1, has_side_effects=True, vmem_limit_bytes=64 * 1024 * 1024 - 65536
        ),
        cost_estimate=pl.CostEstimate(flops=58 * 10**9, bytes_accessed=60 * 10**6, transcendentals=2 * 10**6),
        name="experts",
    )(hidden, all_upstream, probs, expert_gate, expert_up, expert_down)


def moe_by_collectives(hidden_two, all_upstream, dense_probs, expert_gate, expert_up, expert_down):
    local_count = expert_gate.shape[0]
    all_hidden = lax.all_gather(hidden_two, "expert", axis=0, tiled=True)
    all_probs = own_columns(lax.all_gather(dense_probs, "expert", axis=0, tiled=True), local_count)
    mix_part = jnp.zeros(all_hidden.shape, jnp.float32)
    row_part = jnp.zeros(all_hidden.shape, jnp.float32)
    grad_columns, down_parts, gate_parts, up_parts = [], [], [], []
    for e in range(local_count):
        prob = all_probs[:, e : e + 1]
        gate_pre = jnp.dot(all_hidden, expert_gate[e], preferred_element_type=jnp.float32)
        up_pre = jnp.dot(all_hidden, expert_up[e], preferred_element_type=jnp.float32)
        raw_grad = jnp.dot(all_upstream, expert_down[e], preferred_element_type=jnp.float32)
        gate_sig = jax.nn.sigmoid(gate_pre)
        gate_act = gate_pre * gate_sig
        activation = gate_act * up_pre
        grad_columns.append(jnp.sum(activation * raw_grad, axis=-1, keepdims=True))
        weighted = (activation * prob).astype(jnp.bfloat16)
        act_grad = raw_grad * prob
        gate_pre_grad = (act_grad * up_pre * gate_sig * (1.0 + gate_pre * (1.0 - gate_sig))).astype(
            jnp.bfloat16
        )
        up_pre_grad = (act_grad * gate_act).astype(jnp.bfloat16)
        mix_part = mix_part + jnp.dot(
            weighted, expert_down[e].T, preferred_element_type=jnp.float32
        )
        row_part = row_part + jnp.dot(
            gate_pre_grad, expert_gate[e].T, preferred_element_type=jnp.float32
        )
        row_part = row_part + jnp.dot(
            up_pre_grad, expert_up[e].T, preferred_element_type=jnp.float32
        )
        down_parts.append(jnp.dot(all_upstream.T, weighted, preferred_element_type=jnp.float32))
        gate_parts.append(jnp.dot(all_hidden.T, gate_pre_grad, preferred_element_type=jnp.float32))
        up_parts.append(jnp.dot(all_hidden.T, up_pre_grad, preferred_element_type=jnp.float32))
    down_partial = jnp.stack(down_parts)
    gate_partial = jnp.stack(gate_parts)
    up_partial = jnp.stack(up_parts)
    grad_dense = lax.all_to_all(
        jnp.concatenate(grad_columns, axis=1), "expert", split_axis=0, concat_axis=1, tiled=True
    )
    hidden_two_grad = lax.psum_scatter(
        row_part.astype(jnp.bfloat16), "expert", scatter_dimension=0, tiled=True
    ).astype(jnp.float32)
    expert_totals = tuple(
        lax.psum_scatter(part.astype(jnp.bfloat16), "dp", scatter_dimension=1, tiled=True).astype(
            jnp.float32
        )
        for part in (gate_partial, up_partial, down_partial)
    )
    return (mix_part.astype(jnp.bfloat16), hidden_two_grad, grad_dense, expert_totals)


def fits_fused(dp_size, group, row_count):
    return dp_size == 4 and group == 8 and row_count == 256


def body(
    tokens,
    seq_lengths,
    routes,
    w_query,
    w_key,
    w_value,
    w_output,
    w_router,
    attn_gain,
    moe_gain,
    expert_gate,
    expert_up,
    expert_down,
    out_grad,
):
    shards = (w_query, w_key, w_value, w_output, w_router, attn_gain, moe_gain)
    gathered = (
        lax.all_gather(shards[0], "dp", axis=0, tiled=True),
        lax.all_gather(shards[1], "dp", axis=0, tiled=True),
        lax.all_gather(shards[2], "dp", axis=0, tiled=True),
        lax.all_gather(shards[3], "dp", axis=0, tiled=True),
        lax.all_gather(shards[4], "dp", axis=0, tiled=True),
        lax.all_gather(shards[5], "dp", axis=0, tiled=True),
        lax.all_gather(shards[6], "dp", axis=0, tiled=True),
    )
    query_w, key_w, value_w, output_w, router_w, gain_one, gain_two = gathered
    row_count = tokens.shape[0]
    expert_count = w_router.shape[1]
    group_size = QH // KVH
    block_rows = min(512, row_count)
    block_total = row_count // block_rows
    score_scale = HD ** (-0.5)
    doc_id, position = token_layout(seq_lengths[0], row_count)
    cos_table, sin_table = rope_tables(position)
    token_index = jnp.arange(row_count, dtype=jnp.int32)
    block_starts = jnp.arange(block_total, dtype=jnp.int32) * block_rows
    inputs = tokens.astype(jnp.float32)
    scale_one = rms_scale(inputs)
    normed_one = inputs * scale_one
    hidden_one = (normed_one * gain_one.astype(jnp.float32)).astype(jnp.bfloat16)
    query_rot = rotate(
        jnp.dot(hidden_one, query_w, preferred_element_type=jnp.float32), cos_table, sin_table, QH
    ).astype(jnp.bfloat16)
    key_rot = rotate(
        jnp.dot(hidden_one, key_w, preferred_element_type=jnp.float32), cos_table, sin_table, KVH
    ).astype(jnp.bfloat16)
    value_rows = jnp.dot(hidden_one, value_w, preferred_element_type=jnp.float32).astype(
        jnp.bfloat16
    )
    key_heads = key_rot.reshape(row_count, KVH, HD)
    value_heads = value_rows.reshape(row_count, KVH, HD)

    def block_scores(block_start):
        query_block = query_rot.reshape(block_rows, KVH, group_size, HD)
        raw_scores = (
            jnp.einsum("tkgd,ukd->kgtu", query_block, key_heads, preferred_element_type=jnp.float32)
            * score_scale
        )
        block_index = block_start + jnp.arange(block_rows, dtype=jnp.int32)
        allowed = (doc_id[:, None] == doc_id[None, :]) & (
            token_index[None, :] <= block_index[:, None]
        )
        return (query_block, jnp.where(allowed, raw_scores, masked_score))

    def attend_block(block_start):
        query_block, scores = block_scores(block_start)
        row_top = jnp.max(scores, axis=-1, keepdims=True)
        exp_terms = jnp.exp(scores - row_top)
        row_total = jnp.sum(exp_terms, axis=-1, keepdims=True)
        probs_low = (exp_terms / row_total).astype(jnp.bfloat16)
        attended_block = jnp.einsum(
            "kgtu,ukd->tkgd", probs_low, value_heads, preferred_element_type=jnp.float32
        )
        log_total = (row_top + jnp.log(row_total))[..., 0]
        return (attended_block.reshape(block_rows, QH * HD).astype(jnp.bfloat16), log_total)

    attended_blocks, log_blocks = lax.map(attend_block, block_starts)
    attended = attended_blocks.reshape(row_count, QH * HD)
    residual = inputs + jnp.dot(attended, output_w, preferred_element_type=jnp.float32)
    scale_two = rms_scale(residual)
    normed_two = residual * scale_two
    hidden_two = (normed_two * gain_two.astype(jnp.float32)).astype(jnp.bfloat16)
    logits = jnp.dot(hidden_two, router_w, preferred_element_type=jnp.float32)
    expert_ids = jnp.arange(expert_count, dtype=jnp.int32)
    route_hot = (routes[:, :, None] == expert_ids[None, None, :]).astype(jnp.float32)
    chosen = jnp.sum(route_hot * logits[:, None, :], axis=-1)
    gate_probs = jax.nn.softmax(chosen, axis=-1)
    dense_probs = jnp.sum(route_hot * gate_probs[:, :, None], axis=1)
    upstream = out_grad.astype(jnp.float32)
    local_count = expert_gate.shape[0]
    group = lax.axis_size("expert")
    all_upstream = lax.all_gather(out_grad, "expert", axis=0, tiled=True)
    if fits_fused(lax.axis_size("dp"), group, row_count):
        by_owner = jnp.pad(
            dense_probs.T.reshape(group, local_count, row_count), ((0, 0), (0, 8 - local_count), (0, 0))
        )
        mix_part, row_sum, grad_rows, expert_grads, _, _ = moe_call(
            hidden_two,
            all_upstream.reshape(group, row_count, -1),
            by_owner,
            expert_gate,
            expert_up,
            expert_down,
        )
        mix_part = mix_part.reshape(all_upstream.shape)
        hidden_two_grad = row_sum
        grad_dense = grad_rows[:, :local_count].reshape(expert_count, row_count).T
        expert_totals = tuple(expert_grads[2 * kind : 2 * kind + 2] for kind in range(3))
    else:
        mix_part, hidden_two_grad, grad_dense, expert_totals = moe_by_collectives(
            hidden_two, all_upstream, dense_probs, expert_gate, expert_up, expert_down
        )
    gate_grad = jnp.sum(route_hot * grad_dense[:, None, :], axis=-1)
    mixture = lax.psum_scatter(mix_part, "expert", scatter_dimension=0, tiled=True)
    layer_out = (residual + mixture.astype(jnp.float32)).astype(jnp.bfloat16)
    chosen_grad = gate_probs * (gate_grad - jnp.sum(gate_probs * gate_grad, axis=-1, keepdims=True))
    logit_grad = jnp.sum(route_hot * chosen_grad[:, :, None], axis=1).astype(jnp.bfloat16)
    hidden_two_grad = hidden_two_grad + jnp.dot(
        logit_grad, router_w.T, preferred_element_type=jnp.float32
    )
    gain_two_partial = jnp.sum(hidden_two_grad * normed_two, axis=0)
    normed_two_grad = hidden_two_grad * gain_two.astype(jnp.float32)
    residual_grad = upstream + scale_two * (
        normed_two_grad
        - normed_two * jnp.mean(normed_two_grad * normed_two, axis=-1, keepdims=True)
    )
    branch_grad = residual_grad.astype(jnp.bfloat16)
    attended_grad = jnp.dot(branch_grad, output_w.T, preferred_element_type=jnp.float32).astype(
        jnp.bfloat16
    )

    def attend_back(carry, block_data):
        key_acc, value_acc = carry
        block_start, log_total = block_data
        query_block, scores = block_scores(block_start)
        attn_probs = jnp.exp(scores - log_total[..., None])
        probs_low = attn_probs.astype(jnp.bfloat16)
        grad_block = attended_grad.reshape(block_rows, KVH, group_size, HD)
        prob_grad = jnp.einsum(
            "tkgd,ukd->kgtu", grad_block, value_heads, preferred_element_type=jnp.float32
        )
        score_grad = (
            attn_probs * (prob_grad - jnp.sum(attn_probs * prob_grad, axis=-1, keepdims=True))
        ).astype(jnp.bfloat16)
        query_part = (
            jnp.einsum("kgtu,ukd->tkgd", score_grad, key_heads, preferred_element_type=jnp.float32)
            * score_scale
        )
        key_acc = (
            key_acc
            + jnp.einsum(
                "kgtu,tkgd->ukd", score_grad, query_block, preferred_element_type=jnp.float32
            )
            * score_scale
        )
        value_acc = value_acc + jnp.einsum(
            "kgtu,tkgd->ukd", probs_low, grad_block, preferred_element_type=jnp.float32
        )
        return ((key_acc, value_acc), query_part.reshape(block_rows, QH * HD))

    zero_heads = jnp.zeros((row_count, KVH, HD), jnp.float32)
    (key_sums, value_sums), query_blocks = lax.scan(
        attend_back, (zero_heads, zero_heads), (block_starts, log_blocks)
    )
    query_grad = unrotate(
        query_blocks.reshape(row_count, QH * HD), cos_table, sin_table, QH
    ).astype(jnp.bfloat16)
    key_grad = unrotate(key_sums.reshape(row_count, KVH * HD), cos_table, sin_table, KVH).astype(
        jnp.bfloat16
    )
    value_grad = value_sums.reshape(row_count, KVH * HD).astype(jnp.bfloat16)
    hidden_one_grad = jnp.dot(query_grad, query_w.T, preferred_element_type=jnp.float32)
    hidden_one_grad = hidden_one_grad + jnp.dot(
        key_grad, key_w.T, preferred_element_type=jnp.float32
    )
    hidden_one_grad = hidden_one_grad + jnp.dot(
        value_grad, value_w.T, preferred_element_type=jnp.float32
    )
    gain_one_partial = jnp.sum(hidden_one_grad * normed_one, axis=0)
    normed_one_grad = hidden_one_grad * gain_one.astype(jnp.float32)
    in_grad = residual_grad + scale_one * (
        normed_one_grad
        - normed_one * jnp.mean(normed_one_grad * normed_one, axis=-1, keepdims=True)
    )
    query_partial = jnp.dot(hidden_one.T, query_grad, preferred_element_type=jnp.float32)
    key_partial = jnp.dot(hidden_one.T, key_grad, preferred_element_type=jnp.float32)
    value_partial = jnp.dot(hidden_one.T, value_grad, preferred_element_type=jnp.float32)
    output_partial = jnp.dot(attended.T, branch_grad, preferred_element_type=jnp.float32)
    router_partial = jnp.dot(hidden_two.T, logit_grad, preferred_element_type=jnp.float32)
    pieces = jax.tree.map(
        lambda part: part.astype(jnp.float32),
        lax.psum_scatter(
            shortened(
                (
                    query_partial,
                    key_partial,
                    value_partial,
                    output_partial,
                    router_partial,
                    gain_one_partial,
                    gain_two_partial,
                )
            ),
            "dp",
            scatter_dimension=0,
            tiled=True,
        ),
    )
    totals = (
        lax.psum(pieces[0].astype(jnp.bfloat16), "expert").astype(jnp.float32),
        lax.psum(pieces[1].astype(jnp.bfloat16), "expert").astype(jnp.float32),
        lax.psum(pieces[2].astype(jnp.bfloat16), "expert").astype(jnp.float32),
        lax.psum(pieces[3].astype(jnp.bfloat16), "expert").astype(jnp.float32),
        lax.psum(pieces[4].astype(jnp.bfloat16), "expert").astype(jnp.float32),
        lax.psum(pieces[5].astype(jnp.bfloat16), "expert").astype(jnp.float32),
        lax.psum(pieces[6].astype(jnp.bfloat16), "expert").astype(jnp.float32),
    )
    return (
        layer_out,
        in_grad,
        totals[0],
        totals[1],
        totals[2],
        totals[3],
        totals[4],
        totals[5],
        totals[6],
        expert_totals[0],
        expert_totals[1],
        expert_totals[2],
    )


def solution(mesh):
    placed = (
        P(("dp", "expert"), None),
        P(("dp", "expert"), None),
        P(("dp", "expert"), None),
        P("dp", None),
        P("dp", None),
        P("dp", None),
        P("dp", None),
        P("dp", None),
        P("dp"),
        P("dp"),
        P("expert", None, None),
        P("expert", None, None),
        P("expert", None, None),
        P(("dp", "expert"), None),
    )
    return jax.shard_map(
        body,
        mesh=mesh,
        in_specs=placed,
        out_specs=(
            P(("dp", "expert"), None),
            P(("dp", "expert"), None),
            P("dp", None),
            P("dp", None),
            P("dp", None),
            P("dp", None),
            P("dp", None),
            P("dp"),
            P("dp"),
            P("expert", "dp", None),
            P("expert", "dp", None),
            P("expert", "dp", None),
        ),
        check_vma=False,
    )
```

```python
import functools

import jax
import jax.numpy as jnp
from jax import lax
from jax.experimental import pallas as pl
from jax.experimental.pallas import tpu as pltpu
from jax.sharding import PartitionSpec as P

MESH = pl.DeviceIdType.MESH
QH = 24
KVH = 8
HD = 64
TOP = 8


eps = 1e-06
rope_base = 10000.0
masked_score = -1e30


def shortened(value):
    return jax.tree.map(lambda a: a.astype(jnp.bfloat16) if a.dtype == jnp.float32 else a, value)


def rms_scale(values):
    return lax.rsqrt(jnp.mean(values * values, axis=-1, keepdims=True) + eps)


def token_layout(lengths_row, row_count):
    token_index = jnp.arange(row_count, dtype=jnp.int32)
    seq_ends = jnp.cumsum(lengths_row)
    passed = (token_index[:, None] >= seq_ends[None, :]).astype(jnp.int32)
    doc_id = jnp.sum(passed, axis=1)
    seq_start = jnp.sum(passed * lengths_row[None, :], axis=1)
    return (doc_id, token_index - seq_start)


def rope_tables(position):
    half_size = HD // 2
    frequency = rope_base ** (-2.0 * jnp.arange(half_size, dtype=jnp.float32) / HD)
    angles = position.astype(jnp.float32)[:, None] * frequency[None, :]
    return (jnp.cos(angles)[:, None, :], jnp.sin(angles)[:, None, :])


def rotate(values, cos_table, sin_table, head_count):
    half_size = HD // 2
    shaped = values.reshape(values.shape[0], head_count, HD)
    front_half = shaped[..., :half_size]
    back_half = shaped[..., half_size:]
    turned = jnp.concatenate(
        [
            front_half * cos_table - back_half * sin_table,
            back_half * cos_table + front_half * sin_table,
        ],
        axis=-1,
    )
    return turned.reshape(values.shape[0], head_count * HD)


def unrotate(values, cos_table, sin_table, head_count):
    half_size = HD // 2
    shaped = values.reshape(values.shape[0], head_count, HD)
    front_half = shaped[..., :half_size]
    back_half = shaped[..., half_size:]
    turned = jnp.concatenate(
        [
            front_half * cos_table + back_half * sin_table,
            back_half * cos_table - front_half * sin_table,
        ],
        axis=-1,
    )
    return turned.reshape(values.shape[0], head_count * HD)


def own_columns(values, local_count):
    start = lax.axis_index("expert") * local_count
    return lax.dynamic_slice_in_dim(values, start, local_count, axis=1)


NT = (((1,), (1,)), ((), ()))
TN = (((0,), (0,)), ((), ()))


def dot_f32(left, right, dims=(((1,), (0,)), ((), ()))):
    return lax.dot_general(left, right, dims, preferred_element_type=jnp.float32)


def packed(rows, index, step, base=8):
    value = 0
    for place, row in enumerate(rows):
        number = sum(digit * base**power for power, digit in enumerate(row))
        value = value + jnp.where(index == place, number, 0)
    scale = 1
    for power in range(1, len(rows[0])):
        scale = jnp.where(step == power, base**power, scale)
    return (value // scale) % base


BLOCK_ORDER = (
    (0, 4, 1, 5, 2, 6, 3, 7),
    (1, 5, 0, 2, 4, 3, 6, 7),
    (2, 6, 3, 1, 7, 0, 5, 4),
    (3, 7, 2, 6, 1, 5, 0, 4),
)
TAKE_FIRST = (
    (7, 1, 7, 2, 7, 3, 7, 7),
    (7, 0, 7, 7, 3, 7, 7, 7),
    (7, 3, 7, 7, 0, 7, 7, 7),
    (7, 2, 7, 1, 7, 0, 7, 7),
)
TAKE_SECOND = (
    (7, 7, 7, 7, 7, 7, 7, 7),
    (7, 2, 7, 7, 7, 7, 7, 7),
    (7, 1, 7, 7, 7, 7, 7, 7),
    (7, 7, 7, 7, 7, 7, 7, 7),
)
SUM_ORDER = ((3, 2, 1, 0), (3, 2, 0, 1), (0, 1, 3, 2), (0, 1, 2, 3))


def moe_kernel(
    h_in, u_in, p_in, wg_in, wu_in, wd_in,
    d_out, e_out, gg_out, grads_out, core_got, y_got,
    h_all, u_all, p_all, wg, wu, wd, act, gu, ex, ez, rx, rz, d_stage, gg_stage, tile_bf, tile_f32, got_tile, got_y,
    load_sem, h_up, h_down, h_across, h_recv, p_send, p_recv, g_send, g_recv,
    x_send, x_recv, z_send, z_recv, d_sem, c_send, c_recv, y_send, y_recv, tile_sem, out_sem,
    *, comm
):
    A, B, n = 4, 2, 8
    R, D = h_in.shape
    F = wg.shape[2]
    shard = D // 4
    me = lax.axis_index("expert")
    dp = lax.axis_index("dp")
    a, b = me // B, me % B
    y, c = dp // 2, dp % 2
    partner_x = a * B + (1 - b)
    core_peer = 2 * y + (1 - c)
    y_peer = 2 * (1 - y) + c

    def copy(src, dst, send, recv, **target):
        return pltpu.make_async_remote_copy(
            src_ref=src, dst_ref=dst, send_sem=send, recv_sem=recv, device_id=target, device_id_type=MESH
        )

    loads = [
        pltpu.make_async_copy(h_in, h_all.at[me], load_sem.at[0]),
        pltpu.make_async_copy(u_in, u_all, load_sem.at[1]),
        pltpu.make_async_copy(wg_in, wg, load_sem.at[2]),
        pltpu.make_async_copy(wu_in, wu, load_sem.at[3]),
        pltpu.make_async_copy(wd_in, wd, load_sem.at[4]),
        pltpu.make_async_copy(p_in.at[me], p_all.at[me], load_sem.at[5]),
    ]
    for load in loads:
        load.start()

    barrier = pltpu.get_barrier_semaphore()
    for k in range(1, n):
        pl.semaphore_signal(barrier, inc=1, device_id={"expert": (me + k) % n}, device_id_type=MESH)
    pl.semaphore_signal(barrier, inc=1, device_id={"dp": core_peer}, device_id_type=MESH)
    pl.semaphore_signal(barrier, inc=1, device_id={"dp": y_peer}, device_id_type=MESH)
    pl.semaphore_wait(barrier, n + 1)
    loads[0].wait()
    loads[5].wait()

    def send_up(s):
        return copy(h_all.at[s], h_all.at[s], h_up.at[s], h_recv.at[s], expert=me + B)

    def send_down(s):
        return copy(h_all.at[s], h_all.at[s], h_down.at[s], h_recv.at[s], expert=me - B)

    def send_across(s):
        return copy(h_all.at[s], h_all.at[s], h_across.at[s], h_recv.at[s], expert=partner_x)

    def p_copy(peer):
        return copy(p_in.at[peer], p_all.at[me], p_send.at[peer], p_recv.at[me], expert=peer)

    @pl.when(a < A - 1)
    def _():
        send_up(me).start()

    @pl.when(a > 0)
    def _():
        send_down(me).start()

    send_across(me).start()
    for k in range(1, n):
        p_copy((me + k) % n).start()
    for k in range(1, n):
        s = (me + k) % n
        copy(p_in.at[s], p_all.at[s], p_send.at[s], p_recv.at[s], expert=s).wait_recv()
    for load in loads[1:5]:
        load.wait()

    def recv_block(s):
        send_across(s).wait_recv()

    def take(row):
        @pl.when(row < A)
        def _():
            s = row * B + b
            recv_block(s)
            send_across(s).start()

            @pl.when((row < a) & (a < A - 1))
            def _():
                send_up(s).start()

            @pl.when((row > a) & (a > 0))
            def _():
                send_down(s).start()

    def d_copy(s, slot):
        return pltpu.make_async_copy(d_stage.at[slot], d_out.at[s], d_sem.at[slot])

    def g_copy(s):
        return copy(gg_stage.at[s], gg_out.at[me], g_send.at[s], g_recv.at[me], expert=s)

    def compute(step, s, row, across):
        rows = pl.ds(pl.multiple_of(s * R, R), R)
        probs = jnp.transpose(p_all[s])
        grad_cols = []
        for e in range(2):
            gate_pre = dot_f32(h_all[s], wg[e])
            up_pre = dot_f32(h_all[s], wu[e])
            raw = dot_f32(u_all[s], wd[e])
            prob = probs[:, e : e + 1]
            sig = 1.0 / (1.0 + jnp.exp(-gate_pre))
            gate_act = gate_pre * sig
            activation = gate_act * up_pre
            grad_cols.append(jnp.sum(activation * raw, axis=1, keepdims=True))
            act[rows, e * F : (e + 1) * F] = (activation * prob).astype(jnp.bfloat16)
            act_grad = raw * prob
            gate_grad = act_grad * up_pre * sig * (1.0 + gate_pre * (1.0 - sig))
            gu[rows, 2 * e * F : (2 * e + 1) * F] = gate_grad.astype(jnp.bfloat16)
            gu[rows, (2 * e + 1) * F : (2 * e + 2) * F] = (act_grad * gate_act).astype(jnp.bfloat16)
        column = lax.broadcasted_iota(jnp.int32, (R, 128), 1)
        both = jnp.where(column == 0, grad_cols[0], jnp.where(column == 1, grad_cols[1], 0.0))
        gg_stage[s] = jnp.transpose(both)[:8]
        slot = step % 2

        @pl.when(step >= 2)
        def _():
            d_copy(s, slot).wait()

        def columns(tile, _):
            cols = pl.ds(pl.multiple_of(tile * 512, 512), 512)
            mixed = dot_f32(act[rows, 0:F], wd[0, cols, :], NT) + dot_f32(act[rows, F : 2 * F], wd[1, cols, :], NT)
            d_stage[slot, :, cols] = mixed.astype(jnp.bfloat16)
            back = dot_f32(gu[rows, 0:F], wg[0, cols, :], NT)
            back += dot_f32(gu[rows, F : 2 * F], wu[0, cols, :], NT)
            back += dot_f32(gu[rows, 2 * F : 3 * F], wg[1, cols, :], NT)
            back += dot_f32(gu[rows, 3 * F : 4 * F], wu[1, cols, :], NT)

            @pl.when(across)
            def _():
                ex[row, :, cols] = back.astype(jnp.bfloat16)

            @pl.when(jnp.logical_not(across))
            def _():
                ez[row, :, cols] = back.astype(jnp.bfloat16)

            return 0

        lax.fori_loop(0, D // 512, columns, 0)
        d_copy(s, slot).start()

        @pl.when(s != me)
        def _():
            g_copy(s).start()

        @pl.when(s == me)
        def _():
            pltpu.make_async_copy(gg_stage.at[s], gg_out.at[me], g_send.at[s]).start()

    def block_step(step, _):
        take(packed(TAKE_FIRST, a, step))
        take(packed(TAKE_SECOND, a, step))
        code = packed(BLOCK_ORDER, a, step)
        across = code >= A
        row = code % A
        s = row * B + jnp.where(across, 1 - b, b)

        @pl.when(across)
        def _():
            recv_block(s)

        compute(step, s, row, across)
        return 0

    lax.fori_loop(0, n, block_step, 0)

    def x_copy(row):
        return copy(ex.at[row], rx.at[row], x_send.at[row], x_recv.at[row], expert=partner_x)

    def z_up(row):
        return copy(ez.at[row], rz.at[row + 1], z_send.at[row], z_recv.at[row + 1], expert=me + B)

    def z_down(row):
        return copy(ez.at[row], rz.at[row], z_send.at[row], z_recv.at[row], expert=me - B)

    for place in range(A):
        x_copy(packed(SUM_ORDER, a, place)).start()

    def core_copy(slot, which, index):
        return copy(tile_bf.at[slot], core_got.at[which, index], c_send.at[slot], c_recv.at[which, index], dp=core_peer)

    def y_copy(slot, index):
        return copy(tile_bf.at[slot], y_got.at[index], y_send.at[slot], y_recv.at[index], dp=y_peer)

    def weight_tile(group, e, kind, left, right):
        owner = jnp.where(group == 0, core_peer, jnp.where(group == 1, 2 * (1 - y) + 1 - c, jnp.where(group == 2, y_peer, dp)))
        cols = pl.ds(pl.multiple_of(owner * shard, 128), shard)
        total = dot_f32(left[:, :, cols].reshape(n * R, shard), right, TN)
        index = kind * 2 + e
        slot = kind

        @pl.when(group < 2)
        def _():
            @pl.when((group > 0) | (e > 0))
            def _():
                core_copy(slot, 0, index).wait_send()

            tile_bf[slot] = total.astype(jnp.bfloat16)
            core_copy(slot, group, index).start()

        @pl.when(group == 2)
        def _():
            @pl.when(e == 0)
            def _():
                core_copy(slot, 0, index).wait_send()

            @pl.when(e > 0)
            def _():
                y_copy(slot, index).wait_send()

            core_copy(slot, 1, index).wait_recv()
            got = pltpu.make_async_copy(core_got.at[1, index], got_tile, tile_sem)
            got.start()
            got.wait()
            tile_bf[slot] = (total + got_tile[...].astype(jnp.float32)).astype(jnp.bfloat16)
            y_copy(slot, index).start()

        @pl.when(group == 3)
        def _():
            core_copy(slot, 0, index).wait_recv()
            got = pltpu.make_async_copy(core_got.at[0, index], got_tile, tile_sem)
            got.start()
            got.wait()
            tile_f32[index] = total + got_tile[...].astype(jnp.float32)

    def sum_step(place, _):
        def pair(e, _):
            weight_tile(place, e, 0, h_all, gu[:, pl.ds(pl.multiple_of(2 * e * F, 128), F)])
            weight_tile(place, e, 1, h_all, gu[:, pl.ds(pl.multiple_of((2 * e + 1) * F, 128), F)])
            weight_tile(place, e, 2, u_all, act[:, pl.ds(pl.multiple_of(e * F, 128), F)])
            return 0

        lax.fori_loop(0, 2, pair, 0)
        row = packed(SUM_ORDER, a, place)
        x_copy(row).wait_recv()
        below = (a > 0) & (row >= a)
        above = (a < A - 1) & (row <= a)

        @pl.when(below)
        def _():
            z_up(row).wait_recv()

        @pl.when(above)
        def _():
            z_down(row).wait_recv()

        def chunk(index, _):
            part = pl.ds(pl.multiple_of(index * 64, 64), 64)
            total = ez[row, part, :].astype(jnp.float32) + rx[row, part, :].astype(jnp.float32)

            @pl.when(row != a)
            def _():
                @pl.when(below)
                def _():
                    ez[row, part, :] = (total + rz[row + 1, part, :].astype(jnp.float32)).astype(jnp.bfloat16)

                @pl.when(above)
                def _():
                    ez[row, part, :] = (total + rz[row, part, :].astype(jnp.float32)).astype(jnp.bfloat16)

                @pl.when(jnp.logical_not(below | above))
                def _():
                    ez[row, part, :] = total.astype(jnp.bfloat16)

            @pl.when(row == a)
            def _():
                @pl.when(below & above)
                def _():
                    e_out[part, :] = total + rz[row + 1, part, :].astype(jnp.float32) + rz[row, part, :].astype(jnp.float32)

                @pl.when(below & jnp.logical_not(above))
                def _():
                    e_out[part, :] = total + rz[row + 1, part, :].astype(jnp.float32)

                @pl.when(above & jnp.logical_not(below))
                def _():
                    e_out[part, :] = total + rz[row, part, :].astype(jnp.float32)

            return 0

        lax.fori_loop(0, R // 64, chunk, 0)

        @pl.when(row > a)
        def _():
            z_up(row).start()

        @pl.when(row < a)
        def _():
            z_down(row).start()

        return 0

    lax.fori_loop(0, A, sum_step, 0)

    def finish(index, _):
        y_copy(0, index).wait_recv()
        got = pltpu.make_async_copy(y_got.at[index], got_y, tile_sem)
        got.start()
        got.wait()
        tile_f32[index] = tile_f32[index] + got_y[...].astype(jnp.float32)
        out = pltpu.make_async_copy(tile_f32.at[index], grads_out.at[index], out_sem.at[index])
        out.start()
        return 0

    lax.fori_loop(0, 6, finish, 0)

    for kind in range(3):
        y_copy(kind, 0).wait_send()
    for row in range(A):
        x_copy(row).wait_send()

        @pl.when(row != a)
        def _():
            z_up(row).wait_send()

    @pl.when(a < A - 1)
    def _():
        send_up(me).wait_send()

    @pl.when(a > 0)
    def _():
        send_down(me).wait_send()

    for row in range(A):
        s = row * B + b
        send_across(s).wait_send()

        @pl.when((row < a) & (a < A - 1))
        def _():
            send_up(s).wait_send()

        @pl.when((row > a) & (a > 0))
        def _():
            send_down(s).wait_send()

    for k in range(1, n):
        s = (me + k) % n
        p_copy(s).wait_send()
        g_copy(s).wait_send()
        copy(gg_stage.at[s], gg_out.at[s], g_send.at[s], g_recv.at[s], expert=s).wait_recv()
    pltpu.make_async_copy(gg_stage.at[me], gg_out.at[me], g_send.at[me]).wait()
    for slot in range(2):
        d_copy(0, slot).wait()
    for index in range(6):
        pltpu.make_async_copy(tile_f32.at[index], grads_out.at[index], out_sem.at[index]).wait()


def moe_call(hidden, all_upstream, probs, expert_gate, expert_up, expert_down):
    R, D = hidden.shape
    F = expert_gate.shape[2]
    A, n = 4, 8
    shard = D // 4
    bf, f32 = jnp.bfloat16, jnp.float32
    any_spec = pl.BlockSpec(memory_space=pl.ANY)
    vmem = pl.BlockSpec(memory_space=pltpu.VMEM)
    dma = pltpu.SemaphoreType.DMA
    out_shape = (
        jax.ShapeDtypeStruct((n, R, D), bf),
        jax.ShapeDtypeStruct((R, D), f32),
        jax.ShapeDtypeStruct((n, 8, R), f32),
        jax.ShapeDtypeStruct((6, shard, F), f32),
        jax.ShapeDtypeStruct((2, 6, shard, F), bf),
        jax.ShapeDtypeStruct((6, shard, F), bf),
    )
    return pl.pallas_call(
        functools.partial(moe_kernel, comm=True),
        out_shape=out_shape,
        in_specs=[any_spec] * 6,
        out_specs=(any_spec, vmem, any_spec, any_spec, any_spec, any_spec),
        scratch_shapes=[
            pltpu.VMEM((n, R, D), bf),
            pltpu.VMEM((n, R, D), bf),
            pltpu.VMEM((n, 8, R), f32),
            pltpu.VMEM((2, D, F), bf),
            pltpu.VMEM((2, D, F), bf),
            pltpu.VMEM((2, D, F), bf),
            pltpu.VMEM((n * R, 2 * F), bf),
            pltpu.VMEM((n * R, 4 * F), bf),
            pltpu.VMEM((A, R, D), bf),
            pltpu.VMEM((A, R, D), bf),
            pltpu.VMEM((A, R, D), bf),
            pltpu.VMEM((A + 1, R, D), bf),
            pltpu.VMEM((2, R, D), bf),
            pltpu.VMEM((n, 8, R), f32),
            pltpu.VMEM((3, shard, F), bf),
            pltpu.VMEM((6, shard, F), f32),
            pltpu.VMEM((shard, F), bf),
            pltpu.VMEM((shard, F), bf),
            dma((6,)), dma((n,)), dma((n,)), dma((n,)), dma((n,)), dma((n,)), dma((n,)), dma((n,)), dma((n,)),
            dma((A,)), dma((A,)), dma((A,)), dma((A + 1,)), dma((2,)),
            dma((3,)), dma((2, 6)), dma((3,)), dma((6,)), dma, dma((6,)),
        ],
        compiler_params=pltpu.CompilerParams(
            collective_id=1, has_side_effects=True, vmem_limit_bytes=64 * 1024 * 1024 - 65536
        ),
        cost_estimate=pl.CostEstimate(flops=58 * 10**9, bytes_accessed=60 * 10**6, transcendentals=2 * 10**6),
        name="experts",
    )(hidden, all_upstream, probs, expert_gate, expert_up, expert_down)


def reduce_kernel(
    left, right, extra, out,
    core_out, core_in, y_out, y_in, half, x_out, x_in, own, z_out, z_in, full,
    core_send, core_recv, y_send, y_recv, x_send, x_recv, zs_send, zs_recv, zg_send, zg_recv, xg_send, xg_recv,
):
    A, B = 4, 2
    W = core_out.shape[3]
    shard = core_out.shape[2]
    half_rows, piece = shard // B, shard // (A * B)
    chunks = y_in.shape[0]
    me = lax.axis_index("expert")
    dp = lax.axis_index("dp")
    a, b = me // B, me % B
    y, c = dp // 2, dp % 2
    partner_x = a * B + (1 - b)
    core_peer = 2 * y + (1 - c)
    y_peer = 2 * (1 - y) + c

    def copy(src, dst, send, recv, **target):
        return pltpu.make_async_remote_copy(
            src_ref=src, dst_ref=dst, send_sem=send, recv_sem=recv, device_id=target, device_id_type=MESH
        )

    barrier = pltpu.get_barrier_semaphore()
    for target in [{"dp": core_peer}, {"dp": y_peer}, {"expert": partner_x}] + [
        {"expert": (a + k) % A * B + b} for k in range(1, A)
    ]:
        pl.semaphore_signal(barrier, inc=1, device_id=target, device_id_type=MESH)
    pl.semaphore_wait(barrier, 2 + A)

    def partial(chunk, owner):
        rows = pl.ds(pl.multiple_of(owner * shard, 128), shard)
        cols = pl.ds(pl.multiple_of(chunk * W, 128), W)
        which = jnp.where(chunk < 4, 0, 1)
        total = dot_f32(left[which, :, rows], right[:, cols], TN)
        share = extra[pl.ds(pl.multiple_of(owner * shard, 128), shard), :].astype(jnp.float32)
        share = jnp.where(chunk == chunks - 1, share, 0.0)
        return jnp.concatenate([total[:, : W - 128], total[:, W - 128 :] + share], axis=1)

    def core_copy(chunk, which):
        slot = chunk % 2
        return copy(core_out.at[slot, which], core_in.at[chunk, which], core_send.at[slot, which], core_recv.at[chunk, which], dp=core_peer)

    def y_copy(chunk):
        slot = chunk % 2
        return copy(y_out.at[slot], y_in.at[chunk], y_send.at[slot], y_recv.at[chunk], dp=y_peer)

    def x_copy(chunk):
        slot = chunk % 2
        return copy(x_out.at[slot], x_in.at[chunk], x_send.at[slot], x_recv.at[chunk], expert=partner_x)

    def z_scatter(chunk, to, source):
        slot = chunk % 2
        return copy(
            z_out.at[slot, pl.ds(pl.multiple_of(to * piece, 16), piece)], z_in.at[chunk, source],
            zs_send.at[slot, to], zs_recv.at[chunk, source], expert=to * B + b,
        )

    def z_gather(chunk, to, source):
        rows = pl.ds(pl.multiple_of(b * half_rows + source * piece, 16), piece)
        return copy(full.at[chunk, rows], full.at[chunk, rows], zg_send.at[chunk, to], zg_recv.at[chunk, source], expert=to * B + b)

    def x_gather(chunk, side):
        rows = pl.ds(pl.multiple_of(side * half_rows, 16), half_rows)
        return copy(full.at[chunk, rows], full.at[chunk, rows], xg_send.at[chunk], xg_recv.at[chunk], expert=partner_x)

    def to_core(chunk):
        for which, owner in ((0, core_peer), (1, 2 * (1 - y) + 1 - c)):
            value = partial(chunk, owner).astype(jnp.bfloat16)

            @pl.when(chunk >= 2)
            def _():
                core_copy(chunk, which).wait_send()

            core_out[chunk % 2, which] = value
            core_copy(chunk, which).start()

    def to_y(chunk):
        value = partial(chunk, y_peer)
        core_copy(chunk, 1).wait_recv()

        @pl.when(chunk >= 2)
        def _():
            y_copy(chunk).wait_send()

        y_out[chunk % 2] = (value + core_in[chunk, 1].astype(jnp.float32)).astype(jnp.bfloat16)
        y_copy(chunk).start()

    def to_x(chunk):
        value = partial(chunk, dp)
        core_copy(chunk, 0).wait_recv()
        y_copy(chunk).wait_recv()
        value = value + core_in[chunk, 0].astype(jnp.float32) + y_in[chunk].astype(jnp.float32)

        @pl.when(chunk >= 2)
        def _():
            x_copy(chunk).wait_send()

        low, high = value[:half_rows], value[half_rows:]
        half[chunk % 2] = jnp.where(b == 0, low, high)
        x_out[chunk % 2] = jnp.where(b == 0, high, low).astype(jnp.bfloat16)
        x_copy(chunk).start()

    def to_z(chunk):
        x_copy(chunk).wait_recv()

        @pl.when(chunk >= 2)
        def _():
            for k in range(1, A):
                z_scatter(chunk, (a + k) % A, a).wait_send()

        total = half[chunk % 2] + x_in[chunk].astype(jnp.float32)
        half[chunk % 2] = total
        own[chunk % 2] = half[chunk % 2, pl.ds(pl.multiple_of(a * piece, 8), piece)]
        z_out[chunk % 2] = total.astype(jnp.bfloat16)
        for k in range(1, A):
            z_scatter(chunk, (a + k) % A, a).start()

    def spread_z(chunk):
        total = own[chunk % 2]
        for k in range(1, A):
            source = (a + k) % A
            z_scatter(chunk, a, source).wait_recv()
            total = total + z_in[chunk, source].astype(jnp.float32)
        rows = pl.ds(pl.multiple_of(b * half_rows + a * piece, 16), piece)
        full[chunk, rows] = total.astype(jnp.bfloat16)
        for k in range(1, A):
            z_gather(chunk, (a + k) % A, a).start()

    def spread_x(chunk):
        for k in range(1, A):
            z_gather(chunk, a, (a + k) % A).wait_recv()
        x_gather(chunk, b).start()

    def finish(chunk):
        x_gather(chunk, 1 - b).wait_recv()
        cols = pl.ds(pl.multiple_of(chunk * W, 128), W)
        out[:, cols] = full[chunk].astype(jnp.float32)

    stages = (to_core, to_y, to_x, to_z, spread_z, spread_x, finish)

    def step(t, _):
        for delay, stage in enumerate(stages):
            @pl.when((t >= delay) & (t < delay + chunks))
            def _():
                stage(t - delay)

        return 0

    lax.fori_loop(0, chunks + len(stages) - 1, step, 0)

    for chunk in range(chunks - 2, chunks):
        core_copy(chunk, 0).wait_send()
        core_copy(chunk, 1).wait_send()
        y_copy(chunk).wait_send()
        x_copy(chunk).wait_send()
        for k in range(1, A):
            z_scatter(chunk, (a + k) % A, a).wait_send()

    def drain(chunk, _):
        for k in range(1, A):
            z_gather(chunk, (a + k) % A, a).wait_send()
        x_gather(chunk, b).wait_send()
        return 0

    lax.fori_loop(0, chunks, drain, 0)


def reduce_call(left, right, extra):
    D = left.shape[2]
    width = right.shape[1]
    W, A, B = 384, 4, 2
    shard, chunks = D // 4, width // W
    bf, f32 = jnp.bfloat16, jnp.float32
    vmem = pl.BlockSpec(memory_space=pltpu.VMEM)
    dma = pltpu.SemaphoreType.DMA
    piece = shard // (A * B)
    return pl.pallas_call(
        reduce_kernel,
        out_shape=jax.ShapeDtypeStruct((shard, width), f32),
        in_specs=[vmem] * 3,
        out_specs=vmem,
        scratch_shapes=[
            pltpu.VMEM((2, 2, shard, W), bf),
            pltpu.VMEM((chunks, 2, shard, W), bf),
            pltpu.VMEM((2, shard, W), bf),
            pltpu.VMEM((chunks, shard, W), bf),
            pltpu.VMEM((2, shard // B, W), f32),
            pltpu.VMEM((2, shard // B, W), bf),
            pltpu.VMEM((chunks, shard // B, W), bf),
            pltpu.VMEM((2, piece, W), f32),
            pltpu.VMEM((2, shard // B, W), bf),
            pltpu.VMEM((chunks, A, piece, W), bf),
            pltpu.VMEM((chunks, shard, W), bf),
            dma((2, 2)), dma((chunks, 2)), dma((2,)), dma((chunks,)), dma((2,)), dma((chunks,)),
            dma((2, A)), dma((chunks, A)), dma((chunks, A)), dma((chunks, A)), dma((chunks,)), dma((chunks,)),
        ],
        compiler_params=pltpu.CompilerParams(
            collective_id=2, has_side_effects=True, vmem_limit_bytes=56 * 1024 * 1024
        ),
        cost_estimate=pl.CostEstimate(flops=4 * 10**9, bytes_accessed=20 * 10**6, transcendentals=0),
        name="weight_sums",
    )(left, right, extra)


def front_kernel(
    w_q, w_k, w_v, w_o, w_small, u_in,
    all_q, all_k, all_v, all_o, all_small, u_all,
    local_sem, core_send, y_send, pass_send, w_recv, u_up, u_down, u_across, u_recv,
):
    A, B = 4, 2
    me = lax.axis_index("expert")
    dp = lax.axis_index("dp")
    a, b = me // B, me % B
    y, c = dp // 2, dp % 2
    partner_x = a * B + (1 - b)
    core_peer = 2 * y + (1 - c)
    y_peer = 2 * (1 - y) + c
    far_peer = 2 * (1 - y) + 1 - c
    shards = (w_small, w_q, w_k, w_v, w_o)
    gathered = (all_small, all_q, all_k, all_v, all_o)
    count = len(shards)

    def copy(src, dst, send, recv, **target):
        return pltpu.make_async_remote_copy(
            src_ref=src, dst_ref=dst, send_sem=send, recv_sem=recv, device_id=target, device_id_type=MESH
        )

    barrier = pltpu.get_barrier_semaphore()
    for target in [{"dp": core_peer}, {"dp": y_peer}, {"expert": partner_x}] + [
        {"expert": (a + k) % A * B + b} for k in range(1, A)
    ]:
        pl.semaphore_signal(barrier, inc=1, device_id=target, device_id_type=MESH)
    pl.semaphore_wait(barrier, 2 + A)

    def to_core(i):
        return copy(shards[i], gathered[i].at[dp], core_send.at[i], w_recv.at[i, dp], dp=core_peer)

    def to_y(i):
        return copy(shards[i], gathered[i].at[dp], y_send.at[i], w_recv.at[i, dp], dp=y_peer)

    def pass_on(i):
        return copy(gathered[i].at[y_peer], gathered[i].at[y_peer], pass_send.at[i], w_recv.at[i, y_peer], dp=core_peer)

    def wait_shard(i, owner):
        copy(shards[i], gathered[i].at[owner], core_send.at[i], w_recv.at[i, owner], dp=core_peer).wait_recv()

    def keep(i):
        return pltpu.make_async_copy(shards[i], gathered[i].at[dp], local_sem.at[i])

    def u_send_up(src, s):
        return copy(src, u_all.at[s], u_up.at[s], u_recv.at[s], expert=me + B)

    def u_send_down(src, s):
        return copy(src, u_all.at[s], u_down.at[s], u_recv.at[s], expert=me - B)

    def u_send_across(src, s):
        return copy(src, u_all.at[s], u_across.at[s], u_recv.at[s], expert=partner_x)

    keep_u = pltpu.make_async_copy(u_in, u_all.at[me], local_sem.at[count])

    @pl.when(a < A - 1)
    def _():
        u_send_up(u_in, me).start()

    @pl.when(a > 0)
    def _():
        u_send_down(u_in, me).start()

    u_send_across(u_in, me).start()
    for i in range(count):
        to_y(i).start()
        to_core(i).start()
        keep(i).start()
    keep_u.start()

    def take(row):
        @pl.when((row >= 0) & (row < A))
        def _():
            s = row * B + b
            u_send_across(u_all.at[s], s).wait_recv()
            u_send_across(u_all.at[s], s).start()

            @pl.when((row < a) & (a < A - 1))
            def _():
                u_send_up(u_all.at[s], s).start()

            @pl.when((row > a) & (a > 0))
            def _():
                u_send_down(u_all.at[s], s).start()

    def forward(i):
        wait_shard(i, y_peer)
        pass_on(i).start()

    for k in range(1, A):
        take(a - k)
        take(a + k)
    for i in range(count):
        forward(i)

    for row in range(A):
        s = row * B + 1 - b
        u_send_across(u_all.at[s], s).wait_recv()
    for i in range(count):
        wait_shard(i, core_peer)
        wait_shard(i, far_peer)
        keep(i).wait()
        to_y(i).wait_send()
        to_core(i).wait_send()
        pass_on(i).wait_send()
    keep_u.wait()

    @pl.when(a < A - 1)
    def _():
        u_send_up(u_in, me).wait_send()

    @pl.when(a > 0)
    def _():
        u_send_down(u_in, me).wait_send()

    for row in range(A):
        s = row * B + b
        u_send_across(u_all.at[s], s).wait_send()

        @pl.when((row < a) & (a < A - 1))
        def _():
            u_send_up(u_all.at[s], s).wait_send()

        @pl.when((row > a) & (a > 0))
        def _():
            u_send_down(u_all.at[s], s).wait_send()


def front_call(w_query, w_key, w_value, w_output, w_small, out_grad):
    n = 8
    bf = jnp.bfloat16
    any_spec = pl.BlockSpec(memory_space=pl.ANY)
    dma = pltpu.SemaphoreType.DMA
    shards = (w_query, w_key, w_value, w_output, w_small)
    return pl.pallas_call(
        front_kernel,
        out_shape=tuple(jax.ShapeDtypeStruct((4, *w.shape), bf) for w in shards)
        + (jax.ShapeDtypeStruct((n, *out_grad.shape), bf),),
        in_specs=[pl.BlockSpec(memory_space=pltpu.VMEM)] * 6,
        out_specs=(any_spec,) * 6,
        scratch_shapes=[
            dma((6,)), dma((5,)), dma((5,)), dma((5,)), dma((5, 4)), dma((n,)), dma((n,)), dma((n,)), dma((n,)),
        ],
        compiler_params=pltpu.CompilerParams(collective_id=3, has_side_effects=True, vmem_limit_bytes=32 * 1024 * 1024),
        cost_estimate=pl.CostEstimate(flops=0, bytes_accessed=40 * 10**6, transcendentals=0),
        name="gathers",
    )(*shards, out_grad)


def moe_by_collectives(hidden_two, all_upstream, dense_probs, expert_gate, expert_up, expert_down):
    local_count = expert_gate.shape[0]
    all_hidden = lax.all_gather(hidden_two, "expert", axis=0, tiled=True)
    all_probs = own_columns(lax.all_gather(dense_probs, "expert", axis=0, tiled=True), local_count)
    mix_part = jnp.zeros(all_hidden.shape, jnp.float32)
    row_part = jnp.zeros(all_hidden.shape, jnp.float32)
    grad_columns, down_parts, gate_parts, up_parts = [], [], [], []
    for e in range(local_count):
        prob = all_probs[:, e : e + 1]
        gate_pre = jnp.dot(all_hidden, expert_gate[e], preferred_element_type=jnp.float32)
        up_pre = jnp.dot(all_hidden, expert_up[e], preferred_element_type=jnp.float32)
        raw_grad = jnp.dot(all_upstream, expert_down[e], preferred_element_type=jnp.float32)
        gate_sig = jax.nn.sigmoid(gate_pre)
        gate_act = gate_pre * gate_sig
        activation = gate_act * up_pre
        grad_columns.append(jnp.sum(activation * raw_grad, axis=-1, keepdims=True))
        weighted = (activation * prob).astype(jnp.bfloat16)
        act_grad = raw_grad * prob
        gate_pre_grad = (act_grad * up_pre * gate_sig * (1.0 + gate_pre * (1.0 - gate_sig))).astype(
            jnp.bfloat16
        )
        up_pre_grad = (act_grad * gate_act).astype(jnp.bfloat16)
        mix_part = mix_part + jnp.dot(
            weighted, expert_down[e].T, preferred_element_type=jnp.float32
        )
        row_part = row_part + jnp.dot(
            gate_pre_grad, expert_gate[e].T, preferred_element_type=jnp.float32
        )
        row_part = row_part + jnp.dot(
            up_pre_grad, expert_up[e].T, preferred_element_type=jnp.float32
        )
        down_parts.append(jnp.dot(all_upstream.T, weighted, preferred_element_type=jnp.float32))
        gate_parts.append(jnp.dot(all_hidden.T, gate_pre_grad, preferred_element_type=jnp.float32))
        up_parts.append(jnp.dot(all_hidden.T, up_pre_grad, preferred_element_type=jnp.float32))
    down_partial = jnp.stack(down_parts)
    gate_partial = jnp.stack(gate_parts)
    up_partial = jnp.stack(up_parts)
    grad_dense = lax.all_to_all(
        jnp.concatenate(grad_columns, axis=1), "expert", split_axis=0, concat_axis=1, tiled=True
    )
    hidden_two_grad = lax.psum_scatter(
        row_part.astype(jnp.bfloat16), "expert", scatter_dimension=0, tiled=True
    ).astype(jnp.float32)
    expert_totals = tuple(
        lax.psum_scatter(part.astype(jnp.bfloat16), "dp", scatter_dimension=1, tiled=True).astype(
            jnp.float32
        )
        for part in (gate_partial, up_partial, down_partial)
    )
    return (mix_part.astype(jnp.bfloat16), hidden_two_grad, grad_dense, expert_totals)


def sums_by_collectives(
    hidden_one, attended, query_grad, key_grad, value_grad, branch_grad, router_partial, gain_one_partial, gain_two_partial
):
    query_partial = jnp.dot(hidden_one.T, query_grad, preferred_element_type=jnp.float32)
    key_partial = jnp.dot(hidden_one.T, key_grad, preferred_element_type=jnp.float32)
    value_partial = jnp.dot(hidden_one.T, value_grad, preferred_element_type=jnp.float32)
    output_partial = jnp.dot(attended.T, branch_grad, preferred_element_type=jnp.float32)
    pieces = jax.tree.map(
        lambda part: part.astype(jnp.float32),
        lax.psum_scatter(
            shortened(
                (
                    query_partial,
                    key_partial,
                    value_partial,
                    output_partial,
                    router_partial,
                    gain_one_partial,
                    gain_two_partial,
                )
            ),
            "dp",
            scatter_dimension=0,
            tiled=True,
        ),
    )
    totals = (
        lax.psum(pieces[0].astype(jnp.bfloat16), "expert").astype(jnp.float32),
        lax.psum(pieces[1].astype(jnp.bfloat16), "expert").astype(jnp.float32),
        lax.psum(pieces[2].astype(jnp.bfloat16), "expert").astype(jnp.float32),
        lax.psum(pieces[3].astype(jnp.bfloat16), "expert").astype(jnp.float32),
        lax.psum(pieces[4].astype(jnp.bfloat16), "expert").astype(jnp.float32),
        lax.psum(pieces[5].astype(jnp.bfloat16), "expert").astype(jnp.float32),
        lax.psum(pieces[6].astype(jnp.bfloat16), "expert").astype(jnp.float32),
    )
    return totals


def fits_fused(dp_size, group, row_count):
    return dp_size == 4 and group == 8 and row_count == 256


def body(
    tokens,
    seq_lengths,
    routes,
    w_query,
    w_key,
    w_value,
    w_output,
    w_router,
    attn_gain,
    moe_gain,
    expert_gate,
    expert_up,
    expert_down,
    out_grad,
):
    group = lax.axis_size("expert")
    fused = fits_fused(lax.axis_size("dp"), group, tokens.shape[0])
    if fused:
        small = jnp.concatenate([w_router, attn_gain[:, None], moe_gain[:, None]], axis=1)
        small = jnp.pad(small, ((0, 0), (0, 128 - small.shape[1])))
        gathered = front_call(w_query, w_key, w_value, w_output, small, out_grad)
        query_w, key_w, value_w, output_w, small = [
            whole.reshape(-1, whole.shape[2]) for whole in gathered[:5]
        ]
        experts_all = w_router.shape[1]
        router_w, gain_one, gain_two = small[:, :experts_all], small[:, experts_all], small[:, experts_all + 1]
        all_upstream = gathered[5].reshape(-1, out_grad.shape[1])
    else:
        query_w, key_w, value_w, output_w, router_w, gain_one, gain_two = [
            lax.all_gather(shard, "dp", axis=0, tiled=True)
            for shard in (w_query, w_key, w_value, w_output, w_router, attn_gain, moe_gain)
        ]
        all_upstream = lax.all_gather(out_grad, "expert", axis=0, tiled=True)
    row_count = tokens.shape[0]
    expert_count = w_router.shape[1]
    group_size = QH // KVH
    block_rows = min(512, row_count)
    block_total = row_count // block_rows
    score_scale = HD ** (-0.5)
    doc_id, position = token_layout(seq_lengths[0], row_count)
    cos_table, sin_table = rope_tables(position)
    token_index = jnp.arange(row_count, dtype=jnp.int32)
    block_starts = jnp.arange(block_total, dtype=jnp.int32) * block_rows
    inputs = tokens.astype(jnp.float32)
    scale_one = rms_scale(inputs)
    normed_one = inputs * scale_one
    hidden_one = (normed_one * gain_one.astype(jnp.float32)).astype(jnp.bfloat16)
    query_rot = rotate(
        jnp.dot(hidden_one, query_w, preferred_element_type=jnp.float32), cos_table, sin_table, QH
    ).astype(jnp.bfloat16)
    key_rot = rotate(
        jnp.dot(hidden_one, key_w, preferred_element_type=jnp.float32), cos_table, sin_table, KVH
    ).astype(jnp.bfloat16)
    value_rows = jnp.dot(hidden_one, value_w, preferred_element_type=jnp.float32).astype(
        jnp.bfloat16
    )
    key_heads = key_rot.reshape(row_count, KVH, HD)
    value_heads = value_rows.reshape(row_count, KVH, HD)

    def block_scores(block_start):
        query_block = query_rot.reshape(block_rows, KVH, group_size, HD)
        raw_scores = (
            jnp.einsum("tkgd,ukd->kgtu", query_block, key_heads, preferred_element_type=jnp.float32)
            * score_scale
        )
        block_index = block_start + jnp.arange(block_rows, dtype=jnp.int32)
        allowed = (doc_id[:, None] == doc_id[None, :]) & (
            token_index[None, :] <= block_index[:, None]
        )
        return (query_block, jnp.where(allowed, raw_scores, masked_score))

    def attend_block(block_start):
        query_block, scores = block_scores(block_start)
        row_top = jnp.max(scores, axis=-1, keepdims=True)
        exp_terms = jnp.exp(scores - row_top)
        row_total = jnp.sum(exp_terms, axis=-1, keepdims=True)
        probs_low = (exp_terms / row_total).astype(jnp.bfloat16)
        attended_block = jnp.einsum(
            "kgtu,ukd->tkgd", probs_low, value_heads, preferred_element_type=jnp.float32
        )
        log_total = (row_top + jnp.log(row_total))[..., 0]
        return (attended_block.reshape(block_rows, QH * HD).astype(jnp.bfloat16), log_total)

    attended_blocks, log_blocks = lax.map(attend_block, block_starts)
    attended = attended_blocks.reshape(row_count, QH * HD)
    residual = inputs + jnp.dot(attended, output_w, preferred_element_type=jnp.float32)
    scale_two = rms_scale(residual)
    normed_two = residual * scale_two
    hidden_two = (normed_two * gain_two.astype(jnp.float32)).astype(jnp.bfloat16)
    logits = jnp.dot(hidden_two, router_w, preferred_element_type=jnp.float32)
    expert_ids = jnp.arange(expert_count, dtype=jnp.int32)
    route_hot = (routes[:, :, None] == expert_ids[None, None, :]).astype(jnp.float32)
    chosen = jnp.sum(route_hot * logits[:, None, :], axis=-1)
    gate_probs = jax.nn.softmax(chosen, axis=-1)
    dense_probs = jnp.sum(route_hot * gate_probs[:, :, None], axis=1)
    upstream = out_grad.astype(jnp.float32)
    local_count = expert_gate.shape[0]
    if fused:
        by_owner = jnp.pad(
            dense_probs.T.reshape(group, local_count, row_count), ((0, 0), (0, 8 - local_count), (0, 0))
        )
        mix_part, row_sum, grad_rows, expert_grads, _, _ = moe_call(
            hidden_two,
            all_upstream.reshape(group, row_count, -1),
            by_owner,
            expert_gate,
            expert_up,
            expert_down,
        )
        mix_part = mix_part.reshape(all_upstream.shape)
        hidden_two_grad = row_sum
        grad_dense = grad_rows[:, :local_count].reshape(expert_count, row_count).T
        expert_totals = tuple(expert_grads[2 * kind : 2 * kind + 2] for kind in range(3))
    else:
        mix_part, hidden_two_grad, grad_dense, expert_totals = moe_by_collectives(
            hidden_two, all_upstream, dense_probs, expert_gate, expert_up, expert_down
        )
    gate_grad = jnp.sum(route_hot * grad_dense[:, None, :], axis=-1)
    mixture = lax.psum_scatter(mix_part, "expert", scatter_dimension=0, tiled=True)
    chosen_grad = gate_probs * (gate_grad - jnp.sum(gate_probs * gate_grad, axis=-1, keepdims=True))
    logit_grad = jnp.sum(route_hot * chosen_grad[:, :, None], axis=1).astype(jnp.bfloat16)
    hidden_two_grad = hidden_two_grad + jnp.dot(
        logit_grad, router_w.T, preferred_element_type=jnp.float32
    )
    gain_two_partial = jnp.sum(hidden_two_grad * normed_two, axis=0)
    normed_two_grad = hidden_two_grad * gain_two.astype(jnp.float32)
    residual_grad = upstream + scale_two * (
        normed_two_grad
        - normed_two * jnp.mean(normed_two_grad * normed_two, axis=-1, keepdims=True)
    )
    branch_grad = residual_grad.astype(jnp.bfloat16)
    attended_grad = jnp.dot(branch_grad, output_w.T, preferred_element_type=jnp.float32).astype(
        jnp.bfloat16
    )

    def attend_back(carry, block_data):
        key_acc, value_acc = carry
        block_start, log_total = block_data
        query_block, scores = block_scores(block_start)
        attn_probs = jnp.exp(scores - log_total[..., None])
        probs_low = attn_probs.astype(jnp.bfloat16)
        grad_block = attended_grad.reshape(block_rows, KVH, group_size, HD)
        prob_grad = jnp.einsum(
            "tkgd,ukd->kgtu", grad_block, value_heads, preferred_element_type=jnp.float32
        )
        score_grad = (
            attn_probs * (prob_grad - jnp.sum(attn_probs * prob_grad, axis=-1, keepdims=True))
        ).astype(jnp.bfloat16)
        query_part = (
            jnp.einsum("kgtu,ukd->tkgd", score_grad, key_heads, preferred_element_type=jnp.float32)
            * score_scale
        )
        key_acc = (
            key_acc
            + jnp.einsum(
                "kgtu,tkgd->ukd", score_grad, query_block, preferred_element_type=jnp.float32
            )
            * score_scale
        )
        value_acc = value_acc + jnp.einsum(
            "kgtu,tkgd->ukd", probs_low, grad_block, preferred_element_type=jnp.float32
        )
        return ((key_acc, value_acc), query_part.reshape(block_rows, QH * HD))

    zero_heads = jnp.zeros((row_count, KVH, HD), jnp.float32)
    (key_sums, value_sums), query_blocks = lax.scan(
        attend_back, (zero_heads, zero_heads), (block_starts, log_blocks)
    )
    query_grad = unrotate(
        query_blocks.reshape(row_count, QH * HD), cos_table, sin_table, QH
    ).astype(jnp.bfloat16)
    key_grad = unrotate(key_sums.reshape(row_count, KVH * HD), cos_table, sin_table, KVH).astype(
        jnp.bfloat16
    )
    value_grad = value_sums.reshape(row_count, KVH * HD).astype(jnp.bfloat16)
    hidden_one_grad = jnp.dot(query_grad, query_w.T, preferred_element_type=jnp.float32)
    hidden_one_grad = hidden_one_grad + jnp.dot(
        key_grad, key_w.T, preferred_element_type=jnp.float32
    )
    hidden_one_grad = hidden_one_grad + jnp.dot(
        value_grad, value_w.T, preferred_element_type=jnp.float32
    )
    gain_one_partial = jnp.sum(hidden_one_grad * normed_one, axis=0)
    normed_one_grad = hidden_one_grad * gain_one.astype(jnp.float32)
    in_grad = residual_grad + scale_one * (
        normed_one_grad
        - normed_one * jnp.mean(normed_one_grad * normed_one, axis=-1, keepdims=True)
    )
    router_partial = jnp.dot(hidden_two.T, logit_grad, preferred_element_type=jnp.float32)
    if fused:
        extra = jnp.concatenate(
            [router_partial, gain_one_partial[:, None], gain_two_partial[:, None]], axis=1
        )
        spare = 128 - extra.shape[1]
        extra = jnp.pad(extra, ((0, 0), (0, spare))).astype(jnp.bfloat16)
        zero_columns = jnp.zeros((row_count, 128), jnp.bfloat16)
        sums = reduce_call(
            jnp.stack([attended, hidden_one]),
            jnp.concatenate([branch_grad, query_grad, key_grad, value_grad, zero_columns], axis=1),
            extra,
        )
        wide, narrow = query_w.shape[1], key_w.shape[1]
        cuts = (0, wide, 2 * wide, 2 * wide + narrow, 2 * wide + 2 * narrow)
        of_output, of_query, of_key, of_value = [sums[:, i:j] for i, j in zip(cuts, cuts[1:])]
        tail = sums[:, cuts[-1] :]
        totals = (
            of_query,
            of_key,
            of_value,
            of_output,
            tail[:, :expert_count],
            tail[:, expert_count],
            tail[:, expert_count + 1],
        )
    else:
        totals = sums_by_collectives(
            hidden_one, attended, query_grad, key_grad, value_grad, branch_grad, router_partial, gain_one_partial,
            gain_two_partial,
        )
    late_residual, _ = lax.optimization_barrier((residual, totals[0]))
    layer_out = (late_residual + mixture.astype(jnp.float32)).astype(jnp.bfloat16)
    return (
        layer_out,
        in_grad,
        totals[0],
        totals[1],
        totals[2],
        totals[3],
        totals[4],
        totals[5],
        totals[6],
        expert_totals[0],
        expert_totals[1],
        expert_totals[2],
    )


def solution(mesh):
    placed = (
        P(("dp", "expert"), None),
        P(("dp", "expert"), None),
        P(("dp", "expert"), None),
        P("dp", None),
        P("dp", None),
        P("dp", None),
        P("dp", None),
        P("dp", None),
        P("dp"),
        P("dp"),
        P("expert", None, None),
        P("expert", None, None),
        P("expert", None, None),
        P(("dp", "expert"), None),
    )
    return jax.shard_map(
        body,
        mesh=mesh,
        in_specs=placed,
        out_specs=(
            P(("dp", "expert"), None),
            P(("dp", "expert"), None),
            P("dp", None),
            P("dp", None),
            P("dp", None),
            P("dp", None),
            P("dp", None),
            P("dp"),
            P("dp"),
            P("expert", "dp", None),
            P("expert", "dp", None),
            P("expert", "dp", None),
        ),
        check_vma=False,
    )
```

```python
import functools
import math

import jax
import jax.numpy as jnp
from jax import lax
from jax.experimental import pallas as pl
from jax.experimental.pallas import tpu as pltpu
from jax.sharding import PartitionSpec as P

MESH = pl.DeviceIdType.MESH

QH = 24
KVH = 8
HD = 64
TOP = 8


eps = 1e-06
rope_base = 10000.0
masked_score = -1e30


def shortened(value):
    return jax.tree.map(lambda a: a.astype(jnp.bfloat16) if a.dtype == jnp.float32 else a, value)


def rms_scale(values):
    return lax.rsqrt(jnp.mean(values * values, axis=-1, keepdims=True) + eps)


def token_layout(lengths_row, row_count):
    token_index = jnp.arange(row_count, dtype=jnp.int32)
    seq_ends = jnp.cumsum(lengths_row)
    passed = (token_index[:, None] >= seq_ends[None, :]).astype(jnp.int32)
    doc_id = jnp.sum(passed, axis=1)
    seq_start = jnp.sum(passed * lengths_row[None, :], axis=1)
    return (doc_id, token_index - seq_start)


def rope_tables(position):
    half_size = HD // 2
    frequency = rope_base ** (-2.0 * jnp.arange(half_size, dtype=jnp.float32) / HD)
    angles = position.astype(jnp.float32)[:, None] * frequency[None, :]
    return (jnp.cos(angles)[:, None, :], jnp.sin(angles)[:, None, :])


def rotate(values, cos_table, sin_table, head_count):
    half_size = HD // 2
    shaped = values.reshape(values.shape[0], head_count, HD)
    front_half = shaped[..., :half_size]
    back_half = shaped[..., half_size:]
    turned = jnp.concatenate(
        [
            front_half * cos_table - back_half * sin_table,
            back_half * cos_table + front_half * sin_table,
        ],
        axis=-1,
    )
    return turned.reshape(values.shape[0], head_count * HD)


def unrotate(values, cos_table, sin_table, head_count):
    half_size = HD // 2
    shaped = values.reshape(values.shape[0], head_count, HD)
    front_half = shaped[..., :half_size]
    back_half = shaped[..., half_size:]
    turned = jnp.concatenate(
        [
            front_half * cos_table + back_half * sin_table,
            back_half * cos_table - front_half * sin_table,
        ],
        axis=-1,
    )
    return turned.reshape(values.shape[0], head_count * HD)


def own_columns(values, local_count):
    start = lax.axis_index("expert") * local_count
    return lax.dynamic_slice_in_dim(values, start, local_count, axis=1)


def body(
    tokens,
    seq_lengths,
    routes,
    w_query,
    w_key,
    w_value,
    w_output,
    w_router,
    attn_gain,
    moe_gain,
    expert_gate,
    expert_up,
    expert_down,
    out_grad,
):
    shards = (w_query, w_key, w_value, w_output, w_router, attn_gain, moe_gain)
    gathered = (
        lax.all_gather(shards[0], "dp", axis=0, tiled=True),
        lax.all_gather(shards[1], "dp", axis=0, tiled=True),
        lax.all_gather(shards[2], "dp", axis=0, tiled=True),
        lax.all_gather(shards[3], "dp", axis=0, tiled=True),
        lax.all_gather(shards[4], "dp", axis=0, tiled=True),
        lax.all_gather(shards[5], "dp", axis=0, tiled=True),
        lax.all_gather(shards[6], "dp", axis=0, tiled=True),
    )
    query_w, key_w, value_w, output_w, router_w, gain_one, gain_two = gathered
    row_count = tokens.shape[0]
    expert_count = w_router.shape[1]
    group_size = QH // KVH
    block_rows = min(512, row_count)
    block_total = row_count // block_rows
    score_scale = HD ** (-0.5)
    doc_id, position = token_layout(seq_lengths[0], row_count)
    cos_table, sin_table = rope_tables(position)
    token_index = jnp.arange(row_count, dtype=jnp.int32)
    block_starts = jnp.arange(block_total, dtype=jnp.int32) * block_rows
    inputs = tokens.astype(jnp.float32)
    scale_one = rms_scale(inputs)
    normed_one = inputs * scale_one
    hidden_one = (normed_one * gain_one.astype(jnp.float32)).astype(jnp.bfloat16)
    query_rot = rotate(
        jnp.dot(hidden_one, query_w, preferred_element_type=jnp.float32), cos_table, sin_table, QH
    ).astype(jnp.bfloat16)
    key_rot = rotate(
        jnp.dot(hidden_one, key_w, preferred_element_type=jnp.float32), cos_table, sin_table, KVH
    ).astype(jnp.bfloat16)
    value_rows = jnp.dot(hidden_one, value_w, preferred_element_type=jnp.float32).astype(
        jnp.bfloat16
    )
    key_heads = key_rot.reshape(row_count, KVH, HD)
    value_heads = value_rows.reshape(row_count, KVH, HD)

    def block_scores(block_start):
        query_block = query_rot.reshape(block_rows, KVH, group_size, HD)
        raw_scores = (
            jnp.einsum("tkgd,ukd->kgtu", query_block, key_heads, preferred_element_type=jnp.float32)
            * score_scale
        )
        block_index = block_start + jnp.arange(block_rows, dtype=jnp.int32)
        allowed = (doc_id[:, None] == doc_id[None, :]) & (
            token_index[None, :] <= block_index[:, None]
        )
        return (query_block, jnp.where(allowed, raw_scores, masked_score))

    def attend_block(block_start):
        query_block, scores = block_scores(block_start)
        row_top = jnp.max(scores, axis=-1, keepdims=True)
        exp_terms = jnp.exp(scores - row_top)
        row_total = jnp.sum(exp_terms, axis=-1, keepdims=True)
        probs_low = (exp_terms / row_total).astype(jnp.bfloat16)
        attended_block = jnp.einsum(
            "kgtu,ukd->tkgd", probs_low, value_heads, preferred_element_type=jnp.float32
        )
        log_total = (row_top + jnp.log(row_total))[..., 0]
        return (attended_block.reshape(block_rows, QH * HD).astype(jnp.bfloat16), log_total)

    attended_blocks, log_blocks = lax.map(attend_block, block_starts)
    attended = attended_blocks.reshape(row_count, QH * HD)
    residual = inputs + jnp.dot(attended, output_w, preferred_element_type=jnp.float32)
    scale_two = rms_scale(residual)
    normed_two = residual * scale_two
    hidden_two = (normed_two * gain_two.astype(jnp.float32)).astype(jnp.bfloat16)
    logits = jnp.dot(hidden_two, router_w, preferred_element_type=jnp.float32)
    expert_ids = jnp.arange(expert_count, dtype=jnp.int32)
    route_hot = (routes[:, :, None] == expert_ids[None, None, :]).astype(jnp.float32)
    chosen = jnp.sum(route_hot * logits[:, None, :], axis=-1)
    gate_probs = jax.nn.softmax(chosen, axis=-1)
    dense_probs = jnp.sum(route_hot * gate_probs[:, :, None], axis=1)
    upstream = out_grad.astype(jnp.float32)
    local_count = expert_gate.shape[0]
    all_hidden = lax.all_gather(hidden_two, "expert", axis=0, tiled=True)
    all_probs = own_columns(lax.all_gather(dense_probs, "expert", axis=0, tiled=True), local_count)
    all_upstream = lax.all_gather(out_grad, "expert", axis=0, tiled=True)
    mix_part = jnp.zeros(all_hidden.shape, jnp.float32)
    row_part = jnp.zeros(all_hidden.shape, jnp.float32)
    grad_columns, down_parts, gate_parts, up_parts = [], [], [], []
    for e in range(local_count):
        prob = all_probs[:, e : e + 1]
        gate_pre = jnp.dot(all_hidden, expert_gate[e], preferred_element_type=jnp.float32)
        up_pre = jnp.dot(all_hidden, expert_up[e], preferred_element_type=jnp.float32)
        raw_grad = jnp.dot(all_upstream, expert_down[e], preferred_element_type=jnp.float32)
        gate_sig = jax.nn.sigmoid(gate_pre)
        gate_act = gate_pre * gate_sig
        activation = gate_act * up_pre
        grad_columns.append(jnp.sum(activation * raw_grad, axis=-1, keepdims=True))
        weighted = (activation * prob).astype(jnp.bfloat16)
        act_grad = raw_grad * prob
        gate_pre_grad = (act_grad * up_pre * gate_sig * (1.0 + gate_pre * (1.0 - gate_sig))).astype(
            jnp.bfloat16
        )
        up_pre_grad = (act_grad * gate_act).astype(jnp.bfloat16)
        mix_part = mix_part + jnp.dot(
            weighted, expert_down[e].T, preferred_element_type=jnp.float32
        )
        row_part = row_part + jnp.dot(
            gate_pre_grad, expert_gate[e].T, preferred_element_type=jnp.float32
        )
        row_part = row_part + jnp.dot(
            up_pre_grad, expert_up[e].T, preferred_element_type=jnp.float32
        )
        down_parts.append(jnp.dot(all_upstream.T, weighted, preferred_element_type=jnp.float32))
        gate_parts.append(jnp.dot(all_hidden.T, gate_pre_grad, preferred_element_type=jnp.float32))
        up_parts.append(jnp.dot(all_hidden.T, up_pre_grad, preferred_element_type=jnp.float32))
    down_partial = jnp.stack(down_parts)
    gate_partial = jnp.stack(gate_parts)
    up_partial = jnp.stack(up_parts)
    grad_dense = lax.all_to_all(
        jnp.concatenate(grad_columns, axis=1), "expert", split_axis=0, concat_axis=1, tiled=True
    )
    gate_grad = jnp.sum(route_hot * grad_dense[:, None, :], axis=-1)
    mixture = lax.psum_scatter(
        mix_part.astype(jnp.bfloat16), "expert", scatter_dimension=0, tiled=True
    ).astype(jnp.float32)
    layer_out = (residual + mixture).astype(jnp.bfloat16)
    hidden_two_grad = lax.psum_scatter(
        row_part.astype(jnp.bfloat16), "expert", scatter_dimension=0, tiled=True
    ).astype(jnp.float32)
    chosen_grad = gate_probs * (gate_grad - jnp.sum(gate_probs * gate_grad, axis=-1, keepdims=True))
    logit_grad = jnp.sum(route_hot * chosen_grad[:, :, None], axis=1).astype(jnp.bfloat16)
    hidden_two_grad = hidden_two_grad + jnp.dot(
        logit_grad, router_w.T, preferred_element_type=jnp.float32
    )
    gain_two_partial = jnp.sum(hidden_two_grad * normed_two, axis=0)
    normed_two_grad = hidden_two_grad * gain_two.astype(jnp.float32)
    residual_grad = upstream + scale_two * (
        normed_two_grad
        - normed_two * jnp.mean(normed_two_grad * normed_two, axis=-1, keepdims=True)
    )
    branch_grad = residual_grad.astype(jnp.bfloat16)
    attended_grad = jnp.dot(branch_grad, output_w.T, preferred_element_type=jnp.float32).astype(
        jnp.bfloat16
    )

    def attend_back(carry, block_data):
        key_acc, value_acc = carry
        block_start, log_total = block_data
        query_block, scores = block_scores(block_start)
        attn_probs = jnp.exp(scores - log_total[..., None])
        probs_low = attn_probs.astype(jnp.bfloat16)
        grad_block = attended_grad.reshape(block_rows, KVH, group_size, HD)
        prob_grad = jnp.einsum(
            "tkgd,ukd->kgtu", grad_block, value_heads, preferred_element_type=jnp.float32
        )
        score_grad = (
            attn_probs * (prob_grad - jnp.sum(attn_probs * prob_grad, axis=-1, keepdims=True))
        ).astype(jnp.bfloat16)
        query_part = (
            jnp.einsum("kgtu,ukd->tkgd", score_grad, key_heads, preferred_element_type=jnp.float32)
            * score_scale
        )
        key_acc = (
            key_acc
            + jnp.einsum(
                "kgtu,tkgd->ukd", score_grad, query_block, preferred_element_type=jnp.float32
            )
            * score_scale
        )
        value_acc = value_acc + jnp.einsum(
            "kgtu,tkgd->ukd", probs_low, grad_block, preferred_element_type=jnp.float32
        )
        return ((key_acc, value_acc), query_part.reshape(block_rows, QH * HD))

    zero_heads = jnp.zeros((row_count, KVH, HD), jnp.float32)
    (key_sums, value_sums), query_blocks = lax.scan(
        attend_back, (zero_heads, zero_heads), (block_starts, log_blocks)
    )
    query_grad = unrotate(
        query_blocks.reshape(row_count, QH * HD), cos_table, sin_table, QH
    ).astype(jnp.bfloat16)
    key_grad = unrotate(key_sums.reshape(row_count, KVH * HD), cos_table, sin_table, KVH).astype(
        jnp.bfloat16
    )
    value_grad = value_sums.reshape(row_count, KVH * HD).astype(jnp.bfloat16)
    hidden_one_grad = jnp.dot(query_grad, query_w.T, preferred_element_type=jnp.float32)
    hidden_one_grad = hidden_one_grad + jnp.dot(
        key_grad, key_w.T, preferred_element_type=jnp.float32
    )
    hidden_one_grad = hidden_one_grad + jnp.dot(
        value_grad, value_w.T, preferred_element_type=jnp.float32
    )
    gain_one_partial = jnp.sum(hidden_one_grad * normed_one, axis=0)
    normed_one_grad = hidden_one_grad * gain_one.astype(jnp.float32)
    in_grad = residual_grad + scale_one * (
        normed_one_grad
        - normed_one * jnp.mean(normed_one_grad * normed_one, axis=-1, keepdims=True)
    )
    query_partial = jnp.dot(hidden_one.T, query_grad, preferred_element_type=jnp.float32)
    key_partial = jnp.dot(hidden_one.T, key_grad, preferred_element_type=jnp.float32)
    value_partial = jnp.dot(hidden_one.T, value_grad, preferred_element_type=jnp.float32)
    output_partial = jnp.dot(attended.T, branch_grad, preferred_element_type=jnp.float32)
    router_partial = jnp.dot(hidden_two.T, logit_grad, preferred_element_type=jnp.float32)
    pieces = jax.tree.map(
        lambda part: part.astype(jnp.float32),
        lax.psum_scatter(
            shortened(
                (
                    query_partial,
                    key_partial,
                    value_partial,
                    output_partial,
                    router_partial,
                    gain_one_partial,
                    gain_two_partial,
                )
            ),
            "dp",
            scatter_dimension=0,
            tiled=True,
        ),
    )
    totals = (
        lax.psum(pieces[0].astype(jnp.bfloat16), "expert").astype(jnp.float32),
        lax.psum(pieces[1].astype(jnp.bfloat16), "expert").astype(jnp.float32),
        lax.psum(pieces[2].astype(jnp.bfloat16), "expert").astype(jnp.float32),
        lax.psum(pieces[3].astype(jnp.bfloat16), "expert").astype(jnp.float32),
        lax.psum(pieces[4].astype(jnp.bfloat16), "expert").astype(jnp.float32),
        lax.psum(pieces[5].astype(jnp.bfloat16), "expert").astype(jnp.float32),
        lax.psum(pieces[6].astype(jnp.bfloat16), "expert").astype(jnp.float32),
    )
    expert_totals = (
        lax.psum_scatter(
            gate_partial.astype(jnp.bfloat16), "dp", scatter_dimension=1, tiled=True
        ).astype(jnp.float32),
        lax.psum_scatter(
            up_partial.astype(jnp.bfloat16), "dp", scatter_dimension=1, tiled=True
        ).astype(jnp.float32),
        lax.psum_scatter(
            down_partial.astype(jnp.bfloat16), "dp", scatter_dimension=1, tiled=True
        ).astype(jnp.float32),
    )
    return (
        layer_out,
        in_grad,
        totals[0],
        totals[1],
        totals[2],
        totals[3],
        totals[4],
        totals[5],
        totals[6],
        expert_totals[0],
        expert_totals[1],
        expert_totals[2],
    )


NT = (((1,), (1,)), ((), ()))
TN = (((0,), (0,)), ((), ()))


def dot_f32(left, right, dims=(((1,), (0,)), ((), ()))):
    return lax.dot_general(left, right, dims, preferred_element_type=jnp.float32)


def entry(rows, index, step):
    value = 0
    for place, row in enumerate(rows):
        for column, digit in enumerate(row):
            if digit:
                value = jnp.where((index == place) & (step == column), digit, value)
    return value


BLOCK_ORDER = (
    (0, 4, 1, 2, 5, 3, 7, 6),
    (1, 5, 0, 2, 4, 3, 7, 6),
    (2, 6, 3, 1, 7, 0, 4, 5),
    (3, 7, 2, 1, 6, 0, 4, 5),
)
TAKE_FIRST = (
    (15, 1, 15, 2, 5, 3, 7, 6),
    (15, 0, 15, 3, 15, 7, 15, 6),
    (15, 3, 15, 0, 15, 4, 15, 5),
    (15, 2, 15, 1, 6, 0, 4, 5),
)
TAKE_SECOND = (
    (15, 4, 15, 15, 15, 15, 15, 15),
    (15, 2, 15, 4, 15, 15, 15, 15),
    (15, 1, 15, 7, 15, 15, 15, 15),
    (15, 7, 15, 15, 15, 15, 15, 15),
)
TAKE_THIRD = (
    (15, 15, 15, 15, 15, 15, 15, 15),
    (15, 5, 15, 15, 15, 15, 15, 15),
    (15, 6, 15, 15, 15, 15, 15, 15),
    (15, 15, 15, 15, 15, 15, 15, 15),
)
SUM_ORDER = (
    (3, 2, 7, 7, 0),
    (7, 3, 0, 2, 1),
    (7, 0, 3, 1, 2),
    (0, 1, 7, 7, 3),
)
HALVES = 2


def moe_kernel(
    h_in, u_in, p_in, wg_in, wu_in, wd_in,
    d_out, e_out, gg_out, grads_out, core_got, y_out,
    h_all, u_all, p_all, wg, wu, wd, act, gu, ex, ez, rx, rz, d_stage, gg_stage, tile_bf, tile_f32, got_tile,
    load_sem, h_up, h_down, h_across, h_recv, p_send, p_recv, g_send, g_recv,
    x_send, x_recv, z_send, z_recv, d_sem, c_send, c_recv, y_send, tile_sem, out_sem,
    *, comm
):
    A, B, n = 4, 2, 8
    R, D = h_in.shape
    F = wg.shape[2]
    shard = D // 4
    me = lax.axis_index("expert")
    dp = lax.axis_index("dp")
    a, b = me // B, me % B
    y, c = dp // 2, dp % 2
    partner_x = a * B + (1 - b)
    core_peer = 2 * y + (1 - c)
    y_peer = 2 * (1 - y) + c

    def copy(src, dst, send, recv, **target):
        return pltpu.make_async_remote_copy(
            src_ref=src, dst_ref=dst, send_sem=send, recv_sem=recv, device_id=target, device_id_type=MESH
        )

    loads = [
        pltpu.make_async_copy(h_in, h_all.at[me], load_sem.at[0]),
        pltpu.make_async_copy(u_in, u_all, load_sem.at[1]),
        pltpu.make_async_copy(wg_in, wg, load_sem.at[2]),
        pltpu.make_async_copy(wu_in, wu, load_sem.at[3]),
        pltpu.make_async_copy(wd_in, wd, load_sem.at[4]),
        pltpu.make_async_copy(p_in.at[me], p_all.at[me], load_sem.at[5]),
    ]
    for load in loads:
        load.start()

    barrier = pltpu.get_barrier_semaphore()
    for k in range(1, n):
        pl.semaphore_signal(barrier, inc=1, device_id={"expert": (me + k) % n}, device_id_type=MESH)
    pl.semaphore_signal(barrier, inc=1, device_id={"dp": core_peer}, device_id_type=MESH)
    pl.semaphore_wait(barrier, n)
    loads[0].wait()
    loads[5].wait()

    def send_up(s):
        return copy(h_all.at[s], h_all.at[s], h_up.at[s], h_recv.at[s], expert=me + B)

    def send_down(s):
        return copy(h_all.at[s], h_all.at[s], h_down.at[s], h_recv.at[s], expert=me - B)

    def send_across(s):
        return copy(h_all.at[s], h_all.at[s], h_across.at[s], h_recv.at[s], expert=partner_x)

    def p_copy(peer):
        return copy(p_in.at[peer], p_all.at[me], p_send.at[peer], p_recv.at[me], expert=peer)

    @pl.when(a < A - 1)
    def _():
        send_up(me).start()

    @pl.when(a > 0)
    def _():
        send_down(me).start()

    send_across(me).start()
    for k in range(1, n):
        p_copy((me + k) % n).start()
    for k in range(1, n):
        s = (me + k) % n
        copy(p_in.at[s], p_all.at[s], p_send.at[s], p_recv.at[s], expert=s).wait_recv()
    for load in loads[1:5]:
        load.wait()

    def recv_block(s):
        send_across(s).wait_recv()

    def pass_along(row, s):
        @pl.when((row <= a) & (a < A - 1))
        def _():
            send_up(s).start()

        @pl.when((row >= a) & (a > 0))
        def _():
            send_down(s).start()

    def take(code):
        @pl.when(code < n)
        def _():
            across = code >= A
            row = code % A
            s = row * B + jnp.where(across, 1 - b, b)
            recv_block(s)

            @pl.when(jnp.logical_not(across))
            def _():
                pass_along(row, s)

                @pl.when(((a == 0) & (row == 1)) | ((a == A - 1) & (row == A - 2)))
                def _():
                    send_across(s).start()

            @pl.when(across & ((row == 0) | (row == A - 1)))
            def _():
                pass_along(row, s)

                @pl.when((a > 0) & (a < A - 1) & ((row == 0) == (a == 1)))
                def _():
                    near = a * B + 1 - b

                    @pl.when(a == 1)
                    def _():
                        send_up(near).start()

                    @pl.when(a == A - 2)
                    def _():
                        send_down(near).start()

            @pl.when(across & (row == 1) & (a == 2))
            def _():
                send_up(s).start()

            @pl.when(across & (row == 2) & (a == 1))
            def _():
                send_down(s).start()

    def d_copy(s, slot):
        return pltpu.make_async_copy(d_stage.at[slot], d_out.at[s], d_sem.at[slot])

    def g_copy(s):
        return copy(gg_stage.at[s], gg_out.at[me], g_send.at[s], g_recv.at[me], expert=s)

    def compute(step, s, row, across):
        rows = pl.ds(pl.multiple_of(s * R, R), R)
        probs = jnp.transpose(p_all[s])
        grad_cols = []
        for e in range(2):
            gate_pre = dot_f32(h_all[s], wg[e])
            up_pre = dot_f32(h_all[s], wu[e])
            raw = dot_f32(u_all[s], wd[e])
            prob = probs[:, e : e + 1]
            sig = 1.0 / (1.0 + jnp.exp(-gate_pre))
            gate_act = gate_pre * sig
            activation = gate_act * up_pre
            grad_cols.append(jnp.sum(activation * raw, axis=1, keepdims=True))
            act[rows, e * F : (e + 1) * F] = (activation * prob).astype(jnp.bfloat16)
            act_grad = raw * prob
            gate_grad = act_grad * up_pre * sig * (1.0 + gate_pre * (1.0 - sig))
            gu[rows, 2 * e * F : (2 * e + 1) * F] = gate_grad.astype(jnp.bfloat16)
            gu[rows, (2 * e + 1) * F : (2 * e + 2) * F] = (act_grad * gate_act).astype(jnp.bfloat16)
        column = lax.broadcasted_iota(jnp.int32, (R, 128), 1)
        both = jnp.where(column == 0, grad_cols[0], jnp.where(column == 1, grad_cols[1], 0.0))
        gg_stage[s] = jnp.transpose(both)[:8]
        slot = step % 2

        @pl.when(step >= 2)
        def _():
            d_copy(s, slot).wait()

        def columns(tile, _):
            cols = pl.ds(pl.multiple_of(tile * 512, 512), 512)
            mixed = dot_f32(act[rows, 0:F], wd[0, cols, :], NT) + dot_f32(act[rows, F : 2 * F], wd[1, cols, :], NT)
            d_stage[slot, :, cols] = mixed.astype(jnp.bfloat16)
            back = dot_f32(gu[rows, 0:F], wg[0, cols, :], NT)
            back += dot_f32(gu[rows, F : 2 * F], wu[0, cols, :], NT)
            back += dot_f32(gu[rows, 2 * F : 3 * F], wg[1, cols, :], NT)
            back += dot_f32(gu[rows, 3 * F : 4 * F], wu[1, cols, :], NT)

            @pl.when(across)
            def _():
                ex[row, :, cols] = back.astype(jnp.bfloat16)

            @pl.when(jnp.logical_not(across))
            def _():
                ez[row, :, cols] = back.astype(jnp.bfloat16)

            return 0

        lax.fori_loop(0, D // 512, columns, 0)
        d_copy(s, slot).start()

        @pl.when(s != me)
        def _():
            g_copy(s).start()

        @pl.when(s == me)
        def _():
            pltpu.make_async_copy(gg_stage.at[s], gg_out.at[me], g_send.at[s]).start()

    part_rows = R // HALVES

    def part_of(part):
        return pl.ds(pl.multiple_of(part * part_rows, 16), part_rows)

    def x_copy(row, part):
        return copy(ex.at[row, part_of(part)], rx.at[row, part_of(part)], x_send.at[row, part], x_recv.at[row, part], expert=partner_x)

    def z_up(row, part):
        return copy(ez.at[row, part_of(part)], rz.at[row + 1, part_of(part)], z_send.at[row, part], z_recv.at[row + 1, part], expert=me + B)

    def z_down(row, part):
        return copy(ez.at[row, part_of(part)], rz.at[row, part_of(part)], z_send.at[row, part], z_recv.at[row, part], expert=me - B)

    def sum_part(row, part):
        x_copy(row, part).wait_recv()
        below = (a > 0) & (row >= a)
        above = (a < A - 1) & (row <= a)

        @pl.when(below)
        def _():
            z_up(row, part).wait_recv()

        @pl.when(above)
        def _():
            z_down(row, part).wait_recv()

        def chunk(index, _):
            rows = pl.ds(pl.multiple_of(part * part_rows + index * 64, 64), 64)
            total = ez[row, rows, :].astype(jnp.float32) + rx[row, rows, :].astype(jnp.float32)

            @pl.when(row != a)
            def _():
                @pl.when(below)
                def _():
                    ez[row, rows, :] = (total + rz[row + 1, rows, :].astype(jnp.float32)).astype(jnp.bfloat16)

                @pl.when(above)
                def _():
                    ez[row, rows, :] = (total + rz[row, rows, :].astype(jnp.float32)).astype(jnp.bfloat16)

                @pl.when(jnp.logical_not(below | above))
                def _():
                    ez[row, rows, :] = total.astype(jnp.bfloat16)

            @pl.when(row == a)
            def _():
                @pl.when(below & above)
                def _():
                    e_out[rows, :] = total + rz[row + 1, rows, :].astype(jnp.float32) + rz[row, rows, :].astype(jnp.float32)

                @pl.when(below & jnp.logical_not(above))
                def _():
                    e_out[rows, :] = total + rz[row + 1, rows, :].astype(jnp.float32)

                @pl.when(above & jnp.logical_not(below))
                def _():
                    e_out[rows, :] = total + rz[row, rows, :].astype(jnp.float32)

            return 0

        lax.fori_loop(0, part_rows // 64, chunk, 0)

        @pl.when(row > a)
        def _():
            z_up(row, part).start()

        @pl.when(row < a)
        def _():
            z_down(row, part).start()

    def sum_parts(row):
        def one(part, _):
            sum_part(row, part)
            return 0

        lax.fori_loop(0, HALVES, one, 0)

    def block_step(step, _):
        @pl.when((step == n - 1) & ((a == 0) | (a == A - 1)))
        def _():
            sum_parts(jnp.where(a == 0, 1, A - 2))

        take(entry(TAKE_FIRST, a, step))
        take(entry(TAKE_SECOND, a, step))
        take(entry(TAKE_THIRD, a, step))
        code = entry(BLOCK_ORDER, a, step)
        across = code >= A
        row = code % A
        s = row * B + jnp.where(across, 1 - b, b)
        compute(step, s, row, across)

        @pl.when(across)
        def _():
            for part in range(HALVES):
                x_copy(row, part).start()

        return 0

    lax.fori_loop(0, n, block_step, 0)

    def core_copy(slot, which, index):
        return copy(tile_bf.at[slot], core_got.at[which, index], c_send.at[slot], c_recv.at[which, index], dp=core_peer)

    def y_copy(slot, index):
        return pltpu.make_async_copy(tile_bf.at[slot], y_out.at[index], y_send.at[slot])

    def weight_tile(group, e, kind, left, right):
        owner = jnp.where(group == 0, 2 * (1 - y) + 1 - c, jnp.where(group == 1, y_peer, jnp.where(group == 2, core_peer, dp)))
        cols = pl.ds(pl.multiple_of(owner * shard, 128), shard)
        total = dot_f32(left[:, :, cols].reshape(n * R, shard), right, TN)
        index = kind * 2 + e
        slot = kind

        @pl.when((group == 0) | (group == 2))
        def _():
            @pl.when(e > 0)
            def _():
                core_copy(slot, 0, index).wait_send()

            @pl.when((e == 0) & (group == 2))
            def _():
                y_copy(slot, index).wait()

            tile_bf[slot] = total.astype(jnp.bfloat16)
            core_copy(slot, group // 2, index).start()

        @pl.when(group == 1)
        def _():
            @pl.when(e == 0)
            def _():
                core_copy(slot, 0, index).wait_send()

            @pl.when(e > 0)
            def _():
                y_copy(slot, index).wait()

            core_copy(slot, 0, index).wait_recv()
            got = pltpu.make_async_copy(core_got.at[0, index], got_tile, tile_sem)
            got.start()
            got.wait()
            tile_bf[slot] = (total + got_tile[...].astype(jnp.float32)).astype(jnp.bfloat16)
            y_copy(slot, index).start()

        @pl.when(group == 3)
        def _():
            core_copy(slot, 1, index).wait_recv()
            got = pltpu.make_async_copy(core_got.at[1, index], got_tile, tile_sem)
            got.start()
            got.wait()
            tile_f32[index] = total + got_tile[...].astype(jnp.float32)
            pltpu.make_async_copy(tile_f32.at[index], grads_out.at[index], out_sem.at[index]).start()

    def sum_step(place, _):
        row = entry(SUM_ORDER, a, place)

        @pl.when(row < A)
        def _():
            sum_parts(row)

        @pl.when(place < 4)
        def _():
            def pair(e, _):
                weight_tile(place, e, 0, h_all, gu[:, pl.ds(pl.multiple_of(2 * e * F, 128), F)])
                weight_tile(place, e, 1, h_all, gu[:, pl.ds(pl.multiple_of((2 * e + 1) * F, 128), F)])
                weight_tile(place, e, 2, u_all, act[:, pl.ds(pl.multiple_of(e * F, 128), F)])
                return 0

            lax.fori_loop(0, 2, pair, 0)

        return 0

    lax.fori_loop(0, 5, sum_step, 0)

    for kind in range(3):
        core_copy(kind, 1, 3 + kind).wait_send()
    for row in range(A):
        for part in range(HALVES):
            x_copy(row, part).wait_send()

            @pl.when(row != a)
            def _():
                z_up(row, part).wait_send()

    for row in range(A):
        s = row * B + b
        far = row * B + 1 - b

        @pl.when((row <= a) & (a < A - 1))
        def _():
            send_up(s).wait_send()

        @pl.when((row >= a) & (a > 0))
        def _():
            send_down(s).wait_send()

        @pl.when((row <= a) & (a < A - 1) & (row < A - 2))
        def _():
            send_up(far).wait_send()

        @pl.when((row >= a) & (a > 0) & (row > 1))
        def _():
            send_down(far).wait_send()

        @pl.when((row == a) | ((a == 0) & (row == 1)) | ((a == A - 1) & (row == A - 2)))
        def _():
            send_across(s).wait_send()

    for k in range(1, n):
        s = (me + k) % n
        p_copy(s).wait_send()
        g_copy(s).wait_send()
        copy(gg_stage.at[s], gg_out.at[s], g_send.at[s], g_recv.at[s], expert=s).wait_recv()
    pltpu.make_async_copy(gg_stage.at[me], gg_out.at[me], g_send.at[me]).wait()
    for slot in range(2):
        d_copy(0, slot).wait()
    for index in range(6):
        pltpu.make_async_copy(tile_f32.at[index], grads_out.at[index], out_sem.at[index]).wait()


def moe_call(hidden, all_upstream, probs, expert_gate, expert_up, expert_down):
    R, D = hidden.shape
    F = expert_gate.shape[2]
    A, n = 4, 8
    shard = D // 4
    bf, f32 = jnp.bfloat16, jnp.float32
    any_spec = pl.BlockSpec(memory_space=pl.ANY)
    vmem = pl.BlockSpec(memory_space=pltpu.VMEM)
    dma = pltpu.SemaphoreType.DMA
    out_shape = (
        jax.ShapeDtypeStruct((n, R, D), bf),
        jax.ShapeDtypeStruct((R, D), f32),
        jax.ShapeDtypeStruct((n, 8, R), f32),
        jax.ShapeDtypeStruct((6, shard, F), f32),
        jax.ShapeDtypeStruct((2, 6, shard, F), bf),
        jax.ShapeDtypeStruct((6, shard, F), bf),
    )
    return pl.pallas_call(
        functools.partial(moe_kernel, comm=True),
        out_shape=out_shape,
        in_specs=[any_spec] * 6,
        out_specs=(any_spec, vmem, any_spec, any_spec, any_spec, any_spec),
        scratch_shapes=[
            pltpu.VMEM((n, R, D), bf),
            pltpu.VMEM((n, R, D), bf),
            pltpu.VMEM((n, 8, R), f32),
            pltpu.VMEM((2, D, F), bf),
            pltpu.VMEM((2, D, F), bf),
            pltpu.VMEM((2, D, F), bf),
            pltpu.VMEM((n * R, 2 * F), bf),
            pltpu.VMEM((n * R, 4 * F), bf),
            pltpu.VMEM((A, R, D), bf),
            pltpu.VMEM((A, R, D), bf),
            pltpu.VMEM((A, R, D), bf),
            pltpu.VMEM((A + 1, R, D), bf),
            pltpu.VMEM((2, R, D), bf),
            pltpu.VMEM((n, 8, R), f32),
            pltpu.VMEM((3, shard, F), bf),
            pltpu.VMEM((6, shard, F), f32),
            pltpu.VMEM((shard, F), bf),
            dma((6,)), dma((n,)), dma((n,)), dma((n,)), dma((n,)), dma((n,)), dma((n,)), dma((n,)), dma((n,)),
            dma((A, HALVES)), dma((A, HALVES)), dma((A, HALVES)), dma((A + 1, HALVES)), dma((2,)),
            dma((3,)), dma((2, 6)), dma((3,)), dma, dma((6,)),
        ],
        compiler_params=pltpu.CompilerParams(
            collective_id=1, has_side_effects=True, vmem_limit_bytes=64 * 1024 * 1024 - 65536
        ),
        cost_estimate=pl.CostEstimate(flops=58 * 10**9, bytes_accessed=60 * 10**6, transcendentals=2 * 10**6),
        name="experts",
    )(hidden, all_upstream, probs, expert_gate, expert_up, expert_down)


def reduce_kernel(
    left, right, extra, out,
    core_out, core_in, y_out, y_in, half, x_out, x_in, own, z_out, z_in, full,
    core_send, core_recv, y_send, y_recv, x_send, x_recv, zs_send, zs_recv, zg_send, zg_recv, xg_send, xg_recv,
):
    A, B = 4, 2
    W = core_out.shape[3]
    shard = core_out.shape[2]
    half_rows, piece = shard // B, shard // (A * B)
    chunks = y_in.shape[0]
    me = lax.axis_index("expert")
    dp = lax.axis_index("dp")
    a, b = me // B, me % B
    y, c = dp // 2, dp % 2
    partner_x = a * B + (1 - b)
    core_peer = 2 * y + (1 - c)
    y_peer = 2 * (1 - y) + c

    def copy(src, dst, send, recv, **target):
        return pltpu.make_async_remote_copy(
            src_ref=src, dst_ref=dst, send_sem=send, recv_sem=recv, device_id=target, device_id_type=MESH
        )

    barrier = pltpu.get_barrier_semaphore()
    for target in [{"dp": core_peer}, {"dp": y_peer}, {"expert": partner_x}] + [
        {"expert": (a + k) % A * B + b} for k in range(1, A)
    ]:
        pl.semaphore_signal(barrier, inc=1, device_id=target, device_id_type=MESH)
    pl.semaphore_wait(barrier, 2 + A)

    def partial(chunk, owner):
        rows = pl.ds(pl.multiple_of(owner * shard, 128), shard)
        cols = pl.ds(pl.multiple_of(chunk * W, 128), W)
        which = jnp.where(chunk < 4, 0, 1)
        total = dot_f32(left[which, :, rows], right[:, cols], TN)
        share = extra[pl.ds(pl.multiple_of(owner * shard, 128), shard), :].astype(jnp.float32)
        share = jnp.where(chunk == chunks - 1, share, 0.0)
        return jnp.concatenate([total[:, : W - 128], total[:, W - 128 :] + share], axis=1)

    def core_copy(chunk, which):
        slot = chunk % 2
        return copy(core_out.at[slot, which], core_in.at[chunk, which], core_send.at[slot, which], core_recv.at[chunk, which], dp=core_peer)

    def y_copy(chunk):
        slot = chunk % 2
        return copy(y_out.at[slot], y_in.at[chunk], y_send.at[slot], y_recv.at[chunk], dp=y_peer)

    def x_copy(chunk):
        slot = chunk % 2
        return copy(x_out.at[slot], x_in.at[chunk], x_send.at[slot], x_recv.at[chunk], expert=partner_x)

    def z_scatter(chunk, to, source):
        slot = chunk % 2
        return copy(
            z_out.at[slot, pl.ds(pl.multiple_of(to * piece, 16), piece)], z_in.at[chunk, source],
            zs_send.at[slot, to], zs_recv.at[chunk, source], expert=to * B + b,
        )

    def z_gather(chunk, to, source):
        rows = pl.ds(pl.multiple_of(b * half_rows + source * piece, 16), piece)
        return copy(full.at[chunk, rows], full.at[chunk, rows], zg_send.at[chunk, to], zg_recv.at[chunk, source], expert=to * B + b)

    def x_gather(chunk, side):
        rows = pl.ds(pl.multiple_of(side * half_rows, 16), half_rows)
        return copy(full.at[chunk, rows], full.at[chunk, rows], xg_send.at[chunk], xg_recv.at[chunk], expert=partner_x)

    def to_core(chunk):
        for which, owner in ((0, core_peer), (1, 2 * (1 - y) + 1 - c)):
            value = partial(chunk, owner).astype(jnp.bfloat16)

            @pl.when(chunk >= 2)
            def _():
                core_copy(chunk, which).wait_send()

            core_out[chunk % 2, which] = value
            core_copy(chunk, which).start()

    def to_y(chunk):
        value = partial(chunk, y_peer)
        core_copy(chunk, 1).wait_recv()

        @pl.when(chunk >= 2)
        def _():
            y_copy(chunk).wait_send()

        y_out[chunk % 2] = (value + core_in[chunk, 1].astype(jnp.float32)).astype(jnp.bfloat16)
        y_copy(chunk).start()

    def to_x(chunk):
        value = partial(chunk, dp)
        core_copy(chunk, 0).wait_recv()
        y_copy(chunk).wait_recv()
        value = value + core_in[chunk, 0].astype(jnp.float32) + y_in[chunk].astype(jnp.float32)

        @pl.when(chunk >= 2)
        def _():
            x_copy(chunk).wait_send()

        low, high = value[:half_rows], value[half_rows:]
        half[chunk % 2] = jnp.where(b == 0, low, high)
        x_out[chunk % 2] = jnp.where(b == 0, high, low).astype(jnp.bfloat16)
        x_copy(chunk).start()

    def to_z(chunk):
        x_copy(chunk).wait_recv()

        @pl.when(chunk >= 2)
        def _():
            for k in range(1, A):
                z_scatter(chunk, (a + k) % A, a).wait_send()

        total = half[chunk % 2] + x_in[chunk].astype(jnp.float32)
        half[chunk % 2] = total
        own[chunk % 2] = half[chunk % 2, pl.ds(pl.multiple_of(a * piece, 8), piece)]
        z_out[chunk % 2] = total.astype(jnp.bfloat16)
        for k in range(1, A):
            z_scatter(chunk, (a + k) % A, a).start()

    def spread_z(chunk):
        total = own[chunk % 2]
        for k in range(1, A):
            source = (a + k) % A
            z_scatter(chunk, a, source).wait_recv()
            total = total + z_in[chunk, source].astype(jnp.float32)
        rows = pl.ds(pl.multiple_of(b * half_rows + a * piece, 16), piece)
        full[chunk, rows] = total.astype(jnp.bfloat16)
        for k in range(1, A):
            z_gather(chunk, (a + k) % A, a).start()

    def spread_x(chunk):
        for k in range(1, A):
            z_gather(chunk, a, (a + k) % A).wait_recv()
        x_gather(chunk, b).start()

    def finish(chunk):
        x_gather(chunk, 1 - b).wait_recv()
        cols = pl.ds(pl.multiple_of(chunk * W, 128), W)
        out[:, cols] = full[chunk].astype(jnp.float32)

    stages = (to_core, to_y, to_x, to_z, spread_z, spread_x, finish)

    def step(t, _):
        for delay, stage in enumerate(stages):
            @pl.when((t >= delay) & (t < delay + chunks))
            def _():
                stage(t - delay)

        return 0

    lax.fori_loop(0, chunks + len(stages) - 1, step, 0)

    for chunk in range(chunks - 2, chunks):
        core_copy(chunk, 0).wait_send()
        core_copy(chunk, 1).wait_send()
        y_copy(chunk).wait_send()
        x_copy(chunk).wait_send()
        for k in range(1, A):
            z_scatter(chunk, (a + k) % A, a).wait_send()

    def drain(chunk, _):
        for k in range(1, A):
            z_gather(chunk, (a + k) % A, a).wait_send()
        x_gather(chunk, b).wait_send()
        return 0

    lax.fori_loop(0, chunks, drain, 0)


def reduce_call(left, right, extra):
    D = left.shape[2]
    width = right.shape[1]
    W, A, B = 384, 4, 2
    shard, chunks = D // 4, width // W
    bf, f32 = jnp.bfloat16, jnp.float32
    vmem = pl.BlockSpec(memory_space=pltpu.VMEM)
    dma = pltpu.SemaphoreType.DMA
    piece = shard // (A * B)
    return pl.pallas_call(
        reduce_kernel,
        out_shape=jax.ShapeDtypeStruct((shard, width), f32),
        in_specs=[vmem] * 3,
        out_specs=vmem,
        scratch_shapes=[
            pltpu.VMEM((2, 2, shard, W), bf),
            pltpu.VMEM((chunks, 2, shard, W), bf),
            pltpu.VMEM((2, shard, W), bf),
            pltpu.VMEM((chunks, shard, W), bf),
            pltpu.VMEM((2, shard // B, W), f32),
            pltpu.VMEM((2, shard // B, W), bf),
            pltpu.VMEM((chunks, shard // B, W), bf),
            pltpu.VMEM((2, piece, W), f32),
            pltpu.VMEM((2, shard // B, W), bf),
            pltpu.VMEM((chunks, A, piece, W), bf),
            pltpu.VMEM((chunks, shard, W), bf),
            dma((2, 2)), dma((chunks, 2)), dma((2,)), dma((chunks,)), dma((2,)), dma((chunks,)),
            dma((2, A)), dma((chunks, A)), dma((chunks, A)), dma((chunks, A)), dma((chunks,)), dma((chunks,)),
        ],
        compiler_params=pltpu.CompilerParams(
            collective_id=2, has_side_effects=True, vmem_limit_bytes=56 * 1024 * 1024
        ),
        cost_estimate=pl.CostEstimate(flops=4 * 10**9, bytes_accessed=20 * 10**6, transcendentals=0),
        name="weight_sums",
    )(left, right, extra)


def front_kernel(
    lengths, tokens, routes, w_gain, w_small, w_q, w_k, w_v, w_o, u_in,
    out_gain, out_small, out_q, out_k, out_v, out_o, u_all,
    hidden_one, qkv, attended, log_total, cos_out, sin_out, residual, hidden_two, probs_out, by_owner,
    all_gain, all_small, all_q, all_k, all_v, all_o, sums, q_heads, k_heads, v_heads, mixed,
    keep_sem, core_send, y_send, pass_send, w_recv, u_keep, u_up, u_down, u_across, u_recv,
):
    A, B = 4, 2
    R, D = tokens.shape
    shard = D // 4
    me = lax.axis_index("expert")
    dp = lax.axis_index("dp")
    a, b = me // B, me % B
    y, c = dp // 2, dp % 2
    partner_x = a * B + (1 - b)
    core_peer = 2 * y + (1 - c)
    y_peer = 2 * (1 - y) + c
    far_peer = 2 * (1 - y) + 1 - c
    shards = (w_gain, w_small, w_q, w_k, w_v, w_o)
    landed = (all_gain, all_small, all_q, all_k, all_v, all_o)
    kept = (out_gain, out_small, out_q, out_k, out_v, out_o)
    count = len(shards)
    GAIN, SMALL, QUERY, KEY, VALUE, OUTPUT = range(count)

    def copy(src, dst, send, recv, **target):
        return pltpu.make_async_remote_copy(
            src_ref=src, dst_ref=dst, send_sem=send, recv_sem=recv, device_id=target, device_id_type=MESH
        )

    barrier = pltpu.get_barrier_semaphore()
    for target in [{"dp": core_peer}, {"dp": y_peer}, {"expert": partner_x}] + [
        {"expert": (a + k) % A * B + b} for k in range(1, A)
    ]:
        pl.semaphore_signal(barrier, inc=1, device_id=target, device_id_type=MESH)
    pl.semaphore_wait(barrier, 2 + A)

    def to_core(i):
        return copy(shards[i], landed[i].at[dp], core_send.at[i], w_recv.at[i, dp], dp=core_peer)

    def to_y(i):
        return copy(shards[i], landed[i].at[dp], y_send.at[i], w_recv.at[i, dp], dp=y_peer)

    def pass_on(i):
        return copy(landed[i].at[y_peer], landed[i].at[y_peer], pass_send.at[i], w_recv.at[i, y_peer], dp=core_peer)

    def keep_own(i):
        return pltpu.make_async_copy(shards[i], kept[i].at[dp], keep_sem.at[i, dp])

    def keep(i, owner):
        return pltpu.make_async_copy(landed[i].at[owner], kept[i].at[owner], keep_sem.at[i, owner])

    def receive(i, owner):
        copy(shards[i], landed[i].at[owner], core_send.at[i], w_recv.at[i, owner], dp=core_peer).wait_recv()
        keep(i, owner).start()

    def forward(i):
        receive(i, y_peer)
        pass_on(i).start()

    def u_send_up(src, s):
        return copy(src, u_all.at[s], u_up.at[s], u_recv.at[s], expert=me + B)

    def u_send_down(src, s):
        return copy(src, u_all.at[s], u_down.at[s], u_recv.at[s], expert=me - B)

    def u_send_across(src, s):
        return copy(src, u_all.at[s], u_across.at[s], u_recv.at[s], expert=partner_x)

    def take(row):
        @pl.when((row >= 0) & (row < A))
        def _():
            s = row * B + b
            u_send_across(u_all.at[s], s).wait_recv()
            u_send_across(u_all.at[s], s).start()

            @pl.when((row < a) & (a < A - 1))
            def _():
                u_send_up(u_all.at[s], s).start()

            @pl.when((row > a) & (a > 0))
            def _():
                u_send_down(u_all.at[s], s).start()

    keep_u = pltpu.make_async_copy(u_in, u_all.at[me], u_keep)

    @pl.when(a < A - 1)
    def _():
        u_send_up(u_in, me).start()

    @pl.when(a > 0)
    def _():
        u_send_down(u_in, me).start()

    u_send_across(u_in, me).start()
    for i in range(count):
        to_y(i).start()
        to_core(i).start()
        keep_own(i).start()
    keep_u.start()

    row_index = lax.broadcasted_iota(jnp.int32, (R, 128), 0)
    ends = (lengths[0, 0], lengths[0, 0] + lengths[0, 1], lengths[0, 0] + lengths[0, 1] + lengths[0, 2])
    start = jnp.where(row_index >= ends[2], ends[2], jnp.where(row_index >= ends[1], ends[1], jnp.where(row_index >= ends[0], ends[0], 0)))
    position = (row_index - start).astype(jnp.float32)
    lane = lax.broadcasted_iota(jnp.int32, (R, 128), 1)
    pair = (lane % (HD // 2)).astype(jnp.float32)
    frequency = jnp.exp(pair * (-2.0 / HD * math.log(rope_base)))
    angle = position * frequency
    front = lane % HD < HD // 2
    cos_out[...] = jnp.cos(angle)
    sin_out[...] = jnp.where(front, -jnp.sin(angle), jnp.sin(angle))

    def doc_of(index):
        total = 0
        for end in ends:
            total = total + jnp.where(index >= end, 1, 0)
        return total

    rows_t = lax.broadcasted_iota(jnp.int32, (R, R), 0)
    rows_u = lax.broadcasted_iota(jnp.int32, (R, R), 1)
    allowed = (doc_of(rows_t) == doc_of(rows_u)) & (rows_u <= rows_t)

    inputs = tokens[...].astype(jnp.float32)
    scale_one = lax.rsqrt(jnp.mean(inputs * inputs, axis=1, keepdims=True) + eps)

    forward(GAIN)
    receive(GAIN, core_peer)
    receive(GAIN, far_peer)
    all_gain[dp] = w_gain[...]
    for j in range(4):
        cols = slice(j * shard, (j + 1) * shard)
        gain = all_gain[j, 0:1, :].astype(jnp.float32)
        hidden_one[:, cols] = (inputs[:, cols] * scale_one * gain).astype(jnp.bfloat16)

    offsets = {QUERY: 0, KEY: D, VALUE: D + KVH * HD}
    sums[...] = jnp.zeros_like(sums)

    def product(i, owner, own=False):
        cols = pl.ds(pl.multiple_of(owner * shard, 128), shard)
        left = hidden_one[:, cols]
        width = shards[i].shape[1]

        def tile(t, _):
            into = pl.ds(pl.multiple_of(offsets[i] + t * 512, 128), 512)
            part = pl.ds(pl.multiple_of(t * 512, 128), 512)
            weight = shards[i][:, part] if own else landed[i][owner, :, part]
            sums[:, into] += dot_f32(left, weight)
            return 0

        lax.fori_loop(0, width // 512, tile, 0)

    for i in (QUERY, KEY, VALUE):
        product(i, dp, own=True)
    for i in (QUERY, KEY, VALUE):
        receive(i, core_peer)
        product(i, core_peer)
    take(a - 1)
    take(a + 1)
    forward(SMALL)
    receive(SMALL, core_peer)
    forward(QUERY)
    product(QUERY, y_peer)
    receive(QUERY, far_peer)
    product(QUERY, far_peer)
    take(a - 2)
    take(a + 2)
    forward(KEY)
    product(KEY, y_peer)
    receive(KEY, far_peer)
    product(KEY, far_peer)
    forward(VALUE)
    product(VALUE, y_peer)
    receive(VALUE, far_peer)
    product(VALUE, far_peer)

    def rotated(columns):
        value = sums[:, columns]
        other = jnp.where(front, pltpu.roll(value, 128 - HD // 2, 1), pltpu.roll(value, HD // 2, 1))
        return (value * cos_out[...] + other * sin_out[...]).astype(jnp.bfloat16)

    for pair_index in range(QH // 2):
        columns = slice(pair_index * 128, (pair_index + 1) * 128)
        value = rotated(columns)
        qkv[:, columns] = value
        q_heads[2 * pair_index] = value[:, :HD]
        q_heads[2 * pair_index + 1] = value[:, HD:]
    for pair_index in range(KVH // 2):
        columns = slice(D + pair_index * 128, D + (pair_index + 1) * 128)
        value = rotated(columns)
        qkv[:, columns] = value
        k_heads[2 * pair_index] = value[:, :HD]
        k_heads[2 * pair_index + 1] = value[:, HD:]
        columns = slice(D + KVH * HD + pair_index * 128, D + KVH * HD + (pair_index + 1) * 128)
        value = sums[:, columns].astype(jnp.bfloat16)
        qkv[:, columns] = value
        v_heads[2 * pair_index] = value[:, :HD]
        v_heads[2 * pair_index + 1] = value[:, HD:]
    log_total[...] = jnp.zeros_like(log_total)

    def group_step(g, _):
        for k in range(QH // KVH):
            head = g * (QH // KVH) + k
            scores = dot_f32(q_heads[head], k_heads[g], NT) * HD**-0.5
            scores = jnp.where(allowed, scores, masked_score)
            top = jnp.max(scores, axis=1, keepdims=True)
            terms = jnp.exp(scores - top)
            total = jnp.sum(terms, axis=1, keepdims=True)
            low = (terms / total).astype(jnp.bfloat16)
            mixed[head] = dot_f32(low, v_heads[g]).astype(jnp.bfloat16)
            log_total[...] += jnp.where(lane == head, top + jnp.log(total), 0.0)
        return 0

    lax.fori_loop(0, KVH, group_step, 0)
    take(a - 3)
    take(a + 3)
    for pair_index in range(QH // 2):
        attended[:, pair_index * 128 : (pair_index + 1) * 128] = jnp.concatenate(
            [mixed[2 * pair_index], mixed[2 * pair_index + 1]], axis=1
        )

    residual[...] = inputs

    def out_product(owner, own=False):
        cols = pl.ds(pl.multiple_of(owner * shard, 128), shard)
        left = attended[:, cols]

        def tile(t, _):
            part = pl.ds(pl.multiple_of(t * 512, 128), 512)
            weight = w_o[:, part] if own else all_o[owner, :, part]
            residual[:, part] += dot_f32(left, weight)
            return 0

        lax.fori_loop(0, D // 512, tile, 0)

    out_product(dp, own=True)
    receive(OUTPUT, core_peer)
    out_product(core_peer)
    receive(SMALL, far_peer)
    all_small[dp] = w_small[...]
    forward(OUTPUT)
    out_product(y_peer)
    receive(OUTPUT, far_peer)
    out_product(far_peer)

    whole = residual[...]
    scale_two = lax.rsqrt(jnp.mean(whole * whole, axis=1, keepdims=True) + eps)
    logits = jnp.zeros((R, 128), jnp.float32)
    for j in range(4):
        cols = slice(j * shard, (j + 1) * shard)
        gain = all_gain[j, 1:2, :].astype(jnp.float32)
        value = (whole[:, cols] * scale_two * gain).astype(jnp.bfloat16)
        hidden_two[:, cols] = value
        logits = logits + dot_f32(value, all_small[j])
    chosen = lane == routes[:, 0:1]
    for j in range(1, TOP):
        chosen = chosen | (lane == routes[:, j : j + 1])
    logits = jnp.where(chosen, logits, masked_score)
    terms = jnp.where(chosen, jnp.exp(logits - jnp.max(logits, axis=1, keepdims=True)), 0.0)
    probs = terms / jnp.sum(terms, axis=1, keepdims=True)
    probs_out[...] = probs
    turned = jnp.transpose(probs)
    by_owner[...] = jnp.zeros_like(by_owner)
    local = 2
    for owner in range(A * B):
        by_owner[owner, 0:local, :] = turned[owner * local : (owner + 1) * local]

    for row in range(A):
        s = row * B + 1 - b
        u_send_across(u_all.at[s], s).wait_recv()
    for i in range(count):
        keep_own(i).wait()
        for owner in (core_peer, y_peer, far_peer):
            keep(i, owner).wait()
        to_y(i).wait_send()
        to_core(i).wait_send()
        pass_on(i).wait_send()
    keep_u.wait()

    @pl.when(a < A - 1)
    def _():
        u_send_up(u_in, me).wait_send()

    @pl.when(a > 0)
    def _():
        u_send_down(u_in, me).wait_send()

    for row in range(A):
        s = row * B + b
        u_send_across(u_all.at[s], s).wait_send()

        @pl.when((row < a) & (a < A - 1))
        def _():
            u_send_up(u_all.at[s], s).wait_send()

        @pl.when((row > a) & (a > 0))
        def _():
            u_send_down(u_all.at[s], s).wait_send()


def front_call(seq_lengths, tokens, routes, gains, small, w_query, w_key, w_value, w_output, out_grad):
    n = 8
    R, D = tokens.shape
    bf, f32 = jnp.bfloat16, jnp.float32
    any_spec = pl.BlockSpec(memory_space=pl.ANY)
    vmem = pl.BlockSpec(memory_space=pltpu.VMEM)
    dma = pltpu.SemaphoreType.DMA
    shards = (gains, small, w_query, w_key, w_value, w_output)
    whole = w_query.shape[1] + w_key.shape[1] + w_value.shape[1]
    return pl.pallas_call(
        front_kernel,
        out_shape=tuple(jax.ShapeDtypeStruct((4, *w.shape), bf) for w in shards)
        + (
            jax.ShapeDtypeStruct((n, R, D), bf),
            jax.ShapeDtypeStruct((R, D), bf),
            jax.ShapeDtypeStruct((R, whole), bf),
            jax.ShapeDtypeStruct((R, D), bf),
            jax.ShapeDtypeStruct((R, 128), f32),
            jax.ShapeDtypeStruct((R, 128), f32),
            jax.ShapeDtypeStruct((R, 128), f32),
            jax.ShapeDtypeStruct((R, D), f32),
            jax.ShapeDtypeStruct((R, D), bf),
            jax.ShapeDtypeStruct((R, 128), f32),
            jax.ShapeDtypeStruct((n, 8, R), f32),
        ),
        in_specs=[pl.BlockSpec(memory_space=pltpu.SMEM)] + [vmem] * 9,
        out_specs=(any_spec,) * 7 + (vmem,) * 10,
        scratch_shapes=[pltpu.VMEM((4, *w.shape), bf) for w in shards]
        + [
            pltpu.VMEM((R, whole), f32),
            pltpu.VMEM((QH, R, HD), bf),
            pltpu.VMEM((KVH, R, HD), bf),
            pltpu.VMEM((KVH, R, HD), bf),
            pltpu.VMEM((QH, R, HD), bf),
            dma((6, 4)), dma((6,)), dma((6,)), dma((6,)), dma((6, 4)), dma, dma((n,)), dma((n,)), dma((n,)), dma((n,)),
        ],
        compiler_params=pltpu.CompilerParams(
            collective_id=3, has_side_effects=True, vmem_limit_bytes=60 * 1024 * 1024
        ),
        cost_estimate=pl.CostEstimate(flops=4 * 10**9, bytes_accessed=40 * 10**6, transcendentals=2 * 10**6),
        name="front",
    )(seq_lengths, tokens, routes, *shards, out_grad)


def fused_body(
    tokens,
    seq_lengths,
    routes,
    w_query,
    w_key,
    w_value,
    w_output,
    w_router,
    attn_gain,
    moe_gain,
    expert_gate,
    expert_up,
    expert_down,
    out_grad,
):
    row_count, width = tokens.shape
    expert_count = w_router.shape[1]
    local_count = expert_gate.shape[0]
    group_size = QH // KVH
    score_scale = HD ** (-0.5)
    gains = jnp.pad(jnp.stack([attn_gain, moe_gain]), ((0, 14), (0, 0)))
    small = jnp.pad(w_router, ((0, 0), (0, 128 - expert_count)))
    (
        gains, small, query_w, key_w, value_w, output_w, all_upstream,
        hidden_one, qkv, attended, log_total, cos_table, sin_table, residual, hidden_two, probs, by_owner,
    ) = front_call(seq_lengths, tokens, routes, gains, small, w_query, w_key, w_value, w_output, out_grad)
    query_w, key_w, value_w, output_w = [w.reshape(-1, w.shape[2]) for w in (query_w, key_w, value_w, output_w)]
    gain_one, gain_two = gains[:, 0].reshape(-1), gains[:, 1].reshape(-1)
    router_w = small.reshape(width, -1)

    mix_part, row_sum, grad_rows, own_grads, _, far_grads = moe_call(
        hidden_two, all_upstream, by_owner, expert_gate, expert_up, expert_down
    )
    far_grads = lax.ppermute(far_grads, "dp", [(0, 2), (1, 3), (2, 0), (3, 1)])
    mixture = lax.psum_scatter(mix_part.reshape(-1, width), "expert", scatter_dimension=0, tiled=True)

    inputs = tokens.astype(jnp.float32)
    upstream = out_grad.astype(jnp.float32)
    scale_one = rms_scale(inputs)
    normed_one = inputs * scale_one
    scale_two = rms_scale(residual)
    normed_two = residual * scale_two
    grad_dense = grad_rows[:, :local_count].reshape(expert_count, row_count).T
    dense = probs[:, :expert_count]
    logit_grad = (dense * (grad_dense - jnp.sum(dense * grad_dense, axis=-1, keepdims=True))).astype(jnp.bfloat16)
    logit_grad = jnp.pad(logit_grad, ((0, 0), (0, 128 - expert_count)))
    hidden_two_grad = row_sum + jnp.dot(logit_grad, router_w.T, preferred_element_type=jnp.float32)
    gain_two_partial = jnp.sum(hidden_two_grad * normed_two, axis=0)
    normed_two_grad = hidden_two_grad * gain_two.astype(jnp.float32)
    residual_grad = upstream + scale_two * (
        normed_two_grad - normed_two * jnp.mean(normed_two_grad * normed_two, axis=-1, keepdims=True)
    )
    branch_grad = residual_grad.astype(jnp.bfloat16)
    attended_grad = jnp.dot(branch_grad, output_w.T, preferred_element_type=jnp.float32).astype(jnp.bfloat16)

    doc_id, _ = token_layout(seq_lengths[0], row_count)
    token_index = jnp.arange(row_count, dtype=jnp.int32)
    allowed = (doc_id[:, None] == doc_id[None, :]) & (token_index[None, :] <= token_index[:, None])
    query_heads = qkv[:, : QH * HD].reshape(row_count, KVH, group_size, HD)
    key_heads = qkv[:, QH * HD : (QH + KVH) * HD].reshape(row_count, KVH, HD)
    value_heads = qkv[:, (QH + KVH) * HD :].reshape(row_count, KVH, HD)
    scores = jnp.einsum("tkgd,ukd->kgtu", query_heads, key_heads, preferred_element_type=jnp.float32) * score_scale
    scores = jnp.where(allowed, scores, masked_score)
    log_heads = log_total[:, :QH].T.reshape(KVH, group_size, row_count, 1)
    attn_probs = jnp.exp(scores - log_heads)
    probs_low = attn_probs.astype(jnp.bfloat16)
    grad_heads = attended_grad.reshape(row_count, KVH, group_size, HD)
    prob_grad = jnp.einsum("tkgd,ukd->kgtu", grad_heads, value_heads, preferred_element_type=jnp.float32)
    score_grad = (
        attn_probs * (prob_grad - jnp.sum(attn_probs * prob_grad, axis=-1, keepdims=True))
    ).astype(jnp.bfloat16)
    query_sums = (
        jnp.einsum("kgtu,ukd->tkgd", score_grad, key_heads, preferred_element_type=jnp.float32) * score_scale
    )
    key_sums = (
        jnp.einsum("kgtu,tkgd->ukd", score_grad, query_heads, preferred_element_type=jnp.float32) * score_scale
    )
    value_sums = jnp.einsum("kgtu,tkgd->ukd", probs_low, grad_heads, preferred_element_type=jnp.float32)
    half_size = HD // 2
    cosines, sines = cos_table[:, None, :half_size], sin_table[:, None, half_size:HD]
    query_grad = unrotate(query_sums.reshape(row_count, QH * HD), cosines, sines, QH).astype(jnp.bfloat16)
    key_grad = unrotate(key_sums.reshape(row_count, KVH * HD), cosines, sines, KVH).astype(jnp.bfloat16)
    value_grad = value_sums.reshape(row_count, KVH * HD).astype(jnp.bfloat16)
    hidden_one_grad = jnp.dot(query_grad, query_w.T, preferred_element_type=jnp.float32)
    hidden_one_grad = hidden_one_grad + jnp.dot(key_grad, key_w.T, preferred_element_type=jnp.float32)
    hidden_one_grad = hidden_one_grad + jnp.dot(value_grad, value_w.T, preferred_element_type=jnp.float32)
    gain_one_partial = jnp.sum(hidden_one_grad * normed_one, axis=0)
    normed_one_grad = hidden_one_grad * gain_one.astype(jnp.float32)
    in_grad = residual_grad + scale_one * (
        normed_one_grad - normed_one * jnp.mean(normed_one_grad * normed_one, axis=-1, keepdims=True)
    )
    router_partial = jnp.dot(hidden_two.T, logit_grad, preferred_element_type=jnp.float32)
    column = jnp.arange(128, dtype=jnp.int32)[None, :]
    extra = jnp.where(
        column == expert_count,
        gain_one_partial[:, None],
        jnp.where(column == expert_count + 1, gain_two_partial[:, None], router_partial),
    ).astype(jnp.bfloat16)
    zero_columns = jnp.zeros((row_count, 128), jnp.bfloat16)
    sums = reduce_call(
        jnp.stack([attended, hidden_one]),
        jnp.concatenate([branch_grad, query_grad, key_grad, value_grad, zero_columns], axis=1),
        extra,
    )
    wide, narrow = QH * HD, KVH * HD
    cuts = (0, wide, 2 * wide, 2 * wide + narrow, 2 * wide + 2 * narrow)
    of_output, of_query, of_key, of_value = [sums[:, i:j] for i, j in zip(cuts, cuts[1:])]
    tail = sums[:, cuts[-1] :]
    far_grads, residual, _ = lax.optimization_barrier((far_grads, residual, of_query))
    expert_grads = own_grads + far_grads.astype(jnp.float32)
    layer_out = (residual + mixture.astype(jnp.float32)).astype(jnp.bfloat16)
    return (
        layer_out,
        in_grad,
        of_query,
        of_key,
        of_value,
        of_output,
        tail[:, :expert_count],
        tail[:, expert_count],
        tail[:, expert_count + 1],
        *[expert_grads[2 * kind : 2 * kind + 2] for kind in range(3)],
    )


def fits_fused(mesh, tokens_shape):
    devices = mesh.shape["dp"] * mesh.shape["expert"]
    return mesh.shape["dp"] == 4 and mesh.shape["expert"] == 8 and tokens_shape[0] == 256 * devices


def solution(mesh):
    placed = (
        P(("dp", "expert"), None),
        P(("dp", "expert"), None),
        P(("dp", "expert"), None),
        P("dp", None),
        P("dp", None),
        P("dp", None),
        P("dp", None),
        P("dp", None),
        P("dp"),
        P("dp"),
        P("expert", None, None),
        P("expert", None, None),
        P("expert", None, None),
        P(("dp", "expert"), None),
    )
    def layer(tokens, *rest):
        return shard(fused_body if fits_fused(mesh, tokens.shape) else body)(tokens, *rest)

    def shard(step):
        return jax.shard_map(
            step,
            mesh=mesh,
            in_specs=placed,
            out_specs=(
                P(("dp", "expert"), None),
                P(("dp", "expert"), None),
                P("dp", None),
                P("dp", None),
                P("dp", None),
                P("dp", None),
                P("dp", None),
                P("dp"),
                P("dp"),
                P("expert", "dp", None),
                P("expert", "dp", None),
                P("expert", "dp", None),
            ),
            check_vma=False,
        )

    return layer
```

```python
import functools
import math

import jax
import jax.numpy as jnp
from jax import lax
from jax.experimental import pallas as pl
from jax.experimental.pallas import tpu as pltpu
from jax.sharding import PartitionSpec as P

MESH = pl.DeviceIdType.MESH

QH = 24
KVH = 8
HD = 64
TOP = 8


eps = 1e-06
rope_base = 10000.0
masked_score = -1e30


def shortened(value):
    return jax.tree.map(lambda a: a.astype(jnp.bfloat16) if a.dtype == jnp.float32 else a, value)


def rms_scale(values):
    return lax.rsqrt(jnp.mean(values * values, axis=-1, keepdims=True) + eps)


def token_layout(lengths_row, row_count):
    token_index = jnp.arange(row_count, dtype=jnp.int32)
    seq_ends = jnp.cumsum(lengths_row)
    passed = (token_index[:, None] >= seq_ends[None, :]).astype(jnp.int32)
    doc_id = jnp.sum(passed, axis=1)
    seq_start = jnp.sum(passed * lengths_row[None, :], axis=1)
    return (doc_id, token_index - seq_start)


def rope_tables(position):
    half_size = HD // 2
    frequency = rope_base ** (-2.0 * jnp.arange(half_size, dtype=jnp.float32) / HD)
    angles = position.astype(jnp.float32)[:, None] * frequency[None, :]
    return (jnp.cos(angles)[:, None, :], jnp.sin(angles)[:, None, :])


def rotate(values, cos_table, sin_table, head_count):
    half_size = HD // 2
    shaped = values.reshape(values.shape[0], head_count, HD)
    front_half = shaped[..., :half_size]
    back_half = shaped[..., half_size:]
    turned = jnp.concatenate(
        [
            front_half * cos_table - back_half * sin_table,
            back_half * cos_table + front_half * sin_table,
        ],
        axis=-1,
    )
    return turned.reshape(values.shape[0], head_count * HD)


def unrotate(values, cos_table, sin_table, head_count):
    half_size = HD // 2
    shaped = values.reshape(values.shape[0], head_count, HD)
    front_half = shaped[..., :half_size]
    back_half = shaped[..., half_size:]
    turned = jnp.concatenate(
        [
            front_half * cos_table + back_half * sin_table,
            back_half * cos_table - front_half * sin_table,
        ],
        axis=-1,
    )
    return turned.reshape(values.shape[0], head_count * HD)


def own_columns(values, local_count):
    start = lax.axis_index("expert") * local_count
    return lax.dynamic_slice_in_dim(values, start, local_count, axis=1)


def body(
    tokens,
    seq_lengths,
    routes,
    w_query,
    w_key,
    w_value,
    w_output,
    w_router,
    attn_gain,
    moe_gain,
    expert_gate,
    expert_up,
    expert_down,
    out_grad,
):
    shards = (w_query, w_key, w_value, w_output, w_router, attn_gain, moe_gain)
    gathered = (
        lax.all_gather(shards[0], "dp", axis=0, tiled=True),
        lax.all_gather(shards[1], "dp", axis=0, tiled=True),
        lax.all_gather(shards[2], "dp", axis=0, tiled=True),
        lax.all_gather(shards[3], "dp", axis=0, tiled=True),
        lax.all_gather(shards[4], "dp", axis=0, tiled=True),
        lax.all_gather(shards[5], "dp", axis=0, tiled=True),
        lax.all_gather(shards[6], "dp", axis=0, tiled=True),
    )
    query_w, key_w, value_w, output_w, router_w, gain_one, gain_two = gathered
    row_count = tokens.shape[0]
    expert_count = w_router.shape[1]
    group_size = QH // KVH
    block_rows = min(512, row_count)
    block_total = row_count // block_rows
    score_scale = HD ** (-0.5)
    doc_id, position = token_layout(seq_lengths[0], row_count)
    cos_table, sin_table = rope_tables(position)
    token_index = jnp.arange(row_count, dtype=jnp.int32)
    block_starts = jnp.arange(block_total, dtype=jnp.int32) * block_rows
    inputs = tokens.astype(jnp.float32)
    scale_one = rms_scale(inputs)
    normed_one = inputs * scale_one
    hidden_one = (normed_one * gain_one.astype(jnp.float32)).astype(jnp.bfloat16)
    query_rot = rotate(
        jnp.dot(hidden_one, query_w, preferred_element_type=jnp.float32), cos_table, sin_table, QH
    ).astype(jnp.bfloat16)
    key_rot = rotate(
        jnp.dot(hidden_one, key_w, preferred_element_type=jnp.float32), cos_table, sin_table, KVH
    ).astype(jnp.bfloat16)
    value_rows = jnp.dot(hidden_one, value_w, preferred_element_type=jnp.float32).astype(
        jnp.bfloat16
    )
    key_heads = key_rot.reshape(row_count, KVH, HD)
    value_heads = value_rows.reshape(row_count, KVH, HD)

    def block_scores(block_start):
        query_block = query_rot.reshape(block_rows, KVH, group_size, HD)
        raw_scores = (
            jnp.einsum("tkgd,ukd->kgtu", query_block, key_heads, preferred_element_type=jnp.float32)
            * score_scale
        )
        block_index = block_start + jnp.arange(block_rows, dtype=jnp.int32)
        allowed = (doc_id[:, None] == doc_id[None, :]) & (
            token_index[None, :] <= block_index[:, None]
        )
        return (query_block, jnp.where(allowed, raw_scores, masked_score))

    def attend_block(block_start):
        query_block, scores = block_scores(block_start)
        row_top = jnp.max(scores, axis=-1, keepdims=True)
        exp_terms = jnp.exp(scores - row_top)
        row_total = jnp.sum(exp_terms, axis=-1, keepdims=True)
        probs_low = (exp_terms / row_total).astype(jnp.bfloat16)
        attended_block = jnp.einsum(
            "kgtu,ukd->tkgd", probs_low, value_heads, preferred_element_type=jnp.float32
        )
        log_total = (row_top + jnp.log(row_total))[..., 0]
        return (attended_block.reshape(block_rows, QH * HD).astype(jnp.bfloat16), log_total)

    attended_blocks, log_blocks = lax.map(attend_block, block_starts)
    attended = attended_blocks.reshape(row_count, QH * HD)
    residual = inputs + jnp.dot(attended, output_w, preferred_element_type=jnp.float32)
    scale_two = rms_scale(residual)
    normed_two = residual * scale_two
    hidden_two = (normed_two * gain_two.astype(jnp.float32)).astype(jnp.bfloat16)
    logits = jnp.dot(hidden_two, router_w, preferred_element_type=jnp.float32)
    expert_ids = jnp.arange(expert_count, dtype=jnp.int32)
    route_hot = (routes[:, :, None] == expert_ids[None, None, :]).astype(jnp.float32)
    chosen = jnp.sum(route_hot * logits[:, None, :], axis=-1)
    gate_probs = jax.nn.softmax(chosen, axis=-1)
    dense_probs = jnp.sum(route_hot * gate_probs[:, :, None], axis=1)
    upstream = out_grad.astype(jnp.float32)
    local_count = expert_gate.shape[0]
    all_hidden = lax.all_gather(hidden_two, "expert", axis=0, tiled=True)
    all_probs = own_columns(lax.all_gather(dense_probs, "expert", axis=0, tiled=True), local_count)
    all_upstream = lax.all_gather(out_grad, "expert", axis=0, tiled=True)
    mix_part = jnp.zeros(all_hidden.shape, jnp.float32)
    row_part = jnp.zeros(all_hidden.shape, jnp.float32)
    grad_columns, down_parts, gate_parts, up_parts = [], [], [], []
    for e in range(local_count):
        prob = all_probs[:, e : e + 1]
        gate_pre = jnp.dot(all_hidden, expert_gate[e], preferred_element_type=jnp.float32)
        up_pre = jnp.dot(all_hidden, expert_up[e], preferred_element_type=jnp.float32)
        raw_grad = jnp.dot(all_upstream, expert_down[e], preferred_element_type=jnp.float32)
        gate_sig = jax.nn.sigmoid(gate_pre)
        gate_act = gate_pre * gate_sig
        activation = gate_act * up_pre
        grad_columns.append(jnp.sum(activation * raw_grad, axis=-1, keepdims=True))
        weighted = (activation * prob).astype(jnp.bfloat16)
        act_grad = raw_grad * prob
        gate_pre_grad = (act_grad * up_pre * gate_sig * (1.0 + gate_pre * (1.0 - gate_sig))).astype(
            jnp.bfloat16
        )
        up_pre_grad = (act_grad * gate_act).astype(jnp.bfloat16)
        mix_part = mix_part + jnp.dot(
            weighted, expert_down[e].T, preferred_element_type=jnp.float32
        )
        row_part = row_part + jnp.dot(
            gate_pre_grad, expert_gate[e].T, preferred_element_type=jnp.float32
        )
        row_part = row_part + jnp.dot(
            up_pre_grad, expert_up[e].T, preferred_element_type=jnp.float32
        )
        down_parts.append(jnp.dot(all_upstream.T, weighted, preferred_element_type=jnp.float32))
        gate_parts.append(jnp.dot(all_hidden.T, gate_pre_grad, preferred_element_type=jnp.float32))
        up_parts.append(jnp.dot(all_hidden.T, up_pre_grad, preferred_element_type=jnp.float32))
    down_partial = jnp.stack(down_parts)
    gate_partial = jnp.stack(gate_parts)
    up_partial = jnp.stack(up_parts)
    grad_dense = lax.all_to_all(
        jnp.concatenate(grad_columns, axis=1), "expert", split_axis=0, concat_axis=1, tiled=True
    )
    gate_grad = jnp.sum(route_hot * grad_dense[:, None, :], axis=-1)
    mixture = lax.psum_scatter(
        mix_part.astype(jnp.bfloat16), "expert", scatter_dimension=0, tiled=True
    ).astype(jnp.float32)
    layer_out = (residual + mixture).astype(jnp.bfloat16)
    hidden_two_grad = lax.psum_scatter(
        row_part.astype(jnp.bfloat16), "expert", scatter_dimension=0, tiled=True
    ).astype(jnp.float32)
    chosen_grad = gate_probs * (gate_grad - jnp.sum(gate_probs * gate_grad, axis=-1, keepdims=True))
    logit_grad = jnp.sum(route_hot * chosen_grad[:, :, None], axis=1).astype(jnp.bfloat16)
    hidden_two_grad = hidden_two_grad + jnp.dot(
        logit_grad, router_w.T, preferred_element_type=jnp.float32
    )
    gain_two_partial = jnp.sum(hidden_two_grad * normed_two, axis=0)
    normed_two_grad = hidden_two_grad * gain_two.astype(jnp.float32)
    residual_grad = upstream + scale_two * (
        normed_two_grad
        - normed_two * jnp.mean(normed_two_grad * normed_two, axis=-1, keepdims=True)
    )
    branch_grad = residual_grad.astype(jnp.bfloat16)
    attended_grad = jnp.dot(branch_grad, output_w.T, preferred_element_type=jnp.float32).astype(
        jnp.bfloat16
    )

    def attend_back(carry, block_data):
        key_acc, value_acc = carry
        block_start, log_total = block_data
        query_block, scores = block_scores(block_start)
        attn_probs = jnp.exp(scores - log_total[..., None])
        probs_low = attn_probs.astype(jnp.bfloat16)
        grad_block = attended_grad.reshape(block_rows, KVH, group_size, HD)
        prob_grad = jnp.einsum(
            "tkgd,ukd->kgtu", grad_block, value_heads, preferred_element_type=jnp.float32
        )
        score_grad = (
            attn_probs * (prob_grad - jnp.sum(attn_probs * prob_grad, axis=-1, keepdims=True))
        ).astype(jnp.bfloat16)
        query_part = (
            jnp.einsum("kgtu,ukd->tkgd", score_grad, key_heads, preferred_element_type=jnp.float32)
            * score_scale
        )
        key_acc = (
            key_acc
            + jnp.einsum(
                "kgtu,tkgd->ukd", score_grad, query_block, preferred_element_type=jnp.float32
            )
            * score_scale
        )
        value_acc = value_acc + jnp.einsum(
            "kgtu,tkgd->ukd", probs_low, grad_block, preferred_element_type=jnp.float32
        )
        return ((key_acc, value_acc), query_part.reshape(block_rows, QH * HD))

    zero_heads = jnp.zeros((row_count, KVH, HD), jnp.float32)
    (key_sums, value_sums), query_blocks = lax.scan(
        attend_back, (zero_heads, zero_heads), (block_starts, log_blocks)
    )
    query_grad = unrotate(
        query_blocks.reshape(row_count, QH * HD), cos_table, sin_table, QH
    ).astype(jnp.bfloat16)
    key_grad = unrotate(key_sums.reshape(row_count, KVH * HD), cos_table, sin_table, KVH).astype(
        jnp.bfloat16
    )
    value_grad = value_sums.reshape(row_count, KVH * HD).astype(jnp.bfloat16)
    hidden_one_grad = jnp.dot(query_grad, query_w.T, preferred_element_type=jnp.float32)
    hidden_one_grad = hidden_one_grad + jnp.dot(
        key_grad, key_w.T, preferred_element_type=jnp.float32
    )
    hidden_one_grad = hidden_one_grad + jnp.dot(
        value_grad, value_w.T, preferred_element_type=jnp.float32
    )
    gain_one_partial = jnp.sum(hidden_one_grad * normed_one, axis=0)
    normed_one_grad = hidden_one_grad * gain_one.astype(jnp.float32)
    in_grad = residual_grad + scale_one * (
        normed_one_grad
        - normed_one * jnp.mean(normed_one_grad * normed_one, axis=-1, keepdims=True)
    )
    query_partial = jnp.dot(hidden_one.T, query_grad, preferred_element_type=jnp.float32)
    key_partial = jnp.dot(hidden_one.T, key_grad, preferred_element_type=jnp.float32)
    value_partial = jnp.dot(hidden_one.T, value_grad, preferred_element_type=jnp.float32)
    output_partial = jnp.dot(attended.T, branch_grad, preferred_element_type=jnp.float32)
    router_partial = jnp.dot(hidden_two.T, logit_grad, preferred_element_type=jnp.float32)
    pieces = jax.tree.map(
        lambda part: part.astype(jnp.float32),
        lax.psum_scatter(
            shortened(
                (
                    query_partial,
                    key_partial,
                    value_partial,
                    output_partial,
                    router_partial,
                    gain_one_partial,
                    gain_two_partial,
                )
            ),
            "dp",
            scatter_dimension=0,
            tiled=True,
        ),
    )
    totals = (
        lax.psum(pieces[0].astype(jnp.bfloat16), "expert").astype(jnp.float32),
        lax.psum(pieces[1].astype(jnp.bfloat16), "expert").astype(jnp.float32),
        lax.psum(pieces[2].astype(jnp.bfloat16), "expert").astype(jnp.float32),
        lax.psum(pieces[3].astype(jnp.bfloat16), "expert").astype(jnp.float32),
        lax.psum(pieces[4].astype(jnp.bfloat16), "expert").astype(jnp.float32),
        lax.psum(pieces[5].astype(jnp.bfloat16), "expert").astype(jnp.float32),
        lax.psum(pieces[6].astype(jnp.bfloat16), "expert").astype(jnp.float32),
    )
    expert_totals = (
        lax.psum_scatter(
            gate_partial.astype(jnp.bfloat16), "dp", scatter_dimension=1, tiled=True
        ).astype(jnp.float32),
        lax.psum_scatter(
            up_partial.astype(jnp.bfloat16), "dp", scatter_dimension=1, tiled=True
        ).astype(jnp.float32),
        lax.psum_scatter(
            down_partial.astype(jnp.bfloat16), "dp", scatter_dimension=1, tiled=True
        ).astype(jnp.float32),
    )
    return (
        layer_out,
        in_grad,
        totals[0],
        totals[1],
        totals[2],
        totals[3],
        totals[4],
        totals[5],
        totals[6],
        expert_totals[0],
        expert_totals[1],
        expert_totals[2],
    )


NT = (((1,), (1,)), ((), ()))
TN = (((0,), (0,)), ((), ()))


def dot_f32(left, right, dims=(((1,), (0,)), ((), ()))):
    return lax.dot_general(left, right, dims, preferred_element_type=jnp.float32)


def entry(rows, index, step):
    value = 0
    for place, row in enumerate(rows):
        for column, digit in enumerate(row):
            if digit:
                value = jnp.where((index == place) & (step == column), digit, value)
    return value


BLOCK_ORDER = ((0, 1, 4, 5, 6, 2, 7, 3), (1, 0, 5, 4, 6, 2, 7, 3))
BEFORE_STEP = (
    ((), ("W1", "X1", "W4", "A4"), (), ("W5",), ("W6",), ("W2",), ("W7",), ("W3",)),
    ((), ("W2", "N2", "W5", "A5", "W0"), (), ("W4", "A4", "W6", "N6", "A0"), (), ("W7", "N7"), (), ("W3", "N3")),
)
SUMS_ACROSS = (((), (), (), (), (2,), (), (3, 1, 0), ()), ((), (), (), (0,), (2,), (), (3, 1), ()))
SUM_ORDER = ((3, 15, 15, 15, 1, 15, 15, 15, 0), (15, 15, 15, 2, 15, 3, 0, 15, 1))
HALVES = 2


def moe_kernel(
    h_in, u_in, p_in, wg_in, wu_in, wd_in,
    d_out, e_out, gg_out, grads_out, core_got, y_out,
    h_all, u_all, p_all, wg, wu, wd, act, gu, partials, rx, rz, d_stage, gg_stage, tile_bf, tile_f32, got_tile,
    load_sem, h_up, h_down, h_across, h_recv, p_send, p_recv, g_send, g_recv,
    x_send, x_recv, z_send, z_recv, d_sem, c_send, c_recv, y_send, tile_sem, out_sem,
    *, comm
):
    A, B, n = 4, 2, 8
    R, D = h_in.shape
    F = wg.shape[2]
    shard = D // 4
    ez, ex = partials.at[pl.ds(0, A)], partials.at[pl.ds(A, A)]
    me = lax.axis_index("expert")
    dp = lax.axis_index("dp")
    a, b = me // B, me % B
    y, c = dp // 2, dp % 2
    partner_x = a * B + (1 - b)
    core_peer = 2 * y + (1 - c)
    y_peer = 2 * (1 - y) + c

    def copy(src, dst, send, recv, **target):
        return pltpu.make_async_remote_copy(
            src_ref=src, dst_ref=dst, send_sem=send, recv_sem=recv, device_id=target, device_id_type=MESH
        )

    loads = [
        pltpu.make_async_copy(h_in, h_all.at[me], load_sem.at[0]),
        pltpu.make_async_copy(u_in, u_all, load_sem.at[1]),
        pltpu.make_async_copy(wg_in, wg, load_sem.at[2]),
        pltpu.make_async_copy(wu_in, wu, load_sem.at[3]),
        pltpu.make_async_copy(wd_in, wd, load_sem.at[4]),
        pltpu.make_async_copy(p_in.at[me], p_all.at[me], load_sem.at[5]),
    ]
    for load in loads:
        load.start()

    barrier = pltpu.get_barrier_semaphore()
    for k in range(1, n):
        pl.semaphore_signal(barrier, inc=1, device_id={"expert": (me + k) % n}, device_id_type=MESH)
    pl.semaphore_signal(barrier, inc=1, device_id={"dp": core_peer}, device_id_type=MESH)
    pl.semaphore_wait(barrier, n)
    loads[0].wait()
    loads[5].wait()

    def send_up(s):
        return copy(h_all.at[s], h_all.at[s], h_up.at[s], h_recv.at[s], expert=me + B)

    def send_down(s):
        return copy(h_all.at[s], h_all.at[s], h_down.at[s], h_recv.at[s], expert=me - B)

    def send_across(s):
        return copy(h_all.at[s], h_all.at[s], h_across.at[s], h_recv.at[s], expert=partner_x)

    def p_copy(peer):
        return copy(p_in.at[peer], p_all.at[me], p_send.at[peer], p_recv.at[me], expert=peer)

    @pl.when(a < A - 1)
    def _():
        send_up(me).start()

    @pl.when(a > 0)
    def _():
        send_down(me).start()

    send_across(me).start()
    for k in range(1, n):
        p_copy((me + k) % n).start()
    for k in range(1, n):
        s = (me + k) % n
        copy(p_in.at[s], p_all.at[s], p_send.at[s], p_recv.at[s], expert=s).wait_recv()
    for load in loads[1:5]:
        load.wait()

    def recv_block(s):
        send_across(s).wait_recv()

    near = jnp.where(a < A // 2, a, A - 1 - a)
    flipped = a >= A // 2

    def turned(row):
        return jnp.where(flipped, A - 1 - row, row)

    def along(s, upward):
        @pl.when(flipped != upward)
        def _():
            send_up(s).start()

        @pl.when(flipped == upward)
        def _():
            send_down(s).start()

    def move(words):
        for word in words:
            code = int(word[1:])
            s = turned(code % A) * B + (1 - b if code >= A else b)
            if word[0] == "W":
                recv_block(s)
            elif word[0] == "X":
                send_across(s).start()
            else:
                along(s, word[0] == "A")

    def d_copy(s, slot):
        return pltpu.make_async_copy(d_stage.at[slot], d_out.at[s], d_sem.at[slot])

    def g_copy(s):
        return copy(gg_stage.at[s], gg_out.at[me], g_send.at[s], g_recv.at[me], expert=s)

    def compute(step, s, row, across):
        rows = pl.ds(pl.multiple_of(s * R, R), R)
        probs = jnp.transpose(p_all[s])
        grad_cols = []
        for e in range(2):
            gate_pre = dot_f32(h_all[s], wg[e])
            up_pre = dot_f32(h_all[s], wu[e])
            raw = dot_f32(u_all[s], wd[e])
            prob = probs[:, e : e + 1]
            sig = 1.0 / (1.0 + jnp.exp(-gate_pre))
            gate_act = gate_pre * sig
            activation = gate_act * up_pre
            grad_cols.append(jnp.sum(activation * raw, axis=1, keepdims=True))
            act[rows, e * F : (e + 1) * F] = (activation * prob).astype(jnp.bfloat16)
            act_grad = raw * prob
            gate_grad = act_grad * up_pre * sig * (1.0 + gate_pre * (1.0 - sig))
            gu[rows, 2 * e * F : (2 * e + 1) * F] = gate_grad.astype(jnp.bfloat16)
            gu[rows, (2 * e + 1) * F : (2 * e + 2) * F] = (act_grad * gate_act).astype(jnp.bfloat16)
        column = lax.broadcasted_iota(jnp.int32, (R, 128), 1)
        both = jnp.where(column == 0, grad_cols[0], jnp.where(column == 1, grad_cols[1], 0.0))
        gg_stage[s] = jnp.transpose(both)[:8]
        slot = step % 2

        @pl.when(step >= 2)
        def _():
            d_copy(s, slot).wait()

        def columns(tile, _):
            cols = pl.ds(pl.multiple_of(tile * 512, 512), 512)
            mixed = dot_f32(act[rows, 0:F], wd[0, cols, :], NT) + dot_f32(act[rows, F : 2 * F], wd[1, cols, :], NT)
            d_stage[slot, :, cols] = mixed.astype(jnp.bfloat16)
            back = dot_f32(gu[rows, 0:F], wg[0, cols, :], NT)
            back += dot_f32(gu[rows, F : 2 * F], wu[0, cols, :], NT)
            back += dot_f32(gu[rows, 2 * F : 3 * F], wg[1, cols, :], NT)
            back += dot_f32(gu[rows, 3 * F : 4 * F], wu[1, cols, :], NT)

            partials[row + jnp.where(across, A, 0), :, cols] = back.astype(jnp.bfloat16)
            return 0

        lax.fori_loop(0, D // 512, columns, 0, unroll=True)
        d_copy(s, slot).start()

        @pl.when(s != me)
        def _():
            g_copy(s).start()

        @pl.when(s == me)
        def _():
            pltpu.make_async_copy(gg_stage.at[s], gg_out.at[me], g_send.at[s]).start()

    part_rows = R // HALVES

    def part_of(part):
        return pl.ds(pl.multiple_of(part * part_rows, 16), part_rows)

    def x_copy(row, part):
        return copy(ex.at[row, part_of(part)], rx.at[row, part_of(part)], x_send.at[row, part], x_recv.at[row, part], expert=partner_x)

    def z_up(row, part):
        return copy(ez.at[row, part_of(part)], rz.at[row + 1, part_of(part)], z_send.at[row, part], z_recv.at[row + 1, part], expert=me + B)

    def z_down(row, part):
        return copy(ez.at[row, part_of(part)], rz.at[row, part_of(part)], z_send.at[row, part], z_recv.at[row, part], expert=me - B)

    def sum_part(row, part):
        x_copy(row, part).wait_recv()
        below = (a > 0) & (row >= a)
        above = (a < A - 1) & (row <= a)

        @pl.when(below)
        def _():
            z_up(row, part).wait_recv()

        @pl.when(above)
        def _():
            z_down(row, part).wait_recv()

        def chunk(index, _):
            rows = pl.ds(pl.multiple_of(part * part_rows + index * 64, 64), 64)
            total = ez[row, rows, :].astype(jnp.float32) + rx[row, rows, :].astype(jnp.float32)

            @pl.when(row != a)
            def _():
                @pl.when(below)
                def _():
                    ez[row, rows, :] = (total + rz[row + 1, rows, :].astype(jnp.float32)).astype(jnp.bfloat16)

                @pl.when(above)
                def _():
                    ez[row, rows, :] = (total + rz[row, rows, :].astype(jnp.float32)).astype(jnp.bfloat16)

                @pl.when(jnp.logical_not(below | above))
                def _():
                    ez[row, rows, :] = total.astype(jnp.bfloat16)

            @pl.when(row == a)
            def _():
                @pl.when(below & above)
                def _():
                    e_out[rows, :] = total + rz[row + 1, rows, :].astype(jnp.float32) + rz[row, rows, :].astype(jnp.float32)

                @pl.when(below & jnp.logical_not(above))
                def _():
                    e_out[rows, :] = total + rz[row + 1, rows, :].astype(jnp.float32)

                @pl.when(above & jnp.logical_not(below))
                def _():
                    e_out[rows, :] = total + rz[row, rows, :].astype(jnp.float32)

            return 0

        lax.fori_loop(0, part_rows // 64, chunk, 0)

        @pl.when(row > a)
        def _():
            z_up(row, part).start()

        @pl.when(row < a)
        def _():
            z_down(row, part).start()

    def sum_parts(row):
        def one(part, _):
            sum_part(row, part)
            return 0

        lax.fori_loop(0, HALVES, one, 0)

    def block_step(step, _):
        for place in range(A // 2):
            for at, words in enumerate(BEFORE_STEP[place]):
                if words:
                    @pl.when((near == place) & (step == at))
                    def _():
                        move(words)

        code = entry(BLOCK_ORDER, near, step)
        across = code >= A
        row = turned(code % A)
        s = row * B + jnp.where(across, 1 - b, b)
        compute(step, s, row, across)
        for place in range(A // 2):
            for at, rows in enumerate(SUMS_ACROSS[place]):
                if rows:
                    @pl.when((near == place) & (step == at))
                    def _():
                        for row in rows:
                            for part in range(HALVES):
                                x_copy(turned(row), part).start()

        @pl.when((near == 0) & (step == n - 2))
        def _():
            sum_parts(turned(2))

        return 0

    lax.fori_loop(0, n, block_step, 0)

    def core_copy(slot, which, index):
        return copy(tile_bf.at[slot], core_got.at[which, index], c_send.at[slot], c_recv.at[which, index], dp=core_peer)

    def y_copy(slot, index):
        return pltpu.make_async_copy(tile_bf.at[slot], y_out.at[index], y_send.at[slot])

    def weight_tile(group, e, kind, left, right):
        owner = jnp.where(group == 0, 2 * (1 - y) + 1 - c, jnp.where(group == 1, y_peer, jnp.where(group == 2, core_peer, dp)))
        cols = pl.ds(pl.multiple_of(owner * shard, 128), shard)
        total = dot_f32(left[:, :, cols].reshape(n * R, shard), right, TN)
        index = kind * 2 + e
        slot = kind

        @pl.when((group == 0) | (group == 2))
        def _():
            @pl.when(e > 0)
            def _():
                core_copy(slot, 0, index).wait_send()

            @pl.when((e == 0) & (group == 2))
            def _():
                y_copy(slot, index).wait()

            tile_bf[slot] = total.astype(jnp.bfloat16)
            core_copy(slot, group // 2, index).start()

        @pl.when(group == 1)
        def _():
            @pl.when(e == 0)
            def _():
                core_copy(slot, 0, index).wait_send()

            @pl.when(e > 0)
            def _():
                y_copy(slot, index).wait()

            core_copy(slot, 0, index).wait_recv()
            got = pltpu.make_async_copy(core_got.at[0, index], got_tile, tile_sem)
            got.start()
            got.wait()
            tile_bf[slot] = (total + got_tile[...].astype(jnp.float32)).astype(jnp.bfloat16)
            y_copy(slot, index).start()

        @pl.when(group == 3)
        def _():
            core_copy(slot, 1, index).wait_recv()
            got = pltpu.make_async_copy(core_got.at[1, index], got_tile, tile_sem)
            got.start()
            got.wait()
            tile_f32[index] = total + got_tile[...].astype(jnp.float32)
            pltpu.make_async_copy(tile_f32.at[index], grads_out.at[index], out_sem.at[index]).start()

    def sum_step(place, _):
        code = entry(SUM_ORDER, near, place)

        @pl.when(code < A)
        def _():
            sum_parts(turned(code))

        @pl.when(place < 8)
        def _():
            group, e = place // 2, place % 2
            weight_tile(group, e, 0, h_all, gu[:, pl.ds(pl.multiple_of(2 * e * F, 128), F)])
            weight_tile(group, e, 1, h_all, gu[:, pl.ds(pl.multiple_of((2 * e + 1) * F, 128), F)])
            weight_tile(group, e, 2, u_all, act[:, pl.ds(pl.multiple_of(e * F, 128), F)])

        return 0

    lax.fori_loop(0, 9, sum_step, 0)

    for kind in range(3):
        core_copy(kind, 1, 3 + kind).wait_send()
    for row in range(A):
        for part in range(HALVES):
            x_copy(row, part).wait_send()

            @pl.when(row != a)
            def _():
                z_up(row, part).wait_send()

    @pl.when(a < A - 1)
    def _():
        send_up(me).wait_send()

    @pl.when(a > 0)
    def _():
        send_down(me).wait_send()

    send_across(me).wait_send()
    for place in range(A // 2):
        @pl.when(near == place)
        def _():
            for word in [word for words in BEFORE_STEP[place] for word in words]:
                code = int(word[1:])
                s = turned(code % A) * B + (1 - b if code >= A else b)
                if word[0] == "X":
                    send_across(s).wait_send()
                elif word[0] != "W":
                    @pl.when(flipped != (word[0] == "A"))
                    def _():
                        send_up(s).wait_send()

                    @pl.when(flipped == (word[0] == "A"))
                    def _():
                        send_down(s).wait_send()

    for k in range(1, n):
        s = (me + k) % n
        p_copy(s).wait_send()
        g_copy(s).wait_send()
        copy(gg_stage.at[s], gg_out.at[s], g_send.at[s], g_recv.at[s], expert=s).wait_recv()
    pltpu.make_async_copy(gg_stage.at[me], gg_out.at[me], g_send.at[me]).wait()
    for slot in range(2):
        d_copy(0, slot).wait()
    for index in range(6):
        pltpu.make_async_copy(tile_f32.at[index], grads_out.at[index], out_sem.at[index]).wait()


def moe_call(hidden, all_upstream, probs, expert_gate, expert_up, expert_down):
    R, D = hidden.shape
    F = expert_gate.shape[2]
    A, n = 4, 8
    shard = D // 4
    bf, f32 = jnp.bfloat16, jnp.float32
    any_spec = pl.BlockSpec(memory_space=pl.ANY)
    vmem = pl.BlockSpec(memory_space=pltpu.VMEM)
    dma = pltpu.SemaphoreType.DMA
    out_shape = (
        jax.ShapeDtypeStruct((n, R, D), bf),
        jax.ShapeDtypeStruct((R, D), f32),
        jax.ShapeDtypeStruct((n, 8, R), f32),
        jax.ShapeDtypeStruct((6, shard, F), f32),
        jax.ShapeDtypeStruct((2, 6, shard, F), bf),
        jax.ShapeDtypeStruct((6, shard, F), bf),
    )
    return pl.pallas_call(
        functools.partial(moe_kernel, comm=True),
        out_shape=out_shape,
        in_specs=[any_spec] * 6,
        out_specs=(any_spec, vmem, any_spec, any_spec, any_spec, any_spec),
        scratch_shapes=[
            pltpu.VMEM((n, R, D), bf),
            pltpu.VMEM((n, R, D), bf),
            pltpu.VMEM((n, 8, R), f32),
            pltpu.VMEM((2, D, F), bf),
            pltpu.VMEM((2, D, F), bf),
            pltpu.VMEM((2, D, F), bf),
            pltpu.VMEM((n * R, 2 * F), bf),
            pltpu.VMEM((n * R, 4 * F), bf),
            pltpu.VMEM((2 * A, R, D), bf),
            pltpu.VMEM((A, R, D), bf),
            pltpu.VMEM((A + 1, R, D), bf),
            pltpu.VMEM((2, R, D), bf),
            pltpu.VMEM((n, 8, R), f32),
            pltpu.VMEM((3, shard, F), bf),
            pltpu.VMEM((6, shard, F), f32),
            pltpu.VMEM((shard, F), bf),
            dma((6,)), dma((n,)), dma((n,)), dma((n,)), dma((n,)), dma((n,)), dma((n,)), dma((n,)), dma((n,)),
            dma((A, HALVES)), dma((A, HALVES)), dma((A, HALVES)), dma((A + 1, HALVES)), dma((2,)),
            dma((3,)), dma((2, 6)), dma((3,)), dma, dma((6,)),
        ],
        compiler_params=pltpu.CompilerParams(
            collective_id=1, has_side_effects=True, vmem_limit_bytes=64 * 1024 * 1024 - 65536
        ),
        cost_estimate=pl.CostEstimate(flops=58 * 10**9, bytes_accessed=60 * 10**6, transcendentals=2 * 10**6),
        name="experts",
    )(hidden, all_upstream, probs, expert_gate, expert_up, expert_down)


def reduce_kernel(
    left, right, extra, out,
    core_out, core_in, y_out, y_in, half, x_out, x_in, own, z_out, z_in, full,
    core_send, core_recv, y_send, y_recv, x_send, x_recv, zs_send, zs_recv, zg_send, zg_recv, xg_send, xg_recv,
):
    A, B = 4, 2
    W = core_out.shape[3]
    shard = core_out.shape[2]
    half_rows, piece = shard // B, shard // (A * B)
    chunks = y_in.shape[0]
    me = lax.axis_index("expert")
    dp = lax.axis_index("dp")
    a, b = me // B, me % B
    y, c = dp // 2, dp % 2
    partner_x = a * B + (1 - b)
    core_peer = 2 * y + (1 - c)
    y_peer = 2 * (1 - y) + c

    def copy(src, dst, send, recv, **target):
        return pltpu.make_async_remote_copy(
            src_ref=src, dst_ref=dst, send_sem=send, recv_sem=recv, device_id=target, device_id_type=MESH
        )

    barrier = pltpu.get_barrier_semaphore()
    for target in [{"dp": core_peer}, {"dp": y_peer}, {"expert": partner_x}] + [
        {"expert": (a + k) % A * B + b} for k in range(1, A)
    ]:
        pl.semaphore_signal(barrier, inc=1, device_id=target, device_id_type=MESH)
    pl.semaphore_wait(barrier, 2 + A)

    def partial(chunk, owner):
        rows = pl.ds(pl.multiple_of(owner * shard, 128), shard)
        cols = pl.ds(pl.multiple_of(chunk * W, 128), W)
        which = jnp.where(chunk < 4, 0, 1)
        total = dot_f32(left[which, :, rows], right[:, cols], TN)
        share = extra[pl.ds(pl.multiple_of(owner * shard, 128), shard), :].astype(jnp.float32)
        share = jnp.where(chunk == chunks - 1, share, 0.0)
        return jnp.concatenate([total[:, : W - 128], total[:, W - 128 :] + share], axis=1)

    def core_copy(chunk, which):
        slot = chunk % 2
        return copy(core_out.at[slot, which], core_in.at[chunk, which], core_send.at[slot, which], core_recv.at[chunk, which], dp=core_peer)

    def y_copy(chunk):
        slot = chunk % 2
        return copy(y_out.at[slot], y_in.at[chunk], y_send.at[slot], y_recv.at[chunk], dp=y_peer)

    def x_copy(chunk):
        slot = chunk % 2
        return copy(x_out.at[slot], x_in.at[chunk], x_send.at[slot], x_recv.at[chunk], expert=partner_x)

    def z_scatter(chunk, to, source):
        slot = chunk % 2
        return copy(
            z_out.at[slot, pl.ds(pl.multiple_of(to * piece, 16), piece)], z_in.at[chunk, source],
            zs_send.at[slot, to], zs_recv.at[chunk, source], expert=to * B + b,
        )

    def z_gather(chunk, to, source):
        rows = pl.ds(pl.multiple_of(b * half_rows + source * piece, 16), piece)
        return copy(full.at[chunk, rows], full.at[chunk, rows], zg_send.at[chunk, to], zg_recv.at[chunk, source], expert=to * B + b)

    def x_gather(chunk, side):
        rows = pl.ds(pl.multiple_of(side * half_rows, 16), half_rows)
        return copy(full.at[chunk, rows], full.at[chunk, rows], xg_send.at[chunk], xg_recv.at[chunk], expert=partner_x)

    def to_core(chunk):
        for which, owner in ((0, core_peer), (1, 2 * (1 - y) + 1 - c)):
            value = partial(chunk, owner).astype(jnp.bfloat16)

            @pl.when(chunk >= 2)
            def _():
                core_copy(chunk, which).wait_send()

            core_out[chunk % 2, which] = value
            core_copy(chunk, which).start()

    def to_y(chunk):
        value = partial(chunk, y_peer)
        core_copy(chunk, 1).wait_recv()

        @pl.when(chunk >= 2)
        def _():
            y_copy(chunk).wait_send()

        y_out[chunk % 2] = (value + core_in[chunk, 1].astype(jnp.float32)).astype(jnp.bfloat16)
        y_copy(chunk).start()

    def to_x(chunk):
        value = partial(chunk, dp)
        core_copy(chunk, 0).wait_recv()
        y_copy(chunk).wait_recv()
        value = value + core_in[chunk, 0].astype(jnp.float32) + y_in[chunk].astype(jnp.float32)

        @pl.when(chunk >= 2)
        def _():
            x_copy(chunk).wait_send()

        low, high = value[:half_rows], value[half_rows:]
        half[chunk % 2] = jnp.where(b == 0, low, high)
        x_out[chunk % 2] = jnp.where(b == 0, high, low).astype(jnp.bfloat16)
        x_copy(chunk).start()

    def to_z(chunk):
        x_copy(chunk).wait_recv()

        @pl.when(chunk >= 2)
        def _():
            for k in range(1, A):
                z_scatter(chunk, (a + k) % A, a).wait_send()

        total = half[chunk % 2] + x_in[chunk].astype(jnp.float32)
        half[chunk % 2] = total
        own[chunk % 2] = half[chunk % 2, pl.ds(pl.multiple_of(a * piece, 8), piece)]
        z_out[chunk % 2] = total.astype(jnp.bfloat16)
        for k in range(1, A):
            z_scatter(chunk, (a + k) % A, a).start()

    def spread_z(chunk):
        total = own[chunk % 2]
        for k in range(1, A):
            source = (a + k) % A
            z_scatter(chunk, a, source).wait_recv()
            total = total + z_in[chunk, source].astype(jnp.float32)
        rows = pl.ds(pl.multiple_of(b * half_rows + a * piece, 16), piece)
        full[chunk, rows] = total.astype(jnp.bfloat16)
        for k in range(1, A):
            z_gather(chunk, (a + k) % A, a).start()

    def spread_x(chunk):
        for k in range(1, A):
            z_gather(chunk, a, (a + k) % A).wait_recv()
        x_gather(chunk, b).start()

    def finish(chunk):
        x_gather(chunk, 1 - b).wait_recv()
        cols = pl.ds(pl.multiple_of(chunk * W, 128), W)
        out[:, cols] = full[chunk].astype(jnp.float32)

    stages = (to_core, to_y, to_x, to_z, spread_z, spread_x, finish)

    def step(t, _):
        for delay, stage in enumerate(stages):
            @pl.when((t >= delay) & (t < delay + chunks))
            def _():
                stage(t - delay)

        return 0

    lax.fori_loop(0, chunks + len(stages) - 1, step, 0)

    for chunk in range(chunks - 2, chunks):
        core_copy(chunk, 0).wait_send()
        core_copy(chunk, 1).wait_send()
        y_copy(chunk).wait_send()
        x_copy(chunk).wait_send()
        for k in range(1, A):
            z_scatter(chunk, (a + k) % A, a).wait_send()

    def drain(chunk, _):
        for k in range(1, A):
            z_gather(chunk, (a + k) % A, a).wait_send()
        x_gather(chunk, b).wait_send()
        return 0

    lax.fori_loop(0, chunks, drain, 0)


def reduce_call(left, right, extra):
    D = left.shape[2]
    width = right.shape[1]
    W, A, B = 384, 4, 2
    shard, chunks = D // 4, width // W
    bf, f32 = jnp.bfloat16, jnp.float32
    vmem = pl.BlockSpec(memory_space=pltpu.VMEM)
    dma = pltpu.SemaphoreType.DMA
    piece = shard // (A * B)
    return pl.pallas_call(
        reduce_kernel,
        out_shape=jax.ShapeDtypeStruct((shard, width), f32),
        in_specs=[vmem] * 3,
        out_specs=vmem,
        scratch_shapes=[
            pltpu.VMEM((2, 2, shard, W), bf),
            pltpu.VMEM((chunks, 2, shard, W), bf),
            pltpu.VMEM((2, shard, W), bf),
            pltpu.VMEM((chunks, shard, W), bf),
            pltpu.VMEM((2, shard // B, W), f32),
            pltpu.VMEM((2, shard // B, W), bf),
            pltpu.VMEM((chunks, shard // B, W), bf),
            pltpu.VMEM((2, piece, W), f32),
            pltpu.VMEM((2, shard // B, W), bf),
            pltpu.VMEM((chunks, A, piece, W), bf),
            pltpu.VMEM((chunks, shard, W), bf),
            dma((2, 2)), dma((chunks, 2)), dma((2,)), dma((chunks,)), dma((2,)), dma((chunks,)),
            dma((2, A)), dma((chunks, A)), dma((chunks, A)), dma((chunks, A)), dma((chunks,)), dma((chunks,)),
        ],
        compiler_params=pltpu.CompilerParams(
            collective_id=2, has_side_effects=True, vmem_limit_bytes=56 * 1024 * 1024
        ),
        cost_estimate=pl.CostEstimate(flops=4 * 10**9, bytes_accessed=20 * 10**6, transcendentals=0),
        name="weight_sums",
    )(left, right, extra)


def front_kernel(
    lengths, tokens, routes, w_gain, w_small, w_q, w_k, w_v, w_o, u_in,
    out_gain, out_small, out_q, out_k, out_v, out_o, u_all,
    left_out, qkv, log_total, cos_out, sin_out, residual, hidden_two, probs_out, by_owner,
    all_gain, all_small, all_q, all_k, all_v, all_o, sums, q_heads, k_heads, v_heads, mixed,
    keep_sem, core_send, y_send, pass_send, w_recv, u_keep, u_up, u_down, u_across, u_recv,
):
    A, B = 4, 2
    R, D = tokens.shape
    shard = D // 4
    attended, hidden_one = left_out.at[0], left_out.at[1]
    me = lax.axis_index("expert")
    dp = lax.axis_index("dp")
    a, b = me // B, me % B
    y, c = dp // 2, dp % 2
    partner_x = a * B + (1 - b)
    core_peer = 2 * y + (1 - c)
    y_peer = 2 * (1 - y) + c
    far_peer = 2 * (1 - y) + 1 - c
    shards = (w_gain, w_small, w_q, w_k, w_v, w_o)
    landed = (all_gain, all_small, all_q, all_k, all_v, all_o)
    kept = (out_gain, out_small, out_q, out_k, out_v, out_o)
    count = len(shards)
    GAIN, SMALL, QUERY, KEY, VALUE, OUTPUT = range(count)

    def copy(src, dst, send, recv, **target):
        return pltpu.make_async_remote_copy(
            src_ref=src, dst_ref=dst, send_sem=send, recv_sem=recv, device_id=target, device_id_type=MESH
        )

    barrier = pltpu.get_barrier_semaphore()
    for target in [{"dp": core_peer}, {"dp": y_peer}, {"expert": partner_x}] + [
        {"expert": (a + k) % A * B + b} for k in range(1, A)
    ]:
        pl.semaphore_signal(barrier, inc=1, device_id=target, device_id_type=MESH)
    pl.semaphore_wait(barrier, 2 + A)

    def to_core(i):
        return copy(shards[i], landed[i].at[dp], core_send.at[i], w_recv.at[i, dp], dp=core_peer)

    def to_y(i):
        return copy(shards[i], landed[i].at[dp], y_send.at[i], w_recv.at[i, dp], dp=y_peer)

    def pass_on(i):
        return copy(landed[i].at[y_peer], landed[i].at[y_peer], pass_send.at[i], w_recv.at[i, y_peer], dp=core_peer)

    def keep_own(i):
        return pltpu.make_async_copy(shards[i], kept[i].at[dp], keep_sem.at[i, dp])

    def keep(i, owner):
        return pltpu.make_async_copy(landed[i].at[owner], kept[i].at[owner], keep_sem.at[i, owner])

    def receive(i, owner):
        copy(shards[i], landed[i].at[owner], core_send.at[i], w_recv.at[i, owner], dp=core_peer).wait_recv()
        keep(i, owner).start()

    def forward(i):
        receive(i, y_peer)
        pass_on(i).start()

    def u_send_up(src, s):
        return copy(src, u_all.at[s], u_up.at[s], u_recv.at[s], expert=me + B)

    def u_send_down(src, s):
        return copy(src, u_all.at[s], u_down.at[s], u_recv.at[s], expert=me - B)

    def u_send_across(src, s):
        return copy(src, u_all.at[s], u_across.at[s], u_recv.at[s], expert=partner_x)

    def take(row):
        @pl.when((row >= 0) & (row < A))
        def _():
            s = row * B + b
            u_send_across(u_all.at[s], s).wait_recv()
            u_send_across(u_all.at[s], s).start()

            @pl.when((row < a) & (a < A - 1))
            def _():
                u_send_up(u_all.at[s], s).start()

            @pl.when((row > a) & (a > 0))
            def _():
                u_send_down(u_all.at[s], s).start()

    keep_u = pltpu.make_async_copy(u_in, u_all.at[me], u_keep)

    @pl.when(a < A - 1)
    def _():
        u_send_up(u_in, me).start()

    @pl.when(a > 0)
    def _():
        u_send_down(u_in, me).start()

    u_send_across(u_in, me).start()
    for i in range(count):
        to_y(i).start()
        to_core(i).start()
        keep_own(i).start()
    keep_u.start()

    row_index = lax.broadcasted_iota(jnp.int32, (R, 128), 0)
    ends = (lengths[0, 0], lengths[0, 0] + lengths[0, 1], lengths[0, 0] + lengths[0, 1] + lengths[0, 2])
    start = jnp.where(row_index >= ends[2], ends[2], jnp.where(row_index >= ends[1], ends[1], jnp.where(row_index >= ends[0], ends[0], 0)))
    position = (row_index - start).astype(jnp.float32)
    lane = lax.broadcasted_iota(jnp.int32, (R, 128), 1)
    pair = (lane % (HD // 2)).astype(jnp.float32)
    frequency = jnp.exp(pair * (-2.0 / HD * math.log(rope_base)))
    angle = position * frequency
    front = lane % HD < HD // 2
    cos_out[...] = jnp.cos(angle)
    sin_out[...] = jnp.where(front, -jnp.sin(angle), jnp.sin(angle))

    def doc_of(index):
        total = 0
        for end in ends:
            total = total + jnp.where(index >= end, 1, 0)
        return total

    rows_t = lax.broadcasted_iota(jnp.int32, (R, R), 0)
    rows_u = lax.broadcasted_iota(jnp.int32, (R, R), 1)
    allowed = (doc_of(rows_t) == doc_of(rows_u)) & (rows_u <= rows_t)

    inputs = tokens[...].astype(jnp.float32)
    scale_one = lax.rsqrt(jnp.mean(inputs * inputs, axis=1, keepdims=True) + eps)

    forward(GAIN)
    receive(GAIN, core_peer)
    receive(GAIN, far_peer)
    all_gain[dp] = w_gain[...]
    for j in range(4):
        cols = slice(j * shard, (j + 1) * shard)
        gain = all_gain[j, 0:1, :].astype(jnp.float32)
        hidden_one[:, cols] = (inputs[:, cols] * scale_one * gain).astype(jnp.bfloat16)

    offsets = {QUERY: 0, KEY: D, VALUE: D + KVH * HD}
    sums[...] = jnp.zeros_like(sums)

    def product(i, owner, own=False):
        cols = pl.ds(pl.multiple_of(owner * shard, 128), shard)
        left = hidden_one[:, cols]
        width = shards[i].shape[1]

        def tile(t, _):
            into = pl.ds(pl.multiple_of(offsets[i] + t * 512, 128), 512)
            part = pl.ds(pl.multiple_of(t * 512, 128), 512)
            weight = shards[i][:, part] if own else landed[i][owner, :, part]
            sums[:, into] += dot_f32(left, weight)
            return 0

        lax.fori_loop(0, width // 512, tile, 0)

    for i in (QUERY, KEY, VALUE):
        product(i, dp, own=True)
    for i in (QUERY, KEY, VALUE):
        receive(i, core_peer)
        product(i, core_peer)
    take(a - 1)
    take(a + 1)
    forward(SMALL)
    receive(SMALL, core_peer)
    forward(QUERY)
    product(QUERY, y_peer)
    receive(QUERY, far_peer)
    product(QUERY, far_peer)
    take(a - 2)
    take(a + 2)
    forward(KEY)
    product(KEY, y_peer)
    receive(KEY, far_peer)
    product(KEY, far_peer)
    forward(VALUE)
    product(VALUE, y_peer)
    receive(VALUE, far_peer)
    product(VALUE, far_peer)

    def rotated(columns):
        value = sums[:, columns]
        other = jnp.where(front, pltpu.roll(value, 128 - HD // 2, 1), pltpu.roll(value, HD // 2, 1))
        return (value * cos_out[...] + other * sin_out[...]).astype(jnp.bfloat16)

    for pair_index in range(QH // 2):
        columns = slice(pair_index * 128, (pair_index + 1) * 128)
        value = rotated(columns)
        qkv[:, columns] = value
        q_heads[2 * pair_index] = value[:, :HD]
        q_heads[2 * pair_index + 1] = value[:, HD:]
    for pair_index in range(KVH // 2):
        columns = slice(D + pair_index * 128, D + (pair_index + 1) * 128)
        value = rotated(columns)
        qkv[:, columns] = value
        k_heads[2 * pair_index] = value[:, :HD]
        k_heads[2 * pair_index + 1] = value[:, HD:]
        columns = slice(D + KVH * HD + pair_index * 128, D + KVH * HD + (pair_index + 1) * 128)
        value = sums[:, columns].astype(jnp.bfloat16)
        qkv[:, columns] = value
        v_heads[2 * pair_index] = value[:, :HD]
        v_heads[2 * pair_index + 1] = value[:, HD:]
    log_total[...] = jnp.zeros_like(log_total)

    def group_step(g, _):
        for k in range(QH // KVH):
            head = g * (QH // KVH) + k
            scores = dot_f32(q_heads[head], k_heads[g], NT) * HD**-0.5
            scores = jnp.where(allowed, scores, masked_score)
            top = jnp.max(scores, axis=1, keepdims=True)
            terms = jnp.exp(scores - top)
            total = jnp.sum(terms, axis=1, keepdims=True)
            low = (terms / total).astype(jnp.bfloat16)
            mixed[head] = dot_f32(low, v_heads[g]).astype(jnp.bfloat16)
            log_total[...] += jnp.where(lane == head, top + jnp.log(total), 0.0)
        return 0

    lax.fori_loop(0, KVH, group_step, 0)
    take(a - 3)
    take(a + 3)
    for pair_index in range(QH // 2):
        attended[:, pair_index * 128 : (pair_index + 1) * 128] = jnp.concatenate(
            [mixed[2 * pair_index], mixed[2 * pair_index + 1]], axis=1
        )

    residual[...] = inputs

    def out_product(owner, own=False):
        cols = pl.ds(pl.multiple_of(owner * shard, 128), shard)
        left = attended[:, cols]

        def tile(t, _):
            part = pl.ds(pl.multiple_of(t * 512, 128), 512)
            weight = w_o[:, part] if own else all_o[owner, :, part]
            residual[:, part] += dot_f32(left, weight)
            return 0

        lax.fori_loop(0, D // 512, tile, 0)

    out_product(dp, own=True)
    receive(OUTPUT, core_peer)
    out_product(core_peer)
    receive(SMALL, far_peer)
    all_small[dp] = w_small[...]
    forward(OUTPUT)
    out_product(y_peer)
    receive(OUTPUT, far_peer)
    out_product(far_peer)

    whole = residual[...]
    scale_two = lax.rsqrt(jnp.mean(whole * whole, axis=1, keepdims=True) + eps)
    logits = jnp.zeros((R, 128), jnp.float32)
    for j in range(4):
        cols = slice(j * shard, (j + 1) * shard)
        gain = all_gain[j, 1:2, :].astype(jnp.float32)
        value = (whole[:, cols] * scale_two * gain).astype(jnp.bfloat16)
        hidden_two[:, cols] = value
        logits = logits + dot_f32(value, all_small[j])
    chosen = lane == routes[:, 0:1]
    for j in range(1, TOP):
        chosen = chosen | (lane == routes[:, j : j + 1])
    logits = jnp.where(chosen, logits, masked_score)
    terms = jnp.where(chosen, jnp.exp(logits - jnp.max(logits, axis=1, keepdims=True)), 0.0)
    probs = terms / jnp.sum(terms, axis=1, keepdims=True)
    probs_out[...] = probs
    turned = jnp.transpose(probs)
    by_owner[...] = jnp.zeros_like(by_owner)
    local = 2
    for owner in range(A * B):
        by_owner[owner, 0:local, :] = turned[owner * local : (owner + 1) * local]

    for row in range(A):
        s = row * B + 1 - b
        u_send_across(u_all.at[s], s).wait_recv()
    for i in range(count):
        keep_own(i).wait()
        for owner in (core_peer, y_peer, far_peer):
            keep(i, owner).wait()
        to_y(i).wait_send()
        to_core(i).wait_send()
        pass_on(i).wait_send()
    keep_u.wait()

    @pl.when(a < A - 1)
    def _():
        u_send_up(u_in, me).wait_send()

    @pl.when(a > 0)
    def _():
        u_send_down(u_in, me).wait_send()

    for row in range(A):
        s = row * B + b
        u_send_across(u_all.at[s], s).wait_send()

        @pl.when((row < a) & (a < A - 1))
        def _():
            u_send_up(u_all.at[s], s).wait_send()

        @pl.when((row > a) & (a > 0))
        def _():
            u_send_down(u_all.at[s], s).wait_send()


def front_call(seq_lengths, tokens, routes, gains, small, w_query, w_key, w_value, w_output, out_grad):
    n = 8
    R, D = tokens.shape
    bf, f32 = jnp.bfloat16, jnp.float32
    any_spec = pl.BlockSpec(memory_space=pl.ANY)
    vmem = pl.BlockSpec(memory_space=pltpu.VMEM)
    dma = pltpu.SemaphoreType.DMA
    shards = (gains, small, w_query, w_key, w_value, w_output)
    whole = w_query.shape[1] + w_key.shape[1] + w_value.shape[1]
    return pl.pallas_call(
        front_kernel,
        out_shape=tuple(jax.ShapeDtypeStruct((4, *w.shape), bf) for w in shards)
        + (
            jax.ShapeDtypeStruct((n, R, D), bf),
            jax.ShapeDtypeStruct((2, R, D), bf),
            jax.ShapeDtypeStruct((R, whole), bf),
            jax.ShapeDtypeStruct((R, 128), f32),
            jax.ShapeDtypeStruct((R, 128), f32),
            jax.ShapeDtypeStruct((R, 128), f32),
            jax.ShapeDtypeStruct((R, D), f32),
            jax.ShapeDtypeStruct((R, D), bf),
            jax.ShapeDtypeStruct((R, 128), f32),
            jax.ShapeDtypeStruct((n, 8, R), f32),
        ),
        in_specs=[pl.BlockSpec(memory_space=pltpu.SMEM)] + [vmem] * 9,
        out_specs=(any_spec,) * 7 + (vmem,) * 9,
        scratch_shapes=[pltpu.VMEM((4, *w.shape), bf) for w in shards]
        + [
            pltpu.VMEM((R, whole), f32),
            pltpu.VMEM((QH, R, HD), bf),
            pltpu.VMEM((KVH, R, HD), bf),
            pltpu.VMEM((KVH, R, HD), bf),
            pltpu.VMEM((QH, R, HD), bf),
            dma((6, 4)), dma((6,)), dma((6,)), dma((6,)), dma((6, 4)), dma, dma((n,)), dma((n,)), dma((n,)), dma((n,)),
        ],
        compiler_params=pltpu.CompilerParams(
            collective_id=3, has_side_effects=True, vmem_limit_bytes=60 * 1024 * 1024
        ),
        cost_estimate=pl.CostEstimate(flops=4 * 10**9, bytes_accessed=40 * 10**6, transcendentals=2 * 10**6),
        name="front",
    )(seq_lengths, tokens, routes, *shards, out_grad)


def back_kernel(
    lengths, row_sum, grad_rows, probs, small, gains, tokens, out_grad, residual, hidden_two, qkv, log_total,
    cos_table, sin_table, in_q, in_k, in_v, in_o,
    right, extra, in_grad,
    w_q, w_k, w_v, w_o, turned, head_grads, q_heads, k_heads, v_heads, q_sums, k_sums, v_sums, wide, load_sem,
):
    R, D = tokens.shape
    shard = D // 4
    local, groups = 2, grad_rows.shape[0]
    expert_count = local * groups
    loads = [
        pltpu.make_async_copy(src, dst, load_sem.at[i])
        for i, (src, dst) in enumerate(((in_o, w_o), (in_q, w_q), (in_k, w_k), (in_v, w_v)))
    ]
    for load in loads:
        load.start()
    lane = lax.broadcasted_iota(jnp.int32, (R, 128), 1)

    turned[...] = jnp.zeros_like(turned)
    for owner in range(groups):
        turned[owner * local : (owner + 1) * local, :] = grad_rows[owner, 0:local, :]
    gate_grad = jnp.transpose(turned[...])
    dense = probs[...]
    logit_grad = dense * (gate_grad - jnp.sum(dense * gate_grad, axis=1, keepdims=True))
    logit_grad = logit_grad.astype(jnp.bfloat16)

    whole = residual[...]
    scale_two = lax.rsqrt(jnp.mean(whole * whole, axis=1, keepdims=True) + eps)
    mean_two = jnp.zeros((R, 1), jnp.float32)
    marks = [(lane == expert_count + k).astype(jnp.bfloat16) for k in range(2)]
    for j in range(4):
        cols = slice(j * shard, (j + 1) * shard)
        rows = row_sum[:, cols] + dot_f32(logit_grad, small[j], NT)
        normed = whole[:, cols] * scale_two
        product = rows * normed
        high = product.astype(jnp.bfloat16)
        rest = (product - high.astype(jnp.float32)).astype(jnp.bfloat16)
        part = dot_f32(hidden_two[:, cols], logit_grad, TN)
        wide[:, cols] = rows
        extra[cols, :] = (part + dot_f32(high, marks[1], TN) + dot_f32(rest, marks[1], TN)).astype(jnp.bfloat16)
        gain = gains[j, 1:2, :].astype(jnp.float32)
        mean_two = mean_two + jnp.sum(product * gain, axis=1, keepdims=True)
    mean_two = mean_two * (1.0 / D)
    for j in range(4):
        cols = slice(j * shard, (j + 1) * shard)
        gain = gains[j, 1:2, :].astype(jnp.float32)
        normed = whole[:, cols] * scale_two
        value = out_grad[:, cols].astype(jnp.float32) + scale_two * (wide[:, cols] * gain - normed * mean_two)
        in_grad[:, cols] = value
        right[:, cols] = value.astype(jnp.bfloat16)

    loads[0].wait()
    for j in range(4):
        part = dot_f32(right[:, 0:D], w_o[j], NT).astype(jnp.bfloat16)
        for k in range(shard // HD):
            head_grads[j * (shard // HD) + k] = part[:, k * HD : (k + 1) * HD]
    for head in range(QH):
        q_heads[head] = qkv[:, head * HD : (head + 1) * HD]
    for g in range(KVH):
        k_heads[g] = qkv[:, D + g * HD : D + (g + 1) * HD]
        v_heads[g] = qkv[:, D + (KVH + g) * HD : D + (KVH + g + 1) * HD]

    ends = (lengths[0, 0], lengths[0, 0] + lengths[0, 1], lengths[0, 0] + lengths[0, 1] + lengths[0, 2])

    def doc_of(index):
        total = 0
        for end in ends:
            total = total + jnp.where(index >= end, 1, 0)
        return total

    rows_t = lax.broadcasted_iota(jnp.int32, (R, R), 0)
    rows_u = lax.broadcasted_iota(jnp.int32, (R, R), 1)
    allowed = (doc_of(rows_t) == doc_of(rows_u)) & (rows_u <= rows_t)
    score_scale = HD**-0.5

    def group_step(g, _):
        key_total = jnp.zeros((R, HD), jnp.float32)
        value_total = jnp.zeros((R, HD), jnp.float32)
        for k in range(QH // KVH):
            head = g * (QH // KVH) + k
            scores = dot_f32(q_heads[head], k_heads[g], NT) * score_scale
            log_head = jnp.sum(jnp.where(lane == head, log_total[...], 0.0), axis=1, keepdims=True)
            head_probs = jnp.exp(jnp.where(allowed, scores - log_head, masked_score))
            prob_grad = dot_f32(head_grads[head], v_heads[g], NT)
            centre = jnp.sum(head_probs * prob_grad, axis=1, keepdims=True)
            score_grad = (head_probs * (prob_grad - centre)).astype(jnp.bfloat16)
            q_sums[head] = dot_f32(score_grad, k_heads[g]) * score_scale
            key_total = key_total + dot_f32(score_grad, q_heads[head], TN)
            value_total = value_total + dot_f32(head_probs.astype(jnp.bfloat16), head_grads[head], TN)
        k_sums[g] = key_total * score_scale
        v_sums[g] = value_total
        return 0

    lax.fori_loop(0, KVH, group_step, 0)

    front = lane % HD < HD // 2

    def turn_back(first, second):
        value = jnp.concatenate([first, second], axis=1)
        other = jnp.where(front, pltpu.roll(value, 128 - HD // 2, 1), pltpu.roll(value, HD // 2, 1))
        return (value * cos_table[...] - other * sin_table[...]).astype(jnp.bfloat16)

    for i in range(QH // 2):
        right[:, D + i * 128 : D + (i + 1) * 128] = turn_back(q_sums[2 * i], q_sums[2 * i + 1])
    key_at, value_at = D + QH * HD, D + (QH + KVH) * HD
    for i in range(KVH // 2):
        right[:, key_at + i * 128 : key_at + (i + 1) * 128] = turn_back(k_sums[2 * i], k_sums[2 * i + 1])
        right[:, value_at + i * 128 : value_at + (i + 1) * 128] = jnp.concatenate(
            [v_sums[2 * i], v_sums[2 * i + 1]], axis=1
        ).astype(jnp.bfloat16)
    right[:, value_at + KVH * HD :] = jnp.zeros((R, 128), jnp.bfloat16)

    for load in loads[1:]:
        load.wait()
    inputs = tokens[...].astype(jnp.float32)
    scale_one = lax.rsqrt(jnp.mean(inputs * inputs, axis=1, keepdims=True) + eps)
    mean_one = jnp.zeros((R, 1), jnp.float32)
    for j in range(4):
        cols = slice(j * shard, (j + 1) * shard)
        rows = dot_f32(right[:, D:key_at], w_q[j], NT)
        rows = rows + dot_f32(right[:, key_at:value_at], w_k[j], NT)
        rows = rows + dot_f32(right[:, value_at : value_at + KVH * HD], w_v[j], NT)
        wide[:, cols] = rows
        product = rows * (inputs[:, cols] * scale_one)
        high = product.astype(jnp.bfloat16)
        rest = (product - high.astype(jnp.float32)).astype(jnp.bfloat16)
        part = dot_f32(high, marks[0], TN) + dot_f32(rest, marks[0], TN)
        extra[cols, :] = (extra[cols, :].astype(jnp.float32) + part).astype(jnp.bfloat16)
        gain = gains[j, 0:1, :].astype(jnp.float32)
        mean_one = mean_one + jnp.sum(product * gain, axis=1, keepdims=True)
    mean_one = mean_one * (1.0 / D)
    for j in range(4):
        cols = slice(j * shard, (j + 1) * shard)
        gain = gains[j, 0:1, :].astype(jnp.float32)
        normed = inputs[:, cols] * scale_one
        in_grad[:, cols] = in_grad[:, cols] + scale_one * (wide[:, cols] * gain - normed * mean_one)


def back_call(seq_lengths, row_sum, grad_rows, probs, small, gains, tokens, out_grad, residual, hidden_two, qkv, log_total, cos_table, sin_table, *weights):
    R, D = tokens.shape
    bf, f32 = jnp.bfloat16, jnp.float32
    any_spec = pl.BlockSpec(memory_space=pl.ANY)
    vmem = pl.BlockSpec(memory_space=pltpu.VMEM)
    return pl.pallas_call(
        back_kernel,
        out_shape=(
            jax.ShapeDtypeStruct((R, D + qkv.shape[1] + 128), bf),
            jax.ShapeDtypeStruct((D, 128), bf),
            jax.ShapeDtypeStruct((R, D), f32),
        ),
        in_specs=[pl.BlockSpec(memory_space=pltpu.SMEM)] + [vmem] * 13 + [any_spec] * 4,
        out_specs=(vmem,) * 3,
        scratch_shapes=[pltpu.VMEM(w.shape, bf) for w in weights]
        + [
            pltpu.VMEM((128, R), f32),
            pltpu.VMEM((QH, R, HD), bf),
            pltpu.VMEM((QH, R, HD), bf),
            pltpu.VMEM((KVH, R, HD), bf),
            pltpu.VMEM((KVH, R, HD), bf),
            pltpu.VMEM((QH, R, HD), f32),
            pltpu.VMEM((KVH, R, HD), f32),
            pltpu.VMEM((KVH, R, HD), f32),
            pltpu.VMEM((R, D), f32),
            pltpu.SemaphoreType.DMA((4,)),
        ],
        compiler_params=pltpu.CompilerParams(vmem_limit_bytes=60 * 1024 * 1024),
        cost_estimate=pl.CostEstimate(flops=6 * 10**9, bytes_accessed=30 * 10**6, transcendentals=2 * 10**6),
        name="back",
    )(seq_lengths, row_sum, grad_rows, probs, small, gains, tokens, out_grad, residual, hidden_two, qkv, log_total, cos_table, sin_table, *weights)


def fused_body(
    tokens,
    seq_lengths,
    routes,
    w_query,
    w_key,
    w_value,
    w_output,
    w_router,
    attn_gain,
    moe_gain,
    expert_gate,
    expert_up,
    expert_down,
    out_grad,
):
    width = tokens.shape[1]
    expert_count = w_router.shape[1]
    gains = jnp.pad(jnp.stack([attn_gain, moe_gain]), ((0, 14), (0, 0)))
    small = jnp.pad(w_router, ((0, 0), (0, 128 - expert_count)))
    (
        gains, small, query_w, key_w, value_w, output_w, all_upstream,
        left, qkv, log_total, cos_table, sin_table, residual, hidden_two, probs, by_owner,
    ) = front_call(seq_lengths, tokens, routes, gains, small, w_query, w_key, w_value, w_output, out_grad)
    mix_part, row_sum, grad_rows, own_grads, _, far_grads = moe_call(
        hidden_two, all_upstream, by_owner, expert_gate, expert_up, expert_down
    )
    far_grads = lax.ppermute(far_grads, "dp", [(0, 2), (1, 3), (2, 0), (3, 1)])
    mixture = lax.psum_scatter(mix_part.reshape(-1, width), "expert", scatter_dimension=0, tiled=True)

    right, extra, in_grad = back_call(
        seq_lengths, row_sum, grad_rows, probs, small, gains, tokens, out_grad, residual, hidden_two, qkv, log_total,
        cos_table, sin_table, query_w, key_w, value_w, output_w,
    )
    sums = reduce_call(left, right, extra)
    wide, narrow = QH * HD, KVH * HD
    cuts = (0, wide, 2 * wide, 2 * wide + narrow, 2 * wide + 2 * narrow)
    of_output, of_query, of_key, of_value = [sums[:, i:j] for i, j in zip(cuts, cuts[1:])]
    tail = sums[:, cuts[-1] :]
    far_grads, residual, _ = lax.optimization_barrier((far_grads, residual, of_query))
    expert_grads = own_grads + far_grads.astype(jnp.float32)
    layer_out = (residual + mixture.astype(jnp.float32)).astype(jnp.bfloat16)
    return (
        layer_out,
        in_grad,
        of_query,
        of_key,
        of_value,
        of_output,
        tail[:, :expert_count],
        tail[:, expert_count],
        tail[:, expert_count + 1],
        *[expert_grads[2 * kind : 2 * kind + 2] for kind in range(3)],
    )


def fits_fused(mesh, tokens_shape):
    devices = mesh.shape["dp"] * mesh.shape["expert"]
    return mesh.shape["dp"] == 4 and mesh.shape["expert"] == 8 and tokens_shape[0] == 256 * devices


def solution(mesh):
    placed = (
        P(("dp", "expert"), None),
        P(("dp", "expert"), None),
        P(("dp", "expert"), None),
        P("dp", None),
        P("dp", None),
        P("dp", None),
        P("dp", None),
        P("dp", None),
        P("dp"),
        P("dp"),
        P("expert", None, None),
        P("expert", None, None),
        P("expert", None, None),
        P(("dp", "expert"), None),
    )
    def layer(tokens, *rest):
        return shard(fused_body if fits_fused(mesh, tokens.shape) else body)(tokens, *rest)

    def shard(step):
        return jax.shard_map(
            step,
            mesh=mesh,
            in_specs=placed,
            out_specs=(
                P(("dp", "expert"), None),
                P(("dp", "expert"), None),
                P("dp", None),
                P("dp", None),
                P("dp", None),
                P("dp", None),
                P("dp", None),
                P("dp"),
                P("dp"),
                P("expert", "dp", None),
                P("expert", "dp", None),
                P("expert", "dp", None),
            ),
            check_vma=False,
        )

    return layer
```

```python
import functools
import math

import jax
import jax.numpy as jnp
from jax import lax
from jax.experimental import pallas as pl
from jax.experimental.pallas import tpu as pltpu
from jax.sharding import PartitionSpec as P

MESH = pl.DeviceIdType.MESH

QH = 24
KVH = 8
HD = 64
TOP = 8


eps = 1e-06
rope_base = 10000.0
masked_score = -1e30


def shortened(value):
    return jax.tree.map(lambda a: a.astype(jnp.bfloat16) if a.dtype == jnp.float32 else a, value)


def rms_scale(values):
    return lax.rsqrt(jnp.mean(values * values, axis=-1, keepdims=True) + eps)


def token_layout(lengths_row, row_count):
    token_index = jnp.arange(row_count, dtype=jnp.int32)
    seq_ends = jnp.cumsum(lengths_row)
    passed = (token_index[:, None] >= seq_ends[None, :]).astype(jnp.int32)
    doc_id = jnp.sum(passed, axis=1)
    seq_start = jnp.sum(passed * lengths_row[None, :], axis=1)
    return (doc_id, token_index - seq_start)


def rope_tables(position):
    half_size = HD // 2
    frequency = rope_base ** (-2.0 * jnp.arange(half_size, dtype=jnp.float32) / HD)
    angles = position.astype(jnp.float32)[:, None] * frequency[None, :]
    return (jnp.cos(angles)[:, None, :], jnp.sin(angles)[:, None, :])


def rotate(values, cos_table, sin_table, head_count):
    half_size = HD // 2
    shaped = values.reshape(values.shape[0], head_count, HD)
    front_half = shaped[..., :half_size]
    back_half = shaped[..., half_size:]
    turned = jnp.concatenate(
        [
            front_half * cos_table - back_half * sin_table,
            back_half * cos_table + front_half * sin_table,
        ],
        axis=-1,
    )
    return turned.reshape(values.shape[0], head_count * HD)


def unrotate(values, cos_table, sin_table, head_count):
    half_size = HD // 2
    shaped = values.reshape(values.shape[0], head_count, HD)
    front_half = shaped[..., :half_size]
    back_half = shaped[..., half_size:]
    turned = jnp.concatenate(
        [
            front_half * cos_table + back_half * sin_table,
            back_half * cos_table - front_half * sin_table,
        ],
        axis=-1,
    )
    return turned.reshape(values.shape[0], head_count * HD)


def own_columns(values, local_count):
    start = lax.axis_index("expert") * local_count
    return lax.dynamic_slice_in_dim(values, start, local_count, axis=1)


def body(
    tokens,
    seq_lengths,
    routes,
    w_query,
    w_key,
    w_value,
    w_output,
    w_router,
    attn_gain,
    moe_gain,
    expert_gate,
    expert_up,
    expert_down,
    out_grad,
):
    shards = (w_query, w_key, w_value, w_output, w_router, attn_gain, moe_gain)
    gathered = (
        lax.all_gather(shards[0], "dp", axis=0, tiled=True),
        lax.all_gather(shards[1], "dp", axis=0, tiled=True),
        lax.all_gather(shards[2], "dp", axis=0, tiled=True),
        lax.all_gather(shards[3], "dp", axis=0, tiled=True),
        lax.all_gather(shards[4], "dp", axis=0, tiled=True),
        lax.all_gather(shards[5], "dp", axis=0, tiled=True),
        lax.all_gather(shards[6], "dp", axis=0, tiled=True),
    )
    query_w, key_w, value_w, output_w, router_w, gain_one, gain_two = gathered
    row_count = tokens.shape[0]
    expert_count = w_router.shape[1]
    group_size = QH // KVH
    block_rows = min(512, row_count)
    block_total = row_count // block_rows
    score_scale = HD ** (-0.5)
    doc_id, position = token_layout(seq_lengths[0], row_count)
    cos_table, sin_table = rope_tables(position)
    token_index = jnp.arange(row_count, dtype=jnp.int32)
    block_starts = jnp.arange(block_total, dtype=jnp.int32) * block_rows
    inputs = tokens.astype(jnp.float32)
    scale_one = rms_scale(inputs)
    normed_one = inputs * scale_one
    hidden_one = (normed_one * gain_one.astype(jnp.float32)).astype(jnp.bfloat16)
    query_rot = rotate(
        jnp.dot(hidden_one, query_w, preferred_element_type=jnp.float32), cos_table, sin_table, QH
    ).astype(jnp.bfloat16)
    key_rot = rotate(
        jnp.dot(hidden_one, key_w, preferred_element_type=jnp.float32), cos_table, sin_table, KVH
    ).astype(jnp.bfloat16)
    value_rows = jnp.dot(hidden_one, value_w, preferred_element_type=jnp.float32).astype(
        jnp.bfloat16
    )
    key_heads = key_rot.reshape(row_count, KVH, HD)
    value_heads = value_rows.reshape(row_count, KVH, HD)

    def block_scores(block_start):
        query_block = query_rot.reshape(block_rows, KVH, group_size, HD)
        raw_scores = (
            jnp.einsum("tkgd,ukd->kgtu", query_block, key_heads, preferred_element_type=jnp.float32)
            * score_scale
        )
        block_index = block_start + jnp.arange(block_rows, dtype=jnp.int32)
        allowed = (doc_id[:, None] == doc_id[None, :]) & (
            token_index[None, :] <= block_index[:, None]
        )
        return (query_block, jnp.where(allowed, raw_scores, masked_score))

    def attend_block(block_start):
        query_block, scores = block_scores(block_start)
        row_top = jnp.max(scores, axis=-1, keepdims=True)
        exp_terms = jnp.exp(scores - row_top)
        row_total = jnp.sum(exp_terms, axis=-1, keepdims=True)
        probs_low = (exp_terms / row_total).astype(jnp.bfloat16)
        attended_block = jnp.einsum(
            "kgtu,ukd->tkgd", probs_low, value_heads, preferred_element_type=jnp.float32
        )
        log_total = (row_top + jnp.log(row_total))[..., 0]
        return (attended_block.reshape(block_rows, QH * HD).astype(jnp.bfloat16), log_total)

    attended_blocks, log_blocks = lax.map(attend_block, block_starts)
    attended = attended_blocks.reshape(row_count, QH * HD)
    residual = inputs + jnp.dot(attended, output_w, preferred_element_type=jnp.float32)
    scale_two = rms_scale(residual)
    normed_two = residual * scale_two
    hidden_two = (normed_two * gain_two.astype(jnp.float32)).astype(jnp.bfloat16)
    logits = jnp.dot(hidden_two, router_w, preferred_element_type=jnp.float32)
    expert_ids = jnp.arange(expert_count, dtype=jnp.int32)
    route_hot = (routes[:, :, None] == expert_ids[None, None, :]).astype(jnp.float32)
    chosen = jnp.sum(route_hot * logits[:, None, :], axis=-1)
    gate_probs = jax.nn.softmax(chosen, axis=-1)
    dense_probs = jnp.sum(route_hot * gate_probs[:, :, None], axis=1)
    upstream = out_grad.astype(jnp.float32)
    local_count = expert_gate.shape[0]
    all_hidden = lax.all_gather(hidden_two, "expert", axis=0, tiled=True)
    all_probs = own_columns(lax.all_gather(dense_probs, "expert", axis=0, tiled=True), local_count)
    all_upstream = lax.all_gather(out_grad, "expert", axis=0, tiled=True)
    mix_part = jnp.zeros(all_hidden.shape, jnp.float32)
    row_part = jnp.zeros(all_hidden.shape, jnp.float32)
    grad_columns, down_parts, gate_parts, up_parts = [], [], [], []
    for e in range(local_count):
        prob = all_probs[:, e : e + 1]
        gate_pre = jnp.dot(all_hidden, expert_gate[e], preferred_element_type=jnp.float32)
        up_pre = jnp.dot(all_hidden, expert_up[e], preferred_element_type=jnp.float32)
        raw_grad = jnp.dot(all_upstream, expert_down[e], preferred_element_type=jnp.float32)
        gate_sig = jax.nn.sigmoid(gate_pre)
        gate_act = gate_pre * gate_sig
        activation = gate_act * up_pre
        grad_columns.append(jnp.sum(activation * raw_grad, axis=-1, keepdims=True))
        weighted = (activation * prob).astype(jnp.bfloat16)
        act_grad = raw_grad * prob
        gate_pre_grad = (act_grad * up_pre * gate_sig * (1.0 + gate_pre * (1.0 - gate_sig))).astype(
            jnp.bfloat16
        )
        up_pre_grad = (act_grad * gate_act).astype(jnp.bfloat16)
        mix_part = mix_part + jnp.dot(
            weighted, expert_down[e].T, preferred_element_type=jnp.float32
        )
        row_part = row_part + jnp.dot(
            gate_pre_grad, expert_gate[e].T, preferred_element_type=jnp.float32
        )
        row_part = row_part + jnp.dot(
            up_pre_grad, expert_up[e].T, preferred_element_type=jnp.float32
        )
        down_parts.append(jnp.dot(all_upstream.T, weighted, preferred_element_type=jnp.float32))
        gate_parts.append(jnp.dot(all_hidden.T, gate_pre_grad, preferred_element_type=jnp.float32))
        up_parts.append(jnp.dot(all_hidden.T, up_pre_grad, preferred_element_type=jnp.float32))
    down_partial = jnp.stack(down_parts)
    gate_partial = jnp.stack(gate_parts)
    up_partial = jnp.stack(up_parts)
    grad_dense = lax.all_to_all(
        jnp.concatenate(grad_columns, axis=1), "expert", split_axis=0, concat_axis=1, tiled=True
    )
    gate_grad = jnp.sum(route_hot * grad_dense[:, None, :], axis=-1)
    mixture = lax.psum_scatter(
        mix_part.astype(jnp.bfloat16), "expert", scatter_dimension=0, tiled=True
    ).astype(jnp.float32)
    layer_out = (residual + mixture).astype(jnp.bfloat16)
    hidden_two_grad = lax.psum_scatter(
        row_part.astype(jnp.bfloat16), "expert", scatter_dimension=0, tiled=True
    ).astype(jnp.float32)
    chosen_grad = gate_probs * (gate_grad - jnp.sum(gate_probs * gate_grad, axis=-1, keepdims=True))
    logit_grad = jnp.sum(route_hot * chosen_grad[:, :, None], axis=1).astype(jnp.bfloat16)
    hidden_two_grad = hidden_two_grad + jnp.dot(
        logit_grad, router_w.T, preferred_element_type=jnp.float32
    )
    gain_two_partial = jnp.sum(hidden_two_grad * normed_two, axis=0)
    normed_two_grad = hidden_two_grad * gain_two.astype(jnp.float32)
    residual_grad = upstream + scale_two * (
        normed_two_grad
        - normed_two * jnp.mean(normed_two_grad * normed_two, axis=-1, keepdims=True)
    )
    branch_grad = residual_grad.astype(jnp.bfloat16)
    attended_grad = jnp.dot(branch_grad, output_w.T, preferred_element_type=jnp.float32).astype(
        jnp.bfloat16
    )

    def attend_back(carry, block_data):
        key_acc, value_acc = carry
        block_start, log_total = block_data
        query_block, scores = block_scores(block_start)
        attn_probs = jnp.exp(scores - log_total[..., None])
        probs_low = attn_probs.astype(jnp.bfloat16)
        grad_block = attended_grad.reshape(block_rows, KVH, group_size, HD)
        prob_grad = jnp.einsum(
            "tkgd,ukd->kgtu", grad_block, value_heads, preferred_element_type=jnp.float32
        )
        score_grad = (
            attn_probs * (prob_grad - jnp.sum(attn_probs * prob_grad, axis=-1, keepdims=True))
        ).astype(jnp.bfloat16)
        query_part = (
            jnp.einsum("kgtu,ukd->tkgd", score_grad, key_heads, preferred_element_type=jnp.float32)
            * score_scale
        )
        key_acc = (
            key_acc
            + jnp.einsum(
                "kgtu,tkgd->ukd", score_grad, query_block, preferred_element_type=jnp.float32
            )
            * score_scale
        )
        value_acc = value_acc + jnp.einsum(
            "kgtu,tkgd->ukd", probs_low, grad_block, preferred_element_type=jnp.float32
        )
        return ((key_acc, value_acc), query_part.reshape(block_rows, QH * HD))

    zero_heads = jnp.zeros((row_count, KVH, HD), jnp.float32)
    (key_sums, value_sums), query_blocks = lax.scan(
        attend_back, (zero_heads, zero_heads), (block_starts, log_blocks)
    )
    query_grad = unrotate(
        query_blocks.reshape(row_count, QH * HD), cos_table, sin_table, QH
    ).astype(jnp.bfloat16)
    key_grad = unrotate(key_sums.reshape(row_count, KVH * HD), cos_table, sin_table, KVH).astype(
        jnp.bfloat16
    )
    value_grad = value_sums.reshape(row_count, KVH * HD).astype(jnp.bfloat16)
    hidden_one_grad = jnp.dot(query_grad, query_w.T, preferred_element_type=jnp.float32)
    hidden_one_grad = hidden_one_grad + jnp.dot(
        key_grad, key_w.T, preferred_element_type=jnp.float32
    )
    hidden_one_grad = hidden_one_grad + jnp.dot(
        value_grad, value_w.T, preferred_element_type=jnp.float32
    )
    gain_one_partial = jnp.sum(hidden_one_grad * normed_one, axis=0)
    normed_one_grad = hidden_one_grad * gain_one.astype(jnp.float32)
    in_grad = residual_grad + scale_one * (
        normed_one_grad
        - normed_one * jnp.mean(normed_one_grad * normed_one, axis=-1, keepdims=True)
    )
    query_partial = jnp.dot(hidden_one.T, query_grad, preferred_element_type=jnp.float32)
    key_partial = jnp.dot(hidden_one.T, key_grad, preferred_element_type=jnp.float32)
    value_partial = jnp.dot(hidden_one.T, value_grad, preferred_element_type=jnp.float32)
    output_partial = jnp.dot(attended.T, branch_grad, preferred_element_type=jnp.float32)
    router_partial = jnp.dot(hidden_two.T, logit_grad, preferred_element_type=jnp.float32)
    pieces = jax.tree.map(
        lambda part: part.astype(jnp.float32),
        lax.psum_scatter(
            shortened(
                (
                    query_partial,
                    key_partial,
                    value_partial,
                    output_partial,
                    router_partial,
                    gain_one_partial,
                    gain_two_partial,
                )
            ),
            "dp",
            scatter_dimension=0,
            tiled=True,
        ),
    )
    totals = (
        lax.psum(pieces[0].astype(jnp.bfloat16), "expert").astype(jnp.float32),
        lax.psum(pieces[1].astype(jnp.bfloat16), "expert").astype(jnp.float32),
        lax.psum(pieces[2].astype(jnp.bfloat16), "expert").astype(jnp.float32),
        lax.psum(pieces[3].astype(jnp.bfloat16), "expert").astype(jnp.float32),
        lax.psum(pieces[4].astype(jnp.bfloat16), "expert").astype(jnp.float32),
        lax.psum(pieces[5].astype(jnp.bfloat16), "expert").astype(jnp.float32),
        lax.psum(pieces[6].astype(jnp.bfloat16), "expert").astype(jnp.float32),
    )
    expert_totals = (
        lax.psum_scatter(
            gate_partial.astype(jnp.bfloat16), "dp", scatter_dimension=1, tiled=True
        ).astype(jnp.float32),
        lax.psum_scatter(
            up_partial.astype(jnp.bfloat16), "dp", scatter_dimension=1, tiled=True
        ).astype(jnp.float32),
        lax.psum_scatter(
            down_partial.astype(jnp.bfloat16), "dp", scatter_dimension=1, tiled=True
        ).astype(jnp.float32),
    )
    return (
        layer_out,
        in_grad,
        totals[0],
        totals[1],
        totals[2],
        totals[3],
        totals[4],
        totals[5],
        totals[6],
        expert_totals[0],
        expert_totals[1],
        expert_totals[2],
    )


NT = (((1,), (1,)), ((), ()))
TN = (((0,), (0,)), ((), ()))


def dot_f32(left, right, dims=(((1,), (0,)), ((), ()))):
    return lax.dot_general(left, right, dims, preferred_element_type=jnp.float32)


def entry(rows, index, step):
    value = 0
    for place, row in enumerate(rows):
        for column, digit in enumerate(row):
            if digit:
                value = jnp.where((index == place) & (step == column), digit, value)
    return value


BLOCK_ORDER = ((0, 1, 4, 5, 6, 2, 7, 3), (1, 0, 5, 4, 6, 2, 7, 3))
BEFORE_STEP = (
    ((), ("W1", "X1", "W4", "A4"), (), ("W5",), ("W6",), ("W2",), ("W7",), ("W3",)),
    ((), ("W2", "N2", "W5", "A5", "W0"), (), ("W4", "A4", "W6", "N6", "A0"), (), ("W7", "N7"), (), ("W3", "N3")),
)
SUMS_ACROSS = (((), (), (), (), (2,), (), (3, 1, 0), ()), ((), (), (), (0,), (2,), (), (3, 1), ()))
SUM_ORDER = ((3, 15, 15, 15, 1, 15, 15, 15, 0), (15, 15, 15, 2, 15, 3, 0, 15, 1))
HALVES = 2


def moe_kernel(
    h_in, u_in, p_in, wg_in, wu_in, wd_in,
    d_out, e_out, gg_out, grads_out, core_got, y_out,
    h_all, u_all, p_all, wg, wu, wd, act, gu, partials, rx, rz, d_stage, gg_stage, tile_bf, tile_f32, got_tile,
    load_sem, h_up, h_down, h_across, h_recv, p_send, p_recv, g_send, g_recv,
    x_send, x_recv, z_send, z_recv, d_sem, c_send, c_recv, y_send, tile_sem, out_sem,
    *, comm
):
    A, B, n = 4, 2, 8
    R, D = h_in.shape
    F = wg.shape[2]
    shard = D // 4
    ez, ex = partials.at[pl.ds(0, A)], partials.at[pl.ds(A, A)]
    me = lax.axis_index("expert")
    dp = lax.axis_index("dp")
    a, b = me // B, me % B
    y, c = dp // 2, dp % 2
    partner_x = a * B + (1 - b)
    core_peer = 2 * y + (1 - c)
    y_peer = 2 * (1 - y) + c

    def copy(src, dst, send, recv, **target):
        return pltpu.make_async_remote_copy(
            src_ref=src, dst_ref=dst, send_sem=send, recv_sem=recv, device_id=target, device_id_type=MESH
        )

    loads = [
        pltpu.make_async_copy(h_in, h_all.at[me], load_sem.at[0]),
        pltpu.make_async_copy(u_in, u_all, load_sem.at[1]),
        pltpu.make_async_copy(wg_in, wg, load_sem.at[2]),
        pltpu.make_async_copy(wu_in, wu, load_sem.at[3]),
        pltpu.make_async_copy(wd_in, wd, load_sem.at[4]),
        pltpu.make_async_copy(p_in.at[me], p_all.at[me], load_sem.at[5]),
    ]
    for load in loads:
        load.start()

    barrier = pltpu.get_barrier_semaphore()
    for k in range(1, n):
        pl.semaphore_signal(barrier, inc=1, device_id={"expert": (me + k) % n}, device_id_type=MESH)
    pl.semaphore_signal(barrier, inc=1, device_id={"dp": core_peer}, device_id_type=MESH)
    pl.semaphore_wait(barrier, n)
    loads[0].wait()
    loads[5].wait()

    def send_up(s):
        return copy(h_all.at[s], h_all.at[s], h_up.at[s], h_recv.at[s], expert=me + B)

    def send_down(s):
        return copy(h_all.at[s], h_all.at[s], h_down.at[s], h_recv.at[s], expert=me - B)

    def send_across(s):
        return copy(h_all.at[s], h_all.at[s], h_across.at[s], h_recv.at[s], expert=partner_x)

    def p_copy(peer):
        return copy(p_in.at[peer], p_all.at[me], p_send.at[peer], p_recv.at[me], expert=peer)

    @pl.when(a < A - 1)
    def _():
        send_up(me).start()

    @pl.when(a > 0)
    def _():
        send_down(me).start()

    send_across(me).start()
    for k in range(1, n):
        p_copy((me + k) % n).start()
    for k in range(1, n):
        s = (me + k) % n
        copy(p_in.at[s], p_all.at[s], p_send.at[s], p_recv.at[s], expert=s).wait_recv()
    for load in loads[1:5]:
        load.wait()

    def recv_block(s):
        send_across(s).wait_recv()

    near = jnp.where(a < A // 2, a, A - 1 - a)
    flipped = a >= A // 2

    def turned(row):
        return jnp.where(flipped, A - 1 - row, row)

    def along(s, upward):
        @pl.when(flipped != upward)
        def _():
            send_up(s).start()

        @pl.when(flipped == upward)
        def _():
            send_down(s).start()

    def move(words):
        for word in words:
            code = int(word[1:])
            s = turned(code % A) * B + (1 - b if code >= A else b)
            if word[0] == "W":
                recv_block(s)
            elif word[0] == "X":
                send_across(s).start()
            else:
                along(s, word[0] == "A")

    def d_copy(s, slot):
        return pltpu.make_async_copy(d_stage.at[slot], d_out.at[s], d_sem.at[slot])

    def g_copy(s):
        return copy(gg_stage.at[s], gg_out.at[me], g_send.at[s], g_recv.at[me], expert=s)

    def compute(step, s, row, across):
        rows = pl.ds(pl.multiple_of(s * R, R), R)
        probs = jnp.transpose(p_all[s])
        grad_cols = []
        for e in range(2):
            gate_pre = dot_f32(h_all[s], wg[e])
            up_pre = dot_f32(h_all[s], wu[e])
            raw = dot_f32(u_all[s], wd[e])
            prob = probs[:, e : e + 1]
            sig = 1.0 / (1.0 + jnp.exp(-gate_pre))
            gate_act = gate_pre * sig
            activation = gate_act * up_pre
            grad_cols.append(jnp.sum(activation * raw, axis=1, keepdims=True))
            act[rows, e * F : (e + 1) * F] = (activation * prob).astype(jnp.bfloat16)
            act_grad = raw * prob
            gate_grad = act_grad * up_pre * sig * (1.0 + gate_pre * (1.0 - sig))
            gu[rows, 2 * e * F : (2 * e + 1) * F] = gate_grad.astype(jnp.bfloat16)
            gu[rows, (2 * e + 1) * F : (2 * e + 2) * F] = (act_grad * gate_act).astype(jnp.bfloat16)
        column = lax.broadcasted_iota(jnp.int32, (R, 128), 1)
        both = jnp.where(column == 0, grad_cols[0], jnp.where(column == 1, grad_cols[1], 0.0))
        gg_stage[s] = jnp.transpose(both)[:8]
        slot = step % 2

        @pl.when(step >= 2)
        def _():
            d_copy(s, slot).wait()

        def columns(tile, _):
            cols = pl.ds(pl.multiple_of(tile * 512, 512), 512)
            mixed = dot_f32(act[rows, 0:F], wd[0, cols, :], NT) + dot_f32(act[rows, F : 2 * F], wd[1, cols, :], NT)
            d_stage[slot, :, cols] = mixed.astype(jnp.bfloat16)
            back = dot_f32(gu[rows, 0:F], wg[0, cols, :], NT)
            back += dot_f32(gu[rows, F : 2 * F], wu[0, cols, :], NT)
            back += dot_f32(gu[rows, 2 * F : 3 * F], wg[1, cols, :], NT)
            back += dot_f32(gu[rows, 3 * F : 4 * F], wu[1, cols, :], NT)

            partials[row + jnp.where(across, A, 0), :, cols] = back.astype(jnp.bfloat16)
            return 0

        lax.fori_loop(0, D // 512, columns, 0, unroll=True)
        d_copy(s, slot).start()

        @pl.when(s != me)
        def _():
            g_copy(s).start()

        @pl.when(s == me)
        def _():
            pltpu.make_async_copy(gg_stage.at[s], gg_out.at[me], g_send.at[s]).start()

    part_rows = R // HALVES

    def part_of(part):
        return pl.ds(pl.multiple_of(part * part_rows, 16), part_rows)

    def x_copy(row, part):
        return copy(ex.at[row, part_of(part)], rx.at[row, part_of(part)], x_send.at[row, part], x_recv.at[row, part], expert=partner_x)

    def z_up(row, part):
        return copy(ez.at[row, part_of(part)], rz.at[row + 1, part_of(part)], z_send.at[row, part], z_recv.at[row + 1, part], expert=me + B)

    def z_down(row, part):
        return copy(ez.at[row, part_of(part)], rz.at[row, part_of(part)], z_send.at[row, part], z_recv.at[row, part], expert=me - B)

    def sum_part(row, part):
        x_copy(row, part).wait_recv()
        below = (a > 0) & (row >= a)
        above = (a < A - 1) & (row <= a)

        @pl.when(below)
        def _():
            z_up(row, part).wait_recv()

        @pl.when(above)
        def _():
            z_down(row, part).wait_recv()

        def chunk(index, _):
            rows = pl.ds(pl.multiple_of(part * part_rows + index * 64, 64), 64)
            total = ez[row, rows, :].astype(jnp.float32) + rx[row, rows, :].astype(jnp.float32)

            @pl.when(row != a)
            def _():
                @pl.when(below)
                def _():
                    ez[row, rows, :] = (total + rz[row + 1, rows, :].astype(jnp.float32)).astype(jnp.bfloat16)

                @pl.when(above)
                def _():
                    ez[row, rows, :] = (total + rz[row, rows, :].astype(jnp.float32)).astype(jnp.bfloat16)

                @pl.when(jnp.logical_not(below | above))
                def _():
                    ez[row, rows, :] = total.astype(jnp.bfloat16)

            @pl.when(row == a)
            def _():
                @pl.when(below & above)
                def _():
                    e_out[rows, :] = total + rz[row + 1, rows, :].astype(jnp.float32) + rz[row, rows, :].astype(jnp.float32)

                @pl.when(below & jnp.logical_not(above))
                def _():
                    e_out[rows, :] = total + rz[row + 1, rows, :].astype(jnp.float32)

                @pl.when(above & jnp.logical_not(below))
                def _():
                    e_out[rows, :] = total + rz[row, rows, :].astype(jnp.float32)

            return 0

        lax.fori_loop(0, part_rows // 64, chunk, 0)

        @pl.when(row > a)
        def _():
            z_up(row, part).start()

        @pl.when(row < a)
        def _():
            z_down(row, part).start()

    def sum_parts(row):
        def one(part, _):
            sum_part(row, part)
            return 0

        lax.fori_loop(0, HALVES, one, 0)

    def block_step(step, _):
        for place in range(A // 2):
            for at, words in enumerate(BEFORE_STEP[place]):
                if words:
                    @pl.when((near == place) & (step == at))
                    def _():
                        move(words)

        code = entry(BLOCK_ORDER, near, step)
        across = code >= A
        row = turned(code % A)
        s = row * B + jnp.where(across, 1 - b, b)
        compute(step, s, row, across)
        for place in range(A // 2):
            for at, rows in enumerate(SUMS_ACROSS[place]):
                if rows:
                    @pl.when((near == place) & (step == at))
                    def _():
                        for row in rows:
                            for part in range(HALVES):
                                x_copy(turned(row), part).start()

        @pl.when((near == 0) & (step == n - 2))
        def _():
            sum_parts(turned(2))

        return 0

    lax.fori_loop(0, n, block_step, 0)

    def core_copy(slot, which, index):
        return copy(tile_bf.at[slot], core_got.at[which, index], c_send.at[slot], c_recv.at[which, index], dp=core_peer)

    def y_copy(slot, index):
        return pltpu.make_async_copy(tile_bf.at[slot], y_out.at[index], y_send.at[slot])

    def weight_tile(group, e, kind, left, right):
        owner = jnp.where(group == 0, 2 * (1 - y) + 1 - c, jnp.where(group == 1, y_peer, jnp.where(group == 2, core_peer, dp)))
        cols = pl.ds(pl.multiple_of(owner * shard, 128), shard)
        total = dot_f32(left[:, :, cols].reshape(n * R, shard), right, TN)
        index = kind * 2 + e
        slot = kind

        @pl.when((group == 0) | (group == 2))
        def _():
            @pl.when(e > 0)
            def _():
                core_copy(slot, 0, index).wait_send()

            @pl.when((e == 0) & (group == 2))
            def _():
                y_copy(slot, index).wait()

            tile_bf[slot] = total.astype(jnp.bfloat16)
            core_copy(slot, group // 2, index).start()

        @pl.when(group == 1)
        def _():
            @pl.when(e == 0)
            def _():
                core_copy(slot, 0, index).wait_send()

            @pl.when(e > 0)
            def _():
                y_copy(slot, index).wait()

            core_copy(slot, 0, index).wait_recv()
            got = pltpu.make_async_copy(core_got.at[0, index], got_tile, tile_sem)
            got.start()
            got.wait()
            tile_bf[slot] = (total + got_tile[...].astype(jnp.float32)).astype(jnp.bfloat16)
            y_copy(slot, index).start()

        @pl.when(group == 3)
        def _():
            core_copy(slot, 1, index).wait_recv()
            got = pltpu.make_async_copy(core_got.at[1, index], got_tile, tile_sem)
            got.start()
            got.wait()
            tile_f32[index] = total + got_tile[...].astype(jnp.float32)
            pltpu.make_async_copy(tile_f32.at[index], grads_out.at[index], out_sem.at[index]).start()

    def sum_step(place, _):
        code = entry(SUM_ORDER, near, place)

        @pl.when(code < A)
        def _():
            sum_parts(turned(code))

        @pl.when(place < 8)
        def _():
            group, e = place // 2, place % 2
            weight_tile(group, e, 0, h_all, gu[:, pl.ds(pl.multiple_of(2 * e * F, 128), F)])
            weight_tile(group, e, 1, h_all, gu[:, pl.ds(pl.multiple_of((2 * e + 1) * F, 128), F)])
            weight_tile(group, e, 2, u_all, act[:, pl.ds(pl.multiple_of(e * F, 128), F)])

        return 0

    lax.fori_loop(0, 9, sum_step, 0)

    for kind in range(3):
        core_copy(kind, 1, 3 + kind).wait_send()
    for row in range(A):
        for part in range(HALVES):
            x_copy(row, part).wait_send()

            @pl.when(row != a)
            def _():
                z_up(row, part).wait_send()

    @pl.when(a < A - 1)
    def _():
        send_up(me).wait_send()

    @pl.when(a > 0)
    def _():
        send_down(me).wait_send()

    send_across(me).wait_send()
    for place in range(A // 2):
        @pl.when(near == place)
        def _():
            for word in [word for words in BEFORE_STEP[place] for word in words]:
                code = int(word[1:])
                s = turned(code % A) * B + (1 - b if code >= A else b)
                if word[0] == "X":
                    send_across(s).wait_send()
                elif word[0] != "W":
                    @pl.when(flipped != (word[0] == "A"))
                    def _():
                        send_up(s).wait_send()

                    @pl.when(flipped == (word[0] == "A"))
                    def _():
                        send_down(s).wait_send()

    for k in range(1, n):
        s = (me + k) % n
        p_copy(s).wait_send()
        g_copy(s).wait_send()
        copy(gg_stage.at[s], gg_out.at[s], g_send.at[s], g_recv.at[s], expert=s).wait_recv()
    pltpu.make_async_copy(gg_stage.at[me], gg_out.at[me], g_send.at[me]).wait()
    for slot in range(2):
        d_copy(0, slot).wait()
    for index in range(6):
        pltpu.make_async_copy(tile_f32.at[index], grads_out.at[index], out_sem.at[index]).wait()


def moe_call(hidden, all_upstream, probs, expert_gate, expert_up, expert_down):
    R, D = hidden.shape
    F = expert_gate.shape[2]
    A, n = 4, 8
    shard = D // 4
    bf, f32 = jnp.bfloat16, jnp.float32
    any_spec = pl.BlockSpec(memory_space=pl.ANY)
    vmem = pl.BlockSpec(memory_space=pltpu.VMEM)
    dma = pltpu.SemaphoreType.DMA
    out_shape = (
        jax.ShapeDtypeStruct((n, R, D), bf),
        jax.ShapeDtypeStruct((R, D), f32),
        jax.ShapeDtypeStruct((n, 8, R), f32),
        jax.ShapeDtypeStruct((6, shard, F), f32),
        jax.ShapeDtypeStruct((2, 6, shard, F), bf),
        jax.ShapeDtypeStruct((6, shard, F), bf),
    )
    return pl.pallas_call(
        functools.partial(moe_kernel, comm=True),
        out_shape=out_shape,
        in_specs=[any_spec] * 6,
        out_specs=(any_spec, vmem, any_spec, any_spec, any_spec, any_spec),
        scratch_shapes=[
            pltpu.VMEM((n, R, D), bf),
            pltpu.VMEM((n, R, D), bf),
            pltpu.VMEM((n, 8, R), f32),
            pltpu.VMEM((2, D, F), bf),
            pltpu.VMEM((2, D, F), bf),
            pltpu.VMEM((2, D, F), bf),
            pltpu.VMEM((n * R, 2 * F), bf),
            pltpu.VMEM((n * R, 4 * F), bf),
            pltpu.VMEM((2 * A, R, D), bf),
            pltpu.VMEM((A, R, D), bf),
            pltpu.VMEM((A + 1, R, D), bf),
            pltpu.VMEM((2, R, D), bf),
            pltpu.VMEM((n, 8, R), f32),
            pltpu.VMEM((3, shard, F), bf),
            pltpu.VMEM((6, shard, F), f32),
            pltpu.VMEM((shard, F), bf),
            dma((6,)), dma((n,)), dma((n,)), dma((n,)), dma((n,)), dma((n,)), dma((n,)), dma((n,)), dma((n,)),
            dma((A, HALVES)), dma((A, HALVES)), dma((A, HALVES)), dma((A + 1, HALVES)), dma((2,)),
            dma((3,)), dma((2, 6)), dma((3,)), dma, dma((6,)),
        ],
        compiler_params=pltpu.CompilerParams(
            collective_id=1, has_side_effects=True, vmem_limit_bytes=64 * 1024 * 1024 - 65536
        ),
        cost_estimate=pl.CostEstimate(flops=58 * 10**9, bytes_accessed=60 * 10**6, transcendentals=2 * 10**6),
        name="experts",
    )(hidden, all_upstream, probs, expert_gate, expert_up, expert_down)


def reduce_kernel(
    left, right, extra, out,
    core_out, core_in, y_out, y_in, half, x_out, x_in, own, z_out, z_in, full, ready,
    core_send, core_recv, y_send, y_recv, x_send, x_recv, zs_send, zs_recv, zg_send, zg_recv, xg_send, xg_recv, ready_sem,
):
    A, B = 4, 2
    W = core_out.shape[3]
    shard = core_out.shape[2]
    half_rows, piece = shard // B, shard // (A * B)
    chunks = y_in.shape[0]
    me = lax.axis_index("expert")
    dp = lax.axis_index("dp")
    a, b = me // B, me % B
    y, c = dp // 2, dp % 2
    partner_x = a * B + (1 - b)
    core_peer = 2 * y + (1 - c)
    y_peer = 2 * (1 - y) + c

    def copy(src, dst, send, recv, **target):
        return pltpu.make_async_remote_copy(
            src_ref=src, dst_ref=dst, send_sem=send, recv_sem=recv, device_id=target, device_id_type=MESH
        )

    barrier = pltpu.get_barrier_semaphore()
    for target in [{"dp": core_peer}, {"dp": y_peer}, {"expert": partner_x}] + [
        {"expert": (a + k) % A * B + b} for k in range(1, A)
    ]:
        pl.semaphore_signal(barrier, inc=1, device_id=target, device_id_type=MESH)
    pl.semaphore_wait(barrier, 2 + A)

    def partial(chunk, owner):
        rows = pl.ds(pl.multiple_of(owner * shard, 128), shard)
        cols = pl.ds(pl.multiple_of(chunk * W, 128), W)
        which = jnp.where(chunk < left.shape[2] // W, 0, 1)
        total = dot_f32(left[which, :, rows], right[:, cols], TN)
        share = extra[pl.ds(pl.multiple_of(owner * shard, 128), shard), :].astype(jnp.float32)
        share = jnp.where(chunk == chunks - 1, share, 0.0)
        return jnp.concatenate([total[:, : W - 128], total[:, W - 128 :] + share], axis=1)

    def core_copy(chunk, which):
        slot = chunk % 2
        return copy(core_out.at[slot, which], core_in.at[chunk, which], core_send.at[slot, which], core_recv.at[chunk, which], dp=core_peer)

    def y_copy(chunk):
        slot = chunk % 2
        return copy(y_out.at[slot], y_in.at[chunk], y_send.at[slot], y_recv.at[chunk], dp=y_peer)

    def x_copy(chunk):
        slot = chunk % 2
        return copy(x_out.at[slot], x_in.at[chunk], x_send.at[slot], x_recv.at[chunk], expert=partner_x)

    def z_scatter(chunk, to, source):
        slot = chunk % 2
        return copy(
            z_out.at[slot, pl.ds(pl.multiple_of(to * piece, 16), piece)], z_in.at[chunk, source],
            zs_send.at[slot, to], zs_recv.at[chunk, source], expert=to * B + b,
        )

    def z_gather(chunk, to, source):
        rows = pl.ds(pl.multiple_of(b * half_rows + source * piece, 16), piece)
        return copy(full.at[chunk, rows], full.at[chunk, rows], zg_send.at[chunk, to], zg_recv.at[chunk, source], expert=to * B + b)

    def x_gather(chunk, side):
        rows = pl.ds(pl.multiple_of(side * half_rows, 16), half_rows)
        return copy(full.at[chunk, rows], full.at[chunk, rows], xg_send.at[chunk], xg_recv.at[chunk], expert=partner_x)

    def to_core(chunk):
        for which, owner in ((0, core_peer), (1, 2 * (1 - y) + 1 - c)):
            value = partial(chunk, owner).astype(jnp.bfloat16)

            @pl.when(chunk >= 2)
            def _():
                core_copy(chunk, which).wait_send()

            core_out[chunk % 2, which] = value
            core_copy(chunk, which).start()

    def to_y(chunk):
        value = partial(chunk, y_peer)
        core_copy(chunk, 1).wait_recv()

        @pl.when(chunk >= 2)
        def _():
            y_copy(chunk).wait_send()

        y_out[chunk % 2] = (value + core_in[chunk, 1].astype(jnp.float32)).astype(jnp.bfloat16)
        y_copy(chunk).start()

    def to_x(chunk):
        value = partial(chunk, dp)
        core_copy(chunk, 0).wait_recv()
        y_copy(chunk).wait_recv()
        value = value + core_in[chunk, 0].astype(jnp.float32) + y_in[chunk].astype(jnp.float32)

        @pl.when(chunk >= 2)
        def _():
            x_copy(chunk).wait_send()

        low, high = value[:half_rows], value[half_rows:]
        half[chunk % 2] = jnp.where(b == 0, low, high)
        x_out[chunk % 2] = jnp.where(b == 0, high, low).astype(jnp.bfloat16)
        x_copy(chunk).start()

    def to_z(chunk):
        x_copy(chunk).wait_recv()

        @pl.when(chunk >= 2)
        def _():
            for k in range(1, A):
                z_scatter(chunk, (a + k) % A, a).wait_send()

        total = half[chunk % 2] + x_in[chunk].astype(jnp.float32)
        half[chunk % 2] = total
        own[chunk % 2] = half[chunk % 2, pl.ds(pl.multiple_of(a * piece, 8), piece)]
        z_out[chunk % 2] = total.astype(jnp.bfloat16)
        for k in range(1, A):
            z_scatter(chunk, (a + k) % A, a).start()

    def spread_z(chunk):
        total = own[chunk % 2]
        for k in range(1, A):
            source = (a + k) % A
            z_scatter(chunk, a, source).wait_recv()
            total = total + z_in[chunk, source].astype(jnp.float32)
        rows = pl.ds(pl.multiple_of(b * half_rows + a * piece, 16), piece)
        full[chunk, rows] = total.astype(jnp.bfloat16)
        for k in range(1, A):
            z_gather(chunk, (a + k) % A, a).start()

    def spread_x(chunk):
        for k in range(1, A):
            z_gather(chunk, a, (a + k) % A).wait_recv()
        x_gather(chunk, b).start()

    def written(chunk):
        cols = pl.ds(pl.multiple_of(chunk * W, 128), W)
        return pltpu.make_async_copy(ready.at[chunk % 2], out.at[:, cols], ready_sem.at[chunk % 2])

    def finish(chunk):
        x_gather(chunk, 1 - b).wait_recv()

        @pl.when(chunk >= 2)
        def _():
            written(chunk).wait()

        ready[chunk % 2] = full[chunk].astype(jnp.float32)
        written(chunk).start()

    stages = (to_core, to_y, to_x, to_z, spread_z, spread_x, finish)

    def step(t, _):
        for delay, stage in enumerate(stages):
            @pl.when((t >= delay) & (t < delay + chunks))
            def _():
                stage(t - delay)

        return 0

    lax.fori_loop(0, chunks + len(stages) - 1, step, 0)

    for chunk in range(chunks - 2, chunks):
        written(chunk).wait()
        core_copy(chunk, 0).wait_send()
        core_copy(chunk, 1).wait_send()
        y_copy(chunk).wait_send()
        x_copy(chunk).wait_send()
        for k in range(1, A):
            z_scatter(chunk, (a + k) % A, a).wait_send()

    def drain(chunk, _):
        for k in range(1, A):
            z_gather(chunk, (a + k) % A, a).wait_send()
        x_gather(chunk, b).wait_send()
        return 0

    lax.fori_loop(0, chunks, drain, 0)


def reduce_call(left, right, extra):
    D = left.shape[2]
    width = right.shape[1]
    W, A, B = 384, 4, 2
    shard, chunks = D // 4, width // W
    bf, f32 = jnp.bfloat16, jnp.float32
    vmem = pl.BlockSpec(memory_space=pltpu.VMEM)
    dma = pltpu.SemaphoreType.DMA
    piece = shard // (A * B)
    return pl.pallas_call(
        reduce_kernel,
        out_shape=jax.ShapeDtypeStruct((shard, width), f32),
        in_specs=[vmem] * 3,
        out_specs=pl.BlockSpec(memory_space=pl.ANY),
        scratch_shapes=[
            pltpu.VMEM((2, 2, shard, W), bf),
            pltpu.VMEM((chunks, 2, shard, W), bf),
            pltpu.VMEM((2, shard, W), bf),
            pltpu.VMEM((chunks, shard, W), bf),
            pltpu.VMEM((2, shard // B, W), f32),
            pltpu.VMEM((2, shard // B, W), bf),
            pltpu.VMEM((chunks, shard // B, W), bf),
            pltpu.VMEM((2, piece, W), f32),
            pltpu.VMEM((2, shard // B, W), bf),
            pltpu.VMEM((chunks, A, piece, W), bf),
            pltpu.VMEM((chunks, shard, W), bf),
            pltpu.VMEM((2, shard, W), f32),
            dma((2, 2)), dma((chunks, 2)), dma((2,)), dma((chunks,)), dma((2,)), dma((chunks,)),
            dma((2, A)), dma((chunks, A)), dma((chunks, A)), dma((chunks, A)), dma((chunks,)), dma((chunks,)), dma((2,)),
        ],
        compiler_params=pltpu.CompilerParams(
            collective_id=2, has_side_effects=True, vmem_limit_bytes=56 * 1024 * 1024
        ),
        cost_estimate=pl.CostEstimate(flops=4 * 10**9, bytes_accessed=20 * 10**6, transcendentals=0),
        name="weight_sums",
    )(left, right, extra)


PIECES = 3


def front_kernel(
    lengths, tokens, routes, w_gain, w_small, w_q, w_k, w_v, w_o, u_in,
    out_gain, out_small, out_q, out_k, out_v, out_o, u_all,
    left_hbm, qkv_hbm, log_total, cos_out, sin_out, residual, hidden_two, probs_out, by_owner,
    all_gain, all_small, all_q, all_k, all_v, all_o, sums, q_heads, k_heads, v_heads, mixed, left_out, qkv,
    keep_sem, core_send, y_send, pass_send, w_recv, u_keep, u_up, u_down, u_across, u_recv,
    o_send, o_recv, o_pass, o_far, early_sem,
):
    A, B = 4, 2
    R, D = tokens.shape
    shard = D // 4
    attended, hidden_one = left_out.at[0], left_out.at[1]
    me = lax.axis_index("expert")
    dp = lax.axis_index("dp")
    a, b = me // B, me % B
    y, c = dp // 2, dp % 2
    partner_x = a * B + (1 - b)
    core_peer = 2 * y + (1 - c)
    y_peer = 2 * (1 - y) + c
    far_peer = 2 * (1 - y) + 1 - c
    shards = (w_gain, w_small, w_q, w_k, w_v, w_o)
    landed = (all_gain, all_small, all_q, all_k, all_v, all_o)
    kept = (out_gain, out_small, out_q, out_k, out_v, out_o)
    count = len(shards)
    GAIN, SMALL, QUERY, KEY, VALUE, OUTPUT = range(count)

    def copy(src, dst, send, recv, **target):
        return pltpu.make_async_remote_copy(
            src_ref=src, dst_ref=dst, send_sem=send, recv_sem=recv, device_id=target, device_id_type=MESH
        )

    barrier = pltpu.get_barrier_semaphore()
    for target in [{"dp": core_peer}, {"dp": y_peer}, {"expert": partner_x}] + [
        {"expert": (a + k) % A * B + b} for k in range(1, A)
    ]:
        pl.semaphore_signal(barrier, inc=1, device_id=target, device_id_type=MESH)
    pl.semaphore_wait(barrier, 2 + A)

    def to_core(i):
        return copy(shards[i], landed[i].at[dp], core_send.at[i], w_recv.at[i, dp], dp=core_peer)

    def to_y(i):
        return copy(shards[i], landed[i].at[dp], y_send.at[i], w_recv.at[i, dp], dp=y_peer)

    def pass_on(i):
        return copy(landed[i].at[y_peer], landed[i].at[y_peer], pass_send.at[i], w_recv.at[i, y_peer], dp=core_peer)

    def keep_own(i):
        return pltpu.make_async_copy(shards[i], kept[i].at[dp], keep_sem.at[i, dp])

    def keep(i, owner):
        return pltpu.make_async_copy(landed[i].at[owner], kept[i].at[owner], keep_sem.at[i, owner])

    def receive(i, owner):
        copy(shards[i], landed[i].at[owner], core_send.at[i], w_recv.at[i, owner], dp=core_peer).wait_recv()
        keep(i, owner).start()

    def forward(i):
        receive(i, y_peer)
        pass_on(i).start()

    def u_send_up(src, s):
        return copy(src, u_all.at[s], u_up.at[s], u_recv.at[s], expert=me + B)

    def u_send_down(src, s):
        return copy(src, u_all.at[s], u_down.at[s], u_recv.at[s], expert=me - B)

    def u_send_across(src, s):
        return copy(src, u_all.at[s], u_across.at[s], u_recv.at[s], expert=partner_x)

    def take(row):
        @pl.when((row >= 0) & (row < A))
        def _():
            s = row * B + b
            u_send_across(u_all.at[s], s).wait_recv()
            u_send_across(u_all.at[s], s).start()

            @pl.when((row < a) & (a < A - 1))
            def _():
                u_send_up(u_all.at[s], s).start()

            @pl.when((row > a) & (a > 0))
            def _():
                u_send_down(u_all.at[s], s).start()

    def o_part(piece):
        return pl.ds(piece * (shard // PIECES), shard // PIECES)

    def o_to_y(piece):
        rows = o_part(piece)
        return copy(w_o.at[rows], all_o.at[dp, rows], o_send.at[piece], o_recv.at[piece], dp=y_peer)

    def o_from_y(piece):
        rows = o_part(piece)
        return copy(w_o.at[rows], all_o.at[y_peer, rows], o_send.at[piece], o_recv.at[piece], dp=y_peer)

    def o_pass_on(piece):
        rows = o_part(piece)
        return copy(all_o.at[y_peer, rows], all_o.at[y_peer, rows], o_pass.at[piece], o_far.at[piece], dp=core_peer)

    def o_from_core(piece):
        rows = o_part(piece)
        return copy(all_o.at[far_peer, rows], all_o.at[far_peer, rows], o_pass.at[piece], o_far.at[piece], dp=core_peer)

    keep_u = pltpu.make_async_copy(u_in, u_all.at[me], u_keep)

    @pl.when(a < A - 1)
    def _():
        u_send_up(u_in, me).start()

    @pl.when(a > 0)
    def _():
        u_send_down(u_in, me).start()

    u_send_across(u_in, me).start()
    for i in range(count):
        if i == OUTPUT:
            for piece in range(PIECES):
                o_to_y(piece).start()
        else:
            to_y(i).start()
        to_core(i).start()
        keep_own(i).start()
    keep_u.start()

    row_index = lax.broadcasted_iota(jnp.int32, (R, 128), 0)
    ends = (lengths[0, 0], lengths[0, 0] + lengths[0, 1], lengths[0, 0] + lengths[0, 1] + lengths[0, 2])
    start = jnp.where(row_index >= ends[2], ends[2], jnp.where(row_index >= ends[1], ends[1], jnp.where(row_index >= ends[0], ends[0], 0)))
    position = (row_index - start).astype(jnp.float32)
    lane = lax.broadcasted_iota(jnp.int32, (R, 128), 1)
    pair = (lane % (HD // 2)).astype(jnp.float32)
    frequency = jnp.exp(pair * (-2.0 / HD * math.log(rope_base)))
    angle = position * frequency
    front = lane % HD < HD // 2
    cos_out[...] = jnp.cos(angle)
    sin_out[...] = jnp.where(front, -jnp.sin(angle), jnp.sin(angle))

    def doc_of(index):
        total = 0
        for end in ends:
            total = total + jnp.where(index >= end, 1, 0)
        return total

    rows_t = lax.broadcasted_iota(jnp.int32, (R, R), 0)
    rows_u = lax.broadcasted_iota(jnp.int32, (R, R), 1)
    allowed = (doc_of(rows_t) == doc_of(rows_u)) & (rows_u <= rows_t)

    inputs = tokens[...].astype(jnp.float32)
    scale_one = lax.rsqrt(jnp.mean(inputs * inputs, axis=1, keepdims=True) + eps)

    forward(GAIN)
    receive(GAIN, core_peer)
    receive(GAIN, far_peer)
    all_gain[dp] = w_gain[...]
    for j in range(4):
        cols = slice(j * shard, (j + 1) * shard)
        gain = all_gain[j, 0:1, :].astype(jnp.float32)
        hidden_one[:, cols] = (inputs[:, cols] * scale_one * gain).astype(jnp.bfloat16)

    offsets = {QUERY: 0, KEY: D, VALUE: D + KVH * HD}
    sums[...] = jnp.zeros_like(sums)

    def product(i, owner, own=False):
        cols = pl.ds(pl.multiple_of(owner * shard, 128), shard)
        left = hidden_one[:, cols]
        width = shards[i].shape[1]

        def tile(t, _):
            into = pl.ds(pl.multiple_of(offsets[i] + t * 512, 128), 512)
            part = pl.ds(pl.multiple_of(t * 512, 128), 512)
            weight = shards[i][:, part] if own else landed[i][owner, :, part]
            sums[:, into] += dot_f32(left, weight)
            return 0

        lax.fori_loop(0, width // 512, tile, 0)

    for i in (QUERY, KEY, VALUE):
        product(i, dp, own=True)
    for i in (QUERY, KEY, VALUE):
        receive(i, core_peer)
        product(i, core_peer)
    take(a - 1)
    take(a + 1)
    forward(SMALL)
    receive(SMALL, core_peer)
    forward(QUERY)
    product(QUERY, y_peer)
    receive(QUERY, far_peer)
    product(QUERY, far_peer)
    take(a - 2)
    take(a + 2)
    forward(KEY)
    product(KEY, y_peer)
    receive(KEY, far_peer)
    product(KEY, far_peer)
    forward(VALUE)
    product(VALUE, y_peer)
    receive(VALUE, far_peer)
    product(VALUE, far_peer)

    def rotated(columns):
        value = sums[:, columns]
        other = jnp.where(front, pltpu.roll(value, 128 - HD // 2, 1), pltpu.roll(value, HD // 2, 1))
        return (value * cos_out[...] + other * sin_out[...]).astype(jnp.bfloat16)

    for pair_index in range(QH // 2):
        columns = slice(pair_index * 128, (pair_index + 1) * 128)
        value = rotated(columns)
        qkv[:, columns] = value
        q_heads[2 * pair_index] = value[:, :HD]
        q_heads[2 * pair_index + 1] = value[:, HD:]
    for pair_index in range(KVH // 2):
        columns = slice(D + pair_index * 128, D + (pair_index + 1) * 128)
        value = rotated(columns)
        qkv[:, columns] = value
        k_heads[2 * pair_index] = value[:, :HD]
        k_heads[2 * pair_index + 1] = value[:, HD:]
        columns = slice(D + KVH * HD + pair_index * 128, D + KVH * HD + (pair_index + 1) * 128)
        value = sums[:, columns].astype(jnp.bfloat16)
        qkv[:, columns] = value
        v_heads[2 * pair_index] = value[:, :HD]
        v_heads[2 * pair_index + 1] = value[:, HD:]
    log_total[...] = jnp.zeros_like(log_total)

    def group_step(g, _):
        for k in range(QH // KVH):
            head = g * (QH // KVH) + k
            scores = dot_f32(q_heads[head], k_heads[g], NT) * HD**-0.5
            scores = jnp.where(allowed, scores, masked_score)
            top = jnp.max(scores, axis=1, keepdims=True)
            terms = jnp.exp(scores - top)
            total = jnp.sum(terms, axis=1, keepdims=True)
            low = (terms / total).astype(jnp.bfloat16)
            mixed[head] = dot_f32(low, v_heads[g]).astype(jnp.bfloat16)
            log_total[...] += jnp.where(lane == head, top + jnp.log(total), 0.0)
        return 0

    lax.fori_loop(0, KVH, group_step, 0)
    take(a - 3)
    take(a + 3)
    for pair_index in range(QH // 2):
        attended[:, pair_index * 128 : (pair_index + 1) * 128] = jnp.concatenate(
            [mixed[2 * pair_index], mixed[2 * pair_index + 1]], axis=1
        )

    residual[...] = inputs
    early = (
        pltpu.make_async_copy(left_out, left_hbm, early_sem.at[0]),
        pltpu.make_async_copy(qkv, qkv_hbm, early_sem.at[1]),
    )
    for write in early:
        write.start()

    def out_product(owner, own=False):
        cols = pl.ds(pl.multiple_of(owner * shard, 128), shard)
        left = attended[:, cols]

        def tile(t, _):
            part = pl.ds(pl.multiple_of(t * 512, 128), 512)
            weight = w_o[:, part] if own else all_o[owner, :, part]
            residual[:, part] += dot_f32(left, weight)
            return 0

        lax.fori_loop(0, D // 512, tile, 0)

    out_product(dp, own=True)
    receive(OUTPUT, core_peer)
    out_product(core_peer)
    receive(SMALL, far_peer)
    all_small[dp] = w_small[...]

    def piece_product(owner, piece):
        rows = o_part(piece)
        left = attended[:, pl.ds(pl.multiple_of(owner * shard + piece * (shard // PIECES), 128), shard // PIECES)]
        for t in range(D // 512):
            part = slice(t * 512, (t + 1) * 512)
            residual[:, part] += dot_f32(left, all_o[owner, rows, part])

    for piece in range(PIECES):
        o_from_y(piece).wait_recv()
        o_pass_on(piece).start()
        if piece:
            o_from_core(piece - 1).wait_recv()
            piece_product(far_peer, piece - 1)
        piece_product(y_peer, piece)
    keep(OUTPUT, y_peer).start()
    o_from_core(PIECES - 1).wait_recv()
    piece_product(far_peer, PIECES - 1)
    keep(OUTPUT, far_peer).start()

    whole = residual[...]
    scale_two = lax.rsqrt(jnp.mean(whole * whole, axis=1, keepdims=True) + eps)
    logits = jnp.zeros((R, 128), jnp.float32)
    for j in range(4):
        cols = slice(j * shard, (j + 1) * shard)
        gain = all_gain[j, 1:2, :].astype(jnp.float32)
        value = (whole[:, cols] * scale_two * gain).astype(jnp.bfloat16)
        hidden_two[:, cols] = value
        logits = logits + dot_f32(value, all_small[j])
    chosen = lane == routes[:, 0:1]
    for j in range(1, TOP):
        chosen = chosen | (lane == routes[:, j : j + 1])
    logits = jnp.where(chosen, logits, masked_score)
    terms = jnp.where(chosen, jnp.exp(logits - jnp.max(logits, axis=1, keepdims=True)), 0.0)
    probs = terms / jnp.sum(terms, axis=1, keepdims=True)
    probs_out[...] = probs
    turned = jnp.transpose(probs)
    by_owner[...] = jnp.zeros_like(by_owner)
    local = 2
    for owner in range(A * B):
        by_owner[owner, 0:local, :] = turned[owner * local : (owner + 1) * local]

    for row in range(A):
        s = row * B + 1 - b
        u_send_across(u_all.at[s], s).wait_recv()
    for i in range(count):
        keep_own(i).wait()
        for owner in (core_peer, y_peer, far_peer):
            keep(i, owner).wait()
        to_core(i).wait_send()
        if i != OUTPUT:
            to_y(i).wait_send()
            pass_on(i).wait_send()
    for piece in range(PIECES):
        o_to_y(piece).wait_send()
        o_pass_on(piece).wait_send()
    for write in early:
        write.wait()
    keep_u.wait()

    @pl.when(a < A - 1)
    def _():
        u_send_up(u_in, me).wait_send()

    @pl.when(a > 0)
    def _():
        u_send_down(u_in, me).wait_send()

    for row in range(A):
        s = row * B + b
        u_send_across(u_all.at[s], s).wait_send()

        @pl.when((row < a) & (a < A - 1))
        def _():
            u_send_up(u_all.at[s], s).wait_send()

        @pl.when((row > a) & (a > 0))
        def _():
            u_send_down(u_all.at[s], s).wait_send()


def front_call(seq_lengths, tokens, routes, gains, small, w_query, w_key, w_value, w_output, out_grad):
    n = 8
    R, D = tokens.shape
    bf, f32 = jnp.bfloat16, jnp.float32
    any_spec = pl.BlockSpec(memory_space=pl.ANY)
    vmem = pl.BlockSpec(memory_space=pltpu.VMEM)
    dma = pltpu.SemaphoreType.DMA
    shards = (gains, small, w_query, w_key, w_value, w_output)
    whole = w_query.shape[1] + w_key.shape[1] + w_value.shape[1]
    return pl.pallas_call(
        front_kernel,
        out_shape=tuple(jax.ShapeDtypeStruct((4, *w.shape), bf) for w in shards)
        + (
            jax.ShapeDtypeStruct((n, R, D), bf),
            jax.ShapeDtypeStruct((2, R, D), bf),
            jax.ShapeDtypeStruct((R, whole), bf),
            jax.ShapeDtypeStruct((R, 128), f32),
            jax.ShapeDtypeStruct((R, 128), f32),
            jax.ShapeDtypeStruct((R, 128), f32),
            jax.ShapeDtypeStruct((R, D), f32),
            jax.ShapeDtypeStruct((R, D), bf),
            jax.ShapeDtypeStruct((R, 128), f32),
            jax.ShapeDtypeStruct((n, 8, R), f32),
        ),
        in_specs=[pl.BlockSpec(memory_space=pltpu.SMEM)] + [vmem] * 9,
        out_specs=(any_spec,) * 9 + (vmem,) * 7,
        scratch_shapes=[pltpu.VMEM((4, *w.shape), bf) for w in shards]
        + [
            pltpu.VMEM((R, whole), f32),
            pltpu.VMEM((QH, R, HD), bf),
            pltpu.VMEM((KVH, R, HD), bf),
            pltpu.VMEM((KVH, R, HD), bf),
            pltpu.VMEM((QH, R, HD), bf),
            pltpu.VMEM((2, R, D), bf),
            pltpu.VMEM((R, whole), bf),
            dma((6, 4)), dma((6,)), dma((6,)), dma((6,)), dma((6, 4)), dma, dma((n,)), dma((n,)), dma((n,)), dma((n,)),
            dma((PIECES,)), dma((PIECES,)), dma((PIECES,)), dma((PIECES,)), dma((2,)),
        ],
        compiler_params=pltpu.CompilerParams(
            collective_id=3, has_side_effects=True, vmem_limit_bytes=60 * 1024 * 1024
        ),
        cost_estimate=pl.CostEstimate(flops=4 * 10**9, bytes_accessed=40 * 10**6, transcendentals=2 * 10**6),
        name="front",
    )(seq_lengths, tokens, routes, *shards, out_grad)


def back_kernel(
    lengths, row_sum, grad_rows, probs, small, gains, tokens, out_grad, residual, hidden_two, qkv, log_total,
    cos_table, sin_table, in_q, in_k, in_v, in_o,
    right, extra, in_grad,
    w_q, w_k, w_v, w_o, turned, head_grads, q_heads, k_heads, v_heads, q_sums, k_sums, v_sums, wide, load_sem,
):
    R, D = tokens.shape
    shard = D // 4
    local, groups = 2, grad_rows.shape[0]
    expert_count = local * groups
    loads = [
        pltpu.make_async_copy(src, dst, load_sem.at[i])
        for i, (src, dst) in enumerate(((in_o, w_o), (in_q, w_q), (in_k, w_k), (in_v, w_v)))
    ]
    for load in loads:
        load.start()
    lane = lax.broadcasted_iota(jnp.int32, (R, 128), 1)

    turned[...] = jnp.zeros_like(turned)
    for owner in range(groups):
        turned[owner * local : (owner + 1) * local, :] = grad_rows[owner, 0:local, :]
    gate_grad = jnp.transpose(turned[...])
    dense = probs[...]
    logit_grad = dense * (gate_grad - jnp.sum(dense * gate_grad, axis=1, keepdims=True))
    logit_grad = logit_grad.astype(jnp.bfloat16)

    whole = residual[...]
    scale_two = lax.rsqrt(jnp.mean(whole * whole, axis=1, keepdims=True) + eps)
    mean_two = jnp.zeros((R, 1), jnp.float32)
    marks = [(lane == expert_count + k).astype(jnp.bfloat16) for k in range(2)]
    for j in range(4):
        cols = slice(j * shard, (j + 1) * shard)
        rows = row_sum[:, cols] + dot_f32(logit_grad, small[j], NT)
        normed = whole[:, cols] * scale_two
        product = rows * normed
        high = product.astype(jnp.bfloat16)
        rest = (product - high.astype(jnp.float32)).astype(jnp.bfloat16)
        part = dot_f32(hidden_two[:, cols], logit_grad, TN)
        wide[:, cols] = rows
        extra[cols, :] = (part + dot_f32(high, marks[1], TN) + dot_f32(rest, marks[1], TN)).astype(jnp.bfloat16)
        gain = gains[j, 1:2, :].astype(jnp.float32)
        mean_two = mean_two + jnp.sum(product * gain, axis=1, keepdims=True)
    mean_two = mean_two * (1.0 / D)
    for j in range(4):
        cols = slice(j * shard, (j + 1) * shard)
        gain = gains[j, 1:2, :].astype(jnp.float32)
        normed = whole[:, cols] * scale_two
        value = out_grad[:, cols].astype(jnp.float32) + scale_two * (wide[:, cols] * gain - normed * mean_two)
        in_grad[:, cols] = value
        right[:, cols] = value.astype(jnp.bfloat16)

    loads[0].wait()
    for j in range(4):
        part = dot_f32(right[:, 0:D], w_o[j], NT).astype(jnp.bfloat16)
        for k in range(shard // HD):
            head_grads[j * (shard // HD) + k] = part[:, k * HD : (k + 1) * HD]
    for head in range(QH):
        q_heads[head] = qkv[:, head * HD : (head + 1) * HD]
    for g in range(KVH):
        k_heads[g] = qkv[:, D + g * HD : D + (g + 1) * HD]
        v_heads[g] = qkv[:, D + (KVH + g) * HD : D + (KVH + g + 1) * HD]

    ends = (lengths[0, 0], lengths[0, 0] + lengths[0, 1], lengths[0, 0] + lengths[0, 1] + lengths[0, 2])

    def doc_of(index):
        total = 0
        for end in ends:
            total = total + jnp.where(index >= end, 1, 0)
        return total

    rows_t = lax.broadcasted_iota(jnp.int32, (R, R), 0)
    rows_u = lax.broadcasted_iota(jnp.int32, (R, R), 1)
    allowed = (doc_of(rows_t) == doc_of(rows_u)) & (rows_u <= rows_t)
    score_scale = HD**-0.5

    def group_step(g, _):
        key_total = jnp.zeros((R, HD), jnp.float32)
        value_total = jnp.zeros((R, HD), jnp.float32)
        for k in range(QH // KVH):
            head = g * (QH // KVH) + k
            scores = dot_f32(q_heads[head], k_heads[g], NT) * score_scale
            log_head = jnp.sum(jnp.where(lane == head, log_total[...], 0.0), axis=1, keepdims=True)
            head_probs = jnp.exp(jnp.where(allowed, scores - log_head, masked_score))
            prob_grad = dot_f32(head_grads[head], v_heads[g], NT)
            centre = jnp.sum(head_probs * prob_grad, axis=1, keepdims=True)
            score_grad = (head_probs * (prob_grad - centre)).astype(jnp.bfloat16)
            q_sums[head] = dot_f32(score_grad, k_heads[g]) * score_scale
            key_total = key_total + dot_f32(score_grad, q_heads[head], TN)
            value_total = value_total + dot_f32(head_probs.astype(jnp.bfloat16), head_grads[head], TN)
        k_sums[g] = key_total * score_scale
        v_sums[g] = value_total
        return 0

    lax.fori_loop(0, KVH, group_step, 0)

    front = lane % HD < HD // 2

    def turn_back(first, second):
        value = jnp.concatenate([first, second], axis=1)
        other = jnp.where(front, pltpu.roll(value, 128 - HD // 2, 1), pltpu.roll(value, HD // 2, 1))
        return (value * cos_table[...] - other * sin_table[...]).astype(jnp.bfloat16)

    for i in range(QH // 2):
        right[:, D + i * 128 : D + (i + 1) * 128] = turn_back(q_sums[2 * i], q_sums[2 * i + 1])
    key_at, value_at = D + QH * HD, D + (QH + KVH) * HD
    for i in range(KVH // 2):
        right[:, key_at + i * 128 : key_at + (i + 1) * 128] = turn_back(k_sums[2 * i], k_sums[2 * i + 1])
        right[:, value_at + i * 128 : value_at + (i + 1) * 128] = jnp.concatenate(
            [v_sums[2 * i], v_sums[2 * i + 1]], axis=1
        ).astype(jnp.bfloat16)
    right[:, value_at + KVH * HD :] = jnp.zeros((R, 128), jnp.bfloat16)

    for load in loads[1:]:
        load.wait()
    inputs = tokens[...].astype(jnp.float32)
    scale_one = lax.rsqrt(jnp.mean(inputs * inputs, axis=1, keepdims=True) + eps)
    mean_one = jnp.zeros((R, 1), jnp.float32)
    for j in range(4):
        cols = slice(j * shard, (j + 1) * shard)
        rows = dot_f32(right[:, D:key_at], w_q[j], NT)
        rows = rows + dot_f32(right[:, key_at:value_at], w_k[j], NT)
        rows = rows + dot_f32(right[:, value_at : value_at + KVH * HD], w_v[j], NT)
        wide[:, cols] = rows
        product = rows * (inputs[:, cols] * scale_one)
        high = product.astype(jnp.bfloat16)
        rest = (product - high.astype(jnp.float32)).astype(jnp.bfloat16)
        part = dot_f32(high, marks[0], TN) + dot_f32(rest, marks[0], TN)
        extra[cols, :] = (extra[cols, :].astype(jnp.float32) + part).astype(jnp.bfloat16)
        gain = gains[j, 0:1, :].astype(jnp.float32)
        mean_one = mean_one + jnp.sum(product * gain, axis=1, keepdims=True)
    mean_one = mean_one * (1.0 / D)
    for j in range(4):
        cols = slice(j * shard, (j + 1) * shard)
        gain = gains[j, 0:1, :].astype(jnp.float32)
        normed = inputs[:, cols] * scale_one
        in_grad[:, cols] = in_grad[:, cols] + scale_one * (wide[:, cols] * gain - normed * mean_one)


def back_call(seq_lengths, row_sum, grad_rows, probs, small, gains, tokens, out_grad, residual, hidden_two, qkv, log_total, cos_table, sin_table, *weights):
    R, D = tokens.shape
    bf, f32 = jnp.bfloat16, jnp.float32
    any_spec = pl.BlockSpec(memory_space=pl.ANY)
    vmem = pl.BlockSpec(memory_space=pltpu.VMEM)
    return pl.pallas_call(
        back_kernel,
        out_shape=(
            jax.ShapeDtypeStruct((R, D + qkv.shape[1] + 128), bf),
            jax.ShapeDtypeStruct((D, 128), bf),
            jax.ShapeDtypeStruct((R, D), f32),
        ),
        in_specs=[pl.BlockSpec(memory_space=pltpu.SMEM)] + [vmem] * 13 + [any_spec] * 4,
        out_specs=(vmem,) * 3,
        scratch_shapes=[pltpu.VMEM(w.shape, bf) for w in weights]
        + [
            pltpu.VMEM((128, R), f32),
            pltpu.VMEM((QH, R, HD), bf),
            pltpu.VMEM((QH, R, HD), bf),
            pltpu.VMEM((KVH, R, HD), bf),
            pltpu.VMEM((KVH, R, HD), bf),
            pltpu.VMEM((QH, R, HD), f32),
            pltpu.VMEM((KVH, R, HD), f32),
            pltpu.VMEM((KVH, R, HD), f32),
            pltpu.VMEM((R, D), f32),
            pltpu.SemaphoreType.DMA((4,)),
        ],
        compiler_params=pltpu.CompilerParams(vmem_limit_bytes=60 * 1024 * 1024),
        cost_estimate=pl.CostEstimate(flops=6 * 10**9, bytes_accessed=30 * 10**6, transcendentals=2 * 10**6),
        name="back",
    )(seq_lengths, row_sum, grad_rows, probs, small, gains, tokens, out_grad, residual, hidden_two, qkv, log_total, cos_table, sin_table, *weights)


def fused_body(
    tokens,
    seq_lengths,
    routes,
    w_query,
    w_key,
    w_value,
    w_output,
    w_router,
    attn_gain,
    moe_gain,
    expert_gate,
    expert_up,
    expert_down,
    out_grad,
):
    width = tokens.shape[1]
    expert_count = w_router.shape[1]
    gains = jnp.pad(jnp.stack([attn_gain, moe_gain]), ((0, 14), (0, 0)))
    small = jnp.pad(w_router, ((0, 0), (0, 128 - expert_count)))
    (
        gains, small, query_w, key_w, value_w, output_w, all_upstream,
        left, qkv, log_total, cos_table, sin_table, residual, hidden_two, probs, by_owner,
    ) = front_call(seq_lengths, tokens, routes, gains, small, w_query, w_key, w_value, w_output, out_grad)
    mix_part, row_sum, grad_rows, own_grads, _, far_grads = moe_call(
        hidden_two, all_upstream, by_owner, expert_gate, expert_up, expert_down
    )
    far_grads = lax.ppermute(far_grads, "dp", [(0, 2), (1, 3), (2, 0), (3, 1)])
    mixture = lax.psum_scatter(mix_part.reshape(-1, width), "expert", scatter_dimension=0, tiled=True)

    right, extra, in_grad = back_call(
        seq_lengths, row_sum, grad_rows, probs, small, gains, tokens, out_grad, residual, hidden_two, qkv, log_total,
        cos_table, sin_table, query_w, key_w, value_w, output_w,
    )
    sums = reduce_call(left, right, extra)
    wide, narrow = QH * HD, KVH * HD
    cuts = (0, wide, 2 * wide, 2 * wide + narrow, 2 * wide + 2 * narrow)
    of_output, of_query, of_key, of_value = [sums[:, i:j] for i, j in zip(cuts, cuts[1:])]
    tail = sums[:, cuts[-1] :]
    far_grads, residual, _ = lax.optimization_barrier((far_grads, residual, of_query))
    expert_grads = own_grads + far_grads.astype(jnp.float32)
    layer_out = (residual + mixture.astype(jnp.float32)).astype(jnp.bfloat16)
    return (
        layer_out,
        in_grad,
        of_query,
        of_key,
        of_value,
        of_output,
        tail[:, :expert_count],
        tail[:, expert_count],
        tail[:, expert_count + 1],
        *[expert_grads[2 * kind : 2 * kind + 2] for kind in range(3)],
    )


def fits_fused(mesh, tokens_shape):
    devices = mesh.shape["dp"] * mesh.shape["expert"]
    return mesh.shape["dp"] == 4 and mesh.shape["expert"] == 8 and tokens_shape[0] == 256 * devices


def solution(mesh):
    placed = (
        P(("dp", "expert"), None),
        P(("dp", "expert"), None),
        P(("dp", "expert"), None),
        P("dp", None),
        P("dp", None),
        P("dp", None),
        P("dp", None),
        P("dp", None),
        P("dp"),
        P("dp"),
        P("expert", None, None),
        P("expert", None, None),
        P("expert", None, None),
        P(("dp", "expert"), None),
    )
    def layer(tokens, *rest):
        return shard(fused_body if fits_fused(mesh, tokens.shape) else body)(tokens, *rest)

    def shard(step):
        return jax.shard_map(
            step,
            mesh=mesh,
            in_specs=placed,
            out_specs=(
                P(("dp", "expert"), None),
                P(("dp", "expert"), None),
                P("dp", None),
                P("dp", None),
                P("dp", None),
                P("dp", None),
                P("dp", None),
                P("dp"),
                P("dp"),
                P("expert", "dp", None),
                P("expert", "dp", None),
                P("expert", "dp", None),
            ),
            check_vma=False,
        )

    return layer
```

```python
import functools
import math

import jax
import jax.numpy as jnp
from jax import lax
from jax.experimental import pallas as pl
from jax.experimental.pallas import tpu as pltpu
from jax.sharding import PartitionSpec as P

MESH = pl.DeviceIdType.MESH

QH = 24
KVH = 8
HD = 64
TOP = 8


eps = 1e-06
rope_base = 10000.0
masked_score = -1e30


def shortened(value):
    return jax.tree.map(lambda a: a.astype(jnp.bfloat16) if a.dtype == jnp.float32 else a, value)


def rms_scale(values):
    return lax.rsqrt(jnp.mean(values * values, axis=-1, keepdims=True) + eps)


def token_layout(lengths_row, row_count):
    token_index = jnp.arange(row_count, dtype=jnp.int32)
    seq_ends = jnp.cumsum(lengths_row)
    passed = (token_index[:, None] >= seq_ends[None, :]).astype(jnp.int32)
    doc_id = jnp.sum(passed, axis=1)
    seq_start = jnp.sum(passed * lengths_row[None, :], axis=1)
    return (doc_id, token_index - seq_start)


def rope_tables(position):
    half_size = HD // 2
    frequency = rope_base ** (-2.0 * jnp.arange(half_size, dtype=jnp.float32) / HD)
    angles = position.astype(jnp.float32)[:, None] * frequency[None, :]
    return (jnp.cos(angles)[:, None, :], jnp.sin(angles)[:, None, :])


def rotate(values, cos_table, sin_table, head_count):
    half_size = HD // 2
    shaped = values.reshape(values.shape[0], head_count, HD)
    front_half = shaped[..., :half_size]
    back_half = shaped[..., half_size:]
    turned = jnp.concatenate(
        [
            front_half * cos_table - back_half * sin_table,
            back_half * cos_table + front_half * sin_table,
        ],
        axis=-1,
    )
    return turned.reshape(values.shape[0], head_count * HD)


def unrotate(values, cos_table, sin_table, head_count):
    half_size = HD // 2
    shaped = values.reshape(values.shape[0], head_count, HD)
    front_half = shaped[..., :half_size]
    back_half = shaped[..., half_size:]
    turned = jnp.concatenate(
        [
            front_half * cos_table + back_half * sin_table,
            back_half * cos_table - front_half * sin_table,
        ],
        axis=-1,
    )
    return turned.reshape(values.shape[0], head_count * HD)


def own_columns(values, local_count):
    start = lax.axis_index("expert") * local_count
    return lax.dynamic_slice_in_dim(values, start, local_count, axis=1)


def body(
    tokens,
    seq_lengths,
    routes,
    w_query,
    w_key,
    w_value,
    w_output,
    w_router,
    attn_gain,
    moe_gain,
    expert_gate,
    expert_up,
    expert_down,
    out_grad,
):
    shards = (w_query, w_key, w_value, w_output, w_router, attn_gain, moe_gain)
    gathered = (
        lax.all_gather(shards[0], "dp", axis=0, tiled=True),
        lax.all_gather(shards[1], "dp", axis=0, tiled=True),
        lax.all_gather(shards[2], "dp", axis=0, tiled=True),
        lax.all_gather(shards[3], "dp", axis=0, tiled=True),
        lax.all_gather(shards[4], "dp", axis=0, tiled=True),
        lax.all_gather(shards[5], "dp", axis=0, tiled=True),
        lax.all_gather(shards[6], "dp", axis=0, tiled=True),
    )
    query_w, key_w, value_w, output_w, router_w, gain_one, gain_two = gathered
    row_count = tokens.shape[0]
    expert_count = w_router.shape[1]
    group_size = QH // KVH
    block_rows = min(512, row_count)
    block_total = row_count // block_rows
    score_scale = HD ** (-0.5)
    doc_id, position = token_layout(seq_lengths[0], row_count)
    cos_table, sin_table = rope_tables(position)
    token_index = jnp.arange(row_count, dtype=jnp.int32)
    block_starts = jnp.arange(block_total, dtype=jnp.int32) * block_rows
    inputs = tokens.astype(jnp.float32)
    scale_one = rms_scale(inputs)
    normed_one = inputs * scale_one
    hidden_one = (normed_one * gain_one.astype(jnp.float32)).astype(jnp.bfloat16)
    query_rot = rotate(
        jnp.dot(hidden_one, query_w, preferred_element_type=jnp.float32), cos_table, sin_table, QH
    ).astype(jnp.bfloat16)
    key_rot = rotate(
        jnp.dot(hidden_one, key_w, preferred_element_type=jnp.float32), cos_table, sin_table, KVH
    ).astype(jnp.bfloat16)
    value_rows = jnp.dot(hidden_one, value_w, preferred_element_type=jnp.float32).astype(
        jnp.bfloat16
    )
    key_heads = key_rot.reshape(row_count, KVH, HD)
    value_heads = value_rows.reshape(row_count, KVH, HD)

    def block_scores(block_start):
        query_block = query_rot.reshape(block_rows, KVH, group_size, HD)
        raw_scores = (
            jnp.einsum("tkgd,ukd->kgtu", query_block, key_heads, preferred_element_type=jnp.float32)
            * score_scale
        )
        block_index = block_start + jnp.arange(block_rows, dtype=jnp.int32)
        allowed = (doc_id[:, None] == doc_id[None, :]) & (
            token_index[None, :] <= block_index[:, None]
        )
        return (query_block, jnp.where(allowed, raw_scores, masked_score))

    def attend_block(block_start):
        query_block, scores = block_scores(block_start)
        row_top = jnp.max(scores, axis=-1, keepdims=True)
        exp_terms = jnp.exp(scores - row_top)
        row_total = jnp.sum(exp_terms, axis=-1, keepdims=True)
        probs_low = (exp_terms / row_total).astype(jnp.bfloat16)
        attended_block = jnp.einsum(
            "kgtu,ukd->tkgd", probs_low, value_heads, preferred_element_type=jnp.float32
        )
        log_total = (row_top + jnp.log(row_total))[..., 0]
        return (attended_block.reshape(block_rows, QH * HD).astype(jnp.bfloat16), log_total)

    attended_blocks, log_blocks = lax.map(attend_block, block_starts)
    attended = attended_blocks.reshape(row_count, QH * HD)
    residual = inputs + jnp.dot(attended, output_w, preferred_element_type=jnp.float32)
    scale_two = rms_scale(residual)
    normed_two = residual * scale_two
    hidden_two = (normed_two * gain_two.astype(jnp.float32)).astype(jnp.bfloat16)
    logits = jnp.dot(hidden_two, router_w, preferred_element_type=jnp.float32)
    expert_ids = jnp.arange(expert_count, dtype=jnp.int32)
    route_hot = (routes[:, :, None] == expert_ids[None, None, :]).astype(jnp.float32)
    chosen = jnp.sum(route_hot * logits[:, None, :], axis=-1)
    gate_probs = jax.nn.softmax(chosen, axis=-1)
    dense_probs = jnp.sum(route_hot * gate_probs[:, :, None], axis=1)
    upstream = out_grad.astype(jnp.float32)
    local_count = expert_gate.shape[0]
    all_hidden = lax.all_gather(hidden_two, "expert", axis=0, tiled=True)
    all_probs = own_columns(lax.all_gather(dense_probs, "expert", axis=0, tiled=True), local_count)
    all_upstream = lax.all_gather(out_grad, "expert", axis=0, tiled=True)
    mix_part = jnp.zeros(all_hidden.shape, jnp.float32)
    row_part = jnp.zeros(all_hidden.shape, jnp.float32)
    grad_columns, down_parts, gate_parts, up_parts = [], [], [], []
    for e in range(local_count):
        prob = all_probs[:, e : e + 1]
        gate_pre = jnp.dot(all_hidden, expert_gate[e], preferred_element_type=jnp.float32)
        up_pre = jnp.dot(all_hidden, expert_up[e], preferred_element_type=jnp.float32)
        raw_grad = jnp.dot(all_upstream, expert_down[e], preferred_element_type=jnp.float32)
        gate_sig = jax.nn.sigmoid(gate_pre)
        gate_act = gate_pre * gate_sig
        activation = gate_act * up_pre
        grad_columns.append(jnp.sum(activation * raw_grad, axis=-1, keepdims=True))
        weighted = (activation * prob).astype(jnp.bfloat16)
        act_grad = raw_grad * prob
        gate_pre_grad = (act_grad * up_pre * gate_sig * (1.0 + gate_pre * (1.0 - gate_sig))).astype(
            jnp.bfloat16
        )
        up_pre_grad = (act_grad * gate_act).astype(jnp.bfloat16)
        mix_part = mix_part + jnp.dot(
            weighted, expert_down[e].T, preferred_element_type=jnp.float32
        )
        row_part = row_part + jnp.dot(
            gate_pre_grad, expert_gate[e].T, preferred_element_type=jnp.float32
        )
        row_part = row_part + jnp.dot(
            up_pre_grad, expert_up[e].T, preferred_element_type=jnp.float32
        )
        down_parts.append(jnp.dot(all_upstream.T, weighted, preferred_element_type=jnp.float32))
        gate_parts.append(jnp.dot(all_hidden.T, gate_pre_grad, preferred_element_type=jnp.float32))
        up_parts.append(jnp.dot(all_hidden.T, up_pre_grad, preferred_element_type=jnp.float32))
    down_partial = jnp.stack(down_parts)
    gate_partial = jnp.stack(gate_parts)
    up_partial = jnp.stack(up_parts)
    grad_dense = lax.all_to_all(
        jnp.concatenate(grad_columns, axis=1), "expert", split_axis=0, concat_axis=1, tiled=True
    )
    gate_grad = jnp.sum(route_hot * grad_dense[:, None, :], axis=-1)
    mixture = lax.psum_scatter(
        mix_part.astype(jnp.bfloat16), "expert", scatter_dimension=0, tiled=True
    ).astype(jnp.float32)
    layer_out = (residual + mixture).astype(jnp.bfloat16)
    hidden_two_grad = lax.psum_scatter(
        row_part.astype(jnp.bfloat16), "expert", scatter_dimension=0, tiled=True
    ).astype(jnp.float32)
    chosen_grad = gate_probs * (gate_grad - jnp.sum(gate_probs * gate_grad, axis=-1, keepdims=True))
    logit_grad = jnp.sum(route_hot * chosen_grad[:, :, None], axis=1).astype(jnp.bfloat16)
    hidden_two_grad = hidden_two_grad + jnp.dot(
        logit_grad, router_w.T, preferred_element_type=jnp.float32
    )
    gain_two_partial = jnp.sum(hidden_two_grad * normed_two, axis=0)
    normed_two_grad = hidden_two_grad * gain_two.astype(jnp.float32)
    residual_grad = upstream + scale_two * (
        normed_two_grad
        - normed_two * jnp.mean(normed_two_grad * normed_two, axis=-1, keepdims=True)
    )
    branch_grad = residual_grad.astype(jnp.bfloat16)
    attended_grad = jnp.dot(branch_grad, output_w.T, preferred_element_type=jnp.float32).astype(
        jnp.bfloat16
    )

    def attend_back(carry, block_data):
        key_acc, value_acc = carry
        block_start, log_total = block_data
        query_block, scores = block_scores(block_start)
        attn_probs = jnp.exp(scores - log_total[..., None])
        probs_low = attn_probs.astype(jnp.bfloat16)
        grad_block = attended_grad.reshape(block_rows, KVH, group_size, HD)
        prob_grad = jnp.einsum(
            "tkgd,ukd->kgtu", grad_block, value_heads, preferred_element_type=jnp.float32
        )
        score_grad = (
            attn_probs * (prob_grad - jnp.sum(attn_probs * prob_grad, axis=-1, keepdims=True))
        ).astype(jnp.bfloat16)
        query_part = (
            jnp.einsum("kgtu,ukd->tkgd", score_grad, key_heads, preferred_element_type=jnp.float32)
            * score_scale
        )
        key_acc = (
            key_acc
            + jnp.einsum(
                "kgtu,tkgd->ukd", score_grad, query_block, preferred_element_type=jnp.float32
            )
            * score_scale
        )
        value_acc = value_acc + jnp.einsum(
            "kgtu,tkgd->ukd", probs_low, grad_block, preferred_element_type=jnp.float32
        )
        return ((key_acc, value_acc), query_part.reshape(block_rows, QH * HD))

    zero_heads = jnp.zeros((row_count, KVH, HD), jnp.float32)
    (key_sums, value_sums), query_blocks = lax.scan(
        attend_back, (zero_heads, zero_heads), (block_starts, log_blocks)
    )
    query_grad = unrotate(
        query_blocks.reshape(row_count, QH * HD), cos_table, sin_table, QH
    ).astype(jnp.bfloat16)
    key_grad = unrotate(key_sums.reshape(row_count, KVH * HD), cos_table, sin_table, KVH).astype(
        jnp.bfloat16
    )
    value_grad = value_sums.reshape(row_count, KVH * HD).astype(jnp.bfloat16)
    hidden_one_grad = jnp.dot(query_grad, query_w.T, preferred_element_type=jnp.float32)
    hidden_one_grad = hidden_one_grad + jnp.dot(
        key_grad, key_w.T, preferred_element_type=jnp.float32
    )
    hidden_one_grad = hidden_one_grad + jnp.dot(
        value_grad, value_w.T, preferred_element_type=jnp.float32
    )
    gain_one_partial = jnp.sum(hidden_one_grad * normed_one, axis=0)
    normed_one_grad = hidden_one_grad * gain_one.astype(jnp.float32)
    in_grad = residual_grad + scale_one * (
        normed_one_grad
        - normed_one * jnp.mean(normed_one_grad * normed_one, axis=-1, keepdims=True)
    )
    query_partial = jnp.dot(hidden_one.T, query_grad, preferred_element_type=jnp.float32)
    key_partial = jnp.dot(hidden_one.T, key_grad, preferred_element_type=jnp.float32)
    value_partial = jnp.dot(hidden_one.T, value_grad, preferred_element_type=jnp.float32)
    output_partial = jnp.dot(attended.T, branch_grad, preferred_element_type=jnp.float32)
    router_partial = jnp.dot(hidden_two.T, logit_grad, preferred_element_type=jnp.float32)
    pieces = jax.tree.map(
        lambda part: part.astype(jnp.float32),
        lax.psum_scatter(
            shortened(
                (
                    query_partial,
                    key_partial,
                    value_partial,
                    output_partial,
                    router_partial,
                    gain_one_partial,
                    gain_two_partial,
                )
            ),
            "dp",
            scatter_dimension=0,
            tiled=True,
        ),
    )
    totals = (
        lax.psum(pieces[0].astype(jnp.bfloat16), "expert").astype(jnp.float32),
        lax.psum(pieces[1].astype(jnp.bfloat16), "expert").astype(jnp.float32),
        lax.psum(pieces[2].astype(jnp.bfloat16), "expert").astype(jnp.float32),
        lax.psum(pieces[3].astype(jnp.bfloat16), "expert").astype(jnp.float32),
        lax.psum(pieces[4].astype(jnp.bfloat16), "expert").astype(jnp.float32),
        lax.psum(pieces[5].astype(jnp.bfloat16), "expert").astype(jnp.float32),
        lax.psum(pieces[6].astype(jnp.bfloat16), "expert").astype(jnp.float32),
    )
    expert_totals = (
        lax.psum_scatter(
            gate_partial.astype(jnp.bfloat16), "dp", scatter_dimension=1, tiled=True
        ).astype(jnp.float32),
        lax.psum_scatter(
            up_partial.astype(jnp.bfloat16), "dp", scatter_dimension=1, tiled=True
        ).astype(jnp.float32),
        lax.psum_scatter(
            down_partial.astype(jnp.bfloat16), "dp", scatter_dimension=1, tiled=True
        ).astype(jnp.float32),
    )
    return (
        layer_out,
        in_grad,
        totals[0],
        totals[1],
        totals[2],
        totals[3],
        totals[4],
        totals[5],
        totals[6],
        expert_totals[0],
        expert_totals[1],
        expert_totals[2],
    )


NT = (((1,), (1,)), ((), ()))
TN = (((0,), (0,)), ((), ()))


def dot_f32(left, right, dims=(((1,), (0,)), ((), ()))):
    return lax.dot_general(left, right, dims, preferred_element_type=jnp.float32)


def entry(rows, index, step):
    value = 0
    for place, row in enumerate(rows):
        for column, digit in enumerate(row):
            if digit:
                value = jnp.where((index == place) & (step == column), digit, value)
    return value


BLOCK_ORDER = ((0, 1, 4, 5, 6, 2, 7, 3), (1, 0, 5, 4, 6, 2, 7, 3))
BEFORE_STEP = (
    ((), ("W1", "X1", "W4", "A4"), (), ("W5",), ("W6",), ("W2",), ("W7",), ("W3",)),
    ((), ("W2", "N2", "W5", "A5", "W0"), (), ("W4", "A4", "W6", "N6", "A0"), (), ("W7", "N7"), (), ("W3", "N3")),
)
SUMS_ACROSS = (((), (), (), (), (2,), (), (3, 1, 0), ()), ((), (), (), (0,), (2,), (), (3, 1), ()))
SUM_ORDER = ((3, 15, 15, 15, 1, 15, 15, 15, 0), (15, 15, 15, 2, 15, 3, 0, 15, 1))
HALVES = 2


def moe_kernel(
    h_in, u_in, p_in, wg_in, wu_in, wd_in,
    d_out, e_out, gg_out, grads_out, core_got, y_out,
    h_all, u_all, p_all, wg, wu, wd, act, gu, partials, rx, rz, d_stage, gg_stage, tile_bf, tile_f32, got_tile,
    load_sem, h_up, h_down, h_across, h_recv, p_send, p_recv, g_send, g_recv,
    x_send, x_recv, z_send, z_recv, d_sem, c_send, c_recv, y_send, tile_sem, out_sem,
    *, comm
):
    A, B, n = 4, 2, 8
    R, D = h_in.shape
    F = wg.shape[2]
    shard = D // 4
    ez, ex = partials.at[pl.ds(0, A)], partials.at[pl.ds(A, A)]
    me = lax.axis_index("expert")
    dp = lax.axis_index("dp")
    a, b = me // B, me % B
    y, c = dp // 2, dp % 2
    partner_x = a * B + (1 - b)
    core_peer = 2 * y + (1 - c)
    y_peer = 2 * (1 - y) + c

    def copy(src, dst, send, recv, **target):
        return pltpu.make_async_remote_copy(
            src_ref=src, dst_ref=dst, send_sem=send, recv_sem=recv, device_id=target, device_id_type=MESH
        )

    loads = [
        pltpu.make_async_copy(h_in, h_all.at[me], load_sem.at[0]),
        pltpu.make_async_copy(u_in, u_all, load_sem.at[1]),
        pltpu.make_async_copy(wg_in, wg, load_sem.at[2]),
        pltpu.make_async_copy(wu_in, wu, load_sem.at[3]),
        pltpu.make_async_copy(wd_in, wd, load_sem.at[4]),
        pltpu.make_async_copy(p_in.at[me], p_all.at[me], load_sem.at[5]),
    ]
    for load in loads:
        load.start()

    barrier = pltpu.get_barrier_semaphore()
    for k in range(1, n):
        pl.semaphore_signal(barrier, inc=1, device_id={"expert": (me + k) % n}, device_id_type=MESH)
    pl.semaphore_signal(barrier, inc=1, device_id={"dp": core_peer}, device_id_type=MESH)
    pl.semaphore_wait(barrier, n)
    loads[0].wait()
    loads[5].wait()

    def send_up(s):
        return copy(h_all.at[s], h_all.at[s], h_up.at[s], h_recv.at[s], expert=me + B)

    def send_down(s):
        return copy(h_all.at[s], h_all.at[s], h_down.at[s], h_recv.at[s], expert=me - B)

    def send_across(s):
        return copy(h_all.at[s], h_all.at[s], h_across.at[s], h_recv.at[s], expert=partner_x)

    def p_copy(peer):
        return copy(p_in.at[peer], p_all.at[me], p_send.at[peer], p_recv.at[me], expert=peer)

    @pl.when(a < A - 1)
    def _():
        send_up(me).start()

    @pl.when(a > 0)
    def _():
        send_down(me).start()

    send_across(me).start()
    for k in range(1, n):
        p_copy((me + k) % n).start()
    for k in range(1, n):
        s = (me + k) % n
        copy(p_in.at[s], p_all.at[s], p_send.at[s], p_recv.at[s], expert=s).wait_recv()
    for load in loads[1:5]:
        load.wait()

    def recv_block(s):
        send_across(s).wait_recv()

    near = jnp.where(a < A // 2, a, A - 1 - a)
    flipped = a >= A // 2

    def turned(row):
        return jnp.where(flipped, A - 1 - row, row)

    def along(s, upward):
        @pl.when(flipped != upward)
        def _():
            send_up(s).start()

        @pl.when(flipped == upward)
        def _():
            send_down(s).start()

    def move(words):
        for word in words:
            code = int(word[1:])
            s = turned(code % A) * B + (1 - b if code >= A else b)
            if word[0] == "W":
                recv_block(s)
            elif word[0] == "X":
                send_across(s).start()
            else:
                along(s, word[0] == "A")

    def d_copy(s, slot):
        return pltpu.make_async_copy(d_stage.at[slot], d_out.at[s], d_sem.at[slot])

    def g_copy(s):
        return copy(gg_stage.at[s], gg_out.at[me], g_send.at[s], g_recv.at[me], expert=s)

    def compute(step, s, row, across):
        rows = pl.ds(pl.multiple_of(s * R, R), R)
        probs = jnp.transpose(p_all[s])
        grad_cols = []
        for e in range(2):
            gate_pre = dot_f32(h_all[s], wg[e])
            up_pre = dot_f32(h_all[s], wu[e])
            raw = dot_f32(u_all[s], wd[e])
            prob = probs[:, e : e + 1]
            sig = 1.0 / (1.0 + jnp.exp(-gate_pre))
            gate_act = gate_pre * sig
            activation = gate_act * up_pre
            grad_cols.append(jnp.sum(activation * raw, axis=1, keepdims=True))
            act[rows, e * F : (e + 1) * F] = (activation * prob).astype(jnp.bfloat16)
            act_grad = raw * prob
            gate_grad = act_grad * up_pre * sig * (1.0 + gate_pre * (1.0 - sig))
            gu[rows, 2 * e * F : (2 * e + 1) * F] = gate_grad.astype(jnp.bfloat16)
            gu[rows, (2 * e + 1) * F : (2 * e + 2) * F] = (act_grad * gate_act).astype(jnp.bfloat16)
        column = lax.broadcasted_iota(jnp.int32, (R, 128), 1)
        both = jnp.where(column == 0, grad_cols[0], jnp.where(column == 1, grad_cols[1], 0.0))
        gg_stage[s] = jnp.transpose(both)[:8]
        slot = step % 2

        @pl.when(step >= 2)
        def _():
            d_copy(s, slot).wait()

        def columns(tile, _):
            cols = pl.ds(pl.multiple_of(tile * 512, 512), 512)
            mixed = dot_f32(act[rows, 0:F], wd[0, cols, :], NT) + dot_f32(act[rows, F : 2 * F], wd[1, cols, :], NT)
            d_stage[slot, :, cols] = mixed.astype(jnp.bfloat16)
            back = dot_f32(gu[rows, 0:F], wg[0, cols, :], NT)
            back += dot_f32(gu[rows, F : 2 * F], wu[0, cols, :], NT)
            back += dot_f32(gu[rows, 2 * F : 3 * F], wg[1, cols, :], NT)
            back += dot_f32(gu[rows, 3 * F : 4 * F], wu[1, cols, :], NT)

            partials[row + jnp.where(across, A, 0), :, cols] = back.astype(jnp.bfloat16)
            return 0

        lax.fori_loop(0, D // 512, columns, 0, unroll=True)
        d_copy(s, slot).start()

        @pl.when(s != me)
        def _():
            g_copy(s).start()

        @pl.when(s == me)
        def _():
            pltpu.make_async_copy(gg_stage.at[s], gg_out.at[me], g_send.at[s]).start()

    part_rows = R // HALVES

    def part_of(part):
        return pl.ds(pl.multiple_of(part * part_rows, 16), part_rows)

    def x_copy(row, part):
        return copy(ex.at[row, part_of(part)], rx.at[row, part_of(part)], x_send.at[row, part], x_recv.at[row, part], expert=partner_x)

    def z_up(row, part):
        return copy(ez.at[row, part_of(part)], rz.at[row + 1, part_of(part)], z_send.at[row, part], z_recv.at[row + 1, part], expert=me + B)

    def z_down(row, part):
        return copy(ez.at[row, part_of(part)], rz.at[row, part_of(part)], z_send.at[row, part], z_recv.at[row, part], expert=me - B)

    def sum_part(row, part):
        x_copy(row, part).wait_recv()
        below = (a > 0) & (row >= a)
        above = (a < A - 1) & (row <= a)

        @pl.when(below)
        def _():
            z_up(row, part).wait_recv()

        @pl.when(above)
        def _():
            z_down(row, part).wait_recv()

        def chunk(index, _):
            rows = pl.ds(pl.multiple_of(part * part_rows + index * 64, 64), 64)
            total = ez[row, rows, :].astype(jnp.float32) + rx[row, rows, :].astype(jnp.float32)

            @pl.when(row != a)
            def _():
                @pl.when(below)
                def _():
                    ez[row, rows, :] = (total + rz[row + 1, rows, :].astype(jnp.float32)).astype(jnp.bfloat16)

                @pl.when(above)
                def _():
                    ez[row, rows, :] = (total + rz[row, rows, :].astype(jnp.float32)).astype(jnp.bfloat16)

                @pl.when(jnp.logical_not(below | above))
                def _():
                    ez[row, rows, :] = total.astype(jnp.bfloat16)

            @pl.when(row == a)
            def _():
                @pl.when(below & above)
                def _():
                    e_out[rows, :] = total + rz[row + 1, rows, :].astype(jnp.float32) + rz[row, rows, :].astype(jnp.float32)

                @pl.when(below & jnp.logical_not(above))
                def _():
                    e_out[rows, :] = total + rz[row + 1, rows, :].astype(jnp.float32)

                @pl.when(above & jnp.logical_not(below))
                def _():
                    e_out[rows, :] = total + rz[row, rows, :].astype(jnp.float32)

            return 0

        lax.fori_loop(0, part_rows // 64, chunk, 0)

        @pl.when(row > a)
        def _():
            z_up(row, part).start()

        @pl.when(row < a)
        def _():
            z_down(row, part).start()

    def sum_parts(row):
        def one(part, _):
            sum_part(row, part)
            return 0

        lax.fori_loop(0, HALVES, one, 0)

    def block_step(step, _):
        for place in range(A // 2):
            for at, words in enumerate(BEFORE_STEP[place]):
                if words:
                    @pl.when((near == place) & (step == at))
                    def _():
                        move(words)

        code = entry(BLOCK_ORDER, near, step)
        across = code >= A
        row = turned(code % A)
        s = row * B + jnp.where(across, 1 - b, b)
        compute(step, s, row, across)
        for place in range(A // 2):
            for at, rows in enumerate(SUMS_ACROSS[place]):
                if rows:
                    @pl.when((near == place) & (step == at))
                    def _():
                        for row in rows:
                            for part in range(HALVES):
                                x_copy(turned(row), part).start()

        @pl.when((near == 0) & (step == n - 2))
        def _():
            sum_parts(turned(2))

        return 0

    lax.fori_loop(0, n, block_step, 0)

    def core_copy(slot, which, index):
        return copy(tile_bf.at[slot], core_got.at[which, index], c_send.at[slot], c_recv.at[which, index], dp=core_peer)

    def y_copy(slot, index):
        return pltpu.make_async_copy(tile_bf.at[slot], y_out.at[index], y_send.at[slot])

    def weight_tile(group, e, kind, left, right):
        owner = jnp.where(group == 0, 2 * (1 - y) + 1 - c, jnp.where(group == 1, y_peer, jnp.where(group == 2, core_peer, dp)))
        cols = pl.ds(pl.multiple_of(owner * shard, 128), shard)
        total = dot_f32(left[:, :, cols].reshape(n * R, shard), right, TN)
        index = kind * 2 + e
        slot = kind

        @pl.when((group == 0) | (group == 2))
        def _():
            @pl.when(e > 0)
            def _():
                core_copy(slot, 0, index).wait_send()

            @pl.when((e == 0) & (group == 2))
            def _():
                y_copy(slot, index).wait()

            tile_bf[slot] = total.astype(jnp.bfloat16)
            core_copy(slot, group // 2, index).start()

        @pl.when(group == 1)
        def _():
            @pl.when(e == 0)
            def _():
                core_copy(slot, 0, index).wait_send()

            @pl.when(e > 0)
            def _():
                y_copy(slot, index).wait()

            core_copy(slot, 0, index).wait_recv()
            got = pltpu.make_async_copy(core_got.at[0, index], got_tile, tile_sem)
            got.start()
            got.wait()
            tile_bf[slot] = (total + got_tile[...].astype(jnp.float32)).astype(jnp.bfloat16)
            y_copy(slot, index).start()

        @pl.when(group == 3)
        def _():
            core_copy(slot, 1, index).wait_recv()
            got = pltpu.make_async_copy(core_got.at[1, index], got_tile, tile_sem)
            got.start()
            got.wait()
            tile_f32[index] = total + got_tile[...].astype(jnp.float32)
            pltpu.make_async_copy(tile_f32.at[index], grads_out.at[index], out_sem.at[index]).start()

    def sum_step(place, _):
        code = entry(SUM_ORDER, near, place)

        @pl.when(code < A)
        def _():
            sum_parts(turned(code))

        @pl.when(place < 8)
        def _():
            group, e = place // 2, place % 2
            weight_tile(group, e, 0, h_all, gu[:, pl.ds(pl.multiple_of(2 * e * F, 128), F)])
            weight_tile(group, e, 1, h_all, gu[:, pl.ds(pl.multiple_of((2 * e + 1) * F, 128), F)])
            weight_tile(group, e, 2, u_all, act[:, pl.ds(pl.multiple_of(e * F, 128), F)])

        return 0

    lax.fori_loop(0, 9, sum_step, 0)

    for kind in range(3):
        core_copy(kind, 1, 3 + kind).wait_send()
    for row in range(A):
        for part in range(HALVES):
            x_copy(row, part).wait_send()

            @pl.when(row != a)
            def _():
                z_up(row, part).wait_send()

    @pl.when(a < A - 1)
    def _():
        send_up(me).wait_send()

    @pl.when(a > 0)
    def _():
        send_down(me).wait_send()

    send_across(me).wait_send()
    for place in range(A // 2):
        @pl.when(near == place)
        def _():
            for word in [word for words in BEFORE_STEP[place] for word in words]:
                code = int(word[1:])
                s = turned(code % A) * B + (1 - b if code >= A else b)
                if word[0] == "X":
                    send_across(s).wait_send()
                elif word[0] != "W":
                    @pl.when(flipped != (word[0] == "A"))
                    def _():
                        send_up(s).wait_send()

                    @pl.when(flipped == (word[0] == "A"))
                    def _():
                        send_down(s).wait_send()

    for k in range(1, n):
        s = (me + k) % n
        p_copy(s).wait_send()
        g_copy(s).wait_send()
        copy(gg_stage.at[s], gg_out.at[s], g_send.at[s], g_recv.at[s], expert=s).wait_recv()
    pltpu.make_async_copy(gg_stage.at[me], gg_out.at[me], g_send.at[me]).wait()
    for slot in range(2):
        d_copy(0, slot).wait()
    for index in range(6):
        pltpu.make_async_copy(tile_f32.at[index], grads_out.at[index], out_sem.at[index]).wait()


def moe_call(hidden, all_upstream, probs, expert_gate, expert_up, expert_down):
    R, D = hidden.shape
    F = expert_gate.shape[2]
    A, n = 4, 8
    shard = D // 4
    bf, f32 = jnp.bfloat16, jnp.float32
    any_spec = pl.BlockSpec(memory_space=pl.ANY)
    vmem = pl.BlockSpec(memory_space=pltpu.VMEM)
    dma = pltpu.SemaphoreType.DMA
    out_shape = (
        jax.ShapeDtypeStruct((n, R, D), bf),
        jax.ShapeDtypeStruct((R, D), f32),
        jax.ShapeDtypeStruct((n, 8, R), f32),
        jax.ShapeDtypeStruct((6, shard, F), f32),
        jax.ShapeDtypeStruct((2, 6, shard, F), bf),
        jax.ShapeDtypeStruct((6, shard, F), bf),
    )
    return pl.pallas_call(
        functools.partial(moe_kernel, comm=True),
        out_shape=out_shape,
        in_specs=[any_spec] * 6,
        out_specs=(any_spec, vmem, any_spec, any_spec, any_spec, any_spec),
        scratch_shapes=[
            pltpu.VMEM((n, R, D), bf),
            pltpu.VMEM((n, R, D), bf),
            pltpu.VMEM((n, 8, R), f32),
            pltpu.VMEM((2, D, F), bf),
            pltpu.VMEM((2, D, F), bf),
            pltpu.VMEM((2, D, F), bf),
            pltpu.VMEM((n * R, 2 * F), bf),
            pltpu.VMEM((n * R, 4 * F), bf),
            pltpu.VMEM((2 * A, R, D), bf),
            pltpu.VMEM((A, R, D), bf),
            pltpu.VMEM((A + 1, R, D), bf),
            pltpu.VMEM((2, R, D), bf),
            pltpu.VMEM((n, 8, R), f32),
            pltpu.VMEM((3, shard, F), bf),
            pltpu.VMEM((6, shard, F), f32),
            pltpu.VMEM((shard, F), bf),
            dma((6,)), dma((n,)), dma((n,)), dma((n,)), dma((n,)), dma((n,)), dma((n,)), dma((n,)), dma((n,)),
            dma((A, HALVES)), dma((A, HALVES)), dma((A, HALVES)), dma((A + 1, HALVES)), dma((2,)),
            dma((3,)), dma((2, 6)), dma((3,)), dma, dma((6,)),
        ],
        compiler_params=pltpu.CompilerParams(
            collective_id=1, has_side_effects=True, vmem_limit_bytes=64 * 1024 * 1024 - 65536
        ),
        cost_estimate=pl.CostEstimate(flops=58 * 10**9, bytes_accessed=60 * 10**6, transcendentals=2 * 10**6),
        name="experts",
    )(hidden, all_upstream, probs, expert_gate, expert_up, expert_down)


def reduce_kernel(
    left, right, extra, out,
    core_out, core_in, y_out, y_in, half, x_out, x_in, own, z_out, z_in, full, ready,
    core_send, core_recv, y_send, y_recv, x_send, x_recv, zs_send, zs_recv, zg_send, zg_recv, xg_send, xg_recv, ready_sem,
):
    A, B = 4, 2
    W = core_out.shape[3]
    shard = core_out.shape[2]
    half_rows, piece = shard // B, shard // (A * B)
    chunks = y_in.shape[0]
    me = lax.axis_index("expert")
    dp = lax.axis_index("dp")
    a, b = me // B, me % B
    y, c = dp // 2, dp % 2
    partner_x = a * B + (1 - b)
    core_peer = 2 * y + (1 - c)
    y_peer = 2 * (1 - y) + c

    def copy(src, dst, send, recv, **target):
        return pltpu.make_async_remote_copy(
            src_ref=src, dst_ref=dst, send_sem=send, recv_sem=recv, device_id=target, device_id_type=MESH
        )

    barrier = pltpu.get_barrier_semaphore()
    for target in [{"dp": core_peer}, {"dp": y_peer}, {"expert": partner_x}] + [
        {"expert": (a + k) % A * B + b} for k in range(1, A)
    ]:
        pl.semaphore_signal(barrier, inc=1, device_id=target, device_id_type=MESH)
    pl.semaphore_wait(barrier, 2 + A)

    def partial(chunk, owner):
        rows = pl.ds(pl.multiple_of(owner * shard, 128), shard)
        cols = pl.ds(pl.multiple_of(chunk * W, 128), W)
        which = jnp.where(chunk < left.shape[2] // W, 0, 1)
        total = dot_f32(left[which, :, rows], right[:, cols], TN)
        share = extra[pl.ds(pl.multiple_of(owner * shard, 128), shard), :].astype(jnp.float32)
        share = jnp.where(chunk == chunks - 1, share, 0.0)
        return jnp.concatenate([total[:, : W - 128], total[:, W - 128 :] + share], axis=1)

    def core_copy(chunk, which):
        slot = chunk % 2
        return copy(core_out.at[slot, which], core_in.at[chunk, which], core_send.at[slot, which], core_recv.at[chunk, which], dp=core_peer)

    def y_copy(chunk):
        slot = chunk % 2
        return copy(y_out.at[slot], y_in.at[chunk], y_send.at[slot], y_recv.at[chunk], dp=y_peer)

    def x_copy(chunk):
        slot = chunk % 2
        return copy(x_out.at[slot], x_in.at[chunk], x_send.at[slot], x_recv.at[chunk], expert=partner_x)

    def z_scatter(chunk, to, source):
        slot = chunk % 2
        return copy(
            z_out.at[slot, pl.ds(pl.multiple_of(to * piece, 16), piece)], z_in.at[chunk, source],
            zs_send.at[slot, to], zs_recv.at[chunk, source], expert=to * B + b,
        )

    def z_gather(chunk, to, source):
        rows = pl.ds(pl.multiple_of(b * half_rows + source * piece, 16), piece)
        return copy(full.at[chunk, rows], full.at[chunk, rows], zg_send.at[chunk, to], zg_recv.at[chunk, source], expert=to * B + b)

    def x_gather(chunk, side):
        rows = pl.ds(pl.multiple_of(side * half_rows, 16), half_rows)
        return copy(full.at[chunk, rows], full.at[chunk, rows], xg_send.at[chunk], xg_recv.at[chunk], expert=partner_x)

    def to_core(chunk):
        for which, owner in ((0, core_peer), (1, 2 * (1 - y) + 1 - c)):
            value = partial(chunk, owner).astype(jnp.bfloat16)

            @pl.when(chunk >= 2)
            def _():
                core_copy(chunk, which).wait_send()

            core_out[chunk % 2, which] = value
            core_copy(chunk, which).start()

    def to_y(chunk):
        value = partial(chunk, y_peer)
        core_copy(chunk, 1).wait_recv()

        @pl.when(chunk >= 2)
        def _():
            y_copy(chunk).wait_send()

        y_out[chunk % 2] = (value + core_in[chunk, 1].astype(jnp.float32)).astype(jnp.bfloat16)
        y_copy(chunk).start()

    def to_x(chunk):
        value = partial(chunk, dp)
        core_copy(chunk, 0).wait_recv()
        y_copy(chunk).wait_recv()
        value = value + core_in[chunk, 0].astype(jnp.float32) + y_in[chunk].astype(jnp.float32)

        @pl.when(chunk >= 2)
        def _():
            x_copy(chunk).wait_send()

        low, high = value[:half_rows], value[half_rows:]
        half[chunk % 2] = jnp.where(b == 0, low, high)
        x_out[chunk % 2] = jnp.where(b == 0, high, low).astype(jnp.bfloat16)
        x_copy(chunk).start()

    def to_z(chunk):
        x_copy(chunk).wait_recv()

        @pl.when(chunk >= 2)
        def _():
            for k in range(1, A):
                z_scatter(chunk, (a + k) % A, a).wait_send()

        total = half[chunk % 2] + x_in[chunk].astype(jnp.float32)
        half[chunk % 2] = total
        own[chunk % 2] = half[chunk % 2, pl.ds(pl.multiple_of(a * piece, 8), piece)]
        z_out[chunk % 2] = total.astype(jnp.bfloat16)
        for k in range(1, A):
            z_scatter(chunk, (a + k) % A, a).start()

    def spread_z(chunk):
        total = own[chunk % 2]
        for k in range(1, A):
            source = (a + k) % A
            z_scatter(chunk, a, source).wait_recv()
            total = total + z_in[chunk, source].astype(jnp.float32)
        rows = pl.ds(pl.multiple_of(b * half_rows + a * piece, 16), piece)
        full[chunk, rows] = total.astype(jnp.bfloat16)
        for k in range(1, A):
            z_gather(chunk, (a + k) % A, a).start()

    def spread_x(chunk):
        for k in range(1, A):
            z_gather(chunk, a, (a + k) % A).wait_recv()
        x_gather(chunk, b).start()

    def written(chunk):
        cols = pl.ds(pl.multiple_of(chunk * W, 128), W)
        return pltpu.make_async_copy(ready.at[chunk % 2], out.at[:, cols], ready_sem.at[chunk % 2])

    def finish(chunk):
        x_gather(chunk, 1 - b).wait_recv()

        @pl.when(chunk >= 2)
        def _():
            written(chunk).wait()

        ready[chunk % 2] = full[chunk].astype(jnp.float32)
        written(chunk).start()

    stages = (to_core, to_y, to_x, to_z, spread_z, spread_x, finish)

    def step(t, _):
        for delay, stage in enumerate(stages):
            @pl.when((t >= delay) & (t < delay + chunks))
            def _():
                stage(t - delay)

        return 0

    lax.fori_loop(0, chunks + len(stages) - 1, step, 0)

    for chunk in range(chunks - 2, chunks):
        written(chunk).wait()
        core_copy(chunk, 0).wait_send()
        core_copy(chunk, 1).wait_send()
        y_copy(chunk).wait_send()
        x_copy(chunk).wait_send()
        for k in range(1, A):
            z_scatter(chunk, (a + k) % A, a).wait_send()

    def drain(chunk, _):
        for k in range(1, A):
            z_gather(chunk, (a + k) % A, a).wait_send()
        x_gather(chunk, b).wait_send()
        return 0

    lax.fori_loop(0, chunks, drain, 0)


def reduce_call(left, right, extra):
    D = left.shape[2]
    width = right.shape[1]
    W, A, B = 384, 4, 2
    shard, chunks = D // 4, width // W
    bf, f32 = jnp.bfloat16, jnp.float32
    vmem = pl.BlockSpec(memory_space=pltpu.VMEM)
    dma = pltpu.SemaphoreType.DMA
    piece = shard // (A * B)
    return pl.pallas_call(
        reduce_kernel,
        out_shape=jax.ShapeDtypeStruct((shard, width), f32),
        in_specs=[vmem] * 3,
        out_specs=pl.BlockSpec(memory_space=pl.ANY),
        scratch_shapes=[
            pltpu.VMEM((2, 2, shard, W), bf),
            pltpu.VMEM((chunks, 2, shard, W), bf),
            pltpu.VMEM((2, shard, W), bf),
            pltpu.VMEM((chunks, shard, W), bf),
            pltpu.VMEM((2, shard // B, W), f32),
            pltpu.VMEM((2, shard // B, W), bf),
            pltpu.VMEM((chunks, shard // B, W), bf),
            pltpu.VMEM((2, piece, W), f32),
            pltpu.VMEM((2, shard // B, W), bf),
            pltpu.VMEM((chunks, A, piece, W), bf),
            pltpu.VMEM((chunks, shard, W), bf),
            pltpu.VMEM((2, shard, W), f32),
            dma((2, 2)), dma((chunks, 2)), dma((2,)), dma((chunks,)), dma((2,)), dma((chunks,)),
            dma((2, A)), dma((chunks, A)), dma((chunks, A)), dma((chunks, A)), dma((chunks,)), dma((chunks,)), dma((2,)),
        ],
        compiler_params=pltpu.CompilerParams(
            collective_id=2, has_side_effects=True, vmem_limit_bytes=56 * 1024 * 1024
        ),
        cost_estimate=pl.CostEstimate(flops=4 * 10**9, bytes_accessed=20 * 10**6, transcendentals=0),
        name="weight_sums",
    )(left, right, extra)


PIECES = 3


def front_kernel(
    lengths, tokens, routes, w_gain, w_small, w_q, w_k, w_v, w_o, u_in,
    out_gain, out_small, out_q, out_k, out_v, out_o, u_all,
    left_hbm, qkv_hbm, log_total, cos_out, sin_out, residual, hidden_two, probs_out, by_owner,
    all_gain, all_small, all_q, all_k, all_v, all_o, sums, q_heads, k_heads, v_heads, mixed, left_out, qkv,
    keep_sem, core_send, y_send, pass_send, w_recv, u_keep, u_up, u_down, u_across, u_recv,
    o_send, o_recv, o_pass, o_far, early_sem,
):
    A, B = 4, 2
    R, D = tokens.shape
    shard = D // 4
    attended, hidden_one = left_out.at[0], left_out.at[1]
    me = lax.axis_index("expert")
    dp = lax.axis_index("dp")
    a, b = me // B, me % B
    y, c = dp // 2, dp % 2
    partner_x = a * B + (1 - b)
    core_peer = 2 * y + (1 - c)
    y_peer = 2 * (1 - y) + c
    far_peer = 2 * (1 - y) + 1 - c
    shards = (w_gain, w_small, w_q, w_k, w_v, w_o)
    landed = (all_gain, all_small, all_q, all_k, all_v, all_o)
    kept = (out_gain, out_small, out_q, out_k, out_v, out_o)
    count = len(shards)
    GAIN, SMALL, QUERY, KEY, VALUE, OUTPUT = range(count)

    def copy(src, dst, send, recv, **target):
        return pltpu.make_async_remote_copy(
            src_ref=src, dst_ref=dst, send_sem=send, recv_sem=recv, device_id=target, device_id_type=MESH
        )

    barrier = pltpu.get_barrier_semaphore()
    for target in [{"dp": core_peer}, {"dp": y_peer}, {"expert": partner_x}] + [
        {"expert": (a + k) % A * B + b} for k in range(1, A)
    ]:
        pl.semaphore_signal(barrier, inc=1, device_id=target, device_id_type=MESH)
    pl.semaphore_wait(barrier, 2 + A)

    def to_core(i):
        return copy(shards[i], landed[i].at[dp], core_send.at[i], w_recv.at[i, dp], dp=core_peer)

    def to_y(i):
        return copy(shards[i], landed[i].at[dp], y_send.at[i], w_recv.at[i, dp], dp=y_peer)

    def pass_on(i):
        return copy(landed[i].at[y_peer], landed[i].at[y_peer], pass_send.at[i], w_recv.at[i, y_peer], dp=core_peer)

    def keep_own(i):
        return pltpu.make_async_copy(shards[i], kept[i].at[dp], keep_sem.at[i, dp])

    def keep(i, owner):
        return pltpu.make_async_copy(landed[i].at[owner], kept[i].at[owner], keep_sem.at[i, owner])

    def receive(i, owner):
        copy(shards[i], landed[i].at[owner], core_send.at[i], w_recv.at[i, owner], dp=core_peer).wait_recv()
        keep(i, owner).start()

    def forward(i):
        receive(i, y_peer)
        pass_on(i).start()

    def u_send_up(src, s):
        return copy(src, u_all.at[s], u_up.at[s], u_recv.at[s], expert=me + B)

    def u_send_down(src, s):
        return copy(src, u_all.at[s], u_down.at[s], u_recv.at[s], expert=me - B)

    def u_send_across(src, s):
        return copy(src, u_all.at[s], u_across.at[s], u_recv.at[s], expert=partner_x)

    def take(row):
        @pl.when((row >= 0) & (row < A))
        def _():
            s = row * B + b
            u_send_across(u_all.at[s], s).wait_recv()
            u_send_across(u_all.at[s], s).start()

            @pl.when((row < a) & (a < A - 1))
            def _():
                u_send_up(u_all.at[s], s).start()

            @pl.when((row > a) & (a > 0))
            def _():
                u_send_down(u_all.at[s], s).start()

    def o_part(piece):
        return pl.ds(piece * (shard // PIECES), shard // PIECES)

    def o_to_y(piece):
        rows = o_part(piece)
        return copy(w_o.at[rows], all_o.at[dp, rows], o_send.at[piece], o_recv.at[piece], dp=y_peer)

    def o_from_y(piece):
        rows = o_part(piece)
        return copy(w_o.at[rows], all_o.at[y_peer, rows], o_send.at[piece], o_recv.at[piece], dp=y_peer)

    def o_pass_on(piece):
        rows = o_part(piece)
        return copy(all_o.at[y_peer, rows], all_o.at[y_peer, rows], o_pass.at[piece], o_far.at[piece], dp=core_peer)

    def o_from_core(piece):
        rows = o_part(piece)
        return copy(all_o.at[far_peer, rows], all_o.at[far_peer, rows], o_pass.at[piece], o_far.at[piece], dp=core_peer)

    keep_u = pltpu.make_async_copy(u_in, u_all.at[me], u_keep)

    @pl.when(a < A - 1)
    def _():
        u_send_up(u_in, me).start()

    @pl.when(a > 0)
    def _():
        u_send_down(u_in, me).start()

    u_send_across(u_in, me).start()
    for i in range(count):
        if i == OUTPUT:
            for piece in range(PIECES):
                o_to_y(piece).start()
        else:
            to_y(i).start()
        to_core(i).start()
        keep_own(i).start()
    keep_u.start()

    row_index = lax.broadcasted_iota(jnp.int32, (R, 128), 0)
    ends = (lengths[0, 0], lengths[0, 0] + lengths[0, 1], lengths[0, 0] + lengths[0, 1] + lengths[0, 2])
    start = jnp.where(row_index >= ends[2], ends[2], jnp.where(row_index >= ends[1], ends[1], jnp.where(row_index >= ends[0], ends[0], 0)))
    position = (row_index - start).astype(jnp.float32)
    lane = lax.broadcasted_iota(jnp.int32, (R, 128), 1)
    pair = (lane % (HD // 2)).astype(jnp.float32)
    frequency = jnp.exp(pair * (-2.0 / HD * math.log(rope_base)))
    angle = position * frequency
    front = lane % HD < HD // 2
    cos_out[...] = jnp.cos(angle)
    sin_out[...] = jnp.where(front, -jnp.sin(angle), jnp.sin(angle))

    def doc_of(index):
        total = 0
        for end in ends:
            total = total + jnp.where(index >= end, 1, 0)
        return total

    rows_t = lax.broadcasted_iota(jnp.int32, (R, R), 0)
    rows_u = lax.broadcasted_iota(jnp.int32, (R, R), 1)
    allowed = (doc_of(rows_t) == doc_of(rows_u)) & (rows_u <= rows_t)

    inputs = tokens[...].astype(jnp.float32)
    scale_one = lax.rsqrt(jnp.mean(inputs * inputs, axis=1, keepdims=True) + eps)

    forward(GAIN)
    receive(GAIN, core_peer)
    receive(GAIN, far_peer)
    all_gain[dp] = w_gain[...]
    for j in range(4):
        cols = slice(j * shard, (j + 1) * shard)
        gain = all_gain[j, 0:1, :].astype(jnp.float32)
        hidden_one[:, cols] = (inputs[:, cols] * scale_one * gain).astype(jnp.bfloat16)

    offsets = {QUERY: 0, KEY: D, VALUE: D + KVH * HD}
    sums[...] = jnp.zeros_like(sums)

    def product(i, owner, own=False):
        cols = pl.ds(pl.multiple_of(owner * shard, 128), shard)
        left = hidden_one[:, cols]
        width = shards[i].shape[1]

        def tile(t, _):
            into = pl.ds(pl.multiple_of(offsets[i] + t * 512, 128), 512)
            part = pl.ds(pl.multiple_of(t * 512, 128), 512)
            weight = shards[i][:, part] if own else landed[i][owner, :, part]
            sums[:, into] += dot_f32(left, weight)
            return 0

        lax.fori_loop(0, width // 512, tile, 0)

    for i in (QUERY, KEY, VALUE):
        product(i, dp, own=True)
    for i in (QUERY, KEY, VALUE):
        receive(i, core_peer)
        product(i, core_peer)
    take(a - 1)
    take(a + 1)
    forward(SMALL)
    receive(SMALL, core_peer)
    forward(QUERY)
    product(QUERY, y_peer)
    receive(QUERY, far_peer)
    product(QUERY, far_peer)
    take(a - 2)
    take(a + 2)
    forward(KEY)
    product(KEY, y_peer)
    receive(KEY, far_peer)
    product(KEY, far_peer)
    forward(VALUE)
    product(VALUE, y_peer)
    receive(VALUE, far_peer)
    product(VALUE, far_peer)

    def rotated(columns):
        value = sums[:, columns]
        other = jnp.where(front, pltpu.roll(value, 128 - HD // 2, 1), pltpu.roll(value, HD // 2, 1))
        return (value * cos_out[...] + other * sin_out[...]).astype(jnp.bfloat16)

    for pair_index in range(QH // 2):
        columns = slice(pair_index * 128, (pair_index + 1) * 128)
        value = rotated(columns)
        qkv[:, columns] = value
        q_heads[2 * pair_index] = value[:, :HD]
        q_heads[2 * pair_index + 1] = value[:, HD:]
    for pair_index in range(KVH // 2):
        columns = slice(D + pair_index * 128, D + (pair_index + 1) * 128)
        value = rotated(columns)
        qkv[:, columns] = value
        k_heads[2 * pair_index] = value[:, :HD]
        k_heads[2 * pair_index + 1] = value[:, HD:]
        columns = slice(D + KVH * HD + pair_index * 128, D + KVH * HD + (pair_index + 1) * 128)
        value = sums[:, columns].astype(jnp.bfloat16)
        qkv[:, columns] = value
        v_heads[2 * pair_index] = value[:, :HD]
        v_heads[2 * pair_index + 1] = value[:, HD:]
    log_total[...] = jnp.zeros_like(log_total)

    def group_step(g, _):
        for k in range(QH // KVH):
            head = g * (QH // KVH) + k
            scores = dot_f32(q_heads[head], k_heads[g], NT) * HD**-0.5
            scores = jnp.where(allowed, scores, masked_score)
            top = jnp.max(scores, axis=1, keepdims=True)
            terms = jnp.exp(scores - top)
            total = jnp.sum(terms, axis=1, keepdims=True)
            low = (terms / total).astype(jnp.bfloat16)
            mixed[head] = dot_f32(low, v_heads[g]).astype(jnp.bfloat16)
            log_total[...] += jnp.where(lane == head, top + jnp.log(total), 0.0)
        return 0

    lax.fori_loop(0, KVH, group_step, 0)
    take(a - 3)
    take(a + 3)
    for pair_index in range(QH // 2):
        attended[:, pair_index * 128 : (pair_index + 1) * 128] = jnp.concatenate(
            [mixed[2 * pair_index], mixed[2 * pair_index + 1]], axis=1
        )

    residual[...] = inputs
    early = (
        pltpu.make_async_copy(left_out, left_hbm, early_sem.at[0]),
        pltpu.make_async_copy(qkv, qkv_hbm, early_sem.at[1]),
    )
    for write in early:
        write.start()

    def out_product(owner, own=False):
        cols = pl.ds(pl.multiple_of(owner * shard, 128), shard)
        left = attended[:, cols]

        def tile(t, _):
            part = pl.ds(pl.multiple_of(t * 512, 128), 512)
            weight = w_o[:, part] if own else all_o[owner, :, part]
            residual[:, part] += dot_f32(left, weight)
            return 0

        lax.fori_loop(0, D // 512, tile, 0)

    out_product(dp, own=True)
    receive(OUTPUT, core_peer)
    out_product(core_peer)
    receive(SMALL, far_peer)
    all_small[dp] = w_small[...]

    def piece_product(owner, piece):
        rows = o_part(piece)
        left = attended[:, pl.ds(pl.multiple_of(owner * shard + piece * (shard // PIECES), 128), shard // PIECES)]
        for t in range(D // 512):
            part = slice(t * 512, (t + 1) * 512)
            residual[:, part] += dot_f32(left, all_o[owner, rows, part])

    for piece in range(PIECES):
        o_from_y(piece).wait_recv()
        o_pass_on(piece).start()
        if piece:
            o_from_core(piece - 1).wait_recv()
            piece_product(far_peer, piece - 1)
        piece_product(y_peer, piece)
    keep(OUTPUT, y_peer).start()
    o_from_core(PIECES - 1).wait_recv()
    piece_product(far_peer, PIECES - 1)
    keep(OUTPUT, far_peer).start()

    whole = residual[...]
    scale_two = lax.rsqrt(jnp.mean(whole * whole, axis=1, keepdims=True) + eps)
    logits = jnp.zeros((R, 128), jnp.float32)
    for j in range(4):
        cols = slice(j * shard, (j + 1) * shard)
        gain = all_gain[j, 1:2, :].astype(jnp.float32)
        value = (whole[:, cols] * scale_two * gain).astype(jnp.bfloat16)
        hidden_two[:, cols] = value
        logits = logits + dot_f32(value, all_small[j])
    chosen = lane == routes[:, 0:1]
    for j in range(1, TOP):
        chosen = chosen | (lane == routes[:, j : j + 1])
    logits = jnp.where(chosen, logits, masked_score)
    terms = jnp.where(chosen, jnp.exp(logits - jnp.max(logits, axis=1, keepdims=True)), 0.0)
    probs = terms / jnp.sum(terms, axis=1, keepdims=True)
    probs_out[...] = probs
    turned = jnp.transpose(probs)
    by_owner[...] = jnp.zeros_like(by_owner)
    local = 2
    for owner in range(A * B):
        by_owner[owner, 0:local, :] = turned[owner * local : (owner + 1) * local]

    for row in range(A):
        s = row * B + 1 - b
        u_send_across(u_all.at[s], s).wait_recv()
    for i in range(count):
        keep_own(i).wait()
        for owner in (core_peer, y_peer, far_peer):
            keep(i, owner).wait()
        to_core(i).wait_send()
        if i != OUTPUT:
            to_y(i).wait_send()
            pass_on(i).wait_send()
    for piece in range(PIECES):
        o_to_y(piece).wait_send()
        o_pass_on(piece).wait_send()
    for write in early:
        write.wait()
    keep_u.wait()

    @pl.when(a < A - 1)
    def _():
        u_send_up(u_in, me).wait_send()

    @pl.when(a > 0)
    def _():
        u_send_down(u_in, me).wait_send()

    for row in range(A):
        s = row * B + b
        u_send_across(u_all.at[s], s).wait_send()

        @pl.when((row < a) & (a < A - 1))
        def _():
            u_send_up(u_all.at[s], s).wait_send()

        @pl.when((row > a) & (a > 0))
        def _():
            u_send_down(u_all.at[s], s).wait_send()


def front_call(seq_lengths, tokens, routes, gains, small, w_query, w_key, w_value, w_output, out_grad):
    n = 8
    R, D = tokens.shape
    bf, f32 = jnp.bfloat16, jnp.float32
    any_spec = pl.BlockSpec(memory_space=pl.ANY)
    vmem = pl.BlockSpec(memory_space=pltpu.VMEM)
    dma = pltpu.SemaphoreType.DMA
    shards = (gains, small, w_query, w_key, w_value, w_output)
    whole = w_query.shape[1] + w_key.shape[1] + w_value.shape[1]
    return pl.pallas_call(
        front_kernel,
        out_shape=tuple(jax.ShapeDtypeStruct((4, *w.shape), bf) for w in shards)
        + (
            jax.ShapeDtypeStruct((n, R, D), bf),
            jax.ShapeDtypeStruct((2, R, D), bf),
            jax.ShapeDtypeStruct((R, whole), bf),
            jax.ShapeDtypeStruct((R, 128), f32),
            jax.ShapeDtypeStruct((R, 128), f32),
            jax.ShapeDtypeStruct((R, 128), f32),
            jax.ShapeDtypeStruct((R, D), f32),
            jax.ShapeDtypeStruct((R, D), bf),
            jax.ShapeDtypeStruct((R, 128), f32),
            jax.ShapeDtypeStruct((n, 8, R), f32),
        ),
        in_specs=[pl.BlockSpec(memory_space=pltpu.SMEM)] + [vmem] * 9,
        out_specs=(any_spec,) * 9 + (vmem,) * 7,
        scratch_shapes=[pltpu.VMEM((4, *w.shape), bf) for w in shards]
        + [
            pltpu.VMEM((R, whole), f32),
            pltpu.VMEM((QH, R, HD), bf),
            pltpu.VMEM((KVH, R, HD), bf),
            pltpu.VMEM((KVH, R, HD), bf),
            pltpu.VMEM((QH, R, HD), bf),
            pltpu.VMEM((2, R, D), bf),
            pltpu.VMEM((R, whole), bf),
            dma((6, 4)), dma((6,)), dma((6,)), dma((6,)), dma((6, 4)), dma, dma((n,)), dma((n,)), dma((n,)), dma((n,)),
            dma((PIECES,)), dma((PIECES,)), dma((PIECES,)), dma((PIECES,)), dma((2,)),
        ],
        compiler_params=pltpu.CompilerParams(
            collective_id=3, has_side_effects=True, vmem_limit_bytes=60 * 1024 * 1024
        ),
        cost_estimate=pl.CostEstimate(flops=4 * 10**9, bytes_accessed=40 * 10**6, transcendentals=2 * 10**6),
        name="front",
    )(seq_lengths, tokens, routes, *shards, out_grad)


def back_kernel(
    lengths, row_sum, grad_rows, probs, small, gains, tokens_in, out_grad, residual, hidden_two, qkv_in, log_total,
    cos_table, sin_table, in_q, in_k, in_v, in_o,
    right, extra, in_grad,
    tokens, qkv, w_q, w_k, w_v, w_o, turned, head_grads, q_heads, k_heads, v_heads, q_sums, k_sums, v_sums, wide, load_sem,
):
    R, D = tokens.shape
    shard = D // 4
    local, groups = 2, grad_rows.shape[0]
    expert_count = local * groups
    loads = [
        pltpu.make_async_copy(src, dst, load_sem.at[i])
        for i, (src, dst) in enumerate(
            ((qkv_in, qkv), (in_o, w_o), (in_q, w_q), (in_k, w_k), (in_v, w_v), (tokens_in, tokens))
        )
    ]
    for load in loads:
        load.start()
    lane = lax.broadcasted_iota(jnp.int32, (R, 128), 1)

    turned[...] = jnp.zeros_like(turned)
    for owner in range(groups):
        turned[owner * local : (owner + 1) * local, :] = grad_rows[owner, 0:local, :]
    gate_grad = jnp.transpose(turned[...])
    dense = probs[...]
    logit_grad = dense * (gate_grad - jnp.sum(dense * gate_grad, axis=1, keepdims=True))
    logit_grad = logit_grad.astype(jnp.bfloat16)

    whole = residual[...]
    scale_two = lax.rsqrt(jnp.mean(whole * whole, axis=1, keepdims=True) + eps)
    mean_two = jnp.zeros((R, 1), jnp.float32)
    marks = [(lane == expert_count + k).astype(jnp.bfloat16) for k in range(2)]
    for j in range(4):
        cols = slice(j * shard, (j + 1) * shard)
        rows = row_sum[:, cols] + dot_f32(logit_grad, small[j], NT)
        normed = whole[:, cols] * scale_two
        product = rows * normed
        high = product.astype(jnp.bfloat16)
        rest = (product - high.astype(jnp.float32)).astype(jnp.bfloat16)
        part = dot_f32(hidden_two[:, cols], logit_grad, TN)
        wide[:, cols] = rows
        extra[cols, :] = (part + dot_f32(high, marks[1], TN) + dot_f32(rest, marks[1], TN)).astype(jnp.bfloat16)
        gain = gains[j, 1:2, :].astype(jnp.float32)
        mean_two = mean_two + jnp.sum(product * gain, axis=1, keepdims=True)
    mean_two = mean_two * (1.0 / D)
    for j in range(4):
        cols = slice(j * shard, (j + 1) * shard)
        gain = gains[j, 1:2, :].astype(jnp.float32)
        normed = whole[:, cols] * scale_two
        value = out_grad[:, cols].astype(jnp.float32) + scale_two * (wide[:, cols] * gain - normed * mean_two)
        in_grad[:, cols] = value
        right[:, cols] = value.astype(jnp.bfloat16)

    loads[0].wait()
    loads[1].wait()
    for j in range(4):
        part = dot_f32(right[:, 0:D], w_o[j], NT).astype(jnp.bfloat16)
        for k in range(shard // HD):
            head_grads[j * (shard // HD) + k] = part[:, k * HD : (k + 1) * HD]
    for head in range(QH):
        q_heads[head] = qkv[:, head * HD : (head + 1) * HD]
    for g in range(KVH):
        k_heads[g] = qkv[:, D + g * HD : D + (g + 1) * HD]
        v_heads[g] = qkv[:, D + (KVH + g) * HD : D + (KVH + g + 1) * HD]

    ends = (lengths[0, 0], lengths[0, 0] + lengths[0, 1], lengths[0, 0] + lengths[0, 1] + lengths[0, 2])

    def doc_of(index):
        total = 0
        for end in ends:
            total = total + jnp.where(index >= end, 1, 0)
        return total

    rows_t = lax.broadcasted_iota(jnp.int32, (R, R), 0)
    rows_u = lax.broadcasted_iota(jnp.int32, (R, R), 1)
    allowed = (doc_of(rows_t) == doc_of(rows_u)) & (rows_u <= rows_t)
    score_scale = HD**-0.5

    def group_step(g, _):
        key_total = jnp.zeros((R, HD), jnp.float32)
        value_total = jnp.zeros((R, HD), jnp.float32)
        for k in range(QH // KVH):
            head = g * (QH // KVH) + k
            scores = dot_f32(q_heads[head], k_heads[g], NT) * score_scale
            log_head = jnp.sum(jnp.where(lane == head, log_total[...], 0.0), axis=1, keepdims=True)
            head_probs = jnp.exp(jnp.where(allowed, scores - log_head, masked_score))
            prob_grad = dot_f32(head_grads[head], v_heads[g], NT)
            centre = jnp.sum(head_probs * prob_grad, axis=1, keepdims=True)
            score_grad = (head_probs * (prob_grad - centre)).astype(jnp.bfloat16)
            q_sums[head] = dot_f32(score_grad, k_heads[g]) * score_scale
            key_total = key_total + dot_f32(score_grad, q_heads[head], TN)
            value_total = value_total + dot_f32(head_probs.astype(jnp.bfloat16), head_grads[head], TN)
        k_sums[g] = key_total * score_scale
        v_sums[g] = value_total
        return 0

    lax.fori_loop(0, KVH, group_step, 0)

    front = lane % HD < HD // 2

    def turn_back(first, second):
        value = jnp.concatenate([first, second], axis=1)
        other = jnp.where(front, pltpu.roll(value, 128 - HD // 2, 1), pltpu.roll(value, HD // 2, 1))
        return (value * cos_table[...] - other * sin_table[...]).astype(jnp.bfloat16)

    for i in range(QH // 2):
        right[:, D + i * 128 : D + (i + 1) * 128] = turn_back(q_sums[2 * i], q_sums[2 * i + 1])
    key_at, value_at = D + QH * HD, D + (QH + KVH) * HD
    for i in range(KVH // 2):
        right[:, key_at + i * 128 : key_at + (i + 1) * 128] = turn_back(k_sums[2 * i], k_sums[2 * i + 1])
        right[:, value_at + i * 128 : value_at + (i + 1) * 128] = jnp.concatenate(
            [v_sums[2 * i], v_sums[2 * i + 1]], axis=1
        ).astype(jnp.bfloat16)
    right[:, value_at + KVH * HD :] = jnp.zeros((R, 128), jnp.bfloat16)

    for load in loads[2:]:
        load.wait()
    inputs = tokens[...].astype(jnp.float32)
    scale_one = lax.rsqrt(jnp.mean(inputs * inputs, axis=1, keepdims=True) + eps)
    mean_one = jnp.zeros((R, 1), jnp.float32)
    for j in range(4):
        cols = slice(j * shard, (j + 1) * shard)
        rows = dot_f32(right[:, D:key_at], w_q[j], NT)
        rows = rows + dot_f32(right[:, key_at:value_at], w_k[j], NT)
        rows = rows + dot_f32(right[:, value_at : value_at + KVH * HD], w_v[j], NT)
        wide[:, cols] = rows
        product = rows * (inputs[:, cols] * scale_one)
        high = product.astype(jnp.bfloat16)
        rest = (product - high.astype(jnp.float32)).astype(jnp.bfloat16)
        part = dot_f32(high, marks[0], TN) + dot_f32(rest, marks[0], TN)
        extra[cols, :] = (extra[cols, :].astype(jnp.float32) + part).astype(jnp.bfloat16)
        gain = gains[j, 0:1, :].astype(jnp.float32)
        mean_one = mean_one + jnp.sum(product * gain, axis=1, keepdims=True)
    mean_one = mean_one * (1.0 / D)
    for j in range(4):
        cols = slice(j * shard, (j + 1) * shard)
        gain = gains[j, 0:1, :].astype(jnp.float32)
        normed = inputs[:, cols] * scale_one
        in_grad[:, cols] = in_grad[:, cols] + scale_one * (wide[:, cols] * gain - normed * mean_one)


def back_call(seq_lengths, row_sum, grad_rows, probs, small, gains, tokens, out_grad, residual, hidden_two, qkv, log_total, cos_table, sin_table, *weights):
    R, D = tokens.shape
    bf, f32 = jnp.bfloat16, jnp.float32
    any_spec = pl.BlockSpec(memory_space=pl.ANY)
    vmem = pl.BlockSpec(memory_space=pltpu.VMEM)
    return pl.pallas_call(
        back_kernel,
        out_shape=(
            jax.ShapeDtypeStruct((R, D + qkv.shape[1] + 128), bf),
            jax.ShapeDtypeStruct((D, 128), bf),
            jax.ShapeDtypeStruct((R, D), f32),
        ),
        in_specs=[pl.BlockSpec(memory_space=pltpu.SMEM)]
        + [any_spec if i in (5, 9) else vmem for i in range(13)]
        + [any_spec] * 4,
        out_specs=(vmem,) * 3,
        scratch_shapes=[pltpu.VMEM(w.shape, bf) for w in (tokens, qkv, *weights)]
        + [
            pltpu.VMEM((128, R), f32),
            pltpu.VMEM((QH, R, HD), bf),
            pltpu.VMEM((QH, R, HD), bf),
            pltpu.VMEM((KVH, R, HD), bf),
            pltpu.VMEM((KVH, R, HD), bf),
            pltpu.VMEM((QH, R, HD), f32),
            pltpu.VMEM((KVH, R, HD), f32),
            pltpu.VMEM((KVH, R, HD), f32),
            pltpu.VMEM((R, D), f32),
            pltpu.SemaphoreType.DMA((6,)),
        ],
        compiler_params=pltpu.CompilerParams(vmem_limit_bytes=60 * 1024 * 1024),
        cost_estimate=pl.CostEstimate(flops=6 * 10**9, bytes_accessed=30 * 10**6, transcendentals=2 * 10**6),
        name="back",
    )(seq_lengths, row_sum, grad_rows, probs, small, gains, tokens, out_grad, residual, hidden_two, qkv, log_total, cos_table, sin_table, *weights)


def fused_body(
    tokens,
    seq_lengths,
    routes,
    w_query,
    w_key,
    w_value,
    w_output,
    w_router,
    attn_gain,
    moe_gain,
    expert_gate,
    expert_up,
    expert_down,
    out_grad,
):
    width = tokens.shape[1]
    expert_count = w_router.shape[1]
    gain_row = lax.broadcasted_iota(jnp.int32, (16, attn_gain.shape[0]), 0)
    gains = jnp.where(gain_row == 0, attn_gain[None, :], jnp.where(gain_row == 1, moe_gain[None, :], 0))
    gains = gains.astype(jnp.bfloat16)
    small = jnp.pad(w_router, ((0, 0), (0, 128 - expert_count)))
    (
        gains, small, query_w, key_w, value_w, output_w, all_upstream,
        left, qkv, log_total, cos_table, sin_table, residual, hidden_two, probs, by_owner,
    ) = front_call(seq_lengths, tokens, routes, gains, small, w_query, w_key, w_value, w_output, out_grad)
    mix_part, row_sum, grad_rows, own_grads, _, far_grads = moe_call(
        hidden_two, all_upstream, by_owner, expert_gate, expert_up, expert_down
    )
    far_grads = lax.ppermute(far_grads, "dp", [(0, 2), (1, 3), (2, 0), (3, 1)])
    mixture = lax.psum_scatter(mix_part.reshape(-1, width), "expert", scatter_dimension=0, tiled=True)

    right, extra, in_grad = back_call(
        seq_lengths, row_sum, grad_rows, probs, small, gains, tokens, out_grad, residual, hidden_two, qkv, log_total,
        cos_table, sin_table, query_w, key_w, value_w, output_w,
    )
    sums = reduce_call(left, right, extra)
    wide, narrow = QH * HD, KVH * HD
    cuts = (0, wide, 2 * wide, 2 * wide + narrow, 2 * wide + 2 * narrow)
    of_output, of_query, of_key, of_value = [sums[:, i:j] for i, j in zip(cuts, cuts[1:])]
    tail = sums[:, cuts[-1] :]
    far_grads, residual, _ = lax.optimization_barrier((far_grads, residual, of_query))
    expert_grads = own_grads + far_grads.astype(jnp.float32)
    layer_out = (residual + mixture.astype(jnp.float32)).astype(jnp.bfloat16)
    return (
        layer_out,
        in_grad,
        of_query,
        of_key,
        of_value,
        of_output,
        tail[:, :expert_count],
        tail[:, expert_count],
        tail[:, expert_count + 1],
        *[expert_grads[2 * kind : 2 * kind + 2] for kind in range(3)],
    )


def fits_fused(mesh, tokens_shape):
    devices = mesh.shape["dp"] * mesh.shape["expert"]
    return mesh.shape["dp"] == 4 and mesh.shape["expert"] == 8 and tokens_shape[0] == 256 * devices


def solution(mesh):
    placed = (
        P(("dp", "expert"), None),
        P(("dp", "expert"), None),
        P(("dp", "expert"), None),
        P("dp", None),
        P("dp", None),
        P("dp", None),
        P("dp", None),
        P("dp", None),
        P("dp"),
        P("dp"),
        P("expert", None, None),
        P("expert", None, None),
        P("expert", None, None),
        P(("dp", "expert"), None),
    )
    def layer(tokens, *rest):
        return shard(fused_body if fits_fused(mesh, tokens.shape) else body)(tokens, *rest)

    def shard(step):
        return jax.shard_map(
            step,
            mesh=mesh,
            in_specs=placed,
            out_specs=(
                P(("dp", "expert"), None),
                P(("dp", "expert"), None),
                P("dp", None),
                P("dp", None),
                P("dp", None),
                P("dp", None),
                P("dp", None),
                P("dp"),
                P("dp"),
                P("expert", "dp", None),
                P("expert", "dp", None),
                P("expert", "dp", None),
            ),
            check_vma=False,
        )

    return layer
```
